32 devices in a mesh: ctx: 16 (over z, y, x), head: 2 (over core), batch: 1.
Axes of the slice: x: 2, y: 2, z: 4, core: 2. Of those that a mesh axis runs over, the one named last changes fastest.
Arguments:
- queries: bfloat16 [1, 4096, 8, 256], P('batch', 'ctx', 'head'), may hold values from -6 to 6
- keys: bfloat16 [1, 4096, 8, 256], P('batch', 'ctx', 'head'), may hold values from -6 to 6
- values: bfloat16 [1, 4096, 8, 256], P('batch', 'ctx', 'head'), may hold values from -6 to 6
- rates: float32 [1, 8, 4096], P('batch', 'head', 'ctx'), may hold values from 0.25 to 4
- head_scale: float32 [8], P('head'), may hold values from 0.3 to 3
- gain: float32 [8, 256], P('head'), may hold values from 0.25 to 1.75
- w_gate: float32 [8, 256, 256], P('head'), may hold values from -0.375 to 0.375
- w_out: float32 [8, 256, 256], P('head'), may hold values from -0.375 to 0.375
- w_up: float32 [8, 256, 256], P('head'), may hold values from -0.375 to 0.375
- cotangent: bfloat16 [1, 4096, 8, 256], P('batch', 'ctx', 'head'), may hold values from -6 to 6
Outputs:
- grad_q: bfloat16 [1, 4096, 8, 256], P('batch', 'ctx', 'head')
- grad_k: bfloat16 [1, 4096, 8, 256], P('batch', 'ctx', 'head')
- grad_v: bfloat16 [1, 4096, 8, 256], P('batch', 'ctx', 'head')
- grad_gate: float32 [8, 256, 256], P('head', ('ctx', 'batch'))
- grad_out: float32 [8, 256, 256], P('head', ('ctx', 'batch'))
- grad_up: float32 [8, 256, 256], P('head', ('ctx', 'batch'))
The draws below stay inside these ranges and needn't reach their ends.
All inputs are finite; a program needn't handle non-finite values.
Results may differ from the reference program's by a relative error of at most 0.019.
Values sent between devices are 32-bit elements; how exact they have to be, the bound alone decides.
No kernel may reach another device: no remote copies, remote signals or barrier semaphores. Data moves between devices by JAX's collectives and lax.ppermute only.
A program may use at most 64 MiB of HBM per device.

```python
import math
import jax
import jax.numpy as jnp
from jax import lax

DH = 256
FH = 256
HEADS = 8
TOKENS = 4096
BATCH = 1


def levels(own_key, extent, shards, least, largest):
    loudness, own = 1.0, jax.random.fold_in(own_key, 6)
    for dim, shards_of in shards:
        draws = jnp.exp(jax.random.uniform(jax.random.fold_in(own, dim), (shards_of,), jnp.float32, least / len(shards), largest / len(shards)))
        loudness = loudness * jnp.repeat(draws, extent[dim] // shards_of).reshape([-1 if axis == dim else 1 for axis in range(len(extent))])
    return loudness


def scatter_about(rng, dims, width, bound, cuts=(), dtype=jnp.bfloat16):
    result = width * jax.random.normal(rng, dims, jnp.float32)
    if cuts:
        result = result * levels(rng, dims, cuts, -0.22, 0.18)
    return jnp.clip(result, -bound, bound).astype(dtype)


def setup_inputs(seed: int = 0) -> dict:
    splits = jax.random.split(jax.random.key(seed), 11)
    return {
        "queries": scatter_about(splits[0], (BATCH, TOKENS, HEADS, DH), 1.0, 6.0, ((1, 16), (2, 2))),
        "keys": scatter_about(splits[1], (BATCH, TOKENS, HEADS, DH), 1.0, 6.0, ((1, 16), (2, 2))),
        "values": scatter_about(splits[2], (BATCH, TOKENS, HEADS, DH), 1.0, 6.0, ((1, 16), (2, 2))),
        "rates": jnp.clip(jnp.exp(math.log(4.0) - 2.7725887 * jax.random.uniform(splits[3], (BATCH, HEADS, TOKENS), jnp.float32) ** levels(splits[3], (BATCH, HEADS, TOKENS), ((1, 2), (2, 16)), -0.2, 0.2)), 0.25, 4.0),
        "head_scale": jnp.clip(jnp.exp(math.log(3.0) - 2.3025851 * jax.random.uniform(splits[4], (HEADS,), jnp.float32) ** levels(splits[4], (HEADS,), ((0, 2),), -0.2, 0.2)), 0.3, 3.0),
        "gain": jnp.clip(1.0 + 0.15 * jax.random.normal(splits[5], (HEADS, DH), jnp.float32), 0.25, 1.75),
        "w_gate": scatter_about(splits[6], (HEADS, DH, FH), DH ** -0.5, 0.375, ((0, 2),), jnp.float32),
        "w_out": scatter_about(splits[7], (HEADS, FH, DH), FH ** -0.5, 0.375, ((0, 2),), jnp.float32),
        "w_up": scatter_about(splits[8], (HEADS, DH, FH), DH ** -0.5, 0.375, ((0, 2),), jnp.float32),
        "cotangent": scatter_about(splits[9], (BATCH, TOKENS, HEADS, DH), 1.0, 6.0, ((1, 16), (2, 2))),
    }


def silu(x):
    return x * jax.nn.sigmoid(x)

def update_terms(keys, values, rates, w_gate, w_out, w_up, scale):
    gate_b = w_gate.astype(jnp.bfloat16)
    up_b = w_up.astype(jnp.bfloat16)
    out_b = w_out.astype(jnp.bfloat16)
    first = jnp.dot(keys, gate_b, preferred_element_type=jnp.float32)
    third = jnp.dot(keys, up_b, preferred_element_type=jnp.float32)
    sig = jax.nn.sigmoid(first)
    activ = first * sig
    act = (activ * third).astype(jnp.bfloat16)
    scaled = (rates[:, None] * values.astype(jnp.float32)).astype(jnp.bfloat16)
    dact = jnp.dot(scaled, out_b.T, preferred_element_type=jnp.float32)
    deriv = sig * (1.0 + first * (1.0 - sig))
    dfirst = (dact * third * deriv).astype(jnp.bfloat16)
    dthird = (dact * activ).astype(jnp.bfloat16)
    upd_gate = jnp.dot(keys.T, dfirst, preferred_element_type=jnp.float32) * scale
    upd_out = jnp.dot(act.T, scaled, preferred_element_type=jnp.float32) * scale
    upd_up = jnp.dot(keys.T, dthird, preferred_element_type=jnp.float32) * scale
    return (upd_gate, upd_out, upd_up)

def update_back(keys, values, rates, w_gate, w_out, w_up, scale, cots):

    def forward(k_in, v_in, g_in, o_in, u_in):
        return update_terms(k_in, v_in, rates, g_in, o_in, u_in, scale)
    primal, pull = jax.vjp(forward, keys, values, w_gate, w_out, w_up)
    return pull(cots)

def apply_terms(queries, w_gate, w_out, w_up):
    first = jnp.dot(queries, w_gate.astype(jnp.bfloat16), preferred_element_type=jnp.float32)
    third = jnp.dot(queries, w_up.astype(jnp.bfloat16), preferred_element_type=jnp.float32)
    hidden = (silu(first) * third).astype(jnp.bfloat16)
    return jnp.dot(hidden, w_out.astype(jnp.bfloat16), preferred_element_type=jnp.float32)

def apply_back(queries, w_gate, w_out, w_up, dout):
    primal, pull = jax.vjp(apply_terms, queries, w_gate, w_out, w_up)
    return pull(dout)

def norm_back(scaled, dyg, sq, ps, count, head_scale):
    inv = lax.rsqrt(sq / count + 1e-06)
    dos = inv[None, :, None] * dyg - scaled * (inv ** 3 * ps / count)[None, :, None]
    return dos * head_scale[:, None, None]

def reference(queries, keys, values, rates, head_scale, gain, w_gate, w_out, w_up, cotangent):
    scale = 1.0 / math.sqrt(TOKENS * DH)
    count = float(HEADS * DH)
    total_gate = jnp.zeros(w_gate.shape, jnp.float32)
    total_out = jnp.zeros(w_out.shape, jnp.float32)
    total_up = jnp.zeros(w_up.shape, jnp.float32)
    grads_q = []
    grads_k = []
    grads_v = []
    for seq in range(BATCH):
        q_heads = jnp.swapaxes(queries[seq], 0, 1)
        k_heads = jnp.swapaxes(keys[seq], 0, 1)
        v_heads = jnp.swapaxes(values[seq], 0, 1)
        upd = lax.map(lambda a: update_terms(a[0], a[1], a[2], a[3], a[4], a[5], scale), (k_heads, v_heads, rates[seq], w_gate, w_out, w_up))
        new_gate = w_gate + upd[0]
        new_out = w_out + upd[1]
        new_up = w_up + upd[2]
        outs = lax.map(lambda a: apply_terms(a[0], a[1], a[2], a[3]), (q_heads, new_gate, new_out, new_up))
        scaled = outs * head_scale[:, None, None]
        dyg = jnp.swapaxes(cotangent[seq], 0, 1).astype(jnp.float32) * gain[:, None, :]
        sq = lax.optimization_barrier(jnp.sum(scaled * scaled, axis=(0, 2)))
        ps = lax.optimization_barrier(jnp.sum(scaled * dyg, axis=(0, 2)))
        dout = norm_back(scaled, dyg, sq, ps, count, head_scale)
        dq, p_gate, p_out, p_up = lax.map(lambda a: apply_back(a[0], a[1], a[2], a[3], a[4]), (q_heads, new_gate, new_out, new_up, dout))
        dk, dv, e_gate, e_out, e_up = lax.map(lambda a: update_back(a[0], a[1], a[2], a[3], a[4], a[5], scale, (a[6], a[7], a[8])), (k_heads, v_heads, rates[seq], w_gate, w_out, w_up, p_gate, p_out, p_up))
        total_gate = total_gate + (p_gate + e_gate)
        total_out = total_out + (p_out + e_out)
        total_up = total_up + (p_up + e_up)
        grads_q.append(jnp.swapaxes(dq, 0, 1))
        grads_k.append(jnp.swapaxes(dk, 0, 1))
        grads_v.append(jnp.swapaxes(dv, 0, 1))
    return (jnp.stack(grads_q), jnp.stack(grads_k), jnp.stack(grads_v), total_gate, total_out, total_up)
```

```python
import functools
import math

import jax
import jax.numpy as jnp
from jax import lax
from jax.experimental import pallas as pl
from jax.experimental.pallas import tpu as pltpu
from jax.sharding import PartitionSpec as P

F32 = jnp.float32
BF16 = jnp.bfloat16
LANES = 128
VMEM_LIMIT = 40 * 1024 * 1024


def mm(a, b):
    return jnp.dot(a, b, preferred_element_type=F32)


def mm_t(a, b):
    return lax.dot_general(a, b, (((1,), (1,)), ((), ())), preferred_element_type=F32)


def tmm(a, b):
    return lax.dot_general(a, b, (((0,), (0,)), ((), ())), preferred_element_type=F32)


def call(body, out_shape, scratch, flops, *args):
    smem = pl.BlockSpec(memory_space=pltpu.SMEM)
    vmem = pl.BlockSpec(memory_space=pltpu.VMEM)
    size = sum(a.size * a.dtype.itemsize for a in args)
    size += sum(math.prod(o.shape) * o.dtype.itemsize for o in out_shape)
    return pl.pallas_call(
        body,
        out_shape=out_shape,
        in_specs=[smem] + [vmem] * (len(args) - 1),
        out_specs=[vmem] * len(out_shape),
        scratch_shapes=scratch,
        compiler_params=pltpu.CompilerParams(vmem_limit_bytes=VMEM_LIMIT),
        cost_estimate=pl.CostEstimate(flops=flops, bytes_accessed=size, transcendentals=0),
    )(*args)


def put_rows(scratch, x):
    for i in range(scratch.shape[0]):
        scratch[i] = x[:, i * LANES : (i + 1) * LANES]


def take_head(scratch, head, tokens, heads):
    parts = [scratch[i, pl.ds(head, tokens, stride=heads), :] for i in range(scratch.shape[0])]
    return jnp.concatenate(parts, axis=1)


def put_head(scratch, head, x, tokens, heads):
    for i in range(scratch.shape[0]):
        scratch[i, pl.ds(head, tokens, stride=heads), :] = x[:, i * LANES : (i + 1) * LANES]


def rows_of(scratch):
    return jnp.concatenate([scratch[i] for i in range(scratch.shape[0])], axis=1)


def partner(own, step, count):
    if count & (count - 1) == 0:
        return own ^ step
    return lax.rem(step + count - own, count)


def split_update(groups, place, k, v, r, *rest):
    outs, (sk, sv) = rest[:groups], rest[groups:]
    tokens, heads, width = k.shape
    put_rows(sk, k[...].astype(F32).reshape(tokens * heads, width))
    put_rows(sv, v[...].astype(F32).reshape(tokens * heads, width))
    for step in range(groups):
        head = partner(place[0], step, groups)
        outs[step][0] = take_head(sk, head, tokens, heads)
        rate = jnp.broadcast_to(r[pl.ds(head, 1), :], (8, tokens)).T[:, 0:1]
        scaled = take_head(sv, head, tokens, heads) * rate
        outs[step][1] = scaled.astype(BF16).astype(F32)


def split_apply(groups, place, q, cot, gain, *rest):
    outs, (sq, sc) = rest[:groups], rest[groups:]
    tokens, heads, width = q.shape
    put_rows(sq, q[...].astype(F32).reshape(tokens * heads, width))
    put_rows(sc, cot[...].astype(F32).reshape(tokens * heads, width))
    for step in range(groups):
        head = partner(place[0], step, groups)
        outs[step][0] = take_head(sq, head, tokens, heads)
        outs[step][1] = take_head(sc, head, tokens, heads) * gain[pl.ds(head, 1), :]


def send_slices(sums, outs, index, count):
    rows = sums.shape[1] // count
    for step in range(count):
        at = pl.multiple_of(partner(index, step, count) * rows, rows)
        outs[step][...] = sums[:, pl.ds(at, rows), :]


def update_kernel(groups, depth, scale, place, *refs):
    pieces = refs[:groups]
    w_gate, w_out, w_up = refs[groups : groups + 3]
    outs = refs[groups + 3 : groups + 3 + depth]
    sums = refs[groups + 3 + depth]
    gate_b, out_b, up_b = (w[...].astype(BF16) for w in (w_gate, w_out, w_up))
    total = [0.0, 0.0, 0.0]
    for piece in pieces:
        keys = piece[0].astype(BF16)
        scaled = piece[1].astype(BF16)
        first = mm(keys, gate_b)
        third = mm(keys, up_b)
        sig = jax.nn.sigmoid(first)
        activ = first * sig
        act = (activ * third).astype(BF16)
        dact = mm_t(scaled, out_b)
        deriv = sig * (1.0 + first * (1.0 - sig))
        dfirst = (dact * third * deriv).astype(BF16)
        dthird = (dact * activ).astype(BF16)
        total[0] += tmm(keys, dfirst)
        total[1] += tmm(act, scaled)
        total[2] += tmm(keys, dthird)
    for i in range(3):
        sums[i] = total[i] * scale
    send_slices(sums, outs, place[1], depth)
    rows = sums.shape[1] // depth
    at = pl.multiple_of(place[1] * rows, rows)
    for i, w in enumerate((w_gate, w_out, w_up)):
        outs[0][i] += w[pl.ds(at, rows), :]


def assemble(place, parts, whole):
    rows = parts[0].shape[1]
    for step, part in enumerate(parts):
        at = pl.multiple_of(partner(place[1], step, len(parts)) * rows, rows)
        whole[:, pl.ds(at, rows), :] = part[...]


def apply_kernel(groups, depth, place, head_scale, *refs):
    pieces = refs[:groups]
    parts = refs[groups : groups + depth]
    first_ref, third_ref, os_ref, stats, new_b = refs[groups + depth : groups + depth + 5]
    whole = refs[groups + depth + 5]
    assemble(place, parts, whole)
    new_b[...] = whole[...].astype(BF16)
    hs = head_scale[...]
    for step, piece in enumerate(pieces):
        tokens = piece.shape[1]
        queries = piece[0].astype(BF16)
        dyg = piece[1]
        first = mm(queries, new_b[0])
        third = mm(queries, new_b[2])
        hidden = (first * jax.nn.sigmoid(first) * third).astype(BF16)
        scaled = mm(hidden, new_b[1]) * hs
        first_ref[step] = first
        third_ref[step] = third
        os_ref[step] = scaled
        sq = jnp.sum(scaled * scaled, axis=1, keepdims=True)
        ps = jnp.sum(scaled * dyg, axis=1, keepdims=True)
        lane = lax.broadcasted_iota(jnp.int32, (tokens, LANES), 1)
        both = jnp.where(lane == 0, sq, jnp.where(lane == 1, ps, 0.0))
        stats[partner(place[0], step, groups)] = both.T[0:8, :]


def apply_back_kernel(groups, depth, count, place, head_scale, stats, *refs):
    pieces = refs[:groups]
    first_ref, third_ref, os_ref, new_b = refs[groups : groups + 4]
    outs = refs[groups + 4 : groups + 4 + groups]
    slices = refs[groups + 4 + groups : groups + 4 + groups + depth]
    sums = refs[groups + 4 + groups + depth]
    hs = head_scale[...]
    total = [0.0, 0.0, 0.0]
    for step, piece in enumerate(pieces):
        queries = piece[0].astype(BF16)
        dyg = piece[1]
        both = stats[partner(place[0], step, groups)].T
        sq = both[:, 0:1]
        ps = both[:, 1:2]
        inv = lax.rsqrt(sq / count + 1e-06)
        scaled = os_ref[step]
        dos = inv * dyg - scaled * (inv * inv * inv * ps / count)
        dout = (dos * hs).astype(BF16)
        first = first_ref[step]
        third = third_ref[step]
        sig = jax.nn.sigmoid(first)
        activ = first * sig
        hidden = (activ * third).astype(BF16)
        dhidden = mm_t(dout, new_b[1])
        dthird = (dhidden * activ).astype(BF16)
        dfirst = (dhidden * third * (sig * (1.0 + first * (1.0 - sig)))).astype(BF16)
        outs[step][...] = mm_t(dfirst, new_b[0]) + mm_t(dthird, new_b[2])
        total[0] += tmm(queries, dfirst)
        total[1] += tmm(hidden, dout)
        total[2] += tmm(queries, dthird)
    for i in range(3):
        sums[i] = total[i]
    send_slices(sums, slices, place[1], depth)


def update_back_kernel(groups, depth, scale, place, *refs):
    pieces = refs[:groups]
    parts = refs[groups : groups + depth]
    w_gate, w_out, w_up = refs[groups + depth : groups + depth + 3]
    base = groups + depth + 3
    outs = refs[base : base + groups]
    slices = refs[base + groups : base + groups + depth]
    whole, sums = refs[base + groups + depth :]
    assemble(place, parts, whole)
    gate_b, out_b, up_b = (w[...].astype(BF16) for w in (w_gate, w_out, w_up))
    cot_gate, cot_out, cot_up = ((whole[i] * scale).astype(BF16) for i in range(3))
    total = [0.0, 0.0, 0.0]
    for step, piece in enumerate(pieces):
        keys = piece[0].astype(BF16)
        scaled = piece[1].astype(BF16)
        first = mm(keys, gate_b)
        third = mm(keys, up_b)
        sig = jax.nn.sigmoid(first)
        activ = first * sig
        act = (activ * third).astype(BF16)
        dact = mm_t(scaled, out_b)
        slope = sig * (1.0 - sig)
        deriv = sig + first * slope
        second = slope * (2.0 + first * (1.0 - 2.0 * sig))
        third_deriv = third * deriv
        dfirst = (dact * third_deriv).astype(BF16)
        dthird = (dact * activ).astype(BF16)
        bar_dfirst = mm(keys, cot_gate)
        bar_dthird = mm(keys, cot_up)
        bar_act = mm_t(scaled, cot_out)
        bar_activ = bar_dthird * dact + bar_act * third
        bar_dact = (bar_dfirst * third_deriv + bar_dthird * activ).astype(BF16)
        bar_df_dact = bar_dfirst * dact
        bar_third = (bar_df_dact * deriv + bar_act * activ).astype(BF16)
        bar_first = (bar_activ * deriv + bar_df_dact * third * second).astype(BF16)
        outs[step][0] = (
            mm_t(dfirst, cot_gate)
            + mm_t(dthird, cot_up)
            + mm_t(bar_first, gate_b)
            + mm_t(bar_third, up_b)
        )
        outs[step][1] = mm(act, cot_out) + mm(bar_dact, out_b)
        total[0] += tmm(keys, bar_first)
        total[1] += tmm(bar_dact, scaled)
        total[2] += tmm(keys, bar_third)
    for i in range(3):
        sums[i] = total[i]
    send_slices(sums, slices, place[1], depth)


def join_query_kernel(groups, place, *refs):
    pieces, out, scratch = refs[:groups], refs[groups], refs[groups + 1]
    tokens, heads, width = out.shape
    for step, piece in enumerate(pieces):
        put_head(scratch, partner(place[0], step, groups), piece[...], tokens, heads)
    out[...] = rows_of(scratch).reshape(tokens, heads, width).astype(BF16)


def join_update_kernel(groups, place, r, *refs):
    pieces = refs[:groups]
    out_k, out_v, sk, sv = refs[groups:]
    tokens, heads, width = out_k.shape
    for step, piece in enumerate(pieces):
        head = partner(place[0], step, groups)
        put_head(sk, head, piece[0], tokens, heads)
        rate = jnp.broadcast_to(r[pl.ds(head, 1), :], (8, tokens)).T[:, 0:1]
        put_head(sv, head, piece[1] * rate, tokens, heads)
    out_k[...] = rows_of(sk).reshape(tokens, heads, width).astype(BF16)
    out_v[...] = rows_of(sv).reshape(tokens, heads, width).astype(BF16)


def rows_kernel(groups, place, *refs):
    parts, outs, total = refs[: -groups - 1], refs[-groups - 1 : -1], refs[-1]
    whole = parts[0][...]
    for part in parts[1:]:
        whole += part[...]
    total[...] = whole
    send_slices(total, outs, place[0], groups)


def join_rows_kernel(groups, place, *refs):
    parts, outs = refs[:groups], refs[groups:]
    for step, part in enumerate(parts):
        for i in range(3):
            outs[i][partner(place[0], step, groups)] = part[i]


def local(queries, keys, values, rates, head_scale, gain, w_gate, w_out, w_up, cotangent):
    tokens, heads, width = keys.shape[1:]
    hidden = w_gate.shape[2]
    ctx = lax.axis_size("ctx")
    head_axis = lax.axis_size("head")
    groups = heads
    depth = ctx // groups
    scale = 1.0 / math.sqrt(tokens * ctx * width)
    count = float(heads * head_axis * width)
    me = lax.axis_index("ctx")
    mine, layer = lax.rem(me, groups), lax.div(me, groups)
    place = jnp.stack([mine, layer]).astype(jnp.int32)

    def in_plane(x, step):
        perm = [
            (c, c // groups * groups + int(partner_of(c % groups, step, groups)))
            for c in range(ctx)
        ]
        return lax.ppermute(x, "ctx", perm)

    def in_column(x, step):
        perm = [
            (c, int(partner_of(c // groups, step, depth)) * groups + c % groups)
            for c in range(ctx)
        ]
        return lax.ppermute(x, "ctx", perm)

    def exchange(parts, move):
        return [parts[0]] + [move(p, step) for step, p in enumerate(parts) if step]

    def spread(part):
        return [part] + [in_column(part, step) for step in range(1, depth)]

    def shape(dims, dtype=F32):
        return jax.ShapeDtypeStruct(dims, dtype)

    flops = 2 * groups * tokens * width * hidden
    pair = [shape((2, tokens, width))] * groups
    slices = [shape((3, hidden // depth, width))] * depth
    scratch = pltpu.VMEM((width // LANES, tokens * heads, LANES), F32)
    square = pltpu.VMEM((3, hidden, width), F32)

    sent = call(
        functools.partial(split_update, groups), pair, [scratch] * 2, flops // 8,
        place, keys[0], values[0], rates[0],
    )
    pieces = exchange(sent, in_plane)
    own = [lax.dynamic_index_in_dim(w, mine, 0, keepdims=False) for w in (w_gate, w_out, w_up)]
    own_scale = lax.dynamic_index_in_dim(head_scale, mine, 0, keepdims=True)[None, :]
    pieces, queries, cotangent = lax.optimization_barrier((pieces, queries, cotangent))
    terms = call(
        functools.partial(update_kernel, groups, depth, scale), slices, [square], 6 * flops,
        place, *pieces, *own,
    )
    terms = exchange(terms, in_column)
    sent = call(
        functools.partial(split_apply, groups), pair, [scratch] * 2, flops // 8,
        place, queries[0], cotangent[0], gain,
    )
    q_pieces = exchange(sent, in_plane)
    new = spread(functools.reduce(jnp.add, terms))
    kept = shape((groups, tokens, width))
    first, third, scaled, stats, new_b = call(
        functools.partial(apply_kernel, groups, depth),
        [kept, kept, kept, shape((groups, 8, tokens)), shape((3, hidden, width), BF16)],
        [square], 3 * flops, place, own_scale, *q_pieces, *new,
    )
    block = groups * head_axis
    sets = [list(range(i, i + block)) for i in range(0, ctx * head_axis, block)]
    stats = lax.psum(stats, ("ctx", "head"), axis_index_groups=sets)
    out = call(
        functools.partial(apply_back_kernel, groups, depth, count),
        [shape((tokens, width))] * groups + slices, [square], 6 * flops,
        place, own_scale, stats, *q_pieces, first, third, scaled, new_b,
    )
    parts = exchange(out[groups:], in_column)
    part_sum = functools.reduce(jnp.add, parts)
    whole = spread(part_sum)
    q_back = exchange(out[:groups], in_plane)
    (grad_q,) = call(
        functools.partial(join_query_kernel, groups), [shape((tokens, heads, width), BF16)],
        [scratch], flops // 16, place, *q_back,
    )
    out = call(
        functools.partial(update_back_kernel, groups, depth, scale), pair + slices, [square] * 2,
        15 * flops, place, *pieces, *whole, *own,
    )
    ends = exchange(out[groups:], in_column)
    rows = hidden // ctx
    sent = call(
        functools.partial(rows_kernel, groups), [shape((3, rows, width))] * groups,
        [pltpu.VMEM((3, hidden // depth, width), F32)], flops // 100, place, part_sum, *ends,
    )
    back = exchange(out[:groups], in_plane)
    grad_k, grad_v = call(
        functools.partial(join_update_kernel, groups),
        [shape((tokens, heads, width), BF16)] * 2, [scratch] * 2, flops // 8,
        place, rates[0], *back,
    )
    grads = call(
        functools.partial(join_rows_kernel, groups), [shape((heads, rows, width))] * 3, [],
        flops // 100, place, *exchange(sent, in_plane),
    )
    if lax.axis_size("batch") > 1:
        grads = [lax.psum_scatter(x, "batch", scatter_dimension=1, tiled=True) for x in grads]
    return (grad_q[None], grad_k[None], grad_v[None], grads[0], grads[1], grads[2])


def partner_of(own, step, count):
    if count & (count - 1) == 0:
        return own ^ step
    return (step + count - own) % count


def solution(mesh):
    in_specs = (
        P("batch", "ctx", "head", None),
        P("batch", "ctx", "head", None),
        P("batch", "ctx", "head", None),
        P("batch", "head", "ctx"),
        P("head"),
        P("head", None),
        P("head", None, None),
        P("head", None, None),
        P("head", None, None),
        P("batch", "ctx", "head", None),
    )
    out_specs = (
        P("batch", "ctx", "head", None),
        P("batch", "ctx", "head", None),
        P("batch", "ctx", "head", None),
        P("head", ("ctx", "batch"), None),
        P("head", ("ctx", "batch"), None),
        P("head", ("ctx", "batch"), None),
    )
    return jax.shard_map(local, mesh=mesh, in_specs=in_specs, out_specs=out_specs, check_vma=False)
```

```python
import functools
import math

import jax
import jax.numpy as jnp
from jax import lax
from jax.experimental import pallas as pl
from jax.experimental.pallas import tpu as pltpu
from jax.sharding import PartitionSpec as P

F32 = jnp.float32
BF16 = jnp.bfloat16
LANES = 128
VMEM_LIMIT = 40 * 1024 * 1024


def mm(a, b):
    return jnp.dot(a, b, preferred_element_type=F32)


def mm_t(a, b):
    return lax.dot_general(a, b, (((1,), (1,)), ((), ())), preferred_element_type=F32)


def tmm(a, b):
    return lax.dot_general(a, b, (((0,), (0,)), ((), ())), preferred_element_type=F32)


def call(body, out_shape, scratch, flops, *args):
    smem = pl.BlockSpec(memory_space=pltpu.SMEM)
    vmem = pl.BlockSpec(memory_space=pltpu.VMEM)
    size = sum(a.size * a.dtype.itemsize for a in args)
    size += sum(math.prod(o.shape) * o.dtype.itemsize for o in out_shape)
    return pl.pallas_call(
        body,
        out_shape=out_shape,
        in_specs=[smem if a.dtype == jnp.int32 else vmem for a in args],
        out_specs=[vmem] * len(out_shape),
        scratch_shapes=scratch,
        compiler_params=pltpu.CompilerParams(vmem_limit_bytes=VMEM_LIMIT),
        cost_estimate=pl.CostEstimate(flops=flops, bytes_accessed=size, transcendentals=0),
    )(*args)


def put_rows(scratch, x):
    for i in range(scratch.shape[0]):
        scratch[i] = x[:, i * LANES : (i + 1) * LANES]


def take_head(scratch, head, tokens, heads):
    parts = [scratch[i, pl.ds(head, tokens, stride=heads), :] for i in range(scratch.shape[0])]
    return jnp.concatenate(parts, axis=1)


def put_head(scratch, head, x, tokens, heads):
    for i in range(scratch.shape[0]):
        scratch[i, pl.ds(head, tokens, stride=heads), :] = x[:, i * LANES : (i + 1) * LANES]


def rows_of(scratch):
    return jnp.concatenate([scratch[i] for i in range(scratch.shape[0])], axis=1)


def split_update(k, v, r, out, sk, sv):
    tokens, heads, width = k.shape
    put_rows(sk, k[...].astype(F32).reshape(tokens * heads, width))
    put_rows(sv, v[...].astype(F32).reshape(tokens * heads, width))
    for head in range(heads):
        out[head, 0] = take_head(sk, head, tokens, heads)
        scaled = take_head(sv, head, tokens, heads) * rate_column(r, head)
        out[head, 1] = scaled.astype(BF16).astype(F32)


def rate_column(r, head):
    return jnp.broadcast_to(r[head : head + 1, :], (8, r.shape[1])).T[:, 0:1]


def split_apply(groups, place, q, cot, gain, *rest):
    outs, (sq, sc) = rest[:groups], rest[groups:]
    tokens, heads, width = q.shape
    put_rows(sq, q[...].astype(F32).reshape(tokens * heads, width))
    put_rows(sc, cot[...].astype(F32).reshape(tokens * heads, width))
    for step in range(groups):
        head = place[0] ^ step
        outs[step][0] = take_head(sq, head, tokens, heads)
        outs[step][1] = take_head(sc, head, tokens, heads) * gain[pl.ds(head, 1), :]


def cut(total, i, out):
    rows = out.shape[2]
    for z in range(out.shape[0]):
        out[z, i] = total[z * rows : (z + 1) * rows]


def update_kernel(scale, place, pieces, w_gate, w_out, w_up, out):
    weights = (w_gate, w_out, w_up)
    gate_b, out_b, up_b = (w[...].astype(BF16) for w in weights)
    total = [0.0, 0.0, 0.0]
    for source in range(pieces.shape[0]):
        keys = pieces[source, 0].astype(BF16)
        scaled = pieces[source, 1].astype(BF16)
        first = mm(keys, gate_b)
        third = mm(keys, up_b)
        sig = jax.nn.sigmoid(first)
        activ = first * sig
        act = (activ * third).astype(BF16)
        dact = mm_t(scaled, out_b)
        deriv = sig * (1.0 + first * (1.0 - sig))
        dfirst = (dact * third * deriv).astype(BF16)
        dthird = (dact * activ).astype(BF16)
        total[0] += tmm(keys, dfirst)
        total[1] += tmm(act, scaled)
        total[2] += tmm(keys, dthird)
    rows = out.shape[2]
    at = pl.multiple_of(place[1] * rows, rows)
    for i in range(3):
        cut(total[i] * scale, i, out)
        out[place[1], i] += weights[i][pl.ds(at, rows), :]


def sum_spread_kernel(parts, out):
    total = parts[0]
    for z in range(1, parts.shape[0]):
        total += parts[z]
    for z in range(parts.shape[0]):
        out[z] = total


def whole(parts, i):
    return jnp.concatenate([parts[z, i] for z in range(parts.shape[0])], axis=0)


def apply_forward(queries, new_b):
    first = mm(queries, new_b[0])
    third = mm(queries, new_b[2])
    sig = jax.nn.sigmoid(first)
    activ = first * sig
    hidden = (activ * third).astype(BF16)
    return first, third, sig, activ, hidden


def apply_kernel(groups, place, head_scale, parts, *refs):
    pieces, out = refs[:groups], refs[groups]
    new_b = [whole(parts, i).astype(BF16) for i in range(3)]
    for step, piece in enumerate(pieces):
        tokens = piece.shape[1]
        hidden = apply_forward(piece[0].astype(BF16), new_b)[4]
        scaled = mm(hidden, new_b[1]) * head_scale[...]
        sq = jnp.sum(scaled * scaled, axis=1, keepdims=True)
        ps = jnp.sum(scaled * piece[1], axis=1, keepdims=True)
        lane = lax.broadcasted_iota(jnp.int32, (tokens, LANES), 1)
        both = jnp.where(lane == 0, sq, jnp.where(lane == 1, ps, 0.0)).T[0:8, :]
        for copy in range(out.shape[0]):
            out[copy, place[0] ^ step] = both


def apply_back_kernel(groups, count, place, head_scale, parts, stats, *refs):
    pieces, outs, slices = refs[:groups], refs[groups : 2 * groups], refs[2 * groups]
    new_b = [whole(parts, i).astype(BF16) for i in range(3)]
    hs = head_scale[...]
    total = [0.0, 0.0, 0.0]
    for step, piece in enumerate(pieces):
        source = place[0] ^ step
        both = stats[0, source]
        for device in range(1, stats.shape[0]):
            both += stats[device, source]
        both = both.T
        sq = both[:, 0:1]
        ps = both[:, 1:2]
        inv = lax.rsqrt(sq / count + 1e-06)
        queries = piece[0].astype(BF16)
        first, third, sig, activ, hidden = apply_forward(queries, new_b)
        scaled = mm(hidden, new_b[1]) * hs
        dos = inv * piece[1] - scaled * (inv * inv * inv * ps / count)
        dout = (dos * hs).astype(BF16)
        dhidden = mm_t(dout, new_b[1])
        dthird = (dhidden * activ).astype(BF16)
        dfirst = (dhidden * third * (sig * (1.0 + first * (1.0 - sig)))).astype(BF16)
        outs[step][...] = mm_t(dfirst, new_b[0]) + mm_t(dthird, new_b[2])
        total[0] += tmm(queries, dfirst)
        total[1] += tmm(hidden, dout)
        total[2] += tmm(queries, dthird)
    for i in range(3):
        cut(total[i], i, slices)


def update_back_kernel(groups, scale, place, pieces, parts, w_gate, w_out, w_up, *rest):
    outs, slices = rest[:groups], rest[groups]
    gate_b, out_b, up_b = (w[...].astype(BF16) for w in (w_gate, w_out, w_up))
    cot_gate, cot_out, cot_up = ((whole(parts, i) * scale).astype(BF16) for i in range(3))
    total = [0.0, 0.0, 0.0]
    for step, out in enumerate(outs):
        source = place[0] ^ step
        keys = pieces[source, 0].astype(BF16)
        scaled = pieces[source, 1].astype(BF16)
        first = mm(keys, gate_b)
        third = mm(keys, up_b)
        sig = jax.nn.sigmoid(first)
        activ = first * sig
        act = (activ * third).astype(BF16)
        dact = mm_t(scaled, out_b)
        slope = sig * (1.0 - sig)
        deriv = sig + first * slope
        second = slope * (2.0 + first * (1.0 - 2.0 * sig))
        third_deriv = third * deriv
        dfirst = (dact * third_deriv).astype(BF16)
        dthird = (dact * activ).astype(BF16)
        bar_dfirst = mm(keys, cot_gate)
        bar_dthird = mm(keys, cot_up)
        bar_act = mm_t(scaled, cot_out)
        bar_activ = bar_dthird * dact + bar_act * third
        bar_dact = (bar_dfirst * third_deriv + bar_dthird * activ).astype(BF16)
        bar_df_dact = bar_dfirst * dact
        bar_third = (bar_df_dact * deriv + bar_act * activ).astype(BF16)
        bar_first = (bar_activ * deriv + bar_df_dact * third * second).astype(BF16)
        out[0] = (
            mm_t(dfirst, cot_gate)
            + mm_t(dthird, cot_up)
            + mm_t(bar_first, gate_b)
            + mm_t(bar_third, up_b)
        )
        out[1] = mm(act, cot_out) + mm(bar_dact, out_b)
        total[0] += tmm(keys, bar_first)
        total[1] += tmm(bar_dact, scaled)
        total[2] += tmm(keys, bar_third)
    for i in range(3):
        cut(total[i], i, slices)


def join_query_kernel(groups, place, *refs):
    pieces, out, scratch = refs[:groups], refs[groups], refs[groups + 1]
    tokens, heads, width = out.shape
    for step, piece in enumerate(pieces):
        put_head(scratch, place[0] ^ step, piece[...], tokens, heads)
    out[...] = rows_of(scratch).reshape(tokens, heads, width).astype(BF16)


def join_update_kernel(groups, place, r, *refs):
    pieces, (out_k, out_v, sk, sv) = refs[:groups], refs[groups:]
    tokens, heads, width = out_k.shape
    for step, piece in enumerate(pieces):
        head = place[0] ^ step
        rate = jnp.broadcast_to(r[pl.ds(head, 1), :], (8, tokens)).T[:, 0:1]
        put_head(sk, head, piece[0], tokens, heads)
        put_head(sv, head, piece[1] * rate, tokens, heads)
    out_k[...] = rows_of(sk).reshape(tokens, heads, width).astype(BF16)
    out_v[...] = rows_of(sv).reshape(tokens, heads, width).astype(BF16)


def rows_kernel(place, first, second, out):
    total = first[place[1]]
    for z in range(second.shape[0]):
        total += second[z]
    rows = out.shape[2]
    for group in range(out.shape[0]):
        out[group] = total[:, group * rows : (group + 1) * rows]


def local(queries, keys, values, rates, head_scale, gain, w_gate, w_out, w_up, cotangent):
    tokens, heads, width = keys.shape[1:]
    hidden = w_gate.shape[2]
    ctx = lax.axis_size("ctx")
    head_axis = lax.axis_size("head")
    groups = heads
    depth = ctx // groups
    assert groups & (groups - 1) == 0 and depth * groups == ctx
    scale = 1.0 / math.sqrt(tokens * ctx * width)
    count = float(heads * head_axis * width)
    me = lax.axis_index("ctx")
    mine, layer = lax.rem(me, groups), lax.div(me, groups)
    place = jnp.stack([mine, layer]).astype(jnp.int32)
    planes = [[z * groups + p for p in range(groups)] for z in range(depth)]
    columns = [[z * groups + p for z in range(depth)] for p in range(groups)]
    block = groups * head_axis
    planes_heads = [list(range(i, i + block)) for i in range(0, ctx * head_axis, block)]

    def swap(x, axes, sets):
        return lax.all_to_all(x, axes, 0, 0, axis_index_groups=sets, tiled=True)

    def in_plane(x, step):
        return lax.ppermute(x, "ctx", [(c, c ^ step) for c in range(ctx)])

    def exchange(parts):
        return [parts[0]] + [in_plane(p, step) for step, p in enumerate(parts) if step]

    def shape(*dims, dtype=F32):
        return jax.ShapeDtypeStruct(dims, dtype)

    flops = 2 * groups * tokens * width * hidden
    pieces_shape = shape(groups, 2, tokens, width)
    slices = shape(depth, 3, hidden // depth, width)
    scratch = pltpu.VMEM((width // LANES, tokens * heads, LANES), F32)

    (sent,) = call(
        split_update, [pieces_shape], [scratch] * 2, flops // 8, keys[0], values[0], rates[0]
    )
    pieces = swap(sent, "ctx", planes)
    own = [lax.dynamic_index_in_dim(w, mine, 0, keepdims=False) for w in (w_gate, w_out, w_up)]
    own_scale = lax.dynamic_index_in_dim(head_scale, mine, 0, keepdims=True)[None, :]
    pieces, queries, cotangent = lax.optimization_barrier((pieces, queries, cotangent))
    sent = call(
        functools.partial(split_apply, groups), [shape(2, tokens, width)] * groups,
        [scratch] * 2, flops // 8, place, queries[0], cotangent[0], gain,
    )
    q_pieces = exchange(sent)
    (terms,) = call(
        functools.partial(update_kernel, scale), [slices], [], 6 * flops, place, pieces, *own
    )
    terms = swap(terms, "ctx", columns)
    new = swap(call(sum_spread_kernel, [slices], [], flops // 100, terms)[0], "ctx", columns)
    (stats,) = call(
        functools.partial(apply_kernel, groups), [shape(block, groups, 8, tokens)], [],
        3 * flops, place, own_scale, new, *q_pieces,
    )
    stats = swap(stats, ("ctx", "head"), planes_heads)
    out = call(
        functools.partial(apply_back_kernel, groups, count),
        [shape(tokens, width)] * groups + [slices], [], 9 * flops,
        place, own_scale, new, stats, *q_pieces,
    )
    q_back = exchange(out[:groups])
    parts = swap(out[groups], "ctx", columns)
    parts = swap(call(sum_spread_kernel, [slices], [], flops // 100, parts)[0], "ctx", columns)
    (grad_q,) = call(
        functools.partial(join_query_kernel, groups),
        [shape(tokens, heads, width, dtype=BF16)], [scratch], flops // 16, place, *q_back,
    )
    out = call(
        functools.partial(update_back_kernel, groups, scale),
        [shape(2, tokens, width)] * groups + [slices], [], 15 * flops, place, pieces, parts, *own,
    )
    back = exchange(out[:groups])
    ends = swap(out[groups], "ctx", columns)
    rows = hidden // ctx
    (sent,) = call(
        rows_kernel, [shape(groups, 3, rows, width)], [], flops // 100, place, parts, ends
    )
    grads = swap(sent, "ctx", planes)
    grad_k, grad_v = call(
        functools.partial(join_update_kernel, groups),
        [shape(tokens, heads, width, dtype=BF16)] * 2, [scratch] * 2, flops // 8,
        place, rates[0], *back,
    )
    grads = [grads[:, i] for i in range(3)]
    if lax.axis_size("batch") > 1:
        grads = [lax.psum_scatter(x, "batch", scatter_dimension=1, tiled=True) for x in grads]
    return (grad_q[None], grad_k[None], grad_v[None], grads[0], grads[1], grads[2])


def solution(mesh):
    in_specs = (
        P("batch", "ctx", "head", None),
        P("batch", "ctx", "head", None),
        P("batch", "ctx", "head", None),
        P("batch", "head", "ctx"),
        P("head"),
        P("head", None),
        P("head", None, None),
        P("head", None, None),
        P("head", None, None),
        P("batch", "ctx", "head", None),
    )
    out_specs = (
        P("batch", "ctx", "head", None),
        P("batch", "ctx", "head", None),
        P("batch", "ctx", "head", None),
        P("head", ("ctx", "batch"), None),
        P("head", ("ctx", "batch"), None),
        P("head", ("ctx", "batch"), None),
    )
    return jax.shard_map(local, mesh=mesh, in_specs=in_specs, out_specs=out_specs, check_vma=False)
```

```python
import functools
import math

import jax
import jax.numpy as jnp
from jax import lax
from jax.experimental import pallas as pl
from jax.experimental.pallas import tpu as pltpu
from jax.sharding import PartitionSpec as P

F32 = jnp.float32
BF16 = jnp.bfloat16
LANES = 128
VMEM_LIMIT = 40 * 1024 * 1024


def mm(a, b):
    return jnp.dot(a, b, preferred_element_type=F32)


def mm_t(a, b):
    return lax.dot_general(a, b, (((1,), (1,)), ((), ())), preferred_element_type=F32)


def tmm(a, b):
    return lax.dot_general(a, b, (((0,), (0,)), ((), ())), preferred_element_type=F32)


def call(body, out_shape, scratch, flops, *args):
    smem = pl.BlockSpec(memory_space=pltpu.SMEM)
    vmem = pl.BlockSpec(memory_space=pltpu.VMEM)
    size = sum(a.size * a.dtype.itemsize for a in args)
    size += sum(math.prod(o.shape) * o.dtype.itemsize for o in out_shape)
    return pl.pallas_call(
        body,
        out_shape=out_shape,
        in_specs=[smem if a.dtype == jnp.int32 else vmem for a in args],
        out_specs=[vmem] * len(out_shape),
        scratch_shapes=scratch,
        compiler_params=pltpu.CompilerParams(vmem_limit_bytes=VMEM_LIMIT),
        cost_estimate=pl.CostEstimate(flops=flops, bytes_accessed=size, transcendentals=0),
    )(*args)


def put_rows(scratch, x):
    for i in range(scratch.shape[0]):
        scratch[i] = x[:, i * LANES : (i + 1) * LANES]


def take_head(scratch, head, tokens, heads):
    parts = [scratch[i, pl.ds(head, tokens, stride=heads), :] for i in range(scratch.shape[0])]
    return jnp.concatenate(parts, axis=1)


def put_head(scratch, head, x, tokens, heads):
    for i in range(scratch.shape[0]):
        scratch[i, pl.ds(head, tokens, stride=heads), :] = x[:, i * LANES : (i + 1) * LANES]


def rows_of(scratch):
    return jnp.concatenate([scratch[i] for i in range(scratch.shape[0])], axis=1)


def split_kernel(groups, place, x, *rest):
    outs, scratch = rest[:groups], rest[groups]
    tokens, heads, width = x.shape
    put_rows(scratch, x[...].astype(F32).reshape(tokens * heads, width))
    for step in range(groups):
        outs[step][...] = take_head(scratch, place[0] ^ step, tokens, heads)


def split_scaled_kernel(groups, place, x, r, *rest):
    outs = rest[:groups]
    split_kernel(groups, place, x, *rest)
    for step in range(groups):
        scaled = outs[step][...] * rate_column(r, place[0] ^ step)
        outs[step][...] = scaled.astype(BF16).astype(F32)


def split_apply_kernel(groups, place, q, cot, gain, *rest):
    outs, scratch = rest[:groups], rest[groups]
    split_kernel(groups, place, q, *[out.at[0] for out in outs], scratch)
    split_kernel(groups, place, cot, *[out.at[1] for out in outs], scratch)
    for step in range(groups):
        outs[step][1] *= gain[pl.ds(place[0] ^ step, 1), :]


def rate_column(r, head):
    return jnp.broadcast_to(r[pl.ds(head, 1), :], (8, r.shape[1])).T[:, 0:1]


def send_slices(sums, outs, layer):
    rows = sums.shape[1] // len(outs)
    for step, out in enumerate(outs):
        at = pl.multiple_of((layer ^ step) * rows, rows)
        out[...] = sums[:, pl.ds(at, rows), :]


def update_kernel(groups, depth, scale, place, *refs):
    keys_in, scaled_in = refs[:groups], refs[groups : 2 * groups]
    w_gate, w_out, w_up = refs[2 * groups : 2 * groups + 3]
    outs, sums = refs[2 * groups + 3 : -1], refs[-1]
    gate_b, out_b, up_b = (w[...].astype(BF16) for w in (w_gate, w_out, w_up))
    total = [0.0, 0.0, 0.0]
    for key, value in zip(keys_in, scaled_in):
        keys = key[...].astype(BF16)
        scaled = value[...].astype(BF16)
        first = mm(keys, gate_b)
        third = mm(keys, up_b)
        sig = jax.nn.sigmoid(first)
        activ = first * sig
        act = (activ * third).astype(BF16)
        dact = mm_t(scaled, out_b)
        deriv = sig * (1.0 + first * (1.0 - sig))
        dfirst = (dact * third * deriv).astype(BF16)
        dthird = (dact * activ).astype(BF16)
        total[0] += tmm(keys, dfirst)
        total[1] += tmm(act, scaled)
        total[2] += tmm(keys, dthird)
    for i in range(3):
        sums[i] = total[i] * scale
    send_slices(sums, outs, place[1])
    rows = sums.shape[1] // depth
    at = pl.multiple_of(place[1] * rows, rows)
    for i, w in enumerate((w_gate, w_out, w_up)):
        outs[0][i] += w[pl.ds(at, rows), :]


def assemble(place, parts, whole):
    rows = parts[0].shape[1]
    for step, part in enumerate(parts):
        at = pl.multiple_of((place[1] ^ step) * rows, rows)
        whole[:, pl.ds(at, rows), :] = part[...]


def apply_kernel(groups, depth, place, head_scale, *refs):
    pieces = refs[:groups]
    parts = refs[groups : groups + depth]
    first_ref, third_ref, os_ref, new_b, stats, whole = refs[groups + depth :]
    assemble(place, parts, whole)
    new_b[...] = whole[...].astype(BF16)
    for step in range(groups):
        queries = pieces[step][0].astype(BF16)
        tokens = queries.shape[0]
        first = mm(queries, new_b[0])
        third = mm(queries, new_b[2])
        hidden = (first * jax.nn.sigmoid(first) * third).astype(BF16)
        scaled = mm(hidden, new_b[1]) * head_scale[...]
        first_ref[step] = first
        third_ref[step] = third
        os_ref[step] = scaled
        sq = jnp.sum(scaled * scaled, axis=1, keepdims=True)
        ps = jnp.sum(scaled * pieces[step][1], axis=1, keepdims=True)
        lane = lax.broadcasted_iota(jnp.int32, (tokens, LANES), 1)
        both = jnp.where(lane == 0, sq, jnp.where(lane == 1, ps, 0.0)).T
        source = place[0] ^ step
        stats[0, pl.ds(source, 1), :] = both[0:1, :]
        stats[1, pl.ds(source, 1), :] = both[1:2, :]


def apply_back_kernel(groups, count, place, head_scale, *refs):
    pieces = refs[:groups]
    stats = refs[groups : 2 * groups]
    first_ref, third_ref, os_ref, new_b = refs[2 * groups : 2 * groups + 4]
    outs = refs[2 * groups + 4 : 3 * groups + 4]
    slices, sums, both = refs[3 * groups + 4 : -2], refs[-2], refs[-1]
    hs = head_scale[...]
    total_stats = stats[0][...]
    for other in stats[1:]:
        total_stats += other[...]
    both[...] = total_stats
    total = [0.0, 0.0, 0.0]
    for step in range(groups):
        queries = pieces[step][0].astype(BF16)
        source = place[0] ^ step
        sq = rate_column(both.at[0], source)
        ps = rate_column(both.at[1], source)
        inv = lax.rsqrt(sq / count + 1e-06)
        scaled = os_ref[step]
        dos = inv * pieces[step][1] - scaled * (inv * inv * inv * ps / count)
        dout = (dos * hs).astype(BF16)
        first = first_ref[step]
        third = third_ref[step]
        sig = jax.nn.sigmoid(first)
        activ = first * sig
        hidden = (activ * third).astype(BF16)
        dhidden = mm_t(dout, new_b[1])
        dthird = (dhidden * activ).astype(BF16)
        dfirst = (dhidden * third * (sig * (1.0 + first * (1.0 - sig)))).astype(BF16)
        outs[step][...] = mm_t(dfirst, new_b[0]) + mm_t(dthird, new_b[2])
        total[0] += tmm(queries, dfirst)
        total[1] += tmm(hidden, dout)
        total[2] += tmm(queries, dthird)
    for i in range(3):
        sums[i] = total[i]
    send_slices(sums, slices, place[1])


def halving_order(depth):
    sets, bit = [], 1
    while bit < depth:
        sets.append(list(range(bit, depth, 2 * bit)))
        bit *= 2
    return sets


def update_back_kernel(groups, depth, scale, place, *refs):
    keys_in, scaled_in = refs[:groups], refs[groups : 2 * groups]
    parts = refs[2 * groups : 2 * groups + depth]
    w_gate, w_out, w_up = refs[2 * groups + depth : 2 * groups + depth + 3]
    base = 2 * groups + depth + 3
    outs = refs[base : base + groups]
    slices = refs[base + groups : -2]
    whole, sums = refs[-2:]
    assemble(place, parts, whole)
    gate_b, out_b, up_b = (w[...].astype(BF16) for w in (w_gate, w_out, w_up))
    cot_gate, cot_out, cot_up = ((whole[i] * scale).astype(BF16) for i in range(3))
    total = [0.0, 0.0, 0.0]
    for step in range(groups):
        keys = keys_in[step][...].astype(BF16)
        scaled = scaled_in[step][...].astype(BF16)
        first = mm(keys, gate_b)
        third = mm(keys, up_b)
        sig = jax.nn.sigmoid(first)
        activ = first * sig
        act = (activ * third).astype(BF16)
        dact = mm_t(scaled, out_b)
        slope = sig * (1.0 - sig)
        deriv = sig + first * slope
        second = slope * (2.0 + first * (1.0 - 2.0 * sig))
        third_deriv = third * deriv
        dfirst = (dact * third_deriv).astype(BF16)
        dthird = (dact * activ).astype(BF16)
        bar_dfirst = mm(keys, cot_gate)
        bar_dthird = mm(keys, cot_up)
        bar_act = mm_t(scaled, cot_out)
        bar_activ = bar_dthird * dact + bar_act * third
        bar_dact = (bar_dfirst * third_deriv + bar_dthird * activ).astype(BF16)
        bar_df_dact = bar_dfirst * dact
        bar_third = (bar_df_dact * deriv + bar_act * activ).astype(BF16)
        bar_first = (bar_activ * deriv + bar_df_dact * third * second).astype(BF16)
        outs[step][0] = (
            mm_t(dfirst, cot_gate)
            + mm_t(dthird, cot_up)
            + mm_t(bar_first, gate_b)
            + mm_t(bar_third, up_b)
        )
        outs[step][1] = mm(act, cot_out) + mm(bar_dact, out_b)
        total[0] += tmm(keys, bar_first)
        total[1] += tmm(bar_dact, scaled)
        total[2] += tmm(keys, bar_third)
    for i in range(3):
        sums[i] = total[i]
    rows = sums.shape[1] // depth
    for out, members in zip(slices, halving_order(depth) + [[0]]):
        for i, step in enumerate(members):
            at = pl.multiple_of((place[1] ^ step) * rows, rows)
            out[i] = sums[:, pl.ds(at, rows), :]


def join_query_kernel(groups, place, *refs):
    pieces, out, scratch = refs[:groups], refs[groups], refs[groups + 1]
    tokens, heads, width = out.shape
    for step, piece in enumerate(pieces):
        put_head(scratch, place[0] ^ step, piece[...], tokens, heads)
    out[...] = rows_of(scratch).reshape(tokens, heads, width).astype(BF16)


def join_update_kernel(groups, place, r, *refs):
    pieces, (out_k, out_v, sk, sv) = refs[:groups], refs[groups:]
    tokens, heads, width = out_k.shape
    for step, piece in enumerate(pieces):
        head = place[0] ^ step
        put_head(sk, head, piece[0], tokens, heads)
        put_head(sv, head, piece[1] * rate_column(r, head), tokens, heads)
    out_k[...] = rows_of(sk).reshape(tokens, heads, width).astype(BF16)
    out_v[...] = rows_of(sv).reshape(tokens, heads, width).astype(BF16)


def rows_kernel(groups, place, *refs):
    parts, outs, total = refs[: -groups - 1], refs[-groups - 1 : -1], refs[-1]
    summed = parts[0][...]
    for part in parts[1:]:
        summed += part[0]
    total[...] = summed
    send_slices(total, outs, place[0])


def join_rows_kernel(groups, place, *refs):
    parts, outs = refs[:groups], refs[groups:]
    for step, part in enumerate(parts):
        for i, out in enumerate(outs):
            out[place[0] ^ step] = part[i]


def local(queries, keys, values, rates, head_scale, gain, w_gate, w_out, w_up, cotangent):
    tokens, heads, width = keys.shape[1:]
    hidden = w_gate.shape[2]
    ctx = lax.axis_size("ctx")
    head_axis = lax.axis_size("head")
    groups = heads
    depth = ctx // groups
    assert groups & (groups - 1) == 0 and depth & (depth - 1) == 0
    scale = 1.0 / math.sqrt(tokens * ctx * width)
    count = float(heads * head_axis * width)
    me = lax.axis_index("ctx")
    mine, layer = lax.rem(me, groups), lax.div(me, groups)
    place = jnp.stack([mine, layer]).astype(jnp.int32)

    def move(x, axis, step):
        return lax.ppermute(x, axis, [(c, c ^ step) for c in range(lax.axis_size(axis))])

    def in_plane(parts):
        return [parts[0]] + [move(p, "ctx", step) for step, p in enumerate(parts) if step]

    def in_column(parts):
        return [parts[0]] + [move(p, "ctx", i * groups) for i, p in enumerate(parts) if i]

    def after(x, *others):
        return lax.optimization_barrier((x, *others))

    def shape(*dims, dtype=F32):
        return jax.ShapeDtypeStruct(dims, dtype)

    flops = 2 * groups * tokens * width * hidden
    pieces = [shape(tokens, width)] * groups
    slices = [shape(3, hidden // depth, width)] * depth
    joined = shape(tokens, heads, width, dtype=BF16)
    scratch = pltpu.VMEM((width // LANES, tokens * heads, LANES), F32)
    square = pltpu.VMEM((3, hidden, width), F32)

    def split(body, *args):
        return call(functools.partial(body, groups), pieces, [scratch], flops // 16, place, *args)

    k_in = in_plane(split(split_kernel, keys[0]))
    s_in = in_plane(split(split_scaled_kernel, values[0], rates[0]))
    own = [lax.dynamic_index_in_dim(w, mine, 0, keepdims=False) for w in (w_gate, w_out, w_up)]
    own_scale = lax.dynamic_index_in_dim(head_scale, mine, 0, keepdims=True)[None, :]
    q_out = call(
        functools.partial(split_apply_kernel, groups), [shape(2, tokens, width)] * groups,
        [scratch], flops // 8, place, queries[0], cotangent[0], gain,
    )
    k_in, s_in, q_out = after(k_in, s_in, q_out)
    terms = call(
        functools.partial(update_kernel, groups, depth, scale), slices, [square], 6 * flops,
        place, *k_in, *s_in, *own,
    )
    q_in = in_plane(q_out)
    new = functools.reduce(jnp.add, in_column(terms))
    new, q_in[:-1] = after(new, q_in[:-1])
    new = in_column([new] * depth)
    kept = shape(groups, tokens, width)
    first, third, scaled, new_b, stats = call(
        functools.partial(apply_kernel, groups, depth),
        [kept, kept, kept, shape(3, hidden, width, dtype=BF16), shape(2, groups, tokens)],
        [square], 3 * flops, place, own_scale, *q_in, *new,
    )
    bit = 1
    while bit < head_axis:
        stats = stats + move(stats, "head", bit)
        bit *= 2
    out = call(
        functools.partial(apply_back_kernel, groups, count), pieces + slices,
        [square, pltpu.VMEM((2, groups, tokens), F32)], 6 * flops,
        place, own_scale, *q_in, *in_plane([stats] * groups),
        first, third, scaled, new_b,
    )
    part = functools.reduce(jnp.add, in_column(out[groups:]))
    part, q_back = after(part, in_plane(out[:groups]))
    parts = in_column([part] * depth)
    (grad_q,) = call(
        functools.partial(join_query_kernel, groups), [joined], [scratch], flops // 16,
        place, *q_back,
    )
    rows = hidden // depth
    sets = halving_order(depth)
    out = call(
        functools.partial(update_back_kernel, groups, depth, scale),
        [shape(2, tokens, width)] * groups
        + [shape(len(members), 3, rows, width) for members in sets + [[0]]],
        [square] * 2, 15 * flops, place, *k_in, *s_in, *parts, *own,
    )
    back = in_plane(out[:groups])
    ends, rest = list(out[groups:-1]), [part, out[-1]]
    for i in range(len(ends)):
        got = move(ends[i], "ctx", groups << i)
        for j in range(i + 1, len(ends)):
            ends[j] = ends[j] + got[1 << (j - i - 1) :: 1 << (j - i)]
        rest.append(got[:1])
    own_rows = rows // groups
    sent = call(
        functools.partial(rows_kernel, groups), [shape(3, own_rows, width)] * groups,
        [pltpu.VMEM((3, rows, width), F32)], flops // 100, place, *rest,
    )
    grads = call(
        functools.partial(join_rows_kernel, groups), [shape(heads, own_rows, width)] * 3, [],
        flops // 100, place, *in_plane(sent),
    )
    grad_k, grad_v = call(
        functools.partial(join_update_kernel, groups), [joined] * 2, [scratch] * 2, flops // 8,
        place, rates[0], *back,
    )
    if lax.axis_size("batch") > 1:
        grads = [lax.psum_scatter(x, "batch", scatter_dimension=1, tiled=True) for x in grads]
    return (grad_q[None], grad_k[None], grad_v[None], grads[0], grads[1], grads[2])


def solution(mesh):
    in_specs = (
        P("batch", "ctx", "head", None),
        P("batch", "ctx", "head", None),
        P("batch", "ctx", "head", None),
        P("batch", "head", "ctx"),
        P("head"),
        P("head", None),
        P("head", None, None),
        P("head", None, None),
        P("head", None, None),
        P("batch", "ctx", "head", None),
    )
    out_specs = (
        P("batch", "ctx", "head", None),
        P("batch", "ctx", "head", None),
        P("batch", "ctx", "head", None),
        P("head", ("ctx", "batch"), None),
        P("head", ("ctx", "batch"), None),
        P("head", ("ctx", "batch"), None),
    )
    return jax.shard_map(local, mesh=mesh, in_specs=in_specs, out_specs=out_specs, check_vma=False)
```

```python
import functools
import math

import jax
import jax.numpy as jnp
from jax import lax
from jax.experimental import pallas as pl
from jax.experimental.pallas import tpu as pltpu
from jax.sharding import PartitionSpec as P

F32 = jnp.float32
BF16 = jnp.bfloat16
LANES = 128
VMEM_LIMIT = 40 * 1024 * 1024
WHOLE_VMEM = 60 * 1024 * 1024


def mm(a, b):
    return jnp.dot(a, b, preferred_element_type=F32)


def mm_t(a, b):
    return lax.dot_general(a, b, (((1,), (1,)), ((), ())), preferred_element_type=F32)


def tmm(a, b):
    return lax.dot_general(a, b, (((0,), (0,)), ((), ())), preferred_element_type=F32)


def place_of(i, array, left):
    if array.dtype == jnp.int32:
        return pl.BlockSpec(memory_space=pltpu.SMEM)
    return pl.BlockSpec(memory_space=pltpu.HBM if i in left else pltpu.VMEM)


def call(body, out_shape, scratch, flops, *args, left=()):
    vmem = pl.BlockSpec(memory_space=pltpu.VMEM)
    size = sum(a.size * a.dtype.itemsize for a in args)
    size += sum(math.prod(o.shape) * o.dtype.itemsize for o in out_shape)
    return pl.pallas_call(
        body,
        out_shape=out_shape,
        in_specs=[place_of(i, a, left) for i, a in enumerate(args)],
        out_specs=[vmem] * len(out_shape),
        scratch_shapes=scratch,
        compiler_params=pltpu.CompilerParams(
            vmem_limit_bytes=WHOLE_VMEM if left else VMEM_LIMIT
        ),
        cost_estimate=pl.CostEstimate(flops=flops, bytes_accessed=size, transcendentals=0),
    )(*args)


def put_rows(scratch, x):
    for i in range(scratch.shape[0]):
        scratch[i] = x[:, i * LANES : (i + 1) * LANES]


def take_head(scratch, head, tokens, heads):
    parts = [scratch[i, pl.ds(head, tokens, stride=heads), :] for i in range(scratch.shape[0])]
    return jnp.concatenate(parts, axis=1)


def put_head(scratch, head, x, tokens, heads):
    for i in range(scratch.shape[0]):
        scratch[i, pl.ds(head, tokens, stride=heads), :] = x[:, i * LANES : (i + 1) * LANES]


def rows_of(scratch):
    return jnp.concatenate([scratch[i] for i in range(scratch.shape[0])], axis=1)


def split_kernel(groups, place, x, *rest):
    outs, scratch = rest[:groups], rest[groups]
    tokens, heads, width = x.shape
    put_rows(scratch, x[...].astype(F32).reshape(tokens * heads, width))
    for step in range(groups):
        outs[step][...] = take_head(scratch, place[0] ^ step, tokens, heads)


def split_update_kernel(groups, place, r, scales, k, v, w_gate, w_out, w_up, *rest):
    outs, own = rest[:groups], rest[groups]
    scratch, k_here, v_here, sems = rest[groups + 1 :]
    width = k.shape[2]
    first = pltpu.make_async_copy(k, k_here, sems.at[0])
    second = pltpu.make_async_copy(v, v_here, sems.at[1])
    first.start()
    second.start()
    copies = []
    for i, w in enumerate((w_gate, w_out, w_up)):
        to = own.at[pl.ds(i * width, width)]
        copies.append(pltpu.make_async_copy(w.at[place[0]], to, sems.at[2 + i]))
        copies[-1].start()
    own[3 * width :, :] = jnp.broadcast_to(scales[pl.ds(place[0], 1), :], (8, width))
    first.wait()
    split_kernel(groups, place, k_here, *[out.at[0] for out in outs], scratch)
    second.wait()
    split_kernel(groups, place, v_here, *[out.at[1] for out in outs], scratch)
    for step in range(groups):
        scaled = outs[step][1] * rate_column(r, place[0] ^ step)
        outs[step][1] = scaled.astype(BF16).astype(F32)
    for copy in copies:
        copy.wait()


def split_apply_kernel(groups, place, q, cot, gain, *rest):
    outs, scratch = rest[:groups], rest[groups]
    split_kernel(groups, place, q, *[out.at[0] for out in outs], scratch)
    split_kernel(groups, place, cot, *[out.at[1] for out in outs], scratch)
    for step in range(groups):
        outs[step][1] *= gain[pl.ds(place[0] ^ step, 1), :]


def rate_column(r, head):
    return jnp.broadcast_to(r[pl.ds(head, 1), :], (8, r.shape[1])).T[:, 0:1]


def halving_order(depth):
    sets, bit = [], 1
    while bit < depth:
        sets.append(list(range(bit, depth, 2 * bit)))
        bit *= 2
    return sets + [[0]]


def send_slices(sums, outs, rank, depth):
    rows = sums.shape[1] // depth
    for out, members in zip(outs, halving_order(depth)):
        for i, step in enumerate(members):
            at = pl.multiple_of((rank ^ step) * rows, rows)
            out[i] = sums[:, pl.ds(at, rows), :]


def weights_of(own, width):
    return [own[i * width : (i + 1) * width, :].astype(BF16) for i in range(3)]


def update_kernel(groups, depth, scale, place, own, *refs):
    pieces, outs, sums = refs[:groups], refs[groups:-1], refs[-1]
    width = sums.shape[1]
    gate_b, out_b, up_b = weights_of(own, width)
    total = [0.0, 0.0, 0.0]
    for piece in pieces:
        keys = piece[0].astype(BF16)
        scaled = piece[1].astype(BF16)
        first = mm(keys, gate_b)
        third = mm(keys, up_b)
        sig = jax.nn.sigmoid(first)
        activ = first * sig
        act = (activ * third).astype(BF16)
        dact = mm_t(scaled, out_b)
        deriv = sig * (1.0 + first * (1.0 - sig))
        dfirst = (dact * third * deriv).astype(BF16)
        dthird = (dact * activ).astype(BF16)
        total[0] += tmm(keys, dfirst)
        total[1] += tmm(act, scaled)
        total[2] += tmm(keys, dthird)
    for i in range(3):
        sums[i] = total[i] * scale
    send_slices(sums, outs, place[1], depth)
    rows = width // depth
    for i in range(3):
        at = pl.multiple_of(i * width + place[1] * rows, rows)
        outs[-1][0, i] += own[pl.ds(at, rows), :]


def assemble(place, depth, parts, whole):
    rows = whole.shape[1] // depth
    for part, members in zip(parts, gathered_order(depth)):
        for i, step in enumerate(members):
            at = pl.multiple_of((place[1] ^ step) * rows, rows)
            whole[:, pl.ds(at, rows), :] = part[i]


def gathered_order(depth):
    held, bit = [0], depth // 2
    while bit > 1:
        held = held + [step ^ bit for step in held]
        bit //= 2
    return [held, [step ^ 1 for step in held]] if depth > 1 else [held]


def apply_kernel(groups, depth, place, own, *refs):
    pieces = refs[:groups]
    parts = refs[groups:-6]
    first_ref, third_ref, os_ref, new_b, stats, whole = refs[-6:]
    assemble(place, depth, parts, whole)
    new_b[...] = whole[...].astype(BF16)
    for step in range(groups):
        queries = pieces[step][0].astype(BF16)
        tokens = queries.shape[0]
        first = mm(queries, new_b[0])
        third = mm(queries, new_b[2])
        hidden = (first * jax.nn.sigmoid(first) * third).astype(BF16)
        scaled = mm(hidden, new_b[1]) * own[-8:-7, :]
        first_ref[step] = first
        third_ref[step] = third
        os_ref[step] = scaled
        sq = jnp.sum(scaled * scaled, axis=1, keepdims=True)
        ps = jnp.sum(scaled * pieces[step][1], axis=1, keepdims=True)
        lane = lax.broadcasted_iota(jnp.int32, (tokens, LANES), 1)
        both = jnp.where(lane == 0, sq, jnp.where(lane == 1, ps, 0.0)).T
        source = place[0] ^ step
        stats[0, pl.ds(source, 1), :] = both[0:1, :]
        stats[1, pl.ds(source, 1), :] = both[1:2, :]


def apply_back_kernel(groups, depth, count, place, own, *refs):
    pieces = refs[:groups]
    stats = refs[groups : 2 * groups]
    first_ref, third_ref, os_ref, new_b = refs[2 * groups : 2 * groups + 4]
    outs = refs[2 * groups + 4 : 3 * groups + 4]
    slices, sums, both = refs[3 * groups + 4 : -2], refs[-2], refs[-1]
    hs = own[-8:-7, :]
    total_stats = stats[0][...]
    for other in stats[1:]:
        total_stats += other[...]
    both[...] = total_stats
    total = [0.0, 0.0, 0.0]
    for step in range(groups):
        queries = pieces[step][0].astype(BF16)
        source = place[0] ^ step
        sq = rate_column(both.at[0], source)
        ps = rate_column(both.at[1], source)
        inv = lax.rsqrt(sq / count + 1e-06)
        scaled = os_ref[step]
        dos = inv * pieces[step][1] - scaled * (inv * inv * inv * ps / count)
        dout = (dos * hs).astype(BF16)
        first = first_ref[step]
        third = third_ref[step]
        sig = jax.nn.sigmoid(first)
        activ = first * sig
        hidden = (activ * third).astype(BF16)
        dhidden = mm_t(dout, new_b[1])
        dthird = (dhidden * activ).astype(BF16)
        dfirst = (dhidden * third * (sig * (1.0 + first * (1.0 - sig)))).astype(BF16)
        outs[step][...] = mm_t(dfirst, new_b[0]) + mm_t(dthird, new_b[2])
        total[0] += tmm(queries, dfirst)
        total[1] += tmm(hidden, dout)
        total[2] += tmm(queries, dthird)
    for i in range(3):
        sums[i] = total[i]
    send_slices(sums, slices, place[1], depth)


def update_back_kernel(groups, depth, scale, place, own, *refs):
    pieces = refs[:groups]
    count = len(gathered_order(depth))
    parts, refs = refs[groups : groups + count], refs[groups + count :]
    outs, slices = refs[:groups], refs[groups:-2]
    whole, sums = refs[-2:]
    assemble(place, depth, parts, whole)
    gate_b, out_b, up_b = weights_of(own, whole.shape[1])
    cot_gate, cot_out, cot_up = ((whole[i] * scale).astype(BF16) for i in range(3))
    total = [0.0, 0.0, 0.0]
    for step in range(groups):
        keys = pieces[step][0].astype(BF16)
        scaled = pieces[step][1].astype(BF16)
        first = mm(keys, gate_b)
        third = mm(keys, up_b)
        sig = jax.nn.sigmoid(first)
        activ = first * sig
        act = (activ * third).astype(BF16)
        dact = mm_t(scaled, out_b)
        slope = sig * (1.0 - sig)
        deriv = sig + first * slope
        second = slope * (2.0 + first * (1.0 - 2.0 * sig))
        third_deriv = third * deriv
        dfirst = (dact * third_deriv).astype(BF16)
        dthird = (dact * activ).astype(BF16)
        bar_dfirst = mm(keys, cot_gate)
        bar_dthird = mm(keys, cot_up)
        bar_act = mm_t(scaled, cot_out)
        bar_activ = bar_dthird * dact + bar_act * third
        bar_dact = (bar_dfirst * third_deriv + bar_dthird * activ).astype(BF16)
        bar_df_dact = bar_dfirst * dact
        bar_third = (bar_df_dact * deriv + bar_act * activ).astype(BF16)
        bar_first = (bar_activ * deriv + bar_df_dact * third * second).astype(BF16)
        outs[step][0] = (
            mm_t(dfirst, cot_gate)
            + mm_t(dthird, cot_up)
            + mm_t(bar_first, gate_b)
            + mm_t(bar_third, up_b)
        )
        outs[step][1] = mm(act, cot_out) + mm(bar_dact, out_b)
        total[0] += tmm(keys, bar_first)
        total[1] += tmm(bar_dact, scaled)
        total[2] += tmm(keys, bar_third)
    for i in range(3):
        sums[i] = total[i]
    send_slices(sums, slices, place[1], depth)


def join_query_kernel(groups, place, *refs):
    pieces, out, scratch = refs[:groups], refs[groups], refs[groups + 1]
    tokens, heads, width = out.shape
    for step, piece in enumerate(pieces):
        put_head(scratch, place[0] ^ step, piece[...], tokens, heads)
    out[...] = rows_of(scratch).reshape(tokens, heads, width).astype(BF16)


def join_update_kernel(groups, place, r, *refs):
    pieces, (out_k, out_v, sk, sv) = refs[:groups], refs[groups:]
    tokens, heads, width = out_k.shape
    for step, piece in enumerate(pieces):
        head = place[0] ^ step
        put_head(sk, head, piece[0], tokens, heads)
        put_head(sv, head, piece[1] * rate_column(r, head), tokens, heads)
    out_k[...] = rows_of(sk).reshape(tokens, heads, width).astype(BF16)
    out_v[...] = rows_of(sv).reshape(tokens, heads, width).astype(BF16)


def rows_kernel(groups, place, *refs):
    parts, outs, total = refs[: -groups - 1], refs[-groups - 1 : -1], refs[-1]
    summed = parts[0][0]
    for part in parts[1:]:
        summed += part[0]
    total[...] = summed
    rows = total.shape[1] // groups
    for step, out in enumerate(outs):
        at = pl.multiple_of((place[0] ^ step) * rows, rows)
        out[...] = total[:, pl.ds(at, rows), :]


def join_rows_kernel(groups, place, *refs):
    parts, outs = refs[:groups], refs[groups:]
    for step, part in enumerate(parts):
        for i, out in enumerate(outs):
            out[place[0] ^ step] = part[i]


def local(queries, keys, values, rates, head_scale, gain, w_gate, w_out, w_up, cotangent):
    tokens, heads, width = keys.shape[1:]
    hidden = w_gate.shape[2]
    ctx = lax.axis_size("ctx")
    blocks = lax.axis_size("head")
    groups = heads
    depth = ctx // groups
    assert groups & (groups - 1) == 0 and depth & (depth - 1) == 0
    assert blocks & (blocks - 1) == 0 and depth % blocks == 0 and hidden == width
    scale = 1.0 / math.sqrt(tokens * ctx * width)
    count = float(heads * blocks * width)
    me, block = lax.axis_index("ctx"), lax.axis_index("head")
    mine = lax.rem(me, groups)
    low = lax.rem(lax.div(me, groups), blocks)
    rank = lax.div(me, groups * blocks) * blocks + block
    place = jnp.stack([mine, rank]).astype(jnp.int32)

    def shift(x, axis, step):
        return lax.ppermute(x, axis, [(c, c ^ step) for c in range(lax.axis_size(axis))])

    def in_rank(x, bit):
        return shift(x, "head", bit) if bit < blocks else shift(x, "ctx", bit * groups)

    def swap(x, step):
        pairs = []
        for c in range(ctx):
            hi, a, p = c // (groups * blocks), c // groups % blocks, c % groups
            for b in range(blocks):
                to = (hi * blocks + b) * groups + (p ^ step)
                pairs.append((c * blocks + b, to * blocks + a))
        return lax.ppermute(x, ("ctx", "head"), pairs)

    def exchange(parts):
        return [swap(part, step) for step, part in enumerate(parts)]

    def scatter(stacks):
        stacks = list(stacks)
        for i in range(len(stacks) - 1):
            got = in_rank(stacks[i], 1 << i)
            for j in range(i + 1, len(stacks) - 1):
                stacks[j] = stacks[j] + got[1 << (j - i - 1) :: 1 << (j - i)]
            stacks[-1] = stacks[-1] + got[:1]
        return stacks[-1]

    def gather(held, beside):
        bit = depth // 2
        while bit > 1:
            held = jnp.concatenate([held, in_rank(held, bit)])
            bit //= 2
        held, beside = after(held, beside)
        return ([held, in_rank(held, bit)] if bit else [held]), beside

    def fetch(bundle):
        own = jnp.where(block == low, bundle, 0.0)
        for step in range(1, blocks):
            pairs = [
                (c * blocks + a, c * blocks + (a ^ step))
                for c in range(ctx)
                for a in [c // groups % blocks]
            ]
            own = own + lax.ppermute(bundle, ("ctx", "head"), pairs)
        return own

    def after(x, *others):
        return lax.optimization_barrier((x, *others))

    def shape(*dims, dtype=F32):
        return jax.ShapeDtypeStruct(dims, dtype)

    flops = 2 * groups * tokens * width * hidden
    rows = hidden // depth
    pieces = [shape(2, tokens, width)] * groups
    stacks = [shape(len(members), 3, rows, width) for members in halving_order(depth)]
    joined = shape(tokens, heads, width, dtype=BF16)
    scratch = pltpu.VMEM((width // LANES, tokens * heads, LANES), F32)
    square = pltpu.VMEM((3, hidden, width), F32)

    scales = jnp.broadcast_to(head_scale[:, None], (heads, width))
    sent = call(
        functools.partial(split_update_kernel, groups), pieces + [shape(3 * width + 8, width)],
        [scratch] + [pltpu.VMEM((tokens, heads, width), BF16)] * 2
        + [pltpu.SemaphoreType.DMA((5,))], flops // 8,
        place, rates[0], scales, keys[0], values[0], w_gate, w_out, w_up, left=(3, 4, 5, 6, 7),
    )
    own = fetch(sent[-1])
    k_in = exchange(sent[:-1])
    q_out = call(
        functools.partial(split_apply_kernel, groups), pieces, [scratch], flops // 8,
        place, queries[0], cotangent[0], gain,
    )
    terms = call(
        functools.partial(update_kernel, groups, depth, scale), stacks, [square], 6 * flops,
        place, own, *k_in,
    )
    terms, q_out = after(terms, q_out)
    new, q_in = gather(scatter(terms), exchange(q_out))
    kept = shape(groups, tokens, width)
    first, third, scaled, new_b, stats = call(
        functools.partial(apply_kernel, groups, depth),
        [kept, kept, kept, shape(3, hidden, width, dtype=BF16), shape(2, groups, tokens)],
        [square], 3 * flops, place, own, *q_in, *new,
    )
    bit = 1
    while bit < blocks:
        stats = stats + shift(stats, "ctx", bit * groups)
        bit *= 2
    stats = [stats] + [shift(stats, "ctx", step) for step in range(1, groups)]
    out = call(
        functools.partial(apply_back_kernel, groups, depth, count),
        [shape(tokens, width)] * groups + stacks,
        [square, pltpu.VMEM((2, groups, tokens), F32)], 6 * flops,
        place, own, *q_in, *stats, first, third, scaled, new_b,
    )
    q_back = exchange(out[:groups])
    half = groups // 2
    part, q_back[:half] = after(scatter(out[groups:]), q_back[:half])
    parts, q_back[half:] = gather(part, q_back[half:])
    (grad_q,) = call(
        functools.partial(join_query_kernel, groups), [joined], [scratch], flops // 16,
        place, *q_back,
    )
    parts, grad_q = after(parts, grad_q)
    out = call(
        functools.partial(update_back_kernel, groups, depth, scale), pieces + stacks,
        [square] * 2, 15 * flops, place, own, *k_in, *parts,
    )
    back = exchange(out[:groups])
    own_rows = rows // groups
    sent = call(
        functools.partial(rows_kernel, groups), [shape(3, own_rows, width)] * groups,
        [pltpu.VMEM((3, rows, width), F32)], flops // 100, place, part, scatter(out[groups:]),
    )
    grads = call(
        functools.partial(join_rows_kernel, groups), [shape(heads, own_rows, width)] * 3, [],
        flops // 100, place, *exchange(sent),
    )
    grad_k, grad_v = call(
        functools.partial(join_update_kernel, groups), [joined] * 2, [scratch] * 2, flops // 8,
        place, rates[0], *back,
    )
    if lax.axis_size("batch") > 1:
        grads = [lax.psum_scatter(x, "batch", scatter_dimension=1, tiled=True) for x in grads]
    return (grad_q[None], grad_k[None], grad_v[None], grads[0], grads[1], grads[2])


def solution(mesh):
    in_specs = (
        P("batch", "ctx", "head", None),
        P("batch", "ctx", "head", None),
        P("batch", "ctx", "head", None),
        P("batch", "head", "ctx"),
        P("head"),
        P("head", None),
        P("head", None, None),
        P("head", None, None),
        P("head", None, None),
        P("batch", "ctx", "head", None),
    )
    out_specs = (
        P("batch", "ctx", "head", None),
        P("batch", "ctx", "head", None),
        P("batch", "ctx", "head", None),
        P("head", ("ctx", "batch"), None),
        P("head", ("ctx", "batch"), None),
        P("head", ("ctx", "batch"), None),
    )
    return jax.shard_map(local, mesh=mesh, in_specs=in_specs, out_specs=out_specs, check_vma=False)
```

```python
import functools
import math

import jax
import jax.numpy as jnp
from jax import lax
from jax.experimental import pallas as pl
from jax.experimental.pallas import tpu as pltpu
from jax.sharding import PartitionSpec as P

F32 = jnp.float32
BF16 = jnp.bfloat16
LANES = 128
VMEM_LIMIT = 40 * 1024 * 1024


def mm(a, b):
    return jnp.dot(a, b, preferred_element_type=F32)


def mm_t(a, b):
    return lax.dot_general(a, b, (((1,), (1,)), ((), ())), preferred_element_type=F32)


def tmm(a, b):
    return lax.dot_general(a, b, (((0,), (0,)), ((), ())), preferred_element_type=F32)


def call(body, out_shape, scratch, flops, *args):
    smem = pl.BlockSpec(memory_space=pltpu.SMEM)
    vmem = pl.BlockSpec(memory_space=pltpu.VMEM)
    size = sum(a.size * a.dtype.itemsize for a in args)
    size += sum(math.prod(o.shape) * o.dtype.itemsize for o in out_shape)
    return pl.pallas_call(
        body,
        out_shape=out_shape,
        in_specs=[smem if a.dtype == jnp.int32 else vmem for a in args],
        out_specs=[vmem] * len(out_shape),
        scratch_shapes=scratch,
        compiler_params=pltpu.CompilerParams(vmem_limit_bytes=VMEM_LIMIT),
        cost_estimate=pl.CostEstimate(flops=flops, bytes_accessed=size, transcendentals=0),
    )(*args)


def put_rows(scratch, x):
    for i in range(scratch.shape[0]):
        scratch[i] = x[:, i * LANES : (i + 1) * LANES]


def take_head(scratch, head, tokens, heads):
    parts = [scratch[i, pl.ds(head, tokens, stride=heads), :] for i in range(scratch.shape[0])]
    return jnp.concatenate(parts, axis=1)


def put_head(scratch, head, x, tokens, heads):
    for i in range(scratch.shape[0]):
        scratch[i, pl.ds(head, tokens, stride=heads), :] = x[:, i * LANES : (i + 1) * LANES]


def rows_of(scratch):
    return jnp.concatenate([scratch[i] for i in range(scratch.shape[0])], axis=1)


def split_kernel(groups, place, x, *rest):
    outs, scratch = rest[:groups], rest[groups]
    tokens, heads, width = x.shape
    put_rows(scratch, x[...].astype(F32).reshape(tokens * heads, width))
    for step in range(groups):
        outs[step][...] = take_head(scratch, place[0] ^ step, tokens, heads)


def split_scaled_kernel(groups, place, x, r, *rest):
    outs = rest[:groups]
    split_kernel(groups, place, x, *rest)
    for step in range(groups):
        scaled = outs[step][...] * rate_column(r, place[0] ^ step)
        outs[step][...] = scaled.astype(BF16).astype(F32)


def split_apply_kernel(groups, place, q, cot, gain, *rest):
    outs, scratch = rest[:groups], rest[groups]
    split_kernel(groups, place, q, *[out.at[0] for out in outs], scratch)
    split_kernel(groups, place, cot, *[out.at[1] for out in outs], scratch)
    for step in range(groups):
        outs[step][1] *= gain[pl.ds(place[0] ^ step, 1), :]


def rate_column(r, head):
    return jnp.broadcast_to(r[pl.ds(head, 1), :], (8, r.shape[1])).T[:, 0:1]


def send_slices(sums, outs, layer):
    rows = sums.shape[1] // len(outs)
    for step, out in enumerate(outs):
        at = pl.multiple_of((layer ^ step) * rows, rows)
        out[...] = sums[:, pl.ds(at, rows), :]


def merge(own, early, late, kept):
    kept[0] = own[...].astype(BF16)
    for step, (one, two) in enumerate(zip(early, late)):
        kept[step + 1] = (one[...] + two[...]).astype(BF16)


def update_kernel(groups, depth, scale, place, mark, *refs):
    each = 2 * groups - 1
    keys_in, scaled_in = refs[:each], refs[each : 2 * each]
    w_gate, w_out, w_up = refs[2 * each : 2 * each + 3]
    key_kept, scaled_kept = refs[2 * each + 3 : 2 * each + 5]
    outs, sums = refs[2 * each + 5 : -1], refs[-1]
    gate_b, out_b, up_b = (w[...].astype(BF16) for w in (w_gate, w_out, w_up))
    merge(keys_in[0], keys_in[1:groups], keys_in[groups:], key_kept)
    merge(scaled_in[0], scaled_in[1:groups], scaled_in[groups:], scaled_kept)
    total = [0.0, 0.0, 0.0]
    for step in range(groups):
        keys = key_kept[step]
        scaled = scaled_kept[step]
        first = mm(keys, gate_b)
        third = mm(keys, up_b)
        sig = jax.nn.sigmoid(first)
        activ = first * sig
        act = (activ * third).astype(BF16)
        dact = mm_t(scaled, out_b)
        deriv = sig * (1.0 + first * (1.0 - sig))
        dfirst = (dact * third * deriv).astype(BF16)
        dthird = (dact * activ).astype(BF16)
        total[0] += tmm(keys, dfirst)
        total[1] += tmm(act, scaled)
        total[2] += tmm(keys, dthird)
    for i in range(3):
        sums[i] = total[i] * scale
    send_slices(sums, outs, place[1])
    rows = sums.shape[1] // depth
    at = pl.multiple_of(place[1] * rows, rows)
    for i, w in enumerate((w_gate, w_out, w_up)):
        outs[0][i] += w[pl.ds(at, rows), :]


def assemble(place, parts, whole):
    rows = parts[0].shape[1]
    for step, part in enumerate(parts):
        at = pl.multiple_of((place[1] ^ step) * rows, rows)
        whole[:, pl.ds(at, rows), :] = part[...]


def apply_kernel(groups, depth, place, head_scale, *refs):
    pieces = refs[:groups]
    parts = refs[groups : groups + depth]
    first_ref, third_ref, os_ref, new_b, stats, whole = refs[groups + depth :]
    assemble(place, parts, whole)
    new_b[...] = whole[...].astype(BF16)
    for step in range(groups):
        queries = pieces[step][0].astype(BF16)
        tokens = queries.shape[0]
        first = mm(queries, new_b[0])
        third = mm(queries, new_b[2])
        hidden = (first * jax.nn.sigmoid(first) * third).astype(BF16)
        scaled = mm(hidden, new_b[1]) * head_scale[...]
        first_ref[step] = first
        third_ref[step] = third
        os_ref[step] = scaled
        sq = jnp.sum(scaled * scaled, axis=1, keepdims=True)
        ps = jnp.sum(scaled * pieces[step][1], axis=1, keepdims=True)
        lane = lax.broadcasted_iota(jnp.int32, (tokens, LANES), 1)
        both = jnp.where(lane == 0, sq, jnp.where(lane == 1, ps, 0.0)).T
        source = place[0] ^ step
        stats[0, pl.ds(source, 1), :] = both[0:1, :]
        stats[1, pl.ds(source, 1), :] = both[1:2, :]


def apply_back_kernel(groups, count, place, head_scale, *refs):
    pieces = refs[:groups]
    stats = refs[groups : 2 * groups]
    first_ref, third_ref, os_ref, new_b = refs[2 * groups : 2 * groups + 4]
    outs = refs[2 * groups + 4 : 3 * groups + 4]
    slices, sums, both = refs[3 * groups + 4 : -2], refs[-2], refs[-1]
    hs = head_scale[...]
    total_stats = stats[0][...]
    for other in stats[1:]:
        total_stats += other[...]
    both[...] = total_stats
    total = [0.0, 0.0, 0.0]
    for step in range(groups):
        queries = pieces[step][0].astype(BF16)
        source = place[0] ^ step
        sq = rate_column(both.at[0], source)
        ps = rate_column(both.at[1], source)
        inv = lax.rsqrt(sq / count + 1e-06)
        scaled = os_ref[step]
        dos = inv * pieces[step][1] - scaled * (inv * inv * inv * ps / count)
        dout = (dos * hs).astype(BF16)
        first = first_ref[step]
        third = third_ref[step]
        sig = jax.nn.sigmoid(first)
        activ = first * sig
        hidden = (activ * third).astype(BF16)
        dhidden = mm_t(dout, new_b[1])
        dthird = (dhidden * activ).astype(BF16)
        dfirst = (dhidden * third * (sig * (1.0 + first * (1.0 - sig)))).astype(BF16)
        outs[step][...] = mm_t(dfirst, new_b[0]) + mm_t(dthird, new_b[2])
        total[0] += tmm(queries, dfirst)
        total[1] += tmm(hidden, dout)
        total[2] += tmm(queries, dthird)
    for i in range(3):
        sums[i] = total[i]
    send_slices(sums, slices, place[1])


def halving_order(depth):
    sets, bit = [], 1
    while bit < depth:
        sets.append(list(range(bit, depth, 2 * bit)))
        bit *= 2
    return sets


def update_back_kernel(groups, depth, scale, place, mark, *refs):
    keys_in, scaled_in = refs[:2]
    parts = refs[2 : depth + 2]
    w_gate, w_out, w_up = refs[depth + 2 : depth + 5]
    base = depth + 5
    outs = refs[base : base + groups]
    slices = refs[base + groups : -2]
    whole, sums = refs[-2:]
    assemble(place, parts, whole)
    gate_b, out_b, up_b = (w[...].astype(BF16) for w in (w_gate, w_out, w_up))
    cot_gate, cot_out, cot_up = ((whole[i] * scale).astype(BF16) for i in range(3))
    total = [0.0, 0.0, 0.0]
    for step in range(groups):
        keys = keys_in[step]
        scaled = scaled_in[step]
        first = mm(keys, gate_b)
        third = mm(keys, up_b)
        sig = jax.nn.sigmoid(first)
        activ = first * sig
        act = (activ * third).astype(BF16)
        dact = mm_t(scaled, out_b)
        slope = sig * (1.0 - sig)
        deriv = sig + first * slope
        second = slope * (2.0 + first * (1.0 - 2.0 * sig))
        third_deriv = third * deriv
        dfirst = (dact * third_deriv).astype(BF16)
        dthird = (dact * activ).astype(BF16)
        bar_dfirst = mm(keys, cot_gate)
        bar_dthird = mm(keys, cot_up)
        bar_act = mm_t(scaled, cot_out)
        bar_activ = bar_dthird * dact + bar_act * third
        bar_dact = (bar_dfirst * third_deriv + bar_dthird * activ).astype(BF16)
        bar_df_dact = bar_dfirst * dact
        bar_third = (bar_df_dact * deriv + bar_act * activ).astype(BF16)
        bar_first = (bar_activ * deriv + bar_df_dact * third * second).astype(BF16)
        outs[step][0] = (
            mm_t(dfirst, cot_gate)
            + mm_t(dthird, cot_up)
            + mm_t(bar_first, gate_b)
            + mm_t(bar_third, up_b)
        )
        outs[step][1] = mm(act, cot_out) + mm(bar_dact, out_b)
        total[0] += tmm(keys, bar_first)
        total[1] += tmm(bar_dact, scaled)
        total[2] += tmm(keys, bar_third)
    for i in range(3):
        sums[i] = total[i]
    rows = sums.shape[1] // depth
    for out, members in zip(slices, halving_order(depth) + [[0]]):
        for i, step in enumerate(members):
            at = pl.multiple_of((place[1] ^ step) * rows, rows)
            out[i] = sums[:, pl.ds(at, rows), :]


def join_query_kernel(groups, place, *refs):
    pieces, out, scratch = refs[:groups], refs[groups], refs[groups + 1]
    tokens, heads, width = out.shape
    for step, piece in enumerate(pieces):
        put_head(scratch, place[0] ^ step, piece[...], tokens, heads)
    out[...] = rows_of(scratch).reshape(tokens, heads, width).astype(BF16)


def join_update_kernel(groups, place, r, *refs):
    pieces, (out_k, out_v, sk, sv) = refs[:groups], refs[groups:]
    tokens, heads, width = out_k.shape
    for step, piece in enumerate(pieces):
        head = place[0] ^ step
        put_head(sk, head, piece[0], tokens, heads)
        put_head(sv, head, piece[1] * rate_column(r, head), tokens, heads)
    out_k[...] = rows_of(sk).reshape(tokens, heads, width).astype(BF16)
    out_v[...] = rows_of(sv).reshape(tokens, heads, width).astype(BF16)


def rows_kernel(groups, place, *refs):
    parts, outs, total = refs[: -groups - 1], refs[-groups - 1 : -1], refs[-1]
    summed = parts[0][...]
    for part in parts[1:]:
        summed += part[0]
    total[...] = summed
    send_slices(total, outs, place[0])


def join_rows_kernel(groups, place, *refs):
    parts, outs = refs[:groups], refs[groups:]
    for step, part in enumerate(parts):
        for i, out in enumerate(outs):
            out[place[0] ^ step] = part[i]


def local(queries, keys, values, rates, head_scale, gain, w_gate, w_out, w_up, cotangent):
    tokens, heads, width = keys.shape[1:]
    hidden = w_gate.shape[2]
    ctx = lax.axis_size("ctx")
    head_axis = lax.axis_size("head")
    groups = heads
    depth = ctx // groups
    assert groups & (groups - 1) == 0 and depth & (depth - 1) == 0
    scale = 1.0 / math.sqrt(tokens * ctx * width)
    count = float(heads * head_axis * width)
    me = lax.axis_index("ctx")
    mine, layer = lax.rem(me, groups), lax.div(me, groups)
    place = jnp.stack([mine, layer]).astype(jnp.int32)

    def move(x, axis, step):
        return lax.ppermute(x, axis, [(c, c ^ step) for c in range(lax.axis_size(axis))])

    blocks = lax.axis_size("head")
    half = max(blocks // 2, 1)

    def half_move(x, step, late):
        heads_of = range(half, blocks) if late else range(half)
        pairs = [(c * blocks + b, (c ^ step) * blocks + b) for c in range(ctx) for b in heads_of]
        return lax.ppermute(x, ("ctx", "head"), pairs)

    def tell(early, x):
        early = lax.optimization_barrier(early)
        mark = jax.tree.leaves(early)[-1][..., :8, :LANES].reshape(-1, LANES)[:8]
        if blocks < 2:
            return early, mark, x
        pairs = [
            (c * blocks + b, c * blocks + b + half) for c in range(ctx) for b in range(blocks - half)
        ]
        return early, *after(lax.ppermute(mark, ("ctx", "head"), pairs), x)

    def half_plane(parts, late):
        if late and blocks < 2:
            return [jnp.zeros_like(p) for p in parts[1:]]
        return [half_move(p, step, late) for step, p in enumerate(parts) if step]

    def in_plane(parts):
        return [parts[0]] + [move(p, "ctx", step) for step, p in enumerate(parts) if step]

    def in_column(parts):
        return [parts[0]] + [move(p, "ctx", i * groups) for i, p in enumerate(parts) if i]

    def after(x, *others):
        return lax.optimization_barrier((x, *others))

    def shape(*dims, dtype=F32):
        return jax.ShapeDtypeStruct(dims, dtype)

    flops = 2 * groups * tokens * width * hidden
    pieces = [shape(tokens, width)] * groups
    slices = [shape(3, hidden // depth, width)] * depth
    joined = shape(tokens, heads, width, dtype=BF16)
    scratch = pltpu.VMEM((width // LANES, tokens * heads, LANES), F32)
    square = pltpu.VMEM((3, hidden, width), F32)

    def split(body, *args):
        return call(functools.partial(body, groups), pieces, [scratch], flops // 16, place, *args)

    k_out = split(split_kernel, keys[0])
    k_early = half_plane(k_out, False)
    s_out = split(split_scaled_kernel, values[0], rates[0])
    s_early = half_plane(s_out, False)
    (k_early, s_early), first_mark, (k_late, s_late) = tell((k_early, s_early), (k_out, s_out))
    k_late, s_late = half_plane(k_late, True), half_plane(s_late, True)
    own = [lax.dynamic_index_in_dim(w, mine, 0, keepdims=False) for w in (w_gate, w_out, w_up)]
    own_scale = lax.dynamic_index_in_dim(head_scale, mine, 0, keepdims=True)[None, :]
    q_out = call(
        functools.partial(split_apply_kernel, groups), [shape(2, tokens, width)] * groups,
        [scratch], flops // 8, place, queries[0], cotangent[0], gain,
    )
    kept_b = shape(groups, tokens, width, dtype=BF16)
    out = call(
        functools.partial(update_kernel, groups, depth, scale), [kept_b] * 2 + slices, [square],
        6 * flops, place, first_mark, k_out[0], *k_early, *k_late, s_out[0], *s_early, *s_late, *own,
    )
    k_in, s_in, terms = out[0], out[1], out[2:]
    new = functools.reduce(jnp.add, in_column(terms))
    new, q_out = after(new, q_out)
    q_in = in_plane(q_out)
    new = in_column([new] * depth)
    kept = shape(groups, tokens, width)
    first, third, scaled, new_b, stats = call(
        functools.partial(apply_kernel, groups, depth),
        [kept, kept, kept, shape(3, hidden, width, dtype=BF16), shape(2, groups, tokens)],
        [square], 3 * flops, place, own_scale, *q_in, *new,
    )
    bit = 1
    while bit < head_axis:
        stats = stats + move(stats, "head", bit)
        bit *= 2
    out = call(
        functools.partial(apply_back_kernel, groups, count), pieces + slices,
        [square, pltpu.VMEM((2, groups, tokens), F32)], 6 * flops,
        place, own_scale, *q_in, *in_plane([stats] * groups),
        first, third, scaled, new_b,
    )
    q_back = in_plane(out[:groups])
    parts = out[groups:]
    early = [half_move(p, i * groups, False) for i, p in enumerate(parts) if i]
    early, second_mark, later = tell(early, parts[1:])
    if blocks > 1:
        early += [half_move(p, (i + 1) * groups, True) for i, p in enumerate(later)]
    part = functools.reduce(jnp.add, [parts[0]] + early)
    parts = in_column([part] * depth)
    (grad_q,) = call(
        functools.partial(join_query_kernel, groups), [joined], [scratch], flops // 16,
        place, *q_back,
    )
    parts, grad_q = after(parts, grad_q)
    rows = hidden // depth
    sets = halving_order(depth)
    out = call(
        functools.partial(update_back_kernel, groups, depth, scale),
        [shape(2, tokens, width)] * groups
        + [shape(len(members), 3, rows, width) for members in sets + [[0]]],
        [square] * 2, 15 * flops, place, second_mark, k_in, s_in, *parts, *own,
    )
    back = in_plane(out[:groups])
    ends, rest = list(out[groups:-1]), [part, out[-1]]
    for i in range(len(ends)):
        got = move(ends[i], "ctx", groups << i)
        for j in range(i + 1, len(ends)):
            ends[j] = ends[j] + got[1 << (j - i - 1) :: 1 << (j - i)]
        rest.append(got[:1])
    own_rows = rows // groups
    sent = call(
        functools.partial(rows_kernel, groups), [shape(3, own_rows, width)] * groups,
        [pltpu.VMEM((3, rows, width), F32)], flops // 100, place, *rest,
    )
    grads = call(
        functools.partial(join_rows_kernel, groups), [shape(heads, own_rows, width)] * 3, [],
        flops // 100, place, *in_plane(sent),
    )
    grad_k, grad_v = call(
        functools.partial(join_update_kernel, groups), [joined] * 2, [scratch] * 2, flops // 8,
        place, rates[0], *back,
    )
    if lax.axis_size("batch") > 1:
        grads = [lax.psum_scatter(x, "batch", scatter_dimension=1, tiled=True) for x in grads]
    return (grad_q[None], grad_k[None], grad_v[None], grads[0], grads[1], grads[2])


def solution(mesh):
    in_specs = (
        P("batch", "ctx", "head", None),
        P("batch", "ctx", "head", None),
        P("batch", "ctx", "head", None),
        P("batch", "head", "ctx"),
        P("head"),
        P("head", None),
        P("head", None, None),
        P("head", None, None),
        P("head", None, None),
        P("batch", "ctx", "head", None),
    )
    out_specs = (
        P("batch", "ctx", "head", None),
        P("batch", "ctx", "head", None),
        P("batch", "ctx", "head", None),
        P("head", ("ctx", "batch"), None),
        P("head", ("ctx", "batch"), None),
        P("head", ("ctx", "batch"), None),
    )
    return jax.shard_map(local, mesh=mesh, in_specs=in_specs, out_specs=out_specs, check_vma=False)
```

```python
import functools
import math

import jax
import jax.numpy as jnp
from jax import lax
from jax.experimental import pallas as pl
from jax.experimental.pallas import tpu as pltpu
from jax.sharding import PartitionSpec as P

F32 = jnp.float32
BF16 = jnp.bfloat16
LANES = 128
VMEM_LIMIT = 40 * 1024 * 1024


def mm(a, b):
    return jnp.dot(a, b, preferred_element_type=F32)


def mm_t(a, b):
    return lax.dot_general(a, b, (((1,), (1,)), ((), ())), preferred_element_type=F32)


def tmm(a, b):
    return lax.dot_general(a, b, (((0,), (0,)), ((), ())), preferred_element_type=F32)


def call(body, out_shape, scratch, flops, *args):
    smem = pl.BlockSpec(memory_space=pltpu.SMEM)
    vmem = pl.BlockSpec(memory_space=pltpu.VMEM)
    size = sum(a.size * a.dtype.itemsize for a in args)
    size += sum(math.prod(o.shape) * o.dtype.itemsize for o in out_shape)
    return pl.pallas_call(
        body,
        out_shape=out_shape,
        in_specs=[smem if a.dtype == jnp.int32 else vmem for a in args],
        out_specs=[vmem] * len(out_shape),
        scratch_shapes=scratch,
        compiler_params=pltpu.CompilerParams(vmem_limit_bytes=VMEM_LIMIT),
        cost_estimate=pl.CostEstimate(flops=flops, bytes_accessed=size, transcendentals=0),
    )(*args)


def put_rows(scratch, x):
    for i in range(scratch.shape[0]):
        scratch[i] = x[:, i * LANES : (i + 1) * LANES]


def take_head(scratch, head, tokens, heads):
    parts = [scratch[i, pl.ds(head, tokens, stride=heads), :] for i in range(scratch.shape[0])]
    return jnp.concatenate(parts, axis=1)


def put_head(scratch, head, x, tokens, heads):
    for i in range(scratch.shape[0]):
        scratch[i, pl.ds(head, tokens, stride=heads), :] = x[:, i * LANES : (i + 1) * LANES]


def rows_of(scratch):
    return jnp.concatenate([scratch[i] for i in range(scratch.shape[0])], axis=1)


def split_kernel(groups, place, x, *rest):
    outs, scratch = rest[:groups], rest[groups]
    tokens, heads, width = x.shape
    put_rows(scratch, x[...].astype(F32).reshape(tokens * heads, width))
    for step in range(groups):
        outs[step][...] = take_head(scratch, place[0] ^ step, tokens, heads)


def split_scaled_kernel(groups, place, x, r, key, *rest):
    outs = list(rest[:groups])
    outs[1][0] = key[...]
    outs[1] = outs[1].at[1]
    split_kernel(groups, place, x, *outs, *rest[groups:])
    for step in range(groups):
        scaled = outs[step][...] * rate_column(r, place[0] ^ step)
        outs[step][...] = scaled.astype(BF16).astype(F32)


def split_apply_kernel(groups, place, q, cot, gain, *rest):
    outs, scratch = rest[:groups], rest[groups]
    split_kernel(groups, place, q, *[out.at[0] for out in outs], scratch)
    split_kernel(groups, place, cot, *[out.at[1] for out in outs], scratch)
    for step in range(groups):
        outs[step][1] *= gain[pl.ds(place[0] ^ step, 1), :]


def rate_column(r, head):
    return jnp.broadcast_to(r[pl.ds(head, 1), :], (8, r.shape[1])).T[:, 0:1]


def send_slices(sums, outs, layer):
    rows = sums.shape[1] // len(outs)
    for step, out in enumerate(outs):
        at = pl.multiple_of((layer ^ step) * rows, rows)
        out[...] = sums[:, pl.ds(at, rows), :]


def update_kernel(groups, depth, scale, place, *refs):
    pieces = list(zip(refs[:groups], refs[groups : 2 * groups]))
    pieces[1] = (refs[1].at[0], refs[1].at[1])
    refs = refs[2 * groups :]
    w_gate, w_out, w_up = refs[:3]
    key_kept, scaled_kept = refs[3:5]
    outs, sums = refs[5:-1], refs[-1]
    gate_b, out_b, up_b = (w[...].astype(BF16) for w in (w_gate, w_out, w_up))
    total = [0.0, 0.0, 0.0]
    for step, (key, value) in enumerate(pieces):
        keys = key[...].astype(BF16)
        scaled = value[...].astype(BF16)
        key_kept[step] = keys
        scaled_kept[step] = scaled
        first = mm(keys, gate_b)
        third = mm(keys, up_b)
        sig = jax.nn.sigmoid(first)
        activ = first * sig
        act = (activ * third).astype(BF16)
        dact = mm_t(scaled, out_b)
        deriv = sig * (1.0 + first * (1.0 - sig))
        dfirst = (dact * third * deriv).astype(BF16)
        dthird = (dact * activ).astype(BF16)
        total[0] += tmm(keys, dfirst)
        total[1] += tmm(act, scaled)
        total[2] += tmm(keys, dthird)
    for i in range(3):
        sums[i] = total[i] * scale
    send_slices(sums, outs, place[1])
    rows = sums.shape[1] // depth
    at = pl.multiple_of(place[1] * rows, rows)
    for i, w in enumerate((w_gate, w_out, w_up)):
        outs[0][i] += w[pl.ds(at, rows), :]


def assemble(place, parts, whole):
    rows = parts[0].shape[1]
    for step, part in enumerate(parts):
        at = pl.multiple_of((place[1] ^ step) * rows, rows)
        whole[:, pl.ds(at, rows), :] = part[...]


def apply_kernel(groups, depth, place, head_scale, *refs):
    pieces = refs[:groups]
    parts = refs[groups : groups + depth]
    first_ref, third_ref, os_ref, new_b, stats, whole = refs[groups + depth :]
    assemble(place, parts, whole)
    new_b[...] = whole[...].astype(BF16)
    for step in range(groups):
        queries = pieces[step][0].astype(BF16)
        tokens = queries.shape[0]
        first = mm(queries, new_b[0])
        third = mm(queries, new_b[2])
        hidden = (first * jax.nn.sigmoid(first) * third).astype(BF16)
        scaled = mm(hidden, new_b[1]) * head_scale[...]
        first_ref[step] = first
        third_ref[step] = third
        os_ref[step] = scaled
        sq = jnp.sum(scaled * scaled, axis=1, keepdims=True)
        ps = jnp.sum(scaled * pieces[step][1], axis=1, keepdims=True)
        lane = lax.broadcasted_iota(jnp.int32, (tokens, LANES), 1)
        both = jnp.where(lane == 0, sq, jnp.where(lane == 1, ps, 0.0)).T
        source = place[0] ^ step
        stats[0, pl.ds(source, 1), :] = both[0:1, :]
        stats[1, pl.ds(source, 1), :] = both[1:2, :]


def apply_back_kernel(groups, count, place, head_scale, *refs):
    pieces = refs[:groups]
    stats = refs[groups : 2 * groups]
    first_ref, third_ref, os_ref, new_b = refs[2 * groups : 2 * groups + 4]
    outs = refs[2 * groups + 4 : 3 * groups + 4]
    slices, sums, both = refs[3 * groups + 4 : -2], refs[-2], refs[-1]
    hs = head_scale[...]
    total_stats = stats[0][...]
    for other in stats[1:]:
        total_stats += other[...]
    both[...] = total_stats
    total = [0.0, 0.0, 0.0]
    for step in range(groups):
        queries = pieces[step][0].astype(BF16)
        source = place[0] ^ step
        sq = rate_column(both.at[0], source)
        ps = rate_column(both.at[1], source)
        inv = lax.rsqrt(sq / count + 1e-06)
        scaled = os_ref[step]
        dos = inv * pieces[step][1] - scaled * (inv * inv * inv * ps / count)
        dout = (dos * hs).astype(BF16)
        first = first_ref[step]
        third = third_ref[step]
        sig = jax.nn.sigmoid(first)
        activ = first * sig
        hidden = (activ * third).astype(BF16)
        dhidden = mm_t(dout, new_b[1])
        dthird = (dhidden * activ).astype(BF16)
        dfirst = (dhidden * third * (sig * (1.0 + first * (1.0 - sig)))).astype(BF16)
        outs[step][...] = mm_t(dfirst, new_b[0]) + mm_t(dthird, new_b[2])
        total[0] += tmm(queries, dfirst)
        total[1] += tmm(hidden, dout)
        total[2] += tmm(queries, dthird)
    for i in range(3):
        sums[i] = total[i]
    send_slices(sums, slices, place[1])


def paired(groups):
    return [True, True, True, False, False] if groups == 4 else [True] * groups


def back_refs(groups, refs):
    pairs, singles = [], []
    for ref, both in zip(refs, paired(groups)):
        if both:
            pairs.append((ref.at[0], ref.at[1]))
        else:
            singles.append(ref)
    return pairs + ([tuple(singles)] if singles else [])


def halving_order(depth):
    sets, bit = [], 1
    while bit < depth:
        sets.append(list(range(bit, depth, 2 * bit)))
        bit *= 2
    return sets


def update_back_kernel(groups, depth, scale, place, *refs):
    keys_in, scaled_in = refs[:2]
    parts = refs[2 : depth + 2]
    w_gate, w_out, w_up = refs[depth + 2 : depth + 5]
    refs = refs[depth + 5 :]
    count = len(paired(groups))
    outs, slices = back_refs(groups, refs[:count]), refs[count:-2]
    whole, sums = refs[-2:]
    assemble(place, parts, whole)
    gate_b, out_b, up_b = (w[...].astype(BF16) for w in (w_gate, w_out, w_up))
    cot_gate, cot_out, cot_up = ((whole[i] * scale).astype(BF16) for i in range(3))
    total = [0.0, 0.0, 0.0]
    for step in range(groups):
        keys = keys_in[step]
        scaled = scaled_in[step]
        first = mm(keys, gate_b)
        third = mm(keys, up_b)
        sig = jax.nn.sigmoid(first)
        activ = first * sig
        act = (activ * third).astype(BF16)
        dact = mm_t(scaled, out_b)
        slope = sig * (1.0 - sig)
        deriv = sig + first * slope
        second = slope * (2.0 + first * (1.0 - 2.0 * sig))
        third_deriv = third * deriv
        dfirst = (dact * third_deriv).astype(BF16)
        dthird = (dact * activ).astype(BF16)
        bar_dfirst = mm(keys, cot_gate)
        bar_dthird = mm(keys, cot_up)
        bar_act = mm_t(scaled, cot_out)
        bar_activ = bar_dthird * dact + bar_act * third
        bar_dact = (bar_dfirst * third_deriv + bar_dthird * activ).astype(BF16)
        bar_df_dact = bar_dfirst * dact
        bar_third = (bar_df_dact * deriv + bar_act * activ).astype(BF16)
        bar_first = (bar_activ * deriv + bar_df_dact * third * second).astype(BF16)
        outs[step][0][...] = (
            mm_t(dfirst, cot_gate)
            + mm_t(dthird, cot_up)
            + mm_t(bar_first, gate_b)
            + mm_t(bar_third, up_b)
        )
        outs[step][1][...] = mm(act, cot_out) + mm(bar_dact, out_b)
        total[0] += tmm(keys, bar_first)
        total[1] += tmm(bar_dact, scaled)
        total[2] += tmm(keys, bar_third)
    for i in range(3):
        sums[i] = total[i]
    rows = sums.shape[1] // depth
    for out, members in zip(slices, halving_order(depth) + [[0]]):
        for i, step in enumerate(members):
            at = pl.multiple_of((place[1] ^ step) * rows, rows)
            out[i] = sums[:, pl.ds(at, rows), :]


def join_query_kernel(groups, place, *refs):
    pieces, out, scratch = refs[:groups], refs[groups], refs[groups + 1]
    tokens, heads, width = out.shape
    for step, piece in enumerate(pieces):
        put_head(scratch, place[0] ^ step, piece[...], tokens, heads)
    out[...] = rows_of(scratch).reshape(tokens, heads, width).astype(BF16)


def join_update_kernel(groups, place, r, *refs):
    pieces, (out_k, out_v, sk, sv) = back_refs(groups, refs[:-4]), refs[-4:]
    tokens, heads, width = out_k.shape
    for step, (key, value) in enumerate(pieces):
        head = place[0] ^ step
        put_head(sk, head, key[...], tokens, heads)
        put_head(sv, head, value[...] * rate_column(r, head), tokens, heads)
    out_k[...] = rows_of(sk).reshape(tokens, heads, width).astype(BF16)
    out_v[...] = rows_of(sv).reshape(tokens, heads, width).astype(BF16)


def rows_kernel(groups, place, *refs):
    parts, outs, total = refs[: -groups - 1], refs[-groups - 1 : -1], refs[-1]
    summed = parts[0][...]
    for part in parts[1:]:
        summed += part[0]
    total[...] = summed
    send_slices(total, outs, place[0])


def join_rows_kernel(groups, place, *refs):
    parts, outs = refs[:groups], refs[groups:]
    for step, part in enumerate(parts):
        for i, out in enumerate(outs):
            out[place[0] ^ step] = part[i]


def local(queries, keys, values, rates, head_scale, gain, w_gate, w_out, w_up, cotangent):
    tokens, heads, width = keys.shape[1:]
    hidden = w_gate.shape[2]
    ctx = lax.axis_size("ctx")
    head_axis = lax.axis_size("head")
    groups = heads
    depth = ctx // groups
    assert groups & (groups - 1) == 0 and depth & (depth - 1) == 0
    scale = 1.0 / math.sqrt(tokens * ctx * width)
    count = float(heads * head_axis * width)
    me = lax.axis_index("ctx")
    mine, layer = lax.rem(me, groups), lax.div(me, groups)
    place = jnp.stack([mine, layer]).astype(jnp.int32)

    def move(x, axis, step):
        return lax.ppermute(x, axis, [(c, c ^ step) for c in range(lax.axis_size(axis))])

    def in_plane(parts):
        return [parts[0]] + [move(p, "ctx", step) for step, p in enumerate(parts) if step]

    def in_column(parts):
        return [parts[0]] + [move(p, "ctx", i * groups) for i, p in enumerate(parts) if i]

    def after(x, *others):
        return lax.optimization_barrier((x, *others))

    def shape(*dims, dtype=F32):
        return jax.ShapeDtypeStruct(dims, dtype)

    flops = 2 * groups * tokens * width * hidden
    pieces = [shape(tokens, width)] * groups
    slices = [shape(3, hidden // depth, width)] * depth
    joined = shape(tokens, heads, width, dtype=BF16)
    scratch = pltpu.VMEM((width // LANES, tokens * heads, LANES), F32)
    square = pltpu.VMEM((3, hidden, width), F32)

    def split(body, out, *args):
        return call(functools.partial(body, groups), out, [scratch], flops // 16, place, *args)

    both = [shape(2, tokens, width)]
    k_out = split(split_kernel, pieces, keys[0])
    s_out = split(
        split_scaled_kernel, pieces[:1] + both + pieces[2:], values[0], rates[0], k_out[1]
    )
    k_in = [k_out[0], move(s_out[1], "ctx", 1)]
    s_in = [s_out[0], s_out[0]]
    if groups == 4:
        k_in += [move(k_out[2], "ctx", 2), move(move(k_out[3], "ctx", 1), "ctx", 2)]
        s_in += [move(s_out[2], "ctx", 2), move(move(s_out[3], "ctx", 2), "ctx", 1)]
    else:
        k_in += [move(k_out[step], "ctx", step) for step in range(2, groups)]
        s_in += [move(s_out[step], "ctx", step) for step in range(2, groups)]
    own = [lax.dynamic_index_in_dim(w, mine, 0, keepdims=False) for w in (w_gate, w_out, w_up)]
    own_scale = lax.dynamic_index_in_dim(head_scale, mine, 0, keepdims=True)[None, :]
    q_out = call(
        functools.partial(split_apply_kernel, groups), both * groups,
        [scratch], flops // 8, place, queries[0], cotangent[0], gain,
    )
    k_in, s_in, q_out = after(k_in, s_in, q_out)
    kept_b = shape(groups, tokens, width, dtype=BF16)
    out = call(
        functools.partial(update_kernel, groups, depth, scale), [kept_b] * 2 + slices, [square],
        6 * flops, place, *k_in, *s_in, *own,
    )
    k_in, s_in, terms = out[0], out[1], in_column(out[2:])
    q_in = in_plane(q_out)
    new = functools.reduce(jnp.add, terms)
    new, q_in[:-1] = after(new, q_in[:-1])
    new = in_column([new] * depth)
    kept = shape(groups, tokens, width)
    first, third, scaled, new_b, stats = call(
        functools.partial(apply_kernel, groups, depth),
        [kept, kept, kept, shape(3, hidden, width, dtype=BF16), shape(2, groups, tokens)],
        [square], 3 * flops, place, own_scale, *q_in, *new,
    )
    bit = 1
    while bit < head_axis:
        stats = stats + move(stats, "head", bit)
        bit *= 2
    out = call(
        functools.partial(apply_back_kernel, groups, count), pieces + slices,
        [square, pltpu.VMEM((2, groups, tokens), F32)], 6 * flops,
        place, own_scale, *q_in, *in_plane([stats] * groups),
        first, third, scaled, new_b,
    )
    part = functools.reduce(jnp.add, in_column(out[groups:]))
    part, q_back = after(part, in_plane(out[:groups]))
    parts = in_column([part] * depth)
    (grad_q,) = call(
        functools.partial(join_query_kernel, groups), [joined], [scratch], flops // 16,
        place, *q_back,
    )
    parts, grad_q = after(parts, grad_q)
    rows = hidden // depth
    sets = halving_order(depth)
    out = call(
        functools.partial(update_back_kernel, groups, depth, scale),
        [both[0] if two else pieces[0] for two in paired(groups)]
        + [shape(len(members), 3, rows, width) for members in sets + [[0]]],
        [square] * 2, 15 * flops, place, k_in, s_in, *parts, *own,
    )
    sent, out = out[: len(paired(groups))], out[len(paired(groups)) :]
    back = in_plane(sent[:groups] if len(sent) == groups else sent[: groups - 1])
    if len(sent) > groups:
        back.append(move(move(sent[-2], "ctx", 1), "ctx", 2))
        back.append(move(move(sent[-1], "ctx", 2), "ctx", 1))
    ends, rest = list(out[:-1]), [part, out[-1]]
    for i in range(len(ends)):
        got = move(ends[i], "ctx", groups << i)
        for j in range(i + 1, len(ends)):
            ends[j] = ends[j] + got[1 << (j - i - 1) :: 1 << (j - i)]
        rest.append(got[:1])
    own_rows = rows // groups
    sent = call(
        functools.partial(rows_kernel, groups), [shape(3, own_rows, width)] * groups,
        [pltpu.VMEM((3, rows, width), F32)], flops // 100, place, *rest,
    )
    grads = call(
        functools.partial(join_rows_kernel, groups), [shape(heads, own_rows, width)] * 3, [],
        flops // 100, place, *in_plane(sent),
    )
    grad_k, grad_v = call(
        functools.partial(join_update_kernel, groups), [joined] * 2, [scratch] * 2, flops // 8,
        place, rates[0], *back,
    )
    if lax.axis_size("batch") > 1:
        grads = [lax.psum_scatter(x, "batch", scatter_dimension=1, tiled=True) for x in grads]
    return (grad_q[None], grad_k[None], grad_v[None], grads[0], grads[1], grads[2])


def solution(mesh):
    in_specs = (
        P("batch", "ctx", "head", None),
        P("batch", "ctx", "head", None),
        P("batch", "ctx", "head", None),
        P("batch", "head", "ctx"),
        P("head"),
        P("head", None),
        P("head", None, None),
        P("head", None, None),
        P("head", None, None),
        P("batch", "ctx", "head", None),
    )
    out_specs = (
        P("batch", "ctx", "head", None),
        P("batch", "ctx", "head", None),
        P("batch", "ctx", "head", None),
        P("head", ("ctx", "batch"), None),
        P("head", ("ctx", "batch"), None),
        P("head", ("ctx", "batch"), None),
    )
    return jax.shard_map(local, mesh=mesh, in_specs=in_specs, out_specs=out_specs, check_vma=False)
```

```python
import functools
import math

import jax
import jax.numpy as jnp
from jax import lax
from jax.experimental import pallas as pl
from jax.experimental.pallas import tpu as pltpu
from jax.sharding import PartitionSpec as P

F32 = jnp.float32
BF16 = jnp.bfloat16
LANES = 128
VMEM_LIMIT = 24 * 1024 * 1024


def mm(a, b):
    return jnp.dot(a, b, preferred_element_type=F32)


def mm_t(a, b):
    return lax.dot_general(a, b, (((1,), (1,)), ((), ())), preferred_element_type=F32)


def tmm(a, b):
    return lax.dot_general(a, b, (((0,), (0,)), ((), ())), preferred_element_type=F32)


def call(body, out_shape, scratch, flops, *args):
    smem = pl.BlockSpec(memory_space=pltpu.SMEM)
    vmem = pl.BlockSpec(memory_space=pltpu.VMEM)
    size = sum(a.size * a.dtype.itemsize for a in args)
    size += sum(math.prod(o.shape) * o.dtype.itemsize for o in out_shape)
    return pl.pallas_call(
        body,
        out_shape=out_shape,
        in_specs=[smem if a.dtype == jnp.int32 else vmem for a in args],
        out_specs=[vmem] * len(out_shape),
        scratch_shapes=scratch,
        compiler_params=pltpu.CompilerParams(vmem_limit_bytes=VMEM_LIMIT),
        cost_estimate=pl.CostEstimate(flops=flops, bytes_accessed=size, transcendentals=0),
    )(*args)


def put_rows(scratch, x):
    for i in range(scratch.shape[0]):
        scratch[i] = x[:, i * LANES : (i + 1) * LANES]


def take_head(scratch, head, tokens, heads):
    parts = [scratch[i, pl.ds(head, tokens, stride=heads), :] for i in range(scratch.shape[0])]
    return jnp.concatenate(parts, axis=1)


def put_head(scratch, head, x, tokens, heads):
    for i in range(scratch.shape[0]):
        scratch[i, pl.ds(head, tokens, stride=heads), :] = x[:, i * LANES : (i + 1) * LANES]


def rows_of(scratch):
    return jnp.concatenate([scratch[i] for i in range(scratch.shape[0])], axis=1)


def split_kernel(groups, place, x, *rest):
    outs, scratch = rest[:groups], rest[groups]
    tokens, heads, width = x.shape
    put_rows(scratch, x[...].astype(F32).reshape(tokens * heads, width))
    for step in range(groups):
        outs[step][...] = take_head(scratch, place[0] ^ step, tokens, heads)


def split_scaled_kernel(groups, place, x, r, *rest):
    outs = rest[:groups]
    split_kernel(groups, place, x, *rest)
    for step in range(groups):
        scaled = outs[step][...] * rate_column(r, place[0] ^ step)
        outs[step][...] = scaled.astype(BF16).astype(F32)


def split_apply_kernel(groups, place, q, cot, gain, *rest):
    outs, scratch = rest[:groups], rest[groups]
    split_kernel(groups, place, q, *[out.at[0] for out in outs], scratch)
    split_kernel(groups, place, cot, *[out.at[1] for out in outs], scratch)
    for step in range(groups):
        outs[step][1] *= gain[pl.ds(place[0] ^ step, 1), :]


def rate_column(r, head):
    return jnp.broadcast_to(r[pl.ds(head, 1), :], (8, r.shape[1])).T[:, 0:1]


def send_groups(count):
    odd = list(range(3, count, 2))
    return ([odd] if odd else []) + [[r] for r in [1] + list(range(2, count, 2)) if r < count] + [[0]]


def send_slices(sums, outs, own, count):
    rows = sums.shape[1] // count
    for out, members in zip(outs, send_groups(count)):
        for i, step in enumerate(members):
            at = pl.multiple_of((own ^ step) * rows, rows)
            out[i] = sums[:, pl.ds(at, rows), :]


def update_kernel(groups, depth, scale, place, *refs):
    keys_in, scaled_in = refs[:groups], refs[groups : 2 * groups]
    w_gate, w_out, w_up = refs[2 * groups : 2 * groups + 3]
    key_kept, scaled_kept = refs[2 * groups + 3 : 2 * groups + 5]
    outs, sums = refs[2 * groups + 5 : -1], refs[-1]
    gate_b, out_b, up_b = (w[...].astype(BF16) for w in (w_gate, w_out, w_up))
    total = [0.0, 0.0, 0.0]
    for step in range(groups):
        keys = keys_in[step][...].astype(BF16)
        scaled = scaled_in[step][...].astype(BF16)
        key_kept[step] = keys
        scaled_kept[step] = scaled
        first = mm(keys, gate_b)
        third = mm(keys, up_b)
        sig = jax.nn.sigmoid(first)
        activ = first * sig
        act = (activ * third).astype(BF16)
        dact = mm_t(scaled, out_b)
        deriv = sig * (1.0 + first * (1.0 - sig))
        dfirst = (dact * third * deriv).astype(BF16)
        dthird = (dact * activ).astype(BF16)
        total[0] += tmm(keys, dfirst)
        total[1] += tmm(act, scaled)
        total[2] += tmm(keys, dthird)
    for i in range(3):
        sums[i] = total[i] * scale
    send_slices(sums, outs, place[1], depth)
    rows = sums.shape[1] // depth
    at = pl.multiple_of(place[1] * rows, rows)
    for i, w in enumerate((w_gate, w_out, w_up)):
        outs[-1][0, i] += w[pl.ds(at, rows), :]


def assemble(place, parts, whole):
    rows = parts[0].shape[2]
    for step, part in enumerate(parts):
        at = pl.multiple_of((place[1] ^ step) * rows, rows)
        whole[:, pl.ds(at, rows), :] = part[0]


def apply_kernel(groups, depth, place, head_scale, *refs):
    pieces = refs[:groups]
    parts = refs[groups : groups + depth]
    first_ref, third_ref, os_ref, new_b, stats, whole = refs[groups + depth :]
    assemble(place, parts, whole)
    new_b[...] = whole[...].astype(BF16)
    for step in range(groups):
        queries = pieces[step][0].astype(BF16)
        tokens = queries.shape[0]
        first = mm(queries, new_b[0])
        third = mm(queries, new_b[2])
        hidden = (first * jax.nn.sigmoid(first) * third).astype(BF16)
        scaled = mm(hidden, new_b[1]) * head_scale[...]
        first_ref[step] = first
        third_ref[step] = third
        os_ref[step] = scaled
        sq = jnp.sum(scaled * scaled, axis=1, keepdims=True)
        ps = jnp.sum(scaled * pieces[step][1], axis=1, keepdims=True)
        lane = lax.broadcasted_iota(jnp.int32, (tokens, LANES), 1)
        both = jnp.where(lane == 0, sq, jnp.where(lane == 1, ps, 0.0)).T
        source = place[0] ^ step
        stats[0, pl.ds(source, 1), :] = both[0:1, :]
        stats[1, pl.ds(source, 1), :] = both[1:2, :]


def apply_back_kernel(groups, depth, count, place, head_scale, *refs):
    pieces = refs[:groups]
    stats = refs[groups : 2 * groups]
    first_ref, third_ref, os_ref, new_b = refs[2 * groups : 2 * groups + 4]
    outs = refs[2 * groups + 4 : 3 * groups + 4]
    slices, sums, both = refs[3 * groups + 4 : -2], refs[-2], refs[-1]
    hs = head_scale[...]
    total_stats = stats[0][...]
    for other in stats[1:]:
        total_stats += other[...]
    both[...] = total_stats
    total = [0.0, 0.0, 0.0]
    for step in range(groups):
        queries = pieces[step][0].astype(BF16)
        source = place[0] ^ step
        sq = rate_column(both.at[0], source)
        ps = rate_column(both.at[1], source)
        inv = lax.rsqrt(sq / count + 1e-06)
        scaled = os_ref[step]
        dos = inv * pieces[step][1] - scaled * (inv * inv * inv * ps / count)
        dout = (dos * hs).astype(BF16)
        first = first_ref[step]
        third = third_ref[step]
        sig = jax.nn.sigmoid(first)
        activ = first * sig
        hidden = (activ * third).astype(BF16)
        dhidden = mm_t(dout, new_b[1])
        dthird = (dhidden * activ).astype(BF16)
        dfirst = (dhidden * third * (sig * (1.0 + first * (1.0 - sig)))).astype(BF16)
        outs[step][...] = mm_t(dfirst, new_b[0]) + mm_t(dthird, new_b[2])
        total[0] += tmm(queries, dfirst)
        total[1] += tmm(hidden, dout)
        total[2] += tmm(queries, dthird)
    for i in range(3):
        sums[i] = total[i]
    send_slices(sums, slices, place[1], depth)


def update_back_kernel(groups, depth, scale, place, *refs):
    keys_in, scaled_in = refs[:2]
    parts = refs[2 : depth + 2]
    w_gate, w_out, w_up = refs[depth + 2 : depth + 5]
    base = depth + 5
    outs = refs[base : base + groups]
    slices = refs[base + groups : -2]
    whole, sums = refs[-2:]
    assemble(place, parts, whole)
    gate_b, out_b, up_b = (w[...].astype(BF16) for w in (w_gate, w_out, w_up))
    cot_gate, cot_out, cot_up = ((whole[i] * scale).astype(BF16) for i in range(3))
    total = [0.0, 0.0, 0.0]
    for step in range(groups):
        keys = keys_in[step]
        scaled = scaled_in[step]
        first = mm(keys, gate_b)
        third = mm(keys, up_b)
        sig = jax.nn.sigmoid(first)
        activ = first * sig
        act = (activ * third).astype(BF16)
        dact = mm_t(scaled, out_b)
        slope = sig * (1.0 - sig)
        deriv = sig + first * slope
        second = slope * (2.0 + first * (1.0 - 2.0 * sig))
        third_deriv = third * deriv
        dfirst = (dact * third_deriv).astype(BF16)
        dthird = (dact * activ).astype(BF16)
        bar_dfirst = mm(keys, cot_gate)
        bar_dthird = mm(keys, cot_up)
        bar_act = mm_t(scaled, cot_out)
        bar_activ = bar_dthird * dact + bar_act * third
        bar_dact = (bar_dfirst * third_deriv + bar_dthird * activ).astype(BF16)
        bar_df_dact = bar_dfirst * dact
        bar_third = (bar_df_dact * deriv + bar_act * activ).astype(BF16)
        bar_first = (bar_activ * deriv + bar_df_dact * third * second).astype(BF16)
        outs[step][0] = (
            mm_t(dfirst, cot_gate)
            + mm_t(dthird, cot_up)
            + mm_t(bar_first, gate_b)
            + mm_t(bar_third, up_b)
        )
        outs[step][1] = mm(act, cot_out) + mm(bar_dact, out_b)
        total[0] += tmm(keys, bar_first)
        total[1] += tmm(bar_dact, scaled)
        total[2] += tmm(keys, bar_third)
    for i in range(3):
        sums[i] = total[i]
    send_slices(sums, slices, place[1], depth)


def join_query_kernel(groups, place, *refs):
    pieces, out, scratch = refs[:groups], refs[groups], refs[groups + 1]
    tokens, heads, width = out.shape
    for step, piece in enumerate(pieces):
        put_head(scratch, place[0] ^ step, piece[...], tokens, heads)
    out[...] = rows_of(scratch).reshape(tokens, heads, width).astype(BF16)


def join_update_kernel(groups, place, r, *refs):
    pieces, parts = refs[:groups], refs[groups : 2 * groups]
    out_k, out_v = refs[2 * groups : 2 * groups + 2]
    grads, (sk, sv) = refs[2 * groups + 2 : -2], refs[-2:]
    tokens, heads, width = out_k.shape
    for step, piece in enumerate(pieces):
        head = place[0] ^ step
        put_head(sk, head, piece[0], tokens, heads)
        put_head(sv, head, piece[1] * rate_column(r, head), tokens, heads)
        for i, grad in enumerate(grads):
            grad[head] = parts[step][0, i]
    out_k[...] = rows_of(sk).reshape(tokens, heads, width).astype(BF16)
    out_v[...] = rows_of(sv).reshape(tokens, heads, width).astype(BF16)


def rows_kernel(groups, place, *refs):
    count = len(send_groups(groups))
    parts, outs, total = refs[: -count - 1], refs[-count - 1 : -1], refs[-1]
    summed = parts[0][0]
    for part in parts[1:]:
        summed += part[0]
    total[...] = summed
    send_slices(total, outs, place[0], groups)


def local(queries, keys, values, rates, head_scale, gain, w_gate, w_out, w_up, cotangent):
    tokens, heads, width = keys.shape[1:]
    hidden = w_gate.shape[2]
    ctx = lax.axis_size("ctx")
    head_axis = lax.axis_size("head")
    groups = heads
    depth = ctx // groups
    assert groups & (groups - 1) == 0 and depth & (depth - 1) == 0
    scale = 1.0 / math.sqrt(tokens * ctx * width)
    count = float(heads * head_axis * width)
    me = lax.axis_index("ctx")
    mine, layer = lax.rem(me, groups), lax.div(me, groups)
    place = jnp.stack([mine, layer]).astype(jnp.int32)

    def move(x, axis, step):
        return lax.ppermute(x, axis, [(c, c ^ step) for c in range(lax.axis_size(axis))])

    def in_plane(parts):
        return [parts[0]] + [move(p, "ctx", step) for step, p in enumerate(parts) if step]

    def forwarded(got):
        return [got[:1]] if got.shape[0] == 1 else [got[i : i + 1] for i in range(got.shape[0])]

    def scatter(outs, count, unit):
        outs = list(outs)
        evens = list(range(2, count, 2))
        via = forwarded(move(outs.pop(0), "ctx", unit)) if evens else []
        first = [move(outs[0], "ctx", unit)] if count > 1 else []
        even = [move(p + v, "ctx", r * unit) for p, v, r in zip(outs[1:], via, evens)]
        return [outs[-1]] + first + even

    def gather(part, count, unit):
        got = [part] * count
        for r in [2 * i for i in range(1, count // 2)]:
            got[r] = move(part, "ctx", r * unit)
            got[r + 1] = move(got[r], "ctx", unit)
        if count > 1:
            got[1] = move(part, "ctx", unit)
        return got

    def rows_exchange(outs):
        outs, evens = list(outs), list(range(2, groups, 2))
        via = forwarded(move(outs.pop(0), "ctx", 1)) if evens else []
        got = [outs[-1]] + [move(outs[0], "ctx", 1)] * (groups > 1)
        for i, r in enumerate(evens):
            got += [move(outs[1 + i], "ctx", r), move(via[i], "ctx", r)]
        return got

    def after(x, *others):
        return lax.optimization_barrier((x, *others))

    def shape(*dims, dtype=F32):
        return jax.ShapeDtypeStruct(dims, dtype)

    flops = 2 * groups * tokens * width * hidden
    pieces = [shape(tokens, width)] * groups
    slices = [shape(len(m), 3, hidden // depth, width) for m in send_groups(depth)]
    joined = shape(tokens, heads, width, dtype=BF16)
    scratch = pltpu.VMEM((width // LANES, tokens * heads, LANES), F32)
    square = pltpu.VMEM((3, hidden, width), F32)

    def split(body, *args):
        return call(functools.partial(body, groups), pieces, [scratch], flops // 16, place, *args)

    k_in = in_plane(split(split_kernel, keys[0]))
    s_in = in_plane(split(split_scaled_kernel, values[0], rates[0]))
    own = [lax.dynamic_index_in_dim(w, mine, 0, keepdims=False) for w in (w_gate, w_out, w_up)]
    own_scale = lax.dynamic_index_in_dim(head_scale, mine, 0, keepdims=True)[None, :]
    k_in, s_in, queries, cotangent = after(k_in, s_in, queries, cotangent)
    kept_b = shape(groups, tokens, width, dtype=BF16)
    out = call(
        functools.partial(update_kernel, groups, depth, scale), [kept_b] * 2 + slices, [square],
        6 * flops, place, *k_in, *s_in, *own,
    )
    k_in, s_in, terms = out[0], out[1], out[2:]
    q_out = call(
        functools.partial(split_apply_kernel, groups), [shape(2, tokens, width)] * groups,
        [scratch], flops // 8, place, queries[0], cotangent[0], gain,
    )
    q_in = in_plane(q_out)
    new = functools.reduce(jnp.add, scatter(terms, depth, groups))
    new = gather(new, depth, groups)
    kept = shape(groups, tokens, width)
    first, third, scaled, new_b, stats = call(
        functools.partial(apply_kernel, groups, depth),
        [kept, kept, kept, shape(3, hidden, width, dtype=BF16), shape(2, groups, tokens)],
        [square], 3 * flops, place, own_scale, *q_in, *new,
    )
    bit = 1
    while bit < head_axis:
        stats = stats + move(stats, "head", bit)
        bit *= 2
    out = call(
        functools.partial(apply_back_kernel, groups, depth, count), pieces + slices,
        [square, pltpu.VMEM((2, groups, tokens), F32)], 6 * flops,
        place, own_scale, *q_in, *in_plane([stats] * groups),
        first, third, scaled, new_b,
    )
    part = functools.reduce(jnp.add, scatter(out[groups:], depth, groups))
    parts = gather(part, depth, groups)
    (grad_q,) = call(
        functools.partial(join_query_kernel, groups), [joined], [scratch], flops // 16,
        place, *in_plane(out[:groups]),
    )
    parts, grad_q = after(parts, grad_q)
    rows = hidden // depth
    out = call(
        functools.partial(update_back_kernel, groups, depth, scale),
        [shape(2, tokens, width)] * groups + slices, [square] * 2, 15 * flops,
        place, k_in, s_in, *parts, *own,
    )
    back = in_plane(out[:groups])
    ends = scatter(out[groups:], depth, groups)
    own_rows = rows // groups
    sent = call(
        functools.partial(rows_kernel, groups),
        [shape(len(m), 3, own_rows, width) for m in send_groups(groups)],
        [pltpu.VMEM((3, rows, width), F32)], flops // 100, place, part, *ends,
    )
    grad_k, grad_v, *grads = call(
        functools.partial(join_update_kernel, groups),
        [joined] * 2 + [shape(heads, own_rows, width)] * 3, [scratch] * 2, flops // 8,
        place, rates[0], *back, *rows_exchange(sent),
    )
    if lax.axis_size("batch") > 1:
        grads = [lax.psum_scatter(x, "batch", scatter_dimension=1, tiled=True) for x in grads]
    return (grad_q[None], grad_k[None], grad_v[None], grads[0], grads[1], grads[2])


def solution(mesh):
    in_specs = (
        P("batch", "ctx", "head", None),
        P("batch", "ctx", "head", None),
        P("batch", "ctx", "head", None),
        P("batch", "head", "ctx"),
        P("head"),
        P("head", None),
        P("head", None, None),
        P("head", None, None),
        P("head", None, None),
        P("batch", "ctx", "head", None),
    )
    out_specs = (
        P("batch", "ctx", "head", None),
        P("batch", "ctx", "head", None),
        P("batch", "ctx", "head", None),
        P("head", ("ctx", "batch"), None),
        P("head", ("ctx", "batch"), None),
        P("head", ("ctx", "batch"), None),
    )
    return jax.shard_map(local, mesh=mesh, in_specs=in_specs, out_specs=out_specs, check_vma=False)
```

```python
import functools
import math

import jax
import jax.numpy as jnp
from jax import lax
from jax.experimental import pallas as pl
from jax.experimental.pallas import tpu as pltpu
from jax.sharding import PartitionSpec as P

F32 = jnp.float32
BF16 = jnp.bfloat16
LANES = 128
VMEM_LIMIT = 24 * 1024 * 1024


def mm(a, b):
    return jnp.dot(a, b, preferred_element_type=F32)


def mm_t(a, b):
    return lax.dot_general(a, b, (((1,), (1,)), ((), ())), preferred_element_type=F32)


def tmm(a, b):
    return lax.dot_general(a, b, (((0,), (0,)), ((), ())), preferred_element_type=F32)


def call(body, out_shape, scratch, flops, *args):
    smem = pl.BlockSpec(memory_space=pltpu.SMEM)
    vmem = pl.BlockSpec(memory_space=pltpu.VMEM)
    size = sum(a.size * a.dtype.itemsize for a in args)
    size += sum(math.prod(o.shape) * o.dtype.itemsize for o in out_shape)
    return pl.pallas_call(
        body,
        out_shape=out_shape,
        in_specs=[smem if a.dtype == jnp.int32 else vmem for a in args],
        out_specs=[vmem] * len(out_shape),
        scratch_shapes=scratch,
        compiler_params=pltpu.CompilerParams(vmem_limit_bytes=VMEM_LIMIT),
        cost_estimate=pl.CostEstimate(flops=flops, bytes_accessed=size, transcendentals=0),
    )(*args)


def put_rows(scratch, x):
    for i in range(scratch.shape[0]):
        scratch[i] = x[:, i * LANES : (i + 1) * LANES]


def take_head(scratch, head, tokens, heads):
    parts = [scratch[i, pl.ds(head, tokens, stride=heads), :] for i in range(scratch.shape[0])]
    return jnp.concatenate(parts, axis=1)


def put_head(scratch, head, x, tokens, heads):
    for i in range(scratch.shape[0]):
        scratch[i, pl.ds(head, tokens, stride=heads), :] = x[:, i * LANES : (i + 1) * LANES]


def rows_of(scratch):
    return jnp.concatenate([scratch[i] for i in range(scratch.shape[0])], axis=1)


def split_kernel(groups, place, x, *rest):
    outs, scratch = rest[:groups], rest[groups]
    tokens, heads, width = x.shape
    put_rows(scratch, x[...].astype(F32).reshape(tokens * heads, width))
    for step in range(groups):
        outs[step][...] = take_head(scratch, place[0] ^ step, tokens, heads)


def split_scaled_kernel(groups, place, x, r, *rest):
    outs = rest[:groups]
    split_kernel(groups, place, x, *rest)
    for step in range(groups):
        scaled = outs[step][...] * rate_column(r, place[0] ^ step)
        outs[step][...] = scaled.astype(BF16).astype(F32)


def split_apply_kernel(groups, place, q, cot, gain, scale, *rest):
    outs, scale_row, scratch = rest[:groups], rest[groups], rest[groups + 1]
    scale_row[...] = jnp.broadcast_to(scale[...], scale_row.shape)
    split_kernel(groups, place, q, *[out.at[0] for out in outs], scratch)
    split_kernel(groups, place, cot, *[out.at[1] for out in outs], scratch)
    for step in range(groups):
        outs[step][1] *= gain[pl.ds(place[0] ^ step, 1), :]


def rate_column(r, head):
    return jnp.broadcast_to(r[pl.ds(head, 1), :], (8, r.shape[1])).T[:, 0:1]


def send_groups(count):
    odd = list(range(3, count, 2))
    return ([odd] if odd else []) + [[r] for r in [1] + list(range(2, count, 2)) if r < count] + [[0]]


def send_slices(sums, outs, own, count):
    rows = sums.shape[1] // count
    for out, members in zip(outs, send_groups(count)):
        for i, step in enumerate(members):
            at = pl.multiple_of((own ^ step) * rows, rows)
            out[i] = sums[:, pl.ds(at, rows), :]


def update_sums(keys_in, scaled_in, weights, key_kept, scaled_kept):
    gate_b, out_b, up_b = (w[...].astype(BF16) for w in weights)
    total = [0.0, 0.0, 0.0]
    for step, (key, value) in enumerate(zip(keys_in, scaled_in)):
        keys = key[...].astype(BF16)
        scaled = value[...].astype(BF16)
        key_kept[step] = keys
        scaled_kept[step] = scaled
        first = mm(keys, gate_b)
        third = mm(keys, up_b)
        sig = jax.nn.sigmoid(first)
        activ = first * sig
        act = (activ * third).astype(BF16)
        dact = mm_t(scaled, out_b)
        deriv = sig * (1.0 + first * (1.0 - sig))
        dfirst = (dact * third * deriv).astype(BF16)
        dthird = (dact * activ).astype(BF16)
        total[0] += tmm(keys, dfirst)
        total[1] += tmm(act, scaled)
        total[2] += tmm(keys, dthird)
    return total


def update_kernel(count, depth, scale, place, *refs):
    keys_in, scaled_in, weights = refs[:count], refs[count : 2 * count], refs[2 * count :][:3]
    key_kept, scaled_kept = refs[2 * count + 3 : 2 * count + 5]
    outs, sums = refs[2 * count + 5 : -1], refs[-1]
    total = update_sums(keys_in, scaled_in, weights, key_kept, scaled_kept)
    for i in range(3):
        sums[i] = total[i] * scale
    send_slices(sums, outs, place[1], depth)
    rows = sums.shape[1] // depth
    at = pl.multiple_of(place[1] * rows, rows)
    for i, w in enumerate(weights):
        outs[-1][0, i] += w[pl.ds(at, rows), :]


def assemble(place, parts, whole):
    rows = parts[0].shape[2]
    for step, part in enumerate(parts):
        at = pl.multiple_of((place[1] ^ step) * rows, rows)
        whole[:, pl.ds(at, rows), :] = part[0]


def apply_kernel(groups, depth, place, scale_row, *refs):
    pieces = refs[:groups]
    parts = refs[groups : groups + depth]
    activ_ref, slope_ref, hidden_ref, os_ref, new_b, stats, whole = refs[groups + depth :]
    assemble(place, parts, whole)
    new_b[...] = whole[...].astype(BF16)
    for step in range(groups):
        queries = pieces[step][0].astype(BF16)
        tokens = queries.shape[0]
        first = mm(queries, new_b[0])
        third = mm(queries, new_b[2])
        sig = jax.nn.sigmoid(first)
        activ = first * sig
        hidden = (activ * third).astype(BF16)
        scaled = mm(hidden, new_b[1]) * scale_row[0:1, :]
        activ_ref[step] = activ
        slope_ref[step] = third * (sig * (1.0 + first * (1.0 - sig)))
        hidden_ref[step] = hidden
        os_ref[step] = scaled
        sq = jnp.sum(scaled * scaled, axis=1, keepdims=True)
        ps = jnp.sum(scaled * pieces[step][1], axis=1, keepdims=True)
        lane = lax.broadcasted_iota(jnp.int32, (tokens, LANES), 1)
        both = jnp.where(lane == 0, sq, jnp.where(lane == 1, ps, 0.0)).T
        source = place[0] ^ step
        stats[0, pl.ds(source, 1), :] = both[0:1, :]
        stats[1, pl.ds(source, 1), :] = both[1:2, :]


def apply_back_kernel(groups, depth, count, place, scale_row, *refs):
    pieces, stats = refs[:groups], refs[groups : 2 * groups]
    activ_ref, slope_ref, hidden_ref, os_ref, new_b = refs[2 * groups : 2 * groups + 5]
    outs = refs[2 * groups + 5 : 3 * groups + 5]
    slices, sums, both = refs[3 * groups + 5 : -2], refs[-2], refs[-1]
    total_stats = stats[0][...]
    for other in stats[1:]:
        total_stats += other[...]
    both[...] = total_stats
    total = [0.0, 0.0, 0.0]
    for step in range(groups):
        queries = pieces[step][0].astype(BF16)
        source = place[0] ^ step
        sq = rate_column(both.at[0], source)
        ps = rate_column(both.at[1], source)
        inv = lax.rsqrt(sq / count + 1e-06)
        dos = inv * pieces[step][1] - os_ref[step] * (inv * inv * inv * ps / count)
        dout = (dos * scale_row[0:1, :]).astype(BF16)
        dhidden = mm_t(dout, new_b[1])
        dthird = (dhidden * activ_ref[step]).astype(BF16)
        dfirst = (dhidden * slope_ref[step]).astype(BF16)
        outs[step][...] = mm_t(dfirst, new_b[0]) + mm_t(dthird, new_b[2])
        total[0] += tmm(queries, dfirst)
        total[1] += tmm(hidden_ref[step], dout)
        total[2] += tmm(queries, dthird)
    for i in range(3):
        sums[i] = total[i]
    send_slices(sums, slices, place[1], depth)


def update_keep_kernel(k_kept, s_kept, w_gate, w_out, w_up, *outs):
    dact_r, third_r, activ_r, deriv_r, slope_r, second_r, dfirst_r, dthird_r, act_r = outs
    gate_b, out_b, up_b = (w[...].astype(BF16) for w in (w_gate, w_out, w_up))
    for step in range(k_kept.shape[0]):
        keys, scaled = k_kept[step], s_kept[step]
        first = mm(keys, gate_b)
        third = mm(keys, up_b)
        dact = mm_t(scaled, out_b)
        sig = jax.nn.sigmoid(first)
        activ = first * sig
        slope = sig * (1.0 - sig)
        deriv = sig + first * slope
        third_deriv = third * deriv
        dact_r[step] = dact
        third_r[step] = third
        activ_r[step] = activ
        deriv_r[step] = deriv
        slope_r[step] = third_deriv
        second_r[step] = third * (slope * (2.0 + first * (1.0 - 2.0 * sig)))
        dfirst_r[step] = (dact * third_deriv).astype(BF16)
        dthird_r[step] = (dact * activ).astype(BF16)
        act_r[step] = (activ * third).astype(BF16)


def update_back_kernel(groups, depth, scale, place, *refs):
    (k_kept, s_kept), refs = refs[:2], refs[2:]
    kept, refs = refs[:9], refs[9:]
    dact_r, third_r, activ_r, deriv_r, slope_r, second_r, dfirst_r, dthird_r, act_r = kept
    parts, refs = refs[:depth], refs[depth:]
    w_gate, w_out, w_up = refs[:3]
    outs, slices = refs[3 : groups + 3], refs[groups + 3 : -2]
    whole, sums = refs[-2:]
    assemble(place, parts, whole)
    gate_b, out_b, up_b = (w[...].astype(BF16) for w in (w_gate, w_out, w_up))
    cot_gate, cot_out, cot_up = ((whole[i] * scale).astype(BF16) for i in range(3))
    total = [0.0, 0.0, 0.0]
    for step in range(groups):
        keys, scaled = k_kept[step], s_kept[step]
        bar_dfirst = mm(keys, cot_gate)
        bar_dthird = mm(keys, cot_up)
        bar_act = mm_t(scaled, cot_out)
        dact, activ, deriv = dact_r[step], activ_r[step], deriv_r[step]
        bar_activ = bar_dthird * dact + bar_act * third_r[step]
        bar_dact = (bar_dfirst * slope_r[step] + bar_dthird * activ).astype(BF16)
        bar_df_dact = bar_dfirst * dact
        bar_third = (bar_df_dact * deriv + bar_act * activ).astype(BF16)
        bar_first = (bar_activ * deriv + bar_df_dact * second_r[step]).astype(BF16)
        outs[step][0] = (
            mm_t(dfirst_r[step], cot_gate)
            + mm_t(dthird_r[step], cot_up)
            + mm_t(bar_first, gate_b)
            + mm_t(bar_third, up_b)
        )
        outs[step][1] = mm(act_r[step], cot_out) + mm(bar_dact, out_b)
        total[0] += tmm(keys, bar_first)
        total[1] += tmm(bar_dact, scaled)
        total[2] += tmm(keys, bar_third)
    for i in range(3):
        sums[i] = total[i]
    send_slices(sums, slices, place[1], depth)


def join_query_kernel(groups, place, *refs):
    pieces, out, scratch = refs[:groups], refs[groups], refs[groups + 1]
    tokens, heads, width = out.shape
    for step, piece in enumerate(pieces):
        put_head(scratch, place[0] ^ step, piece[...], tokens, heads)
    out[...] = rows_of(scratch).reshape(tokens, heads, width).astype(BF16)


def join_update_kernel(groups, place, r, *refs):
    pieces, parts = refs[:groups], refs[groups : 2 * groups]
    out_k, out_v = refs[2 * groups : 2 * groups + 2]
    grads, (sk, sv) = refs[2 * groups + 2 : -2], refs[-2:]
    tokens, heads, width = out_k.shape
    for step, piece in enumerate(pieces):
        head = place[0] ^ step
        put_head(sk, head, piece[0], tokens, heads)
        put_head(sv, head, piece[1] * rate_column(r, head), tokens, heads)
        for i, grad in enumerate(grads):
            grad[head] = parts[step][0, i]
    out_k[...] = rows_of(sk).reshape(tokens, heads, width).astype(BF16)
    out_v[...] = rows_of(sv).reshape(tokens, heads, width).astype(BF16)


def rows_kernel(groups, place, *refs):
    parts, outs, total = refs[: -groups - 1], refs[-groups - 1 : -1], refs[-1]
    summed = parts[0][0]
    for part in parts[1:]:
        summed += part[0]
    total[...] = summed
    rows = total.shape[1] // groups
    for step, out in enumerate(outs):
        at = pl.multiple_of((place[0] ^ step) * rows, rows)
        out[0] = total[:, pl.ds(at, rows), :]


def local(queries, keys, values, rates, head_scale, gain, w_gate, w_out, w_up, cotangent):
    tokens, heads, width = keys.shape[1:]
    hidden = w_gate.shape[2]
    ctx = lax.axis_size("ctx")
    head_axis = lax.axis_size("head")
    groups = heads
    depth = ctx // groups
    assert groups & (groups - 1) == 0 and depth & (depth - 1) == 0
    scale = 1.0 / math.sqrt(tokens * ctx * width)
    count = float(heads * head_axis * width)
    me = lax.axis_index("ctx")
    mine, layer = lax.rem(me, groups), lax.div(me, groups)
    place = jnp.stack([mine, layer]).astype(jnp.int32)

    def move(x, axis, step):
        return lax.ppermute(x, axis, [(c, c ^ step) for c in range(lax.axis_size(axis))])

    def in_plane(parts):
        return [parts[0]] + [move(p, "ctx", step) for step, p in enumerate(parts) if step]

    def forwarded(got):
        return [got[:1]] if got.shape[0] == 1 else [got[i : i + 1] for i in range(got.shape[0])]

    def scatter(outs, count, unit, one_by_one=True):
        outs = list(outs)
        evens = list(range(2, count, 2))
        via = forwarded(move(outs.pop(0), "ctx", unit)) if evens else []
        if one_by_one:
            via, outs[0] = after(via, outs[0])
        first = [move(outs[0], "ctx", unit)] if count > 1 else []
        even = [move(p + v, "ctx", r * unit) for p, v, r in zip(outs[1:], via, evens)]
        return [outs[-1]] + first + even

    def gather(part, count, unit):
        got = [part] * count
        for r in [2 * i for i in range(1, count // 2)]:
            got[r] = move(part, "ctx", r * unit)
            got[r + 1] = move(got[r], "ctx", unit)
        if count > 1:
            got[1] = move(part, "ctx", unit)
        return got

    def after(x, *others):
        return lax.optimization_barrier((x, *others))

    def shape(*dims, dtype=F32):
        return jax.ShapeDtypeStruct(dims, dtype)

    flops = 2 * groups * tokens * width * hidden
    pieces = [shape(tokens, width)] * groups
    slices = [shape(len(m), 3, hidden // depth, width) for m in send_groups(depth)]
    joined = shape(tokens, heads, width, dtype=BF16)
    scratch = pltpu.VMEM((width // LANES, tokens * heads, LANES), F32)
    square = pltpu.VMEM((3, hidden, width), F32)

    def split(body, *args):
        return call(functools.partial(body, groups), pieces, [scratch], 16 * flops, place, *args)

    k_in = in_plane(split(split_kernel, keys[0]))
    s_in = in_plane(split(split_scaled_kernel, values[0], rates[0]))
    own = [lax.dynamic_index_in_dim(w, mine, 0, keepdims=False) for w in (w_gate, w_out, w_up)]
    own_scale = lax.dynamic_index_in_dim(head_scale, mine, 0, keepdims=True)[None, :]
    k_in, s_in, queries, cotangent = after(k_in, s_in, queries, cotangent)

    def kept(*dims, dtype=F32):
        return shape(*dims, tokens, width, dtype=dtype)

    out = call(
        functools.partial(update_kernel, groups, depth, scale),
        [kept(groups, dtype=BF16)] * 2 + slices, [square], 6 * flops,
        place, *k_in, *s_in, *own,
    )
    early, terms = out[:2], out[2:]
    *q_out, scale_row = call(
        functools.partial(split_apply_kernel, groups),
        [shape(2, tokens, width)] * groups + [shape(8, width)],
        [scratch], flops // 8, place, queries[0], cotangent[0], gain, own_scale,
    )
    q_in = in_plane(q_out)
    new = functools.reduce(jnp.add, scatter(terms, depth, groups))
    new = gather(new, depth, groups)
    *passed, stats = call(
        functools.partial(apply_kernel, groups, depth),
        [kept(groups), kept(groups), kept(groups, dtype=BF16), kept(groups)]
        + [shape(3, hidden, width, dtype=BF16), shape(2, groups, tokens)],
        [square], 3 * flops, place, scale_row, *q_in, *new,
    )
    bit = 1
    while bit < head_axis:
        stats = stats + move(stats, "head", bit)
        bit *= 2
    out = call(
        functools.partial(apply_back_kernel, groups, depth, count), pieces + slices,
        [square, pltpu.VMEM((2, groups, tokens), F32)], 6 * flops,
        place, scale_row, *q_in, *in_plane([stats] * groups), *passed,
    )
    out, early = after(out, early)
    saved = call(
        update_keep_kernel, [kept(groups)] * 6 + [kept(groups, dtype=BF16)] * 3, [], 3 * flops,
        *early, *own,
    )
    part = functools.reduce(jnp.add, scatter(out[groups:], depth, groups))
    parts = gather(part, depth, groups)
    (grad_q,) = call(
        functools.partial(join_query_kernel, groups), [joined], [scratch], flops // 16,
        place, *in_plane(out[:groups]),
    )
    parts, grad_q, saved = after(parts, grad_q, saved)
    rows = hidden // depth
    out = call(
        functools.partial(update_back_kernel, groups, depth, scale),
        [shape(2, tokens, width)] * groups + slices, [square] * 2, 12 * flops,
        place, *early, *saved, *parts, *own,
    )
    back = in_plane(out[:groups])
    ends = scatter(out[groups:], depth, groups, one_by_one=False)
    own_rows = rows // groups
    sent = call(
        functools.partial(rows_kernel, groups),
        [shape(1, 3, own_rows, width)] * groups,
        [pltpu.VMEM((3, rows, width), F32)], flops // 100, place, part, *ends,
    )
    grad_k, grad_v, *grads = call(
        functools.partial(join_update_kernel, groups),
        [joined] * 2 + [shape(heads, own_rows, width)] * 3, [scratch] * 2, flops // 8,
        place, rates[0], *back, *in_plane(sent),
    )
    if lax.axis_size("batch") > 1:
        grads = [lax.psum_scatter(x, "batch", scatter_dimension=1, tiled=True) for x in grads]
    return (grad_q[None], grad_k[None], grad_v[None], grads[0], grads[1], grads[2])


def solution(mesh):
    in_specs = (
        P("batch", "ctx", "head", None),
        P("batch", "ctx", "head", None),
        P("batch", "ctx", "head", None),
        P("batch", "head", "ctx"),
        P("head"),
        P("head", None),
        P("head", None, None),
        P("head", None, None),
        P("head", None, None),
        P("batch", "ctx", "head", None),
    )
    out_specs = (
        P("batch", "ctx", "head", None),
        P("batch", "ctx", "head", None),
        P("batch", "ctx", "head", None),
        P("head", ("ctx", "batch"), None),
        P("head", ("ctx", "batch"), None),
        P("head", ("ctx", "batch"), None),
    )
    return jax.shard_map(local, mesh=mesh, in_specs=in_specs, out_specs=out_specs, check_vma=False)
```

```python
import functools
import math

import jax
import jax.numpy as jnp
from jax import lax
from jax.experimental import pallas as pl
from jax.experimental.pallas import tpu as pltpu
from jax.sharding import PartitionSpec as P

F32 = jnp.float32
BF16 = jnp.bfloat16
LANES = 128
VMEM_LIMIT = 24 * 1024 * 1024


def mm(a, b):
    return jnp.dot(a, b, preferred_element_type=F32)


def mm_t(a, b):
    return lax.dot_general(a, b, (((1,), (1,)), ((), ())), preferred_element_type=F32)


def tmm(a, b):
    return lax.dot_general(a, b, (((0,), (0,)), ((), ())), preferred_element_type=F32)


def call(body, out_shape, scratch, flops, *args):
    smem = pl.BlockSpec(memory_space=pltpu.SMEM)
    vmem = pl.BlockSpec(memory_space=pltpu.VMEM)
    size = sum(a.size * a.dtype.itemsize for a in args)
    size += sum(math.prod(o.shape) * o.dtype.itemsize for o in out_shape)
    return pl.pallas_call(
        body,
        out_shape=out_shape,
        in_specs=[smem if a.dtype == jnp.int32 else vmem for a in args],
        out_specs=[vmem] * len(out_shape),
        scratch_shapes=scratch,
        compiler_params=pltpu.CompilerParams(vmem_limit_bytes=VMEM_LIMIT),
        cost_estimate=pl.CostEstimate(flops=flops, bytes_accessed=size, transcendentals=0),
    )(*args)


def put_rows(scratch, x):
    for i in range(scratch.shape[0]):
        scratch[i] = x[:, i * LANES : (i + 1) * LANES]


def take_head(scratch, head, tokens, heads):
    parts = [scratch[i, pl.ds(head, tokens, stride=heads), :] for i in range(scratch.shape[0])]
    return jnp.concatenate(parts, axis=1)


def put_head(scratch, head, x, tokens, heads):
    for i in range(scratch.shape[0]):
        scratch[i, pl.ds(head, tokens, stride=heads), :] = x[:, i * LANES : (i + 1) * LANES]


def rows_of(scratch):
    return jnp.concatenate([scratch[i] for i in range(scratch.shape[0])], axis=1)


def split_kernel(groups, place, x, *rest):
    outs, scratch = rest[:groups], rest[groups]
    tokens, heads, width = x.shape
    put_rows(scratch, x[...].astype(F32).reshape(tokens * heads, width))
    for step in range(groups):
        outs[step][...] = take_head(scratch, place[0] ^ step, tokens, heads)


def split_scaled_kernel(groups, place, x, r, *rest):
    outs = rest[:groups]
    split_kernel(groups, place, x, *rest)
    for step in range(groups):
        scaled = outs[step][...] * rate_column(r, place[0] ^ step)
        outs[step][...] = scaled.astype(BF16).astype(F32)


def split_apply_kernel(groups, place, q, cot, gain, scale, *rest):
    outs, scale_row, scratch = rest[:groups], rest[groups], rest[groups + 1]
    scale_row[...] = jnp.broadcast_to(scale[...], scale_row.shape)
    split_kernel(groups, place, q, *[out.at[0] for out in outs], scratch)
    split_kernel(groups, place, cot, *[out.at[1] for out in outs], scratch)
    for step in range(groups):
        outs[step][1] *= gain[pl.ds(place[0] ^ step, 1), :]


def rate_column(r, head):
    return jnp.broadcast_to(r[pl.ds(head, 1), :], (8, r.shape[1])).T[:, 0:1]


def send_groups(count):
    odd = list(range(3, count, 2))
    return ([odd] if odd else []) + [[r] for r in [1] + list(range(2, count, 2)) if r < count] + [[0]]


def send_slices(sums, outs, own, count):
    rows = sums.shape[1] // count
    for out, members in zip(outs, send_groups(count)):
        for i, step in enumerate(members):
            at = pl.multiple_of((own ^ step) * rows, rows)
            out[i] = sums[:, pl.ds(at, rows), :]


def update_sums(keys_in, scaled_in, weights, key_kept, scaled_kept):
    gate_b, out_b, up_b = (w[...].astype(BF16) for w in weights)
    total = [0.0, 0.0, 0.0]
    for step, (key, value) in enumerate(zip(keys_in, scaled_in)):
        keys = key[...].astype(BF16)
        scaled = value[...].astype(BF16)
        key_kept[step] = keys
        scaled_kept[step] = scaled
        first = mm(keys, gate_b)
        third = mm(keys, up_b)
        sig = jax.nn.sigmoid(first)
        activ = first * sig
        act = (activ * third).astype(BF16)
        dact = mm_t(scaled, out_b)
        deriv = sig * (1.0 + first * (1.0 - sig))
        dfirst = (dact * third * deriv).astype(BF16)
        dthird = (dact * activ).astype(BF16)
        total[0] += tmm(keys, dfirst)
        total[1] += tmm(act, scaled)
        total[2] += tmm(keys, dthird)
    return total


def update_kernel(count, depth, scale, place, *refs):
    keys_in, scaled_in, weights = refs[:count], refs[count : 2 * count], refs[2 * count :][:3]
    key_kept, scaled_kept = refs[2 * count + 3 : 2 * count + 5]
    outs, sums = refs[2 * count + 5 : -1], refs[-1]
    total = update_sums(keys_in, scaled_in, weights, key_kept, scaled_kept)
    for i in range(3):
        sums[i] = total[i] * scale
    send_slices(sums, outs, place[1], depth)
    rows = sums.shape[1] // depth
    at = pl.multiple_of(place[1] * rows, rows)
    for i, w in enumerate(weights):
        outs[-1][0, i] += w[pl.ds(at, rows), :]


def assemble(place, parts, whole):
    rows = parts[0].shape[2]
    for step, part in enumerate(parts):
        at = pl.multiple_of((place[1] ^ step) * rows, rows)
        whole[:, pl.ds(at, rows), :] = part[0]


def apply_kernel(groups, depth, place, scale_row, *refs):
    pieces = refs[:groups]
    parts = refs[groups : groups + depth]
    activ_ref, slope_ref, hidden_ref, os_ref, new_b, stats, whole = refs[groups + depth :]
    assemble(place, parts, whole)
    new_b[...] = whole[...].astype(BF16)
    for step in range(groups):
        queries = pieces[step][0].astype(BF16)
        tokens = queries.shape[0]
        first = mm(queries, new_b[0])
        third = mm(queries, new_b[2])
        sig = jax.nn.sigmoid(first)
        activ = first * sig
        hidden = (activ * third).astype(BF16)
        scaled = mm(hidden, new_b[1]) * scale_row[0:1, :]
        activ_ref[step] = activ
        slope_ref[step] = third * (sig * (1.0 + first * (1.0 - sig)))
        hidden_ref[step] = hidden
        os_ref[step] = scaled
        sq = jnp.sum(scaled * scaled, axis=1, keepdims=True)
        ps = jnp.sum(scaled * pieces[step][1], axis=1, keepdims=True)
        lane = lax.broadcasted_iota(jnp.int32, (tokens, LANES), 1)
        both = jnp.where(lane == 0, sq, jnp.where(lane == 1, ps, 0.0)).T
        source = place[0] ^ step
        stats[0, pl.ds(source, 1), :] = both[0:1, :]
        stats[1, pl.ds(source, 1), :] = both[1:2, :]


def apply_back_kernel(groups, depth, count, place, scale_row, *refs):
    pieces, stats = refs[:groups], refs[groups : 2 * groups]
    activ_ref, slope_ref, hidden_ref, os_ref, new_b = refs[2 * groups : 2 * groups + 5]
    outs = refs[2 * groups + 5 : 3 * groups + 5]
    slices, sums, both = refs[3 * groups + 5 : -2], refs[-2], refs[-1]
    total_stats = stats[0][...]
    for other in stats[1:]:
        total_stats += other[...]
    both[...] = total_stats
    total = [0.0, 0.0, 0.0]
    for step in range(groups):
        queries = pieces[step][0].astype(BF16)
        source = place[0] ^ step
        sq = rate_column(both.at[0], source)
        ps = rate_column(both.at[1], source)
        inv = lax.rsqrt(sq / count + 1e-06)
        dos = inv * pieces[step][1] - os_ref[step] * (inv * inv * inv * ps / count)
        dout = (dos * scale_row[0:1, :]).astype(BF16)
        dhidden = mm_t(dout, new_b[1])
        dthird = (dhidden * activ_ref[step]).astype(BF16)
        dfirst = (dhidden * slope_ref[step]).astype(BF16)
        outs[step][...] = mm_t(dfirst, new_b[0]) + mm_t(dthird, new_b[2])
        total[0] += tmm(queries, dfirst)
        total[1] += tmm(hidden_ref[step], dout)
        total[2] += tmm(queries, dthird)
    for i in range(3):
        sums[i] = total[i]
    send_slices(sums, slices, place[1], depth)


def update_keep_kernel(k_kept, s_kept, w_gate, w_out, w_up, *outs):
    dact_r, third_r, activ_r, deriv_r, slope_r, second_r, dfirst_r, dthird_r, act_r = outs
    gate_b, out_b, up_b = (w[...].astype(BF16) for w in (w_gate, w_out, w_up))
    for step in range(k_kept.shape[0]):
        keys, scaled = k_kept[step], s_kept[step]
        first = mm(keys, gate_b)
        third = mm(keys, up_b)
        dact = mm_t(scaled, out_b)
        sig = jax.nn.sigmoid(first)
        activ = first * sig
        slope = sig * (1.0 - sig)
        deriv = sig + first * slope
        third_deriv = third * deriv
        dact_r[step] = dact
        third_r[step] = third
        activ_r[step] = activ
        deriv_r[step] = deriv
        slope_r[step] = third_deriv
        second_r[step] = third * (slope * (2.0 + first * (1.0 - 2.0 * sig)))
        dfirst_r[step] = (dact * third_deriv).astype(BF16)
        dthird_r[step] = (dact * activ).astype(BF16)
        act_r[step] = (activ * third).astype(BF16)


def update_back_kernel(groups, depth, scale, place, *refs):
    (k_kept, s_kept), refs = refs[:2], refs[2:]
    kept, refs = refs[:9], refs[9:]
    dact_r, third_r, activ_r, deriv_r, slope_r, second_r, dfirst_r, dthird_r, act_r = kept
    parts, refs = refs[:depth], refs[depth:]
    w_gate, w_out, w_up = refs[:3]
    outs, slices = refs[3 : groups + 3], refs[groups + 3 : -2]
    whole, sums = refs[-2:]
    assemble(place, parts, whole)
    gate_b, out_b, up_b = (w[...].astype(BF16) for w in (w_gate, w_out, w_up))
    cot_gate, cot_out, cot_up = ((whole[i] * scale).astype(BF16) for i in range(3))
    total = [0.0, 0.0, 0.0]
    for step in range(groups):
        keys, scaled = k_kept[step], s_kept[step]
        bar_dfirst = mm(keys, cot_gate)
        bar_dthird = mm(keys, cot_up)
        bar_act = mm_t(scaled, cot_out)
        dact, activ, deriv = dact_r[step], activ_r[step], deriv_r[step]
        bar_activ = bar_dthird * dact + bar_act * third_r[step]
        bar_dact = (bar_dfirst * slope_r[step] + bar_dthird * activ).astype(BF16)
        bar_df_dact = bar_dfirst * dact
        bar_third = (bar_df_dact * deriv + bar_act * activ).astype(BF16)
        bar_first = (bar_activ * deriv + bar_df_dact * second_r[step]).astype(BF16)
        outs[step][0] = (
            mm_t(dfirst_r[step], cot_gate)
            + mm_t(dthird_r[step], cot_up)
            + mm_t(bar_first, gate_b)
            + mm_t(bar_third, up_b)
        )
        outs[step][1] = mm(act_r[step], cot_out) + mm(bar_dact, out_b)
        total[0] += tmm(keys, bar_first)
        total[1] += tmm(bar_dact, scaled)
        total[2] += tmm(keys, bar_third)
    for i in range(3):
        sums[i] = total[i]
    send_slices(sums, slices, place[1], depth)


def join_query_kernel(groups, place, *refs):
    pieces, out, scratch = refs[:groups], refs[groups], refs[groups + 1]
    tokens, heads, width = out.shape
    for step, piece in enumerate(pieces):
        put_head(scratch, place[0] ^ step, piece[...], tokens, heads)
    out[...] = rows_of(scratch).reshape(tokens, heads, width).astype(BF16)


def join_update_kernel(groups, place, r, *refs):
    pieces, parts = refs[:groups], refs[groups : 2 * groups]
    out_k, out_v = refs[2 * groups : 2 * groups + 2]
    grads, (sk, sv) = refs[2 * groups + 2 : -2], refs[-2:]
    tokens, heads, width = out_k.shape
    for step, piece in enumerate(pieces):
        head = place[0] ^ step
        put_head(sk, head, piece[0], tokens, heads)
        put_head(sv, head, piece[1] * rate_column(r, head), tokens, heads)
        for i, grad in enumerate(grads):
            grad[head] = parts[step][0, i]
    out_k[...] = rows_of(sk).reshape(tokens, heads, width).astype(BF16)
    out_v[...] = rows_of(sv).reshape(tokens, heads, width).astype(BF16)


def rows_kernel(groups, place, *refs):
    parts, outs, total = refs[: -groups - 1], refs[-groups - 1 : -1], refs[-1]
    summed = parts[0][0]
    for part in parts[1:]:
        summed += part[0]
    total[...] = summed
    rows = total.shape[1] // groups
    for step, out in enumerate(outs):
        at = pl.multiple_of((place[0] ^ step) * rows, rows)
        out[0] = total[:, pl.ds(at, rows), :]


def local(queries, keys, values, rates, head_scale, gain, w_gate, w_out, w_up, cotangent):
    tokens, heads, width = keys.shape[1:]
    hidden = w_gate.shape[2]
    ctx = lax.axis_size("ctx")
    head_axis = lax.axis_size("head")
    groups = heads
    depth = ctx // groups
    assert groups & (groups - 1) == 0 and depth & (depth - 1) == 0
    scale = 1.0 / math.sqrt(tokens * ctx * width)
    count = float(heads * head_axis * width)
    me = lax.axis_index("ctx")
    mine, layer = lax.rem(me, groups), lax.div(me, groups)
    place = jnp.stack([mine, layer]).astype(jnp.int32)

    def move(x, axis, step):
        return lax.ppermute(x, axis, [(c, c ^ step) for c in range(lax.axis_size(axis))])

    def in_plane(parts):
        return [parts[0]] + [move(p, "ctx", step) for step, p in enumerate(parts) if step]

    def forwarded(got):
        return [got[:1]] if got.shape[0] == 1 else [got[i : i + 1] for i in range(got.shape[0])]

    def scatter(outs, count, unit):
        outs = list(outs)
        evens = list(range(2, count, 2))
        via = forwarded(move(outs.pop(0), "ctx", unit)) if evens else []
        via, outs[0] = after(via, outs[0])
        first = [move(outs[0], "ctx", unit)] if count > 1 else []
        even = [move(p + v, "ctx", r * unit) for p, v, r in zip(outs[1:], via, evens)]
        return [outs[-1]] + first + even

    def gather(part, count, unit, beside):
        got = [part] * count
        evens = range(2, count, 2)
        for r in evens:
            got[r] = move(part, "ctx", r * unit)
        if count > 1:
            got[1] = move(part, "ctx", unit)
        got, beside = after(got, beside)
        for r in evens:
            got[r + 1] = move(got[r], "ctx", unit)
        return got, beside

    def after(x, *others):
        return lax.optimization_barrier((x, *others))

    def shape(*dims, dtype=F32):
        return jax.ShapeDtypeStruct(dims, dtype)

    flops = 2 * groups * tokens * width * hidden
    pieces = [shape(tokens, width)] * groups
    slices = [shape(len(m), 3, hidden // depth, width) for m in send_groups(depth)]
    joined = shape(tokens, heads, width, dtype=BF16)
    scratch = pltpu.VMEM((width // LANES, tokens * heads, LANES), F32)
    square = pltpu.VMEM((3, hidden, width), F32)

    def split(body, *args):
        return call(functools.partial(body, groups), pieces, [scratch], 16 * flops, place, *args)

    k_in = in_plane(split(split_kernel, keys[0]))
    s_in = in_plane(split(split_scaled_kernel, values[0], rates[0]))
    own = [lax.dynamic_index_in_dim(w, mine, 0, keepdims=False) for w in (w_gate, w_out, w_up)]
    own_scale = lax.dynamic_index_in_dim(head_scale, mine, 0, keepdims=True)[None, :]
    *q_out, scale_row = call(
        functools.partial(split_apply_kernel, groups),
        [shape(2, tokens, width)] * groups + [shape(8, width)],
        [scratch], flops // 8, place, queries[0], cotangent[0], gain, own_scale,
    )
    k_in, s_in, q_out = after(k_in, s_in, q_out)

    def kept(*dims, dtype=F32):
        return shape(*dims, tokens, width, dtype=dtype)

    out = call(
        functools.partial(update_kernel, groups, depth, scale),
        [kept(groups, dtype=BF16)] * 2 + slices, [square], 6 * flops,
        place, *k_in, *s_in, *own,
    )
    early, terms = out[:2], out[2:]
    q_in = in_plane(q_out)
    new = functools.reduce(jnp.add, scatter(terms, depth, groups))
    new, q_in[:-1] = after(new, q_in[:-1])
    new, q_in[-1] = gather(new, depth, groups, q_in[-1])
    *passed, stats = call(
        functools.partial(apply_kernel, groups, depth),
        [kept(groups), kept(groups), kept(groups, dtype=BF16), kept(groups)]
        + [shape(3, hidden, width, dtype=BF16), shape(2, groups, tokens)],
        [square], 3 * flops, place, scale_row, *q_in, *new,
    )
    bit = 1
    while bit < head_axis:
        stats = stats + move(stats, "head", bit)
        bit *= 2
    out = call(
        functools.partial(apply_back_kernel, groups, depth, count), pieces + slices,
        [square, pltpu.VMEM((2, groups, tokens), F32)], 6 * flops,
        place, scale_row, *q_in, *in_plane([stats] * groups), *passed,
    )
    out, early = after(out, early)
    saved = call(
        update_keep_kernel, [kept(groups)] * 6 + [kept(groups, dtype=BF16)] * 3, [], 3 * flops,
        *early, *own,
    )
    part = functools.reduce(jnp.add, scatter(out[groups:], depth, groups))
    parts, q_back = gather(part, depth, groups, in_plane(out[:groups]))
    (grad_q,) = call(
        functools.partial(join_query_kernel, groups), [joined], [scratch], flops // 16,
        place, *q_back,
    )
    parts, grad_q, saved = after(parts, grad_q, saved)
    rows = hidden // depth
    out = call(
        functools.partial(update_back_kernel, groups, depth, scale),
        [shape(2, tokens, width)] * groups + slices, [square] * 2, 12 * flops,
        place, *early, *saved, *parts, *own,
    )
    back = in_plane(out[:groups])
    ends = scatter(out[groups:], depth, groups)
    own_rows = rows // groups
    sent = call(
        functools.partial(rows_kernel, groups),
        [shape(1, 3, own_rows, width)] * groups,
        [pltpu.VMEM((3, rows, width), F32)], flops // 100, place, part, *ends,
    )
    grad_k, grad_v, *grads = call(
        functools.partial(join_update_kernel, groups),
        [joined] * 2 + [shape(heads, own_rows, width)] * 3, [scratch] * 2, flops // 8,
        place, rates[0], *back, *in_plane(sent),
    )
    if lax.axis_size("batch") > 1:
        grads = [lax.psum_scatter(x, "batch", scatter_dimension=1, tiled=True) for x in grads]
    return (grad_q[None], grad_k[None], grad_v[None], grads[0], grads[1], grads[2])


def solution(mesh):
    in_specs = (
        P("batch", "ctx", "head", None),
        P("batch", "ctx", "head", None),
        P("batch", "ctx", "head", None),
        P("batch", "head", "ctx"),
        P("head"),
        P("head", None),
        P("head", None, None),
        P("head", None, None),
        P("head", None, None),
        P("batch", "ctx", "head", None),
    )
    out_specs = (
        P("batch", "ctx", "head", None),
        P("batch", "ctx", "head", None),
        P("batch", "ctx", "head", None),
        P("head", ("ctx", "batch"), None),
        P("head", ("ctx", "batch"), None),
        P("head", ("ctx", "batch"), None),
    )
    return jax.shard_map(local, mesh=mesh, in_specs=in_specs, out_specs=out_specs, check_vma=False)
```

```python
import functools
import math

import jax
import jax.numpy as jnp
from jax import lax
from jax.experimental import pallas as pl
from jax.experimental.pallas import tpu as pltpu
from jax.sharding import PartitionSpec as P

F32 = jnp.float32
BF16 = jnp.bfloat16
LANES = 128
VMEM_LIMIT = 24 * 1024 * 1024


def mm(a, b):
    return jnp.dot(a, b, preferred_element_type=F32)


def mm_t(a, b):
    return lax.dot_general(a, b, (((1,), (1,)), ((), ())), preferred_element_type=F32)


def tmm(a, b):
    return lax.dot_general(a, b, (((0,), (0,)), ((), ())), preferred_element_type=F32)


def call(body, out_shape, scratch, flops, *args, final=False):
    smem = pl.BlockSpec(memory_space=pltpu.SMEM)
    vmem = pl.BlockSpec(memory_space=pltpu.VMEM)
    size = sum(a.size * a.dtype.itemsize for a in args)
    size += sum(math.prod(o.shape) * o.dtype.itemsize for o in out_shape)
    return pl.pallas_call(
        body,
        out_shape=out_shape if final else [pltpu.VMEM(o.shape, o.dtype) for o in out_shape],
        in_specs=[smem if a.dtype == jnp.int32 else vmem for a in args],
        out_specs=[vmem] * len(out_shape),
        scratch_shapes=scratch,
        compiler_params=pltpu.CompilerParams(vmem_limit_bytes=VMEM_LIMIT),
        cost_estimate=pl.CostEstimate(flops=flops, bytes_accessed=size, transcendentals=0),
    )(*args)


def put_rows(scratch, x):
    for i in range(scratch.shape[0]):
        scratch[i] = x[:, i * LANES : (i + 1) * LANES]


def take_head(scratch, head, tokens, heads):
    parts = [scratch[i, pl.ds(head, tokens, stride=heads), :] for i in range(scratch.shape[0])]
    return jnp.concatenate(parts, axis=1)


def put_head(scratch, head, x, tokens, heads):
    for i in range(scratch.shape[0]):
        scratch[i, pl.ds(head, tokens, stride=heads), :] = x[:, i * LANES : (i + 1) * LANES]


def rows_of(scratch):
    return jnp.concatenate([scratch[i] for i in range(scratch.shape[0])], axis=1)


def split_kernel(groups, place, x, *rest):
    outs, scratch = rest[:groups], rest[groups]
    tokens, heads, width = x.shape
    put_rows(scratch, x[...].astype(F32).reshape(tokens * heads, width))
    for step in range(groups):
        outs[step][...] = take_head(scratch, place[0] ^ step, tokens, heads)


def split_scaled_kernel(groups, place, x, r, *rest):
    outs = rest[:groups]
    split_kernel(groups, place, x, *rest)
    for step in range(groups):
        scaled = outs[step][...] * rate_column(r, place[0] ^ step)
        outs[step][...] = scaled.astype(BF16).astype(F32)


def packing(groups):
    if groups == 4:
        return [[(0, 0), (0, 1)], [(1, 0), (1, 1), (3, 0)], [(2, 0), (2, 1), (3, 1)]]
    return [[(step, 0), (step, 1)] for step in range(groups)]


def unpacked(groups, refs):
    found = {}
    for ref, members in zip(refs, packing(groups)):
        for i, member in enumerate(members):
            found[member] = ref.at[i]
    for i, ref in enumerate(refs[len(packing(groups)) :]):
        found[(groups - 1, i)] = ref
    return [found[(step, 0)] for step in range(groups)], [found[(step, 1)] for step in range(groups)]


def split_apply_kernel(groups, place, q, cot, gain, scale, *rest):
    outs, scale_row, scratch = rest[:-2], rest[-2], rest[-1]
    scale_row[...] = jnp.broadcast_to(scale[...], scale_row.shape)
    to_q, to_dyg = unpacked(groups, outs)
    split_kernel(groups, place, q, *to_q, scratch)
    split_kernel(groups, place, cot, *to_dyg, scratch)
    for step in range(groups):
        to_dyg[step][...] *= gain[pl.ds(place[0] ^ step, 1), :]


def packed_count(groups):
    return len(packing(groups)) + 2 * (groups == 4)


def rate_column(r, head):
    return jnp.broadcast_to(r[pl.ds(head, 1), :], (8, r.shape[1])).T[:, 0:1]


def send_groups(count):
    odd = list(range(3, count, 2))
    return ([odd] if odd else []) + [[r] for r in [1] + list(range(2, count, 2)) if r < count] + [[0]]


def send_slices(sums, outs, own, count):
    rows = sums.shape[1] // count
    for out, members in zip(outs, send_groups(count)):
        for i, step in enumerate(members):
            at = pl.multiple_of((own ^ step) * rows, rows)
            out[i] = sums[:, pl.ds(at, rows), :]


def update_sums(keys_in, scaled_in, weights, key_kept, scaled_kept):
    gate_b, out_b, up_b = (w[...].astype(BF16) for w in weights)
    total = [0.0, 0.0, 0.0]
    for step, (key, value) in enumerate(zip(keys_in, scaled_in)):
        keys = key[...].astype(BF16)
        scaled = value[...].astype(BF16)
        key_kept[step] = keys
        scaled_kept[step] = scaled
        first = mm(keys, gate_b)
        third = mm(keys, up_b)
        sig = jax.nn.sigmoid(first)
        activ = first * sig
        act = (activ * third).astype(BF16)
        dact = mm_t(scaled, out_b)
        deriv = sig * (1.0 + first * (1.0 - sig))
        dfirst = (dact * third * deriv).astype(BF16)
        dthird = (dact * activ).astype(BF16)
        total[0] += tmm(keys, dfirst)
        total[1] += tmm(act, scaled)
        total[2] += tmm(keys, dthird)
    return total


def update_kernel(count, depth, scale, place, *refs):
    keys_in, scaled_in, weights = refs[:count], refs[count : 2 * count], refs[2 * count :][:3]
    key_kept, scaled_kept = refs[2 * count + 3 : 2 * count + 5]
    outs, sums = refs[2 * count + 5 : -1], refs[-1]
    total = update_sums(keys_in, scaled_in, weights, key_kept, scaled_kept)
    for i in range(3):
        sums[i] = total[i] * scale
    send_slices(sums, outs, place[1], depth)
    rows = sums.shape[1] // depth
    at = pl.multiple_of(place[1] * rows, rows)
    for i, w in enumerate(weights):
        outs[-1][0, i] += w[pl.ds(at, rows), :]


def assemble(place, parts, whole):
    rows = parts[0].shape[2]
    for step, part in enumerate(parts):
        at = pl.multiple_of((place[1] ^ step) * rows, rows)
        whole[:, pl.ds(at, rows), :] = part[0]


def apply_kernel(groups, depth, place, scale_row, *refs):
    count = packed_count(groups)
    (q_in, dyg_in), parts = unpacked(groups, refs[:count]), refs[count : count + depth]
    activ_ref, slope_ref, hidden_ref, os_ref, new_b, stats, whole = refs[count + depth :]
    assemble(place, parts, whole)
    new_b[...] = whole[...].astype(BF16)
    for step in range(groups):
        queries = q_in[step][...].astype(BF16)
        tokens = queries.shape[0]
        first = mm(queries, new_b[0])
        third = mm(queries, new_b[2])
        sig = jax.nn.sigmoid(first)
        activ = first * sig
        hidden = (activ * third).astype(BF16)
        scaled = mm(hidden, new_b[1]) * scale_row[0:1, :]
        activ_ref[step] = activ
        slope_ref[step] = third * (sig * (1.0 + first * (1.0 - sig)))
        hidden_ref[step] = hidden
        os_ref[step] = scaled
        sq = jnp.sum(scaled * scaled, axis=1, keepdims=True)
        ps = jnp.sum(scaled * dyg_in[step][...], axis=1, keepdims=True)
        lane = lax.broadcasted_iota(jnp.int32, (tokens, LANES), 1)
        both = jnp.where(lane == 0, sq, jnp.where(lane == 1, ps, 0.0)).T
        source = place[0] ^ step
        stats[0, pl.ds(source, 1), :] = both[0:1, :]
        stats[1, pl.ds(source, 1), :] = both[1:2, :]


def apply_back_kernel(groups, depth, count, place, scale_row, *refs):
    packed = packed_count(groups)
    q_in, dyg_in = unpacked(groups, refs[:packed])
    refs = refs[packed:]
    stats, refs = refs[:groups], refs[groups:]
    activ_ref, slope_ref, hidden_ref, os_ref, new_b = refs[:5]
    outs, slices, sums, both = refs[5 : groups + 5], refs[groups + 5 : -2], refs[-2], refs[-1]
    total_stats = stats[0][...]
    for other in stats[1:]:
        total_stats += other[...]
    both[...] = total_stats
    total = [0.0, 0.0, 0.0]
    for step in range(groups):
        queries = q_in[step][...].astype(BF16)
        source = place[0] ^ step
        sq = rate_column(both.at[0], source)
        ps = rate_column(both.at[1], source)
        inv = lax.rsqrt(sq / count + 1e-06)
        dos = inv * dyg_in[step][...] - os_ref[step] * (inv * inv * inv * ps / count)
        dout = (dos * scale_row[0:1, :]).astype(BF16)
        dhidden = mm_t(dout, new_b[1])
        dthird = (dhidden * activ_ref[step]).astype(BF16)
        dfirst = (dhidden * slope_ref[step]).astype(BF16)
        outs[step][...] = mm_t(dfirst, new_b[0]) + mm_t(dthird, new_b[2])
        total[0] += tmm(queries, dfirst)
        total[1] += tmm(hidden_ref[step], dout)
        total[2] += tmm(queries, dthird)
    for i in range(3):
        sums[i] = total[i]
    send_slices(sums, slices, place[1], depth)


def update_keep_kernel(k_kept, s_kept, w_gate, w_out, w_up, *outs):
    dact_r, third_r, activ_r, deriv_r, slope_r, second_r, dfirst_r, dthird_r, act_r = outs
    gate_b, out_b, up_b = (w[...].astype(BF16) for w in (w_gate, w_out, w_up))
    for step in range(k_kept.shape[0]):
        keys, scaled = k_kept[step], s_kept[step]
        first = mm(keys, gate_b)
        third = mm(keys, up_b)
        dact = mm_t(scaled, out_b)
        sig = jax.nn.sigmoid(first)
        activ = first * sig
        slope = sig * (1.0 - sig)
        deriv = sig + first * slope
        third_deriv = third * deriv
        dact_r[step] = dact
        third_r[step] = third
        activ_r[step] = activ
        deriv_r[step] = deriv
        slope_r[step] = third_deriv
        second_r[step] = third * (slope * (2.0 + first * (1.0 - 2.0 * sig)))
        dfirst_r[step] = (dact * third_deriv).astype(BF16)
        dthird_r[step] = (dact * activ).astype(BF16)
        act_r[step] = (activ * third).astype(BF16)


def update_back_kernel(groups, depth, scale, place, *refs):
    (k_kept, s_kept), refs = refs[:2], refs[2:]
    kept, refs = refs[:9], refs[9:]
    dact_r, third_r, activ_r, deriv_r, slope_r, second_r, dfirst_r, dthird_r, act_r = kept
    parts, refs = refs[:depth], refs[depth:]
    w_gate, w_out, w_up = refs[:3]
    outs, slices = refs[3 : groups + 3], refs[groups + 3 : -2]
    whole, sums = refs[-2:]
    assemble(place, parts, whole)
    gate_b, out_b, up_b = (w[...].astype(BF16) for w in (w_gate, w_out, w_up))
    cot_gate, cot_out, cot_up = ((whole[i] * scale).astype(BF16) for i in range(3))
    total = [0.0, 0.0, 0.0]
    for step in range(groups):
        keys, scaled = k_kept[step], s_kept[step]
        bar_dfirst = mm(keys, cot_gate)
        bar_dthird = mm(keys, cot_up)
        bar_act = mm_t(scaled, cot_out)
        dact, activ, deriv = dact_r[step], activ_r[step], deriv_r[step]
        bar_activ = bar_dthird * dact + bar_act * third_r[step]
        bar_dact = (bar_dfirst * slope_r[step] + bar_dthird * activ).astype(BF16)
        bar_df_dact = bar_dfirst * dact
        bar_third = (bar_df_dact * deriv + bar_act * activ).astype(BF16)
        bar_first = (bar_activ * deriv + bar_df_dact * second_r[step]).astype(BF16)
        outs[step][0] = (
            mm_t(dfirst_r[step], cot_gate)
            + mm_t(dthird_r[step], cot_up)
            + mm_t(bar_first, gate_b)
            + mm_t(bar_third, up_b)
        )
        outs[step][1] = mm(act_r[step], cot_out) + mm(bar_dact, out_b)
        total[0] += tmm(keys, bar_first)
        total[1] += tmm(bar_dact, scaled)
        total[2] += tmm(keys, bar_third)
    for i in range(3):
        sums[i] = total[i]
    send_slices(sums, slices, place[1], depth)


def join_query_kernel(groups, place, *refs):
    pieces, out, scratch = refs[:groups], refs[groups], refs[groups + 1]
    tokens, heads, width = out.shape
    for step, piece in enumerate(pieces):
        put_head(scratch, place[0] ^ step, piece[...], tokens, heads)
    out[...] = rows_of(scratch).reshape(tokens, heads, width).astype(BF16)


def join_update_kernel(groups, place, r, *refs):
    pieces, parts = refs[:groups], refs[groups : 2 * groups]
    out_k, out_v = refs[2 * groups : 2 * groups + 2]
    grads, (sk, sv) = refs[2 * groups + 2 : -2], refs[-2:]
    tokens, heads, width = out_k.shape
    for step, piece in enumerate(pieces):
        head = place[0] ^ step
        put_head(sk, head, piece[0], tokens, heads)
        put_head(sv, head, piece[1] * rate_column(r, head), tokens, heads)
        for i, grad in enumerate(grads):
            grad[head] = parts[step][0, i]
    out_k[...] = rows_of(sk).reshape(tokens, heads, width).astype(BF16)
    out_v[...] = rows_of(sv).reshape(tokens, heads, width).astype(BF16)


def rows_kernel(groups, place, *refs):
    parts, outs, total = refs[: -groups - 1], refs[-groups - 1 : -1], refs[-1]
    summed = parts[0][0]
    for part in parts[1:]:
        summed += part[0]
    total[...] = summed
    rows = total.shape[1] // groups
    for step, out in enumerate(outs):
        at = pl.multiple_of((place[0] ^ step) * rows, rows)
        out[0] = total[:, pl.ds(at, rows), :]


def local(queries, keys, values, rates, head_scale, gain, w_gate, w_out, w_up, cotangent):
    tokens, heads, width = keys.shape[1:]
    hidden = w_gate.shape[2]
    ctx = lax.axis_size("ctx")
    head_axis = lax.axis_size("head")
    groups = heads
    depth = ctx // groups
    assert groups & (groups - 1) == 0 and depth & (depth - 1) == 0
    scale = 1.0 / math.sqrt(tokens * ctx * width)
    count = float(heads * head_axis * width)
    me = lax.axis_index("ctx")
    mine, layer = lax.rem(me, groups), lax.div(me, groups)
    place = jnp.stack([mine, layer]).astype(jnp.int32)

    def move(x, axis, step):
        return lax.ppermute(x, axis, [(c, c ^ step) for c in range(lax.axis_size(axis))])

    def in_plane(parts):
        return [parts[0]] + [move(p, "ctx", step) for step, p in enumerate(parts) if step]

    def forwarded(got):
        return [got[:1]] if got.shape[0] == 1 else [got[i : i + 1] for i in range(got.shape[0])]

    def scatter(outs, count, unit, one_by_one=True):
        outs = list(outs)
        evens = list(range(2, count, 2))
        via = forwarded(move(outs.pop(0), "ctx", unit)) if evens else []
        if one_by_one:
            via, outs[0] = after(via, outs[0])
        first = [move(outs[0], "ctx", unit)] if count > 1 else []
        even = [move(p + v, "ctx", r * unit) for p, v, r in zip(outs[1:], via, evens)]
        return [outs[-1]] + first + even

    def gather(part, count, unit, beside):
        got = [part] * count
        evens = range(2, count, 2)
        for r in evens:
            got[r] = move(part, "ctx", r * unit)
        if count > 1:
            got[1] = move(part, "ctx", unit)
        got, beside = after(got, beside)
        for r in evens:
            got[r + 1] = move(got[r], "ctx", unit)
        return got, beside

    def after(x, *others):
        return lax.optimization_barrier((x, *others))

    def shape(*dims, dtype=F32):
        return jax.ShapeDtypeStruct(dims, dtype)

    flops = 2 * groups * tokens * width * hidden
    pieces = [shape(tokens, width)] * groups
    slices = [shape(len(m), 3, hidden // depth, width) for m in send_groups(depth)]
    joined = shape(tokens, heads, width, dtype=BF16)
    scratch = pltpu.VMEM((width // LANES, tokens * heads, LANES), F32)
    square = pltpu.VMEM((3, hidden, width), F32)

    def split(body, *args):
        return call(functools.partial(body, groups), pieces, [scratch], 16 * flops, place, *args)

    k_in = in_plane(split(split_kernel, keys[0]))
    s_in = in_plane(split(split_scaled_kernel, values[0], rates[0]))
    own = [lax.dynamic_index_in_dim(w, mine, 0, keepdims=False) for w in (w_gate, w_out, w_up)]
    own_scale = lax.dynamic_index_in_dim(head_scale, mine, 0, keepdims=True)[None, :]
    def kept(*dims, dtype=F32):
        return shape(*dims, tokens, width, dtype=dtype)

    *q_out, scale_row = call(
        functools.partial(split_apply_kernel, groups),
        [kept(len(members)) for members in packing(groups)] + [shape(8, width)],
        [scratch], flops // 8, place, queries[0], cotangent[0], gain, own_scale,
    )
    k_in, s_in, q_out = after(k_in, s_in, q_out)
    q_in = q_out[:1] + [move(q_out[i], "ctx", i) for i in range(1, len(q_out))]
    out = call(
        functools.partial(update_kernel, groups, depth, scale),
        [kept(groups, dtype=BF16)] * 2 + slices, [square], 6 * flops,
        place, *k_in, *s_in, *own,
    )
    early, terms = out[:2], out[2:]
    new = functools.reduce(jnp.add, scatter(terms, depth, groups))
    new, q_in[1:] = gather(new, depth, groups, q_in[1:])
    if groups == 4:
        q_in += [move(q_in[1][2], "ctx", 2), move(q_in[2][2], "ctx", 1)]
    *passed, stats = call(
        functools.partial(apply_kernel, groups, depth),
        [kept(groups), kept(groups), kept(groups, dtype=BF16), kept(groups)]
        + [shape(3, hidden, width, dtype=BF16), shape(2, groups, tokens)],
        [square], 3 * flops, place, scale_row, *q_in, *new,
    )
    bit = 1
    while bit < head_axis:
        stats = stats + move(stats, "head", bit)
        bit *= 2
    out = call(
        functools.partial(apply_back_kernel, groups, depth, count), pieces + slices,
        [square, pltpu.VMEM((2, groups, tokens), F32)], 6 * flops,
        place, scale_row, *q_in, *in_plane([stats] * groups), *passed,
    )
    out, early = after(out, early)
    saved = call(
        update_keep_kernel, [kept(groups)] * 6 + [kept(groups, dtype=BF16)] * 3, [], 3 * flops,
        *early, *own,
    )
    part = functools.reduce(jnp.add, scatter(out[groups:], depth, groups))
    parts, q_back = gather(part, depth, groups, in_plane(out[:groups]))
    (grad_q,) = call(
        functools.partial(join_query_kernel, groups), [joined], [scratch], flops // 16,
        place, *q_back, final=True,
    )
    parts, grad_q, saved = after(parts, grad_q, saved)
    rows = hidden // depth
    out = call(
        functools.partial(update_back_kernel, groups, depth, scale),
        [shape(2, tokens, width)] * groups + slices, [square] * 2, 12 * flops,
        place, *early, *saved, *parts, *own,
    )
    back = in_plane(out[:groups])
    ends = scatter(out[groups:], depth, groups, one_by_one=False)
    own_rows = rows // groups
    sent = call(
        functools.partial(rows_kernel, groups),
        [shape(1, 3, own_rows, width)] * groups,
        [pltpu.VMEM((3, rows, width), F32)], flops // 100, place, part, *ends,
    )
    grad_k, grad_v, *grads = call(
        functools.partial(join_update_kernel, groups),
        [joined] * 2 + [shape(heads, own_rows, width)] * 3, [scratch] * 2, flops // 8,
        place, rates[0], *back, *in_plane(sent), final=True,
    )
    if lax.axis_size("batch") > 1:
        grads = [lax.psum_scatter(x, "batch", scatter_dimension=1, tiled=True) for x in grads]
    return (grad_q[None], grad_k[None], grad_v[None], grads[0], grads[1], grads[2])


def solution(mesh):
    in_specs = (
        P("batch", "ctx", "head", None),
        P("batch", "ctx", "head", None),
        P("batch", "ctx", "head", None),
        P("batch", "head", "ctx"),
        P("head"),
        P("head", None),
        P("head", None, None),
        P("head", None, None),
        P("head", None, None),
        P("batch", "ctx", "head", None),
    )
    out_specs = (
        P("batch", "ctx", "head", None),
        P("batch", "ctx", "head", None),
        P("batch", "ctx", "head", None),
        P("head", ("ctx", "batch"), None),
        P("head", ("ctx", "batch"), None),
        P("head", ("ctx", "batch"), None),
    )
    return jax.shard_map(local, mesh=mesh, in_specs=in_specs, out_specs=out_specs, check_vma=False)
```

```python
import functools
import math

import jax
import jax.numpy as jnp
from jax import lax
from jax.experimental import pallas as pl
from jax.experimental.pallas import tpu as pltpu
from jax.sharding import PartitionSpec as P

F32 = jnp.float32
BF16 = jnp.bfloat16
LANES = 128
MIB = 1024 * 1024


def mm(a, b):
    return jnp.dot(a, b, preferred_element_type=F32)


def mm_t(a, b):
    return lax.dot_general(a, b, (((1,), (1,)), ((), ())), preferred_element_type=F32)


def tmm(a, b):
    return lax.dot_general(a, b, (((0,), (0,)), ((), ())), preferred_element_type=F32)


def call(body, out_shape, scratch, flops, *args, final=False, mib=16):
    smem = pl.BlockSpec(memory_space=pltpu.SMEM)
    vmem = pl.BlockSpec(memory_space=pltpu.VMEM)
    size = sum(a.size * a.dtype.itemsize for a in args)
    size += sum(math.prod(o.shape) * o.dtype.itemsize for o in out_shape)
    return pl.pallas_call(
        body,
        out_shape=out_shape if final else [pltpu.VMEM(o.shape, o.dtype) for o in out_shape],
        in_specs=[smem if a.dtype == jnp.int32 else vmem for a in args],
        out_specs=[vmem] * len(out_shape),
        scratch_shapes=scratch,
        compiler_params=pltpu.CompilerParams(vmem_limit_bytes=mib * MIB),
        cost_estimate=pl.CostEstimate(flops=flops, bytes_accessed=size, transcendentals=0),
    )(*args)


def put_rows(scratch, x):
    for i in range(scratch.shape[0]):
        scratch[i] = x[:, i * LANES : (i + 1) * LANES]


def take_head(scratch, head, tokens, heads):
    parts = [scratch[i, pl.ds(head, tokens, stride=heads), :] for i in range(scratch.shape[0])]
    return jnp.concatenate(parts, axis=1)


def put_head(scratch, head, x, tokens, heads):
    for i in range(scratch.shape[0]):
        scratch[i, pl.ds(head, tokens, stride=heads), :] = x[:, i * LANES : (i + 1) * LANES]


def rows_of(scratch):
    return jnp.concatenate([scratch[i] for i in range(scratch.shape[0])], axis=1)


def split_kernel(groups, place, x, *rest):
    outs, scratch = rest[:groups], rest[groups]
    tokens, heads, width = x.shape
    put_rows(scratch, x[...].astype(F32).reshape(tokens * heads, width))
    for step, out in enumerate(outs):
        out[...] = take_head(scratch, place[0] ^ step, tokens, heads).astype(out.dtype)


def split_scaled_kernel(groups, place, x, r, *rest):
    outs = rest[:groups]
    split_kernel(groups, place, x, *rest)
    for step in range(groups):
        scaled = outs[step][...].astype(F32) * rate_column(r, place[0] ^ step)
        outs[step][...] = scaled.astype(BF16).astype(outs[step].dtype)


def packing(groups):
    if groups == 4:
        return [[(0, 0), (0, 1)], [(1, 0), (1, 1), (3, 0)], [(2, 0), (2, 1), (3, 1)]]
    return [[(step, 0), (step, 1)] for step in range(groups)]


def unpacked(groups, refs):
    found = {}
    for ref, members in zip(refs, packing(groups)):
        for i, member in enumerate(members):
            found[member] = ref.at[i]
    for i, ref in enumerate(refs[len(packing(groups)) :]):
        found[(groups - 1, i)] = ref
    return [found[(step, 0)] for step in range(groups)], [found[(step, 1)] for step in range(groups)]


def split_apply_kernel(groups, place, q, cot, gain, scale, *rest):
    outs, scale_row, scratch = rest[:-2], rest[-2], rest[-1]
    scale_row[...] = jnp.broadcast_to(scale[...], scale_row.shape)
    to_q, to_dyg = unpacked(groups, outs)
    split_kernel(groups, place, q, *to_q, scratch)
    split_kernel(groups, place, cot, *to_dyg, scratch)
    for step in range(groups):
        to_dyg[step][...] *= gain[pl.ds(place[0] ^ step, 1), :]


def packed_count(groups):
    return len(packing(groups)) + 2 * (groups == 4)


def rate_column(r, head):
    return jnp.broadcast_to(r[pl.ds(head, 1), :], (8, r.shape[1])).T[:, 0:1]


def send_groups(count):
    odd = list(range(3, count, 2))
    return ([odd] if odd else []) + [[r] for r in [1] + list(range(2, count, 2)) if r < count] + [[0]]


def send_slices(sums, outs, own, count):
    rows = sums.shape[1] // count
    for out, members in zip(outs, send_groups(count)):
        for i, step in enumerate(members):
            at = pl.multiple_of((own ^ step) * rows, rows)
            out[i] = sums[:, pl.ds(at, rows), :]


def update_sums(keys_in, scaled_in, weights, key_kept, scaled_kept):
    gate_b, out_b, up_b = (w[...].astype(BF16) for w in weights)
    total = [0.0, 0.0, 0.0]
    for step, (key, value) in enumerate(zip(keys_in, scaled_in)):
        keys = key[...].astype(BF16)
        scaled = value[...].astype(BF16)
        key_kept[step] = keys
        scaled_kept[step] = scaled
        first = mm(keys, gate_b)
        third = mm(keys, up_b)
        sig = jax.nn.sigmoid(first)
        activ = first * sig
        act = (activ * third).astype(BF16)
        dact = mm_t(scaled, out_b)
        deriv = sig * (1.0 + first * (1.0 - sig))
        dfirst = (dact * third * deriv).astype(BF16)
        dthird = (dact * activ).astype(BF16)
        total[0] += tmm(keys, dfirst)
        total[1] += tmm(act, scaled)
        total[2] += tmm(keys, dthird)
    return total


def update_kernel(count, depth, scale, place, *refs):
    keys_in, scaled_in, weights = refs[:count], refs[count : 2 * count], refs[2 * count :][:3]
    key_kept, scaled_kept = refs[2 * count + 3 : 2 * count + 5]
    outs, sums = refs[2 * count + 5 : -1], refs[-1]
    total = update_sums(keys_in, scaled_in, weights, key_kept, scaled_kept)
    for i in range(3):
        sums[i] = total[i] * scale
    send_slices(sums, outs, place[1], depth)
    rows = sums.shape[1] // depth
    at = pl.multiple_of(place[1] * rows, rows)
    for i, w in enumerate(weights):
        outs[-1][0, i] += w[pl.ds(at, rows), :]


def assemble(place, parts, whole):
    rows = parts[0].shape[2]
    for step, part in enumerate(parts):
        at = pl.multiple_of((place[1] ^ step) * rows, rows)
        whole[:, pl.ds(at, rows), :] = part[0]


def apply_kernel(groups, depth, place, scale_row, *refs):
    count = packed_count(groups)
    (q_in, dyg_in), parts = unpacked(groups, refs[:count]), refs[count : count + depth]
    activ_ref, slope_ref, hidden_ref, os_ref, new_b, stats, whole = refs[count + depth :]
    assemble(place, parts, whole)
    new_b[...] = whole[...].astype(BF16)
    for step in range(groups):
        queries = q_in[step][...].astype(BF16)
        tokens = queries.shape[0]
        first = mm(queries, new_b[0])
        third = mm(queries, new_b[2])
        sig = jax.nn.sigmoid(first)
        activ = first * sig
        hidden = (activ * third).astype(BF16)
        scaled = mm(hidden, new_b[1]) * scale_row[0:1, :]
        activ_ref[step] = activ
        slope_ref[step] = third * (sig * (1.0 + first * (1.0 - sig)))
        hidden_ref[step] = hidden
        os_ref[step] = scaled
        sq = jnp.sum(scaled * scaled, axis=1, keepdims=True)
        ps = jnp.sum(scaled * dyg_in[step][...], axis=1, keepdims=True)
        lane = lax.broadcasted_iota(jnp.int32, (tokens, LANES), 1)
        both = jnp.where(lane == 0, sq, jnp.where(lane == 1, ps, 0.0)).T
        source = place[0] ^ step
        stats[0, pl.ds(source, 1), :] = both[0:1, :]
        stats[1, pl.ds(source, 1), :] = both[1:2, :]


def apply_back_kernel(groups, depth, count, place, scale_row, *refs):
    packed = packed_count(groups)
    q_in, dyg_in = unpacked(groups, refs[:packed])
    refs = refs[packed:]
    stats, refs = refs[:groups], refs[groups:]
    activ_ref, slope_ref, hidden_ref, os_ref, new_b = refs[:5]
    outs, slices, sums, both = refs[5 : groups + 5], refs[groups + 5 : -2], refs[-2], refs[-1]
    total_stats = stats[0][...]
    for other in stats[1:]:
        total_stats += other[...]
    both[...] = total_stats
    total = [0.0, 0.0, 0.0]
    for step in range(groups):
        queries = q_in[step][...].astype(BF16)
        source = place[0] ^ step
        sq = rate_column(both.at[0], source)
        ps = rate_column(both.at[1], source)
        inv = lax.rsqrt(sq / count + 1e-06)
        dos = inv * dyg_in[step][...] - os_ref[step] * (inv * inv * inv * ps / count)
        dout = (dos * scale_row[0:1, :]).astype(BF16)
        dhidden = mm_t(dout, new_b[1])
        dthird = (dhidden * activ_ref[step]).astype(BF16)
        dfirst = (dhidden * slope_ref[step]).astype(BF16)
        outs[step][...] = mm_t(dfirst, new_b[0]) + mm_t(dthird, new_b[2])
        total[0] += tmm(queries, dfirst)
        total[1] += tmm(hidden_ref[step], dout)
        total[2] += tmm(queries, dthird)
    for i in range(3):
        sums[i] = total[i]
    send_slices(sums, slices, place[1], depth)


def update_keep_kernel(k_kept, s_kept, w_gate, w_out, w_up, *outs):
    dact_r, third_r, activ_r, deriv_r, slope_r, second_r, dfirst_r, dthird_r, act_r = outs
    gate_b, out_b, up_b = (w[...].astype(BF16) for w in (w_gate, w_out, w_up))
    for step in range(k_kept.shape[0]):
        keys, scaled = k_kept[step], s_kept[step]
        first = mm(keys, gate_b)
        third = mm(keys, up_b)
        dact = mm_t(scaled, out_b)
        sig = jax.nn.sigmoid(first)
        activ = first * sig
        slope = sig * (1.0 - sig)
        deriv = sig + first * slope
        third_deriv = third * deriv
        dact_r[step] = dact
        third_r[step] = third
        activ_r[step] = activ
        deriv_r[step] = deriv
        slope_r[step] = third_deriv
        second_r[step] = third * (slope * (2.0 + first * (1.0 - 2.0 * sig)))
        dfirst_r[step] = (dact * third_deriv).astype(BF16)
        dthird_r[step] = (dact * activ).astype(BF16)
        act_r[step] = (activ * third).astype(BF16)


def update_back_kernel(groups, depth, scale, place, *refs):
    (k_kept, s_kept), refs = refs[:2], refs[2:]
    kept, refs = refs[:9], refs[9:]
    dact_r, third_r, activ_r, deriv_r, slope_r, second_r, dfirst_r, dthird_r, act_r = kept
    parts, refs = refs[:depth], refs[depth:]
    w_gate, w_out, w_up = refs[:3]
    outs, slices = refs[3 : groups + 3], refs[groups + 3 : -2]
    whole, sums = refs[-2:]
    assemble(place, parts, whole)
    gate_b, out_b, up_b = (w[...].astype(BF16) for w in (w_gate, w_out, w_up))
    cot_gate, cot_out, cot_up = ((whole[i] * scale).astype(BF16) for i in range(3))
    total = [0.0, 0.0, 0.0]
    for step in range(groups):
        keys, scaled = k_kept[step], s_kept[step]
        bar_dfirst = mm(keys, cot_gate)
        bar_dthird = mm(keys, cot_up)
        bar_act = mm_t(scaled, cot_out)
        dact, activ, deriv = dact_r[step], activ_r[step], deriv_r[step]
        bar_activ = bar_dthird * dact + bar_act * third_r[step]
        bar_dact = (bar_dfirst * slope_r[step] + bar_dthird * activ).astype(BF16)
        bar_df_dact = bar_dfirst * dact
        bar_third = (bar_df_dact * deriv + bar_act * activ).astype(BF16)
        bar_first = (bar_activ * deriv + bar_df_dact * second_r[step]).astype(BF16)
        outs[step][0] = (
            mm_t(dfirst_r[step], cot_gate)
            + mm_t(dthird_r[step], cot_up)
            + mm_t(bar_first, gate_b)
            + mm_t(bar_third, up_b)
        )
        outs[step][1] = mm(act_r[step], cot_out) + mm(bar_dact, out_b)
        total[0] += tmm(keys, bar_first)
        total[1] += tmm(bar_dact, scaled)
        total[2] += tmm(keys, bar_third)
    for i in range(3):
        sums[i] = total[i]
    send_slices(sums, slices, place[1], depth)


def join_query_kernel(groups, place, *refs):
    pieces, out, scratch = refs[:groups], refs[groups], refs[groups + 1]
    tokens, heads, width = out.shape
    for step, piece in enumerate(pieces):
        put_head(scratch, place[0] ^ step, piece[...], tokens, heads)
    out[...] = rows_of(scratch).reshape(tokens, heads, width).astype(BF16)


def join_update_kernel(groups, place, r, *refs):
    pieces, parts = refs[:groups], refs[groups : 2 * groups]
    out_k, out_v = refs[2 * groups : 2 * groups + 2]
    grads, (sk, sv) = refs[2 * groups + 2 : -2], refs[-2:]
    tokens, heads, width = out_k.shape
    for step, piece in enumerate(pieces):
        head = place[0] ^ step
        put_head(sk, head, piece[0], tokens, heads)
        put_head(sv, head, piece[1] * rate_column(r, head), tokens, heads)
        for i, grad in enumerate(grads):
            grad[head] = parts[step][0, i]
    out_k[...] = rows_of(sk).reshape(tokens, heads, width).astype(BF16)
    out_v[...] = rows_of(sv).reshape(tokens, heads, width).astype(BF16)


def rows_kernel(groups, place, *refs):
    parts, outs, total = refs[: -groups - 1], refs[-groups - 1 : -1], refs[-1]
    summed = parts[0][0]
    for part in parts[1:]:
        summed += part[0]
    total[...] = summed
    rows = total.shape[1] // groups
    for step, out in enumerate(outs):
        at = pl.multiple_of((place[0] ^ step) * rows, rows)
        out[0] = total[:, pl.ds(at, rows), :]


def local(queries, keys, values, rates, head_scale, gain, w_gate, w_out, w_up, cotangent):
    tokens, heads, width = keys.shape[1:]
    hidden = w_gate.shape[2]
    ctx = lax.axis_size("ctx")
    head_axis = lax.axis_size("head")
    groups = heads
    depth = ctx // groups
    assert groups & (groups - 1) == 0 and depth & (depth - 1) == 0
    scale = 1.0 / math.sqrt(tokens * ctx * width)
    count = float(heads * head_axis * width)
    me = lax.axis_index("ctx")
    mine, layer = lax.rem(me, groups), lax.div(me, groups)
    place = jnp.stack([mine, layer]).astype(jnp.int32)

    def move(x, axis, step):
        return lax.ppermute(x, axis, [(c, c ^ step) for c in range(lax.axis_size(axis))])

    def in_plane(parts):
        return [parts[0]] + [move(p, "ctx", step) for step, p in enumerate(parts) if step]

    def forwarded(got):
        return [got[:1]] if got.shape[0] == 1 else [got[i : i + 1] for i in range(got.shape[0])]

    def scatter(outs, count, unit, one_by_one=True):
        outs = list(outs)
        evens = list(range(2, count, 2))
        via = forwarded(move(outs.pop(0), "ctx", unit)) if evens else []
        if one_by_one:
            via, outs[0] = after(via, outs[0])
        first = [move(outs[0], "ctx", unit)] if count > 1 else []
        even = [move(p + v, "ctx", r * unit) for p, v, r in zip(outs[1:], via, evens)]
        return [outs[-1]] + first + even

    def gather(part, count, unit, beside=()):
        got = [part] * count
        evens = range(2, count, 2)
        for r in evens:
            got[r] = move(part, "ctx", r * unit)
        if count > 1:
            got[1] = move(part, "ctx", unit)
            got[1], beside = after(got[1], beside)
        for r in evens:
            got[r + 1] = move(got[r], "ctx", unit)
        return got, beside

    def after(x, *others):
        return lax.optimization_barrier((x, *others))

    def shape(*dims, dtype=F32):
        return jax.ShapeDtypeStruct(dims, dtype)

    flops = 2 * groups * tokens * width * hidden
    pieces = [shape(tokens, width)] * groups
    slices = [shape(len(m), 3, hidden // depth, width) for m in send_groups(depth)]
    joined = shape(tokens, heads, width, dtype=BF16)
    scratch = pltpu.VMEM((width // LANES, tokens * heads, LANES), F32)
    square = pltpu.VMEM((3, hidden, width), F32)

    def split(body, *args):
        outs = [shape(tokens, width, dtype=BF16)] + pieces[1:]
        body = functools.partial(body, groups)
        return call(body, outs, [scratch], 16 * flops, place, *args, mib=8)

    k_in = in_plane(split(split_kernel, keys[0]))
    s_in = in_plane(split(split_scaled_kernel, values[0], rates[0]))
    own = [lax.dynamic_index_in_dim(w, mine, 0, keepdims=False) for w in (w_gate, w_out, w_up)]
    own_scale = lax.dynamic_index_in_dim(head_scale, mine, 0, keepdims=True)[None, :]
    def kept(*dims, dtype=F32):
        return shape(*dims, tokens, width, dtype=dtype)

    *q_out, scale_row = call(
        functools.partial(split_apply_kernel, groups),
        [kept(len(members)) for members in packing(groups)] + [shape(8, width)],
        [scratch], flops // 8, place, queries[0], cotangent[0], gain, own_scale, mib=8,
    )
    k_in, s_in, q_out = after(k_in, s_in, q_out)
    q_in = q_out[:1] + [move(q_out[i], "ctx", i) for i in range(1, len(q_out))]
    out = call(
        functools.partial(update_kernel, groups, depth, scale),
        [kept(groups, dtype=BF16)] * 2 + slices, [square], 6 * flops,
        place, *k_in, *s_in, *own,
    )
    early, terms = out[:2], out[2:]
    new = functools.reduce(jnp.add, scatter(terms, depth, groups))
    new, q_in[1:] = gather(new, depth, groups, q_in[1:])
    if groups == 4:
        q_in += [move(q_in[1][2], "ctx", 2), move(q_in[2][2], "ctx", 1)]
    *passed, stats = call(
        functools.partial(apply_kernel, groups, depth),
        [kept(groups), kept(groups), kept(groups, dtype=BF16), kept(groups)]
        + [shape(3, hidden, width, dtype=BF16), shape(2, groups, tokens)],
        [square], 3 * flops, place, scale_row, *q_in, *new,
    )
    bit = 1
    while bit < head_axis:
        stats = stats + move(stats, "head", bit)
        bit *= 2
    out = call(
        functools.partial(apply_back_kernel, groups, depth, count), pieces + slices,
        [square, pltpu.VMEM((2, groups, tokens), F32)], 6 * flops,
        place, scale_row, *q_in, *in_plane([stats] * groups), *passed,
    )
    out, early = after(out, early)
    saved = call(
        update_keep_kernel, [kept(groups)] * 6 + [kept(groups, dtype=BF16)] * 3, [], 3 * flops,
        *early, *own,
    )
    part = functools.reduce(jnp.add, scatter(out[groups:], depth, groups))
    parts, _ = gather(part, depth, groups)
    q_back = in_plane(out[:groups])
    (grad_q,) = call(
        functools.partial(join_query_kernel, groups), [joined], [scratch], flops // 16,
        place, *q_back, final=True, mib=8,
    )
    parts, grad_q, saved = after(parts, grad_q, saved)
    rows = hidden // depth
    out = call(
        functools.partial(update_back_kernel, groups, depth, scale),
        [shape(2, tokens, width)] * groups + slices, [square] * 2, 12 * flops,
        place, *early, *saved, *parts, *own, mib=24,
    )
    back = in_plane(out[:groups])
    ends = scatter(out[groups:], depth, groups, one_by_one=False)
    own_rows = rows // groups
    sent = call(
        functools.partial(rows_kernel, groups),
        [shape(1, 3, own_rows, width)] * groups,
        [pltpu.VMEM((3, rows, width), F32)], flops // 100, place, part, *ends, mib=8,
    )
    grad_k, grad_v, *grads = call(
        functools.partial(join_update_kernel, groups),
        [joined] * 2 + [shape(heads, own_rows, width)] * 3, [scratch] * 2, flops // 8,
        place, rates[0], *back, *in_plane(sent), final=True, mib=8,
    )
    if lax.axis_size("batch") > 1:
        grads = [lax.psum_scatter(x, "batch", scatter_dimension=1, tiled=True) for x in grads]
    return (grad_q[None], grad_k[None], grad_v[None], grads[0], grads[1], grads[2])


def solution(mesh):
    in_specs = (
        P("batch", "ctx", "head", None),
        P("batch", "ctx", "head", None),
        P("batch", "ctx", "head", None),
        P("batch", "head", "ctx"),
        P("head"),
        P("head", None),
        P("head", None, None),
        P("head", None, None),
        P("head", None, None),
        P("batch", "ctx", "head", None),
    )
    out_specs = (
        P("batch", "ctx", "head", None),
        P("batch", "ctx", "head", None),
        P("batch", "ctx", "head", None),
        P("head", ("ctx", "batch"), None),
        P("head", ("ctx", "batch"), None),
        P("head", ("ctx", "batch"), None),
    )
    return jax.shard_map(local, mesh=mesh, in_specs=in_specs, out_specs=out_specs, check_vma=False)
```

```python
import functools
import math

import jax
import jax.numpy as jnp
from jax import lax
from jax.experimental import pallas as pl
from jax.experimental.pallas import tpu as pltpu
from jax.sharding import PartitionSpec as P

F32 = jnp.float32
BF16 = jnp.bfloat16
LANES = 128
MIB = 1024 * 1024


def mm(a, b):
    return jnp.dot(a, b, preferred_element_type=F32)


def mm_t(a, b):
    return lax.dot_general(a, b, (((1,), (1,)), ((), ())), preferred_element_type=F32)


def tmm(a, b):
    return lax.dot_general(a, b, (((0,), (0,)), ((), ())), preferred_element_type=F32)


def call(body, out_shape, scratch, flops, *args, mib=16):
    smem = pl.BlockSpec(memory_space=pltpu.SMEM)
    vmem = pl.BlockSpec(memory_space=pltpu.VMEM)
    size = sum(a.size * a.dtype.itemsize for a in args)
    size += sum(math.prod(o.shape) * o.dtype.itemsize for o in out_shape)
    return pl.pallas_call(
        body,
        out_shape=out_shape,
        in_specs=[smem if a.dtype == jnp.int32 else vmem for a in args],
        out_specs=[vmem] * len(out_shape),
        scratch_shapes=scratch,
        compiler_params=pltpu.CompilerParams(vmem_limit_bytes=mib * MIB),
        cost_estimate=pl.CostEstimate(flops=flops, bytes_accessed=size, transcendentals=0),
    )(*args)


def put_rows(scratch, x):
    for i in range(scratch.shape[0]):
        scratch[i] = x[:, i * LANES : (i + 1) * LANES]


def take_head(scratch, head, tokens, heads):
    parts = [scratch[i, pl.ds(head, tokens, stride=heads), :] for i in range(scratch.shape[0])]
    return jnp.concatenate(parts, axis=1)


def put_head(scratch, head, x, tokens, heads):
    for i in range(scratch.shape[0]):
        scratch[i, pl.ds(head, tokens, stride=heads), :] = x[:, i * LANES : (i + 1) * LANES]


def rows_of(scratch):
    return jnp.concatenate([scratch[i] for i in range(scratch.shape[0])], axis=1)


def split_kernel(groups, place, x, *rest):
    outs, scratch = rest[:groups], rest[groups]
    tokens, heads, width = x.shape
    put_rows(scratch, x[...].astype(F32).reshape(tokens * heads, width))
    for step, out in enumerate(outs):
        out[...] = take_head(scratch, place[0] ^ step, tokens, heads).astype(out.dtype)


def split_scaled_kernel(groups, place, x, r, *rest):
    outs = rest[:groups]
    split_kernel(groups, place, x, *rest)
    for step in range(groups):
        scaled = outs[step][...].astype(F32) * rate_column(r, place[0] ^ step)
        outs[step][...] = scaled.astype(BF16).astype(outs[step].dtype)


def split_apply_kernel(groups, place, q, cot, gain, scale, *rest):
    outs, scale_row, scratch = rest[:groups], rest[groups], rest[groups + 1]
    scale_row[...] = jnp.broadcast_to(scale[...], scale_row.shape)
    split_kernel(groups, place, q, *[out.at[0] for out in outs], scratch)
    split_kernel(groups, place, cot, *[out.at[1] for out in outs], scratch)
    for step in range(groups):
        outs[step][1] *= gain[pl.ds(place[0] ^ step, 1), :]


def rate_column(r, head):
    return jnp.broadcast_to(r[pl.ds(head, 1), :], (8, r.shape[1])).T[:, 0:1]


def send_groups(count):
    odd = list(range(3, count, 2))
    return ([odd] if odd else []) + [[r] for r in [1] + list(range(2, count, 2)) if r < count] + [[0]]


def send_slices(sums, outs, own, count):
    rows = sums.shape[1] // count
    for out, members in zip(outs, send_groups(count)):
        for i, step in enumerate(members):
            at = pl.multiple_of((own ^ step) * rows, rows)
            out[i] = sums[:, pl.ds(at, rows), :]


def update_sums(keys_in, scaled_in, weights, key_kept, scaled_kept):
    gate_b, out_b, up_b = (w[...].astype(BF16) for w in weights)
    total = [0.0, 0.0, 0.0]
    for step, (key, value) in enumerate(zip(keys_in, scaled_in)):
        keys = key[...].astype(BF16)
        scaled = value[...].astype(BF16)
        key_kept[step] = keys
        scaled_kept[step] = scaled
        first = mm(keys, gate_b)
        third = mm(keys, up_b)
        sig = jax.nn.sigmoid(first)
        activ = first * sig
        act = (activ * third).astype(BF16)
        dact = mm_t(scaled, out_b)
        deriv = sig * (1.0 + first * (1.0 - sig))
        dfirst = (dact * third * deriv).astype(BF16)
        dthird = (dact * activ).astype(BF16)
        total[0] += tmm(keys, dfirst)
        total[1] += tmm(act, scaled)
        total[2] += tmm(keys, dthird)
    return total


def update_kernel(count, depth, scale, place, *refs):
    keys_in, scaled_in, weights = refs[:count], refs[count : 2 * count], refs[2 * count :][:3]
    key_kept, scaled_kept = refs[2 * count + 3 : 2 * count + 5]
    outs, sums = refs[2 * count + 5 : -1], refs[-1]
    total = update_sums(keys_in, scaled_in, weights, key_kept, scaled_kept)
    for i in range(3):
        sums[i] = total[i] * scale
    send_slices(sums, outs, place[1], depth)
    rows = sums.shape[1] // depth
    at = pl.multiple_of(place[1] * rows, rows)
    for i, w in enumerate(weights):
        outs[-1][0, i] += w[pl.ds(at, rows), :]


def assemble(place, parts, whole):
    rows = parts[0].shape[2]
    for step, part in enumerate(parts):
        at = pl.multiple_of((place[1] ^ step) * rows, rows)
        whole[:, pl.ds(at, rows), :] = part[0]


def apply_kernel(groups, depth, place, scale_row, *refs):
    pieces = refs[:groups]
    parts = refs[groups : groups + depth]
    activ_ref, slope_ref, hidden_ref, os_ref, new_b, stats, whole = refs[groups + depth :]
    assemble(place, parts, whole)
    new_b[...] = whole[...].astype(BF16)
    for step in range(groups):
        queries = pieces[step][0].astype(BF16)
        tokens = queries.shape[0]
        first = mm(queries, new_b[0])
        third = mm(queries, new_b[2])
        sig = jax.nn.sigmoid(first)
        activ = first * sig
        hidden = (activ * third).astype(BF16)
        scaled = mm(hidden, new_b[1]) * scale_row[0:1, :]
        activ_ref[step] = activ
        slope_ref[step] = third * (sig * (1.0 + first * (1.0 - sig)))
        hidden_ref[step] = hidden
        os_ref[step] = scaled
        sq = jnp.sum(scaled * scaled, axis=1, keepdims=True)
        ps = jnp.sum(scaled * pieces[step][1], axis=1, keepdims=True)
        lane = lax.broadcasted_iota(jnp.int32, (tokens, LANES), 1)
        both = jnp.where(lane == 0, sq, jnp.where(lane == 1, ps, 0.0)).T
        source = place[0] ^ step
        stats[0, pl.ds(source, 1), :] = both[0:1, :]
        stats[1, pl.ds(source, 1), :] = both[1:2, :]


def apply_back_kernel(groups, depth, count, place, scale_row, *refs):
    pieces, stats = refs[:groups], refs[groups : 2 * groups]
    activ_ref, slope_ref, hidden_ref, os_ref, new_b = refs[2 * groups : 2 * groups + 5]
    outs = refs[2 * groups + 5 : 3 * groups + 5]
    slices, sums, both = refs[3 * groups + 5 : -2], refs[-2], refs[-1]
    total_stats = stats[0][...]
    for other in stats[1:]:
        total_stats += other[...]
    both[...] = total_stats
    total = [0.0, 0.0, 0.0]
    for step in range(groups):
        queries = pieces[step][0].astype(BF16)
        source = place[0] ^ step
        sq = rate_column(both.at[0], source)
        ps = rate_column(both.at[1], source)
        inv = lax.rsqrt(sq / count + 1e-06)
        dos = inv * pieces[step][1] - os_ref[step] * (inv * inv * inv * ps / count)
        dout = (dos * scale_row[0:1, :]).astype(BF16)
        dhidden = mm_t(dout, new_b[1])
        dthird = (dhidden * activ_ref[step]).astype(BF16)
        dfirst = (dhidden * slope_ref[step]).astype(BF16)
        outs[step][...] = mm_t(dfirst, new_b[0]) + mm_t(dthird, new_b[2])
        total[0] += tmm(queries, dfirst)
        total[1] += tmm(hidden_ref[step], dout)
        total[2] += tmm(queries, dthird)
    for i in range(3):
        sums[i] = total[i]
    send_slices(sums, slices, place[1], depth)


def update_keep_kernel(k_kept, s_kept, w_gate, w_out, w_up, *outs):
    dact_r, third_r, activ_r, deriv_r, slope_r, second_r, dfirst_r, dthird_r, act_r = outs
    gate_b, out_b, up_b = (w[...].astype(BF16) for w in (w_gate, w_out, w_up))
    for step in range(k_kept.shape[0]):
        keys, scaled = k_kept[step], s_kept[step]
        first = mm(keys, gate_b)
        third = mm(keys, up_b)
        dact = mm_t(scaled, out_b)
        sig = jax.nn.sigmoid(first)
        activ = first * sig
        slope = sig * (1.0 - sig)
        deriv = sig + first * slope
        third_deriv = third * deriv
        dact_r[step] = dact
        third_r[step] = third
        activ_r[step] = activ
        deriv_r[step] = deriv
        slope_r[step] = third_deriv
        second_r[step] = third * (slope * (2.0 + first * (1.0 - 2.0 * sig)))
        dfirst_r[step] = (dact * third_deriv).astype(BF16)
        dthird_r[step] = (dact * activ).astype(BF16)
        act_r[step] = (activ * third).astype(BF16)


def update_back_kernel(groups, depth, scale, place, *refs):
    (k_kept, s_kept), refs = refs[:2], refs[2:]
    kept, refs = refs[:9], refs[9:]
    dact_r, third_r, activ_r, deriv_r, slope_r, second_r, dfirst_r, dthird_r, act_r = kept
    parts, refs = refs[:depth], refs[depth:]
    w_gate, w_out, w_up = refs[:3]
    outs, slices = refs[3 : groups + 3], refs[groups + 3 : -2]
    whole, sums = refs[-2:]
    assemble(place, parts, whole)
    gate_b, out_b, up_b = (w[...].astype(BF16) for w in (w_gate, w_out, w_up))
    cot_gate, cot_out, cot_up = ((whole[i] * scale).astype(BF16) for i in range(3))
    total = [0.0, 0.0, 0.0]
    for step in range(groups):
        keys, scaled = k_kept[step], s_kept[step]
        bar_dfirst = mm(keys, cot_gate)
        bar_dthird = mm(keys, cot_up)
        bar_act = mm_t(scaled, cot_out)
        dact, activ, deriv = dact_r[step], activ_r[step], deriv_r[step]
        bar_activ = bar_dthird * dact + bar_act * third_r[step]
        bar_dact = (bar_dfirst * slope_r[step] + bar_dthird * activ).astype(BF16)
        bar_df_dact = bar_dfirst * dact
        bar_third = (bar_df_dact * deriv + bar_act * activ).astype(BF16)
        bar_first = (bar_activ * deriv + bar_df_dact * second_r[step]).astype(BF16)
        outs[step][0] = (
            mm_t(dfirst_r[step], cot_gate)
            + mm_t(dthird_r[step], cot_up)
            + mm_t(bar_first, gate_b)
            + mm_t(bar_third, up_b)
        )
        outs[step][1] = mm(act_r[step], cot_out) + mm(bar_dact, out_b)
        total[0] += tmm(keys, bar_first)
        total[1] += tmm(bar_dact, scaled)
        total[2] += tmm(keys, bar_third)
    for i in range(3):
        sums[i] = total[i]
    send_slices(sums, slices, place[1], depth)


def join_query_kernel(groups, place, *refs):
    pieces, out, scratch = refs[:groups], refs[groups], refs[groups + 1]
    tokens, heads, width = out.shape
    for step, piece in enumerate(pieces):
        put_head(scratch, place[0] ^ step, piece[...], tokens, heads)
    out[...] = rows_of(scratch).reshape(tokens, heads, width).astype(BF16)


def join_update_kernel(groups, place, r, *refs):
    pieces, parts = refs[:groups], refs[groups : 2 * groups]
    out_k, out_v = refs[2 * groups : 2 * groups + 2]
    grads, (sk, sv) = refs[2 * groups + 2 : -2], refs[-2:]
    tokens, heads, width = out_k.shape
    for step, piece in enumerate(pieces):
        head = place[0] ^ step
        put_head(sk, head, piece[0], tokens, heads)
        put_head(sv, head, piece[1] * rate_column(r, head), tokens, heads)
        for i, grad in enumerate(grads):
            grad[head] = parts[step][0, i]
    out_k[...] = rows_of(sk).reshape(tokens, heads, width).astype(BF16)
    out_v[...] = rows_of(sv).reshape(tokens, heads, width).astype(BF16)


def rows_kernel(groups, place, *refs):
    parts, outs, total = refs[: -groups - 1], refs[-groups - 1 : -1], refs[-1]
    summed = parts[0][0]
    for part in parts[1:]:
        summed += part[0]
    total[...] = summed
    rows = total.shape[1] // groups
    for step, out in enumerate(outs):
        at = pl.multiple_of((place[0] ^ step) * rows, rows)
        out[0] = total[:, pl.ds(at, rows), :]


def local(queries, keys, values, rates, head_scale, gain, w_gate, w_out, w_up, cotangent):
    tokens, heads, width = keys.shape[1:]
    hidden = w_gate.shape[2]
    ctx = lax.axis_size("ctx")
    head_axis = lax.axis_size("head")
    groups = heads
    depth = ctx // groups
    assert groups & (groups - 1) == 0 and depth & (depth - 1) == 0
    scale = 1.0 / math.sqrt(tokens * ctx * width)
    count = float(heads * head_axis * width)
    me = lax.axis_index("ctx")
    mine, layer = lax.rem(me, groups), lax.div(me, groups)
    place = jnp.stack([mine, layer]).astype(jnp.int32)

    def move(x, axis, step):
        return lax.ppermute(x, axis, [(c, c ^ step) for c in range(lax.axis_size(axis))])

    def in_plane(parts):
        return [parts[0]] + [move(p, "ctx", step) for step, p in enumerate(parts) if step]

    def forwarded(got):
        return [got[:1]] if got.shape[0] == 1 else [got[i : i + 1] for i in range(got.shape[0])]

    def scatter(outs, count, unit, one_by_one=True):
        outs = list(outs)
        evens = list(range(2, count, 2))
        via = forwarded(move(outs.pop(0), "ctx", unit)) if evens else []
        if one_by_one:
            via, outs[0] = after(via, outs[0])
        first = [move(outs[0], "ctx", unit)] if count > 1 else []
        even = [move(p + v, "ctx", r * unit) for p, v, r in zip(outs[1:], via, evens)]
        return [outs[-1]] + first + even

    def gather(part, count, unit):
        got = [part] * count
        for r in [2 * i for i in range(1, count // 2)]:
            got[r] = move(part, "ctx", r * unit)
            got[r + 1] = move(got[r], "ctx", unit)
        if count > 1:
            got[1] = move(part, "ctx", unit)
        return got

    def after(x, *others):
        return lax.optimization_barrier((x, *others))

    def shape(*dims, dtype=F32):
        return jax.ShapeDtypeStruct(dims, dtype)

    flops = 2 * groups * tokens * width * hidden
    pieces = [shape(tokens, width)] * groups
    slices = [shape(len(m), 3, hidden // depth, width) for m in send_groups(depth)]
    joined = shape(tokens, heads, width, dtype=BF16)
    scratch = pltpu.VMEM((width // LANES, tokens * heads, LANES), F32)
    square = pltpu.VMEM((3, hidden, width), F32)

    def split(body, *args):
        outs = [shape(tokens, width, dtype=BF16)] + pieces[1:]
        body = functools.partial(body, groups)
        return call(body, outs, [scratch], 16 * flops, place, *args, mib=8)

    k_in = in_plane(split(split_kernel, keys[0]))
    s_in = in_plane(split(split_scaled_kernel, values[0], rates[0]))
    own = [lax.dynamic_index_in_dim(w, mine, 0, keepdims=False) for w in (w_gate, w_out, w_up)]
    own_scale = lax.dynamic_index_in_dim(head_scale, mine, 0, keepdims=True)[None, :]
    k_in, s_in, queries, cotangent = after(k_in, s_in, queries, cotangent)

    def kept(*dims, dtype=F32):
        return shape(*dims, tokens, width, dtype=dtype)

    out = call(
        functools.partial(update_kernel, groups, depth, scale),
        [kept(groups, dtype=BF16)] * 2 + slices, [square], 6 * flops,
        place, *k_in, *s_in, *own,
    )
    early, terms = out[:2], out[2:]
    *q_out, scale_row = call(
        functools.partial(split_apply_kernel, groups),
        [shape(2, tokens, width)] * groups + [shape(8, width)],
        [scratch], flops // 8, place, queries[0], cotangent[0], gain, own_scale,
    )
    q_in = in_plane(q_out[:-1])
    new = functools.reduce(jnp.add, scatter(terms, depth, groups))
    new, q_in, q_last = after(new, q_in, q_out[-1])
    q_in.append(move(q_last, "ctx", groups - 1))
    new = gather(new, depth, groups)
    *passed, stats = call(
        functools.partial(apply_kernel, groups, depth),
        [kept(groups), kept(groups), kept(groups, dtype=BF16), kept(groups)]
        + [shape(3, hidden, width, dtype=BF16), shape(2, groups, tokens)],
        [square], 3 * flops, place, scale_row, *q_in, *new,
    )
    bit = 1
    while bit < head_axis:
        stats = stats + move(stats, "head", bit)
        bit *= 2
    out = call(
        functools.partial(apply_back_kernel, groups, depth, count), pieces + slices,
        [square, pltpu.VMEM((2, groups, tokens), F32)], 6 * flops,
        place, scale_row, *q_in, *in_plane([stats] * groups), *passed,
    )
    out, early = after(out, early)
    saved = call(
        update_keep_kernel, [kept(groups)] * 6 + [kept(groups, dtype=BF16)] * 3, [], 3 * flops,
        *early, *own,
    )
    part = functools.reduce(jnp.add, scatter(out[groups:], depth, groups))
    parts = gather(part, depth, groups)
    (grad_q,) = call(
        functools.partial(join_query_kernel, groups), [joined], [scratch], flops // 16,
        place, *in_plane(out[:groups]),
    )
    parts, grad_q, saved = after(parts, grad_q, saved)
    rows = hidden // depth
    out = call(
        functools.partial(update_back_kernel, groups, depth, scale),
        [shape(2, tokens, width)] * groups + slices, [square] * 2, 12 * flops,
        place, *early, *saved, *parts, *own, mib=24,
    )
    back = in_plane(out[:groups])
    ends = scatter(out[groups:], depth, groups, one_by_one=False)
    own_rows = rows // groups
    sent = call(
        functools.partial(rows_kernel, groups),
        [shape(1, 3, own_rows, width)] * groups,
        [pltpu.VMEM((3, rows, width), F32)], flops // 100, place, part, *ends,
    )
    grad_k, grad_v, *grads = call(
        functools.partial(join_update_kernel, groups),
        [joined] * 2 + [shape(heads, own_rows, width)] * 3, [scratch] * 2, flops // 8,
        place, rates[0], *back, *in_plane(sent),
    )
    if lax.axis_size("batch") > 1:
        grads = [lax.psum_scatter(x, "batch", scatter_dimension=1, tiled=True) for x in grads]
    return (grad_q[None], grad_k[None], grad_v[None], grads[0], grads[1], grads[2])


def solution(mesh):
    in_specs = (
        P("batch", "ctx", "head", None),
        P("batch", "ctx", "head", None),
        P("batch", "ctx", "head", None),
        P("batch", "head", "ctx"),
        P("head"),
        P("head", None),
        P("head", None, None),
        P("head", None, None),
        P("head", None, None),
        P("batch", "ctx", "head", None),
    )
    out_specs = (
        P("batch", "ctx", "head", None),
        P("batch", "ctx", "head", None),
        P("batch", "ctx", "head", None),
        P("head", ("ctx", "batch"), None),
        P("head", ("ctx", "batch"), None),
        P("head", ("ctx", "batch"), None),
    )
    return jax.shard_map(local, mesh=mesh, in_specs=in_specs, out_specs=out_specs, check_vma=False)
```

```python
import functools
import math

import jax
import jax.numpy as jnp
from jax import lax
from jax.experimental import pallas as pl
from jax.experimental.pallas import tpu as pltpu
from jax.sharding import PartitionSpec as P

F32 = jnp.float32
BF16 = jnp.bfloat16
LANES = 128
MIB = 1024 * 1024


def mm(a, b):
    return jnp.dot(a, b, preferred_element_type=F32)


def mm_t(a, b):
    return lax.dot_general(a, b, (((1,), (1,)), ((), ())), preferred_element_type=F32)


def tmm(a, b):
    return lax.dot_general(a, b, (((0,), (0,)), ((), ())), preferred_element_type=F32)


def call(body, out_shape, scratch, flops, *args, mib=16):
    smem = pl.BlockSpec(memory_space=pltpu.SMEM)
    vmem = pl.BlockSpec(memory_space=pltpu.VMEM)
    size = sum(a.size * a.dtype.itemsize for a in args)
    size += sum(math.prod(o.shape) * o.dtype.itemsize for o in out_shape)
    return pl.pallas_call(
        body,
        out_shape=out_shape,
        in_specs=[smem if a.dtype == jnp.int32 else vmem for a in args],
        out_specs=[vmem] * len(out_shape),
        scratch_shapes=scratch,
        compiler_params=pltpu.CompilerParams(vmem_limit_bytes=mib * MIB),
        cost_estimate=pl.CostEstimate(flops=flops, bytes_accessed=size, transcendentals=0),
    )(*args)


def put_rows(scratch, x):
    for i in range(scratch.shape[0]):
        scratch[i] = x[:, i * LANES : (i + 1) * LANES]


def take_head(scratch, head, tokens, heads):
    parts = [scratch[i, pl.ds(head, tokens, stride=heads), :] for i in range(scratch.shape[0])]
    return jnp.concatenate(parts, axis=1)


def put_head(scratch, head, x, tokens, heads):
    for i in range(scratch.shape[0]):
        scratch[i, pl.ds(head, tokens, stride=heads), :] = x[:, i * LANES : (i + 1) * LANES]


def rows_of(scratch):
    return jnp.concatenate([scratch[i] for i in range(scratch.shape[0])], axis=1)


def split_kernel(groups, place, x, *rest):
    outs, scratch = rest[:groups], rest[groups]
    tokens, heads, width = x.shape
    put_rows(scratch, x[...].astype(F32).reshape(tokens * heads, width))
    for step, out in enumerate(outs):
        out[...] = take_head(scratch, place[0] ^ step, tokens, heads).astype(out.dtype)


def split_scaled_kernel(groups, place, x, r, *rest):
    outs = rest[:groups]
    split_kernel(groups, place, x, *rest)
    for step in range(groups):
        scaled = outs[step][...].astype(F32) * rate_column(r, place[0] ^ step)
        outs[step][...] = scaled.astype(BF16).astype(outs[step].dtype)


def split_apply_kernel(groups, place, q, cot, gain, scale, *rest):
    outs, scale_row, scratch = rest[:groups], rest[groups], rest[groups + 1]
    scale_row[...] = jnp.broadcast_to(scale[...], scale_row.shape)
    split_kernel(groups, place, q, *[out.at[0] for out in outs], scratch)
    split_kernel(groups, place, cot, *[out.at[1] for out in outs], scratch)
    for step in range(groups):
        outs[step][1] *= gain[pl.ds(place[0] ^ step, 1), :]


def packing(groups):
    if groups == 4:
        return [[(0, 0), (0, 1)], [(1, 0), (1, 1), (3, 0)], [(2, 0), (2, 1), (3, 1)]]
    return [[(step, 0), (step, 1)] for step in range(groups)]


def unpacked(groups, refs):
    found = {}
    for ref, members in zip(refs, packing(groups)):
        for i, member in enumerate(members):
            found[member] = ref.at[i]
    for i, ref in enumerate(refs[len(packing(groups)) :]):
        found[(groups - 1, i)] = ref
    return [(found[(step, 0)], found[(step, 1)]) for step in range(groups)]


def rate_column(r, head):
    return jnp.broadcast_to(r[pl.ds(head, 1), :], (8, r.shape[1])).T[:, 0:1]


def send_groups(count):
    odd = list(range(3, count, 2))
    return ([odd] if odd else []) + [[r] for r in [1] + list(range(2, count, 2)) if r < count] + [[0]]


def send_slices(sums, outs, own, count):
    rows = sums.shape[1] // count
    for out, members in zip(outs, send_groups(count)):
        for i, step in enumerate(members):
            at = pl.multiple_of((own ^ step) * rows, rows)
            out[i] = sums[:, pl.ds(at, rows), :]


def update_sums(keys_in, scaled_in, weights, key_kept, scaled_kept):
    gate_b, out_b, up_b = (w[...].astype(BF16) for w in weights)
    total = [0.0, 0.0, 0.0]
    for step, (key, value) in enumerate(zip(keys_in, scaled_in)):
        keys = key[...].astype(BF16)
        scaled = value[...].astype(BF16)
        key_kept[step] = keys
        scaled_kept[step] = scaled
        first = mm(keys, gate_b)
        third = mm(keys, up_b)
        sig = jax.nn.sigmoid(first)
        activ = first * sig
        act = (activ * third).astype(BF16)
        dact = mm_t(scaled, out_b)
        deriv = sig * (1.0 + first * (1.0 - sig))
        dfirst = (dact * third * deriv).astype(BF16)
        dthird = (dact * activ).astype(BF16)
        total[0] += tmm(keys, dfirst)
        total[1] += tmm(act, scaled)
        total[2] += tmm(keys, dthird)
    return total


def update_kernel(count, depth, scale, place, *refs):
    keys_in, scaled_in, weights = refs[:count], refs[count : 2 * count], refs[2 * count :][:3]
    key_kept, scaled_kept = refs[2 * count + 3 : 2 * count + 5]
    outs, sums = refs[2 * count + 5 : -1], refs[-1]
    total = update_sums(keys_in, scaled_in, weights, key_kept, scaled_kept)
    for i in range(3):
        sums[i] = total[i] * scale
    send_slices(sums, outs, place[1], depth)
    rows = sums.shape[1] // depth
    at = pl.multiple_of(place[1] * rows, rows)
    for i, w in enumerate(weights):
        outs[-1][0, i] += w[pl.ds(at, rows), :]


def assemble(place, parts, whole):
    rows = parts[0].shape[2]
    for step, part in enumerate(parts):
        at = pl.multiple_of((place[1] ^ step) * rows, rows)
        whole[:, pl.ds(at, rows), :] = part[0]


def apply_kernel(groups, depth, place, scale_row, *refs):
    pieces = refs[:groups]
    parts = refs[groups : groups + depth]
    activ_ref, slope_ref, hidden_ref, os_ref, new_b, stats, whole = refs[groups + depth :]
    assemble(place, parts, whole)
    new_b[...] = whole[...].astype(BF16)
    for step in range(groups):
        queries = pieces[step][0].astype(BF16)
        tokens = queries.shape[0]
        first = mm(queries, new_b[0])
        third = mm(queries, new_b[2])
        sig = jax.nn.sigmoid(first)
        activ = first * sig
        hidden = (activ * third).astype(BF16)
        scaled = mm(hidden, new_b[1]) * scale_row[0:1, :]
        activ_ref[step] = activ
        slope_ref[step] = third * (sig * (1.0 + first * (1.0 - sig)))
        hidden_ref[step] = hidden
        os_ref[step] = scaled
        sq = jnp.sum(scaled * scaled, axis=1, keepdims=True)
        ps = jnp.sum(scaled * pieces[step][1], axis=1, keepdims=True)
        lane = lax.broadcasted_iota(jnp.int32, (tokens, LANES), 1)
        both = jnp.where(lane == 0, sq, jnp.where(lane == 1, ps, 0.0)).T
        source = place[0] ^ step
        stats[0, pl.ds(source, 1), :] = both[0:1, :]
        stats[1, pl.ds(source, 1), :] = both[1:2, :]


def apply_back_kernel(groups, depth, count, place, scale_row, *refs):
    pieces, stats = refs[:groups], refs[groups : 2 * groups]
    activ_ref, slope_ref, hidden_ref, os_ref, new_b = refs[2 * groups : 2 * groups + 5]
    outs = refs[2 * groups + 5 : 3 * groups + 5]
    slices, sums, both = refs[3 * groups + 5 : -2], refs[-2], refs[-1]
    total_stats = stats[0][...]
    for other in stats[1:]:
        total_stats += other[...]
    both[...] = total_stats
    total = [0.0, 0.0, 0.0]
    for step in range(groups):
        queries = pieces[step][0].astype(BF16)
        source = place[0] ^ step
        sq = rate_column(both.at[0], source)
        ps = rate_column(both.at[1], source)
        inv = lax.rsqrt(sq / count + 1e-06)
        dos = inv * pieces[step][1] - os_ref[step] * (inv * inv * inv * ps / count)
        dout = (dos * scale_row[0:1, :]).astype(BF16)
        dhidden = mm_t(dout, new_b[1])
        dthird = (dhidden * activ_ref[step]).astype(BF16)
        dfirst = (dhidden * slope_ref[step]).astype(BF16)
        outs[step][...] = mm_t(dfirst, new_b[0]) + mm_t(dthird, new_b[2])
        total[0] += tmm(queries, dfirst)
        total[1] += tmm(hidden_ref[step], dout)
        total[2] += tmm(queries, dthird)
    for i in range(3):
        sums[i] = total[i]
    send_slices(sums, slices, place[1], depth)


def update_keep_kernel(k_kept, s_kept, w_gate, w_out, w_up, *outs):
    dact_r, third_r, activ_r, deriv_r, slope_r, second_r, dfirst_r, dthird_r, act_r = outs
    gate_b, out_b, up_b = (w[...].astype(BF16) for w in (w_gate, w_out, w_up))
    for step in range(k_kept.shape[0]):
        keys, scaled = k_kept[step], s_kept[step]
        first = mm(keys, gate_b)
        third = mm(keys, up_b)
        dact = mm_t(scaled, out_b)
        sig = jax.nn.sigmoid(first)
        activ = first * sig
        slope = sig * (1.0 - sig)
        deriv = sig + first * slope
        third_deriv = third * deriv
        dact_r[step] = dact
        third_r[step] = third
        activ_r[step] = activ
        deriv_r[step] = deriv
        slope_r[step] = third_deriv
        second_r[step] = third * (slope * (2.0 + first * (1.0 - 2.0 * sig)))
        dfirst_r[step] = (dact * third_deriv).astype(BF16)
        dthird_r[step] = (dact * activ).astype(BF16)
        act_r[step] = (activ * third).astype(BF16)


def update_back_kernel(groups, depth, scale, place, *refs):
    (k_kept, s_kept), refs = refs[:2], refs[2:]
    kept, refs = refs[:9], refs[9:]
    dact_r, third_r, activ_r, deriv_r, slope_r, second_r, dfirst_r, dthird_r, act_r = kept
    parts, refs = refs[:depth], refs[depth:]
    w_gate, w_out, w_up = refs[:3]
    packed = len(packing(groups))
    outs, slices = unpacked(groups, refs[3 : packed + 3]), refs[packed + 3 : -2]
    whole, sums = refs[-2:]
    assemble(place, parts, whole)
    gate_b, out_b, up_b = (w[...].astype(BF16) for w in (w_gate, w_out, w_up))
    cot_gate, cot_out, cot_up = ((whole[i] * scale).astype(BF16) for i in range(3))
    total = [0.0, 0.0, 0.0]
    for step in range(groups):
        keys, scaled = k_kept[step], s_kept[step]
        bar_dfirst = mm(keys, cot_gate)
        bar_dthird = mm(keys, cot_up)
        bar_act = mm_t(scaled, cot_out)
        dact, activ, deriv = dact_r[step], activ_r[step], deriv_r[step]
        bar_activ = bar_dthird * dact + bar_act * third_r[step]
        bar_dact = (bar_dfirst * slope_r[step] + bar_dthird * activ).astype(BF16)
        bar_df_dact = bar_dfirst * dact
        bar_third = (bar_df_dact * deriv + bar_act * activ).astype(BF16)
        bar_first = (bar_activ * deriv + bar_df_dact * second_r[step]).astype(BF16)
        outs[step][0][...] = (
            mm_t(dfirst_r[step], cot_gate)
            + mm_t(dthird_r[step], cot_up)
            + mm_t(bar_first, gate_b)
            + mm_t(bar_third, up_b)
        )
        outs[step][1][...] = mm(act_r[step], cot_out) + mm(bar_dact, out_b)
        total[0] += tmm(keys, bar_first)
        total[1] += tmm(bar_dact, scaled)
        total[2] += tmm(keys, bar_third)
    for i in range(3):
        sums[i] = total[i]
    send_slices(sums, slices, place[1], depth)


def join_query_kernel(groups, place, *refs):
    pieces, out, scratch = refs[:groups], refs[groups], refs[groups + 1]
    tokens, heads, width = out.shape
    for step, piece in enumerate(pieces):
        put_head(scratch, place[0] ^ step, piece[...], tokens, heads)
    out[...] = rows_of(scratch).reshape(tokens, heads, width).astype(BF16)


def join_update_kernel(groups, place, r, *refs):
    (out_k, out_v, *grads), (sk, sv) = refs[-7:-2], refs[-2:]
    pieces, parts = unpacked(groups, refs[: -7 - groups]), refs[-7 - groups : -7]
    tokens, heads, width = out_k.shape
    for step, piece in enumerate(pieces):
        head = place[0] ^ step
        put_head(sk, head, piece[0][...], tokens, heads)
        put_head(sv, head, piece[1][...] * rate_column(r, head), tokens, heads)
        for i, grad in enumerate(grads):
            grad[head] = parts[step][0, i]
    out_k[...] = rows_of(sk).reshape(tokens, heads, width).astype(BF16)
    out_v[...] = rows_of(sv).reshape(tokens, heads, width).astype(BF16)


def rows_kernel(groups, place, *refs):
    parts, outs, total = refs[: -groups - 1], refs[-groups - 1 : -1], refs[-1]
    summed = parts[0][0]
    for part in parts[1:]:
        summed += part[0]
    total[...] = summed
    rows = total.shape[1] // groups
    for step, out in enumerate(outs):
        at = pl.multiple_of((place[0] ^ step) * rows, rows)
        out[0] = total[:, pl.ds(at, rows), :]


def local(queries, keys, values, rates, head_scale, gain, w_gate, w_out, w_up, cotangent):
    tokens, heads, width = keys.shape[1:]
    hidden = w_gate.shape[2]
    ctx = lax.axis_size("ctx")
    head_axis = lax.axis_size("head")
    groups = heads
    depth = ctx // groups
    assert groups & (groups - 1) == 0 and depth & (depth - 1) == 0
    scale = 1.0 / math.sqrt(tokens * ctx * width)
    count = float(heads * head_axis * width)
    me = lax.axis_index("ctx")
    mine, layer = lax.rem(me, groups), lax.div(me, groups)
    place = jnp.stack([mine, layer]).astype(jnp.int32)

    def move(x, axis, step):
        return lax.ppermute(x, axis, [(c, c ^ step) for c in range(lax.axis_size(axis))])

    def in_plane(parts):
        return [parts[0]] + [move(p, "ctx", step) for step, p in enumerate(parts) if step]

    def forwarded(got):
        return [got[:1]] if got.shape[0] == 1 else [got[i : i + 1] for i in range(got.shape[0])]

    def scatter(outs, count, unit):
        outs = list(outs)
        evens = list(range(2, count, 2))
        via = forwarded(move(outs.pop(0), "ctx", unit)) if evens else []
        via, outs[0] = after(via, outs[0])
        first = [move(outs[0], "ctx", unit)] if count > 1 else []
        even = [move(p + v, "ctx", r * unit) for p, v, r in zip(outs[1:], via, evens)]
        return [outs[-1]] + first + even

    def gather(part, count, unit):
        got = [part] * count
        for r in [2 * i for i in range(1, count // 2)]:
            got[r] = move(part, "ctx", r * unit)
            got[r + 1] = move(got[r], "ctx", unit)
        if count > 1:
            got[1] = move(part, "ctx", unit)
        return got

    def after(x, *others):
        return lax.optimization_barrier((x, *others))

    def shape(*dims, dtype=F32):
        return jax.ShapeDtypeStruct(dims, dtype)

    flops = 2 * groups * tokens * width * hidden
    pieces = [shape(tokens, width)] * groups
    slices = [shape(len(m), 3, hidden // depth, width) for m in send_groups(depth)]
    joined = shape(tokens, heads, width, dtype=BF16)
    scratch = pltpu.VMEM((width // LANES, tokens * heads, LANES), F32)
    square = pltpu.VMEM((3, hidden, width), F32)

    def split(body, *args):
        outs = [shape(tokens, width, dtype=BF16)] + pieces[1:]
        body = functools.partial(body, groups)
        return call(body, outs, [scratch], 16 * flops, place, *args, mib=8)

    k_in = in_plane(split(split_kernel, keys[0]))
    s_in = in_plane(split(split_scaled_kernel, values[0], rates[0]))
    own = [lax.dynamic_index_in_dim(w, mine, 0, keepdims=False) for w in (w_gate, w_out, w_up)]
    own_scale = lax.dynamic_index_in_dim(head_scale, mine, 0, keepdims=True)[None, :]
    k_in, s_in, queries, cotangent = after(k_in, s_in, queries, cotangent)

    def kept(*dims, dtype=F32):
        return shape(*dims, tokens, width, dtype=dtype)

    out = call(
        functools.partial(update_kernel, groups, depth, scale),
        [kept(groups, dtype=BF16)] * 2 + slices, [square], 6 * flops,
        place, *k_in, *s_in, *own,
    )
    early, terms = out[:2], out[2:]
    *q_out, scale_row = call(
        functools.partial(split_apply_kernel, groups),
        [shape(2, tokens, width)] * groups + [shape(8, width)],
        [scratch], flops // 8, place, queries[0], cotangent[0], gain, own_scale,
    )
    q_in = in_plane(q_out[:-1])
    new = functools.reduce(jnp.add, scatter(terms, depth, groups))
    new, q_in, q_last = after(new, q_in, q_out[-1])
    q_in.append(move(q_last, "ctx", groups - 1))
    new = gather(new, depth, groups)
    *passed, stats = call(
        functools.partial(apply_kernel, groups, depth),
        [kept(groups), kept(groups), kept(groups, dtype=BF16), kept(groups)]
        + [shape(3, hidden, width, dtype=BF16), shape(2, groups, tokens)],
        [square], 3 * flops, place, scale_row, *q_in, *new,
    )
    bit = 1
    while bit < head_axis:
        stats = stats + move(stats, "head", bit)
        bit *= 2
    out = call(
        functools.partial(apply_back_kernel, groups, depth, count), pieces + slices,
        [square, pltpu.VMEM((2, groups, tokens), F32)], 6 * flops,
        place, scale_row, *q_in, *in_plane([stats] * groups), *passed,
    )
    out, early = after(out, early)
    saved = call(
        update_keep_kernel, [kept(groups)] * 6 + [kept(groups, dtype=BF16)] * 3, [], 3 * flops,
        *early, *own,
    )
    part = functools.reduce(jnp.add, scatter(out[groups:], depth, groups))
    parts = gather(part, depth, groups)
    (grad_q,) = call(
        functools.partial(join_query_kernel, groups), [joined], [scratch], flops // 16,
        place, *in_plane(out[:groups]),
    )
    parts, grad_q, saved = after(parts, grad_q, saved)
    rows = hidden // depth
    out = call(
        functools.partial(update_back_kernel, groups, depth, scale),
        [kept(len(members)) for members in packing(groups)] + slices, [square] * 2, 12 * flops,
        place, *early, *saved, *parts, *own, mib=24,
    )
    packed = len(packing(groups))
    back = in_plane(out[:packed])
    ends = scatter(out[packed:], depth, groups)
    if groups == 4:
        ends, back = after(ends, back)
        back += [move(back[1][2], "ctx", 2), move(back[2][2], "ctx", 1)]
    own_rows = rows // groups
    sent = call(
        functools.partial(rows_kernel, groups),
        [shape(1, 3, own_rows, width)] * groups,
        [pltpu.VMEM((3, rows, width), F32)], flops // 100, place, part, *ends,
    )
    grad_k, grad_v, *grads = call(
        functools.partial(join_update_kernel, groups),
        [joined] * 2 + [shape(heads, own_rows, width)] * 3, [scratch] * 2, flops // 8,
        place, rates[0], *back, *in_plane(sent),
    )
    if lax.axis_size("batch") > 1:
        grads = [lax.psum_scatter(x, "batch", scatter_dimension=1, tiled=True) for x in grads]
    return (grad_q[None], grad_k[None], grad_v[None], grads[0], grads[1], grads[2])


def solution(mesh):
    in_specs = (
        P("batch", "ctx", "head", None),
        P("batch", "ctx", "head", None),
        P("batch", "ctx", "head", None),
        P("batch", "head", "ctx"),
        P("head"),
        P("head", None),
        P("head", None, None),
        P("head", None, None),
        P("head", None, None),
        P("batch", "ctx", "head", None),
    )
    out_specs = (
        P("batch", "ctx", "head", None),
        P("batch", "ctx", "head", None),
        P("batch", "ctx", "head", None),
        P("head", ("ctx", "batch"), None),
        P("head", ("ctx", "batch"), None),
        P("head", ("ctx", "batch"), None),
    )
    return jax.shard_map(local, mesh=mesh, in_specs=in_specs, out_specs=out_specs, check_vma=False)
```

```python
import functools
import math

import jax
import jax.numpy as jnp
from jax import lax
from jax.experimental import pallas as pl
from jax.experimental.pallas import tpu as pltpu
from jax.sharding import PartitionSpec as P

F32 = jnp.float32
BF16 = jnp.bfloat16
LANES = 128
MIB = 1024 * 1024


def mm(a, b):
    return jnp.dot(a, b, preferred_element_type=F32)


def mm_t(a, b):
    return lax.dot_general(a, b, (((1,), (1,)), ((), ())), preferred_element_type=F32)


def tmm(a, b):
    return lax.dot_general(a, b, (((0,), (0,)), ((), ())), preferred_element_type=F32)


def call(body, out_shape, scratch, flops, *args, mib=16):
    smem = pl.BlockSpec(memory_space=pltpu.SMEM)
    vmem = pl.BlockSpec(memory_space=pltpu.VMEM)
    size = sum(a.size * a.dtype.itemsize for a in args)
    size += sum(math.prod(o.shape) * o.dtype.itemsize for o in out_shape)
    return pl.pallas_call(
        body,
        out_shape=out_shape,
        in_specs=[smem if a.dtype == jnp.int32 else vmem for a in args],
        out_specs=[vmem] * len(out_shape),
        scratch_shapes=scratch,
        compiler_params=pltpu.CompilerParams(vmem_limit_bytes=mib * MIB),
        cost_estimate=pl.CostEstimate(flops=flops, bytes_accessed=size, transcendentals=0),
    )(*args)


def put_rows(scratch, x):
    for i in range(scratch.shape[0]):
        scratch[i] = x[:, i * LANES : (i + 1) * LANES]


def take_head(scratch, head, tokens, heads):
    parts = [scratch[i, pl.ds(head, tokens, stride=heads), :] for i in range(scratch.shape[0])]
    return jnp.concatenate(parts, axis=1)


def put_head(scratch, head, x, tokens, heads):
    for i in range(scratch.shape[0]):
        scratch[i, pl.ds(head, tokens, stride=heads), :] = x[:, i * LANES : (i + 1) * LANES]


def rows_of(scratch):
    return jnp.concatenate([scratch[i] for i in range(scratch.shape[0])], axis=1)


def split_kernel(groups, place, x, *rest):
    outs, scratch = rest[:groups], rest[groups]
    tokens, heads, width = x.shape
    put_rows(scratch, x[...].astype(F32).reshape(tokens * heads, width))
    for step, out in enumerate(outs):
        out[...] = take_head(scratch, place[0] ^ step, tokens, heads).astype(out.dtype)


def split_scaled_kernel(groups, place, x, r, *rest):
    outs = rest[:groups]
    split_kernel(groups, place, x, *rest)
    for step in range(groups):
        scaled = outs[step][...].astype(F32) * rate_column(r, place[0] ^ step)
        outs[step][...] = scaled.astype(BF16).astype(outs[step].dtype)


def split_apply_kernel(groups, place, q, cot, gain, scale, *rest):
    outs, scale_row, scratch = rest[:groups], rest[groups], rest[groups + 1]
    scale_row[...] = jnp.broadcast_to(scale[...], scale_row.shape)
    split_kernel(groups, place, q, *[out.at[0] for out in outs], scratch)
    split_kernel(groups, place, cot, *[out.at[1] for out in outs], scratch)
    for step in range(groups):
        outs[step][1] *= gain[pl.ds(place[0] ^ step, 1), :]


def packing(groups):
    if groups == 4:
        return [[(0, 0), (0, 1)], [(1, 0), (1, 1), (3, 0)], [(2, 0), (2, 1), (3, 1)]]
    return [[(step, 0), (step, 1)] for step in range(groups)]


def unpacked(groups, refs):
    found = {}
    for ref, members in zip(refs, packing(groups)):
        for i, member in enumerate(members):
            found[member] = ref.at[i]
    for i, ref in enumerate(refs[len(packing(groups)) :]):
        found[(groups - 1, i)] = ref
    return [(found[(step, 0)], found[(step, 1)]) for step in range(groups)]


def rate_column(r, head):
    return jnp.broadcast_to(r[pl.ds(head, 1), :], (8, r.shape[1])).T[:, 0:1]


def send_groups(count):
    odd = list(range(3, count, 2))
    return ([odd] if odd else []) + [[r] for r in [1] + list(range(2, count, 2)) if r < count] + [[0]]


def send_slices(sums, outs, own, count):
    rows = sums.shape[1] // count
    for out, members in zip(outs, send_groups(count)):
        for i, step in enumerate(members):
            at = pl.multiple_of((own ^ step) * rows, rows)
            out[i] = sums[:, pl.ds(at, rows), :]


def update_sums(keys_in, scaled_in, weights, key_kept, scaled_kept):
    gate_b, out_b, up_b = (w[...].astype(BF16) for w in weights)
    total = [0.0, 0.0, 0.0]
    for step, (key, value) in enumerate(zip(keys_in, scaled_in)):
        keys = key[...].astype(BF16)
        scaled = value[...].astype(BF16)
        key_kept[step] = keys
        scaled_kept[step] = scaled
        first = mm(keys, gate_b)
        third = mm(keys, up_b)
        sig = jax.nn.sigmoid(first)
        activ = first * sig
        act = (activ * third).astype(BF16)
        dact = mm_t(scaled, out_b)
        deriv = sig * (1.0 + first * (1.0 - sig))
        dfirst = (dact * third * deriv).astype(BF16)
        dthird = (dact * activ).astype(BF16)
        total[0] += tmm(keys, dfirst)
        total[1] += tmm(act, scaled)
        total[2] += tmm(keys, dthird)
    return total


def update_kernel(count, depth, scale, place, *refs):
    keys_in, scaled_in, weights = refs[:count], refs[count : 2 * count], refs[2 * count :][:3]
    key_kept, scaled_kept = refs[2 * count + 3 : 2 * count + 5]
    outs, sums = refs[2 * count + 5 : -1], refs[-1]
    total = update_sums(keys_in, scaled_in, weights, key_kept, scaled_kept)
    for i in range(3):
        sums[i] = total[i] * scale
    send_slices(sums, outs, place[1], depth)
    rows = sums.shape[1] // depth
    at = pl.multiple_of(place[1] * rows, rows)
    for i, w in enumerate(weights):
        outs[-1][0, i] += w[pl.ds(at, rows), :]


def assemble(place, parts, whole):
    rows = parts[0].shape[2]
    for step, part in enumerate(parts):
        at = pl.multiple_of((place[1] ^ step) * rows, rows)
        whole[:, pl.ds(at, rows), :] = part[0]


def apply_kernel(groups, depth, place, scale_row, *refs):
    pieces = refs[:groups]
    parts = refs[groups : groups + depth]
    activ_ref, slope_ref, hidden_ref, os_ref, new_b, stats, whole = refs[groups + depth :]
    assemble(place, parts, whole)
    new_b[...] = whole[...].astype(BF16)
    for step in range(groups):
        queries = pieces[step][0].astype(BF16)
        tokens = queries.shape[0]
        first = mm(queries, new_b[0])
        third = mm(queries, new_b[2])
        sig = jax.nn.sigmoid(first)
        activ = first * sig
        hidden = (activ * third).astype(BF16)
        scaled = mm(hidden, new_b[1]) * scale_row[0:1, :]
        activ_ref[step] = activ
        slope_ref[step] = third * (sig * (1.0 + first * (1.0 - sig)))
        hidden_ref[step] = hidden
        os_ref[step] = scaled
        sq = jnp.sum(scaled * scaled, axis=1, keepdims=True)
        ps = jnp.sum(scaled * pieces[step][1], axis=1, keepdims=True)
        lane = lax.broadcasted_iota(jnp.int32, (tokens, LANES), 1)
        both = jnp.where(lane == 0, sq, jnp.where(lane == 1, ps, 0.0)).T
        source = place[0] ^ step
        stats[0, pl.ds(source, 1), :] = both[0:1, :]
        stats[1, pl.ds(source, 1), :] = both[1:2, :]


def apply_back_kernel(groups, depth, count, place, scale_row, stats, *refs):
    pieces, refs = refs[:groups], refs[groups:]
    activ_ref, slope_ref, hidden_ref, os_ref, new_b = refs[:5]
    dfirst_ref, dthird_ref, slices, sums = refs[5], refs[6], refs[7:-1], refs[-1]
    total = [0.0, 0.0, 0.0]
    for step in range(groups):
        queries = pieces[step][0].astype(BF16)
        source = place[0] ^ step
        sq = rate_column(stats.at[0], source)
        ps = rate_column(stats.at[1], source)
        inv = lax.rsqrt(sq / count + 1e-06)
        dos = inv * pieces[step][1] - os_ref[step] * (inv * inv * inv * ps / count)
        dout = (dos * scale_row[0:1, :]).astype(BF16)
        dhidden = mm_t(dout, new_b[1])
        dthird = (dhidden * activ_ref[step]).astype(BF16)
        dfirst = (dhidden * slope_ref[step]).astype(BF16)
        dfirst_ref[step] = dfirst
        dthird_ref[step] = dthird
        total[0] += tmm(queries, dfirst)
        total[1] += tmm(hidden_ref[step], dout)
        total[2] += tmm(queries, dthird)
    for i in range(3):
        sums[i] = total[i]
    send_slices(sums, slices, place[1], depth)


def query_back_kernel(dfirst, dthird, new_b, *outs):
    for step, out in enumerate(outs):
        out[...] = mm_t(dfirst[step], new_b[0]) + mm_t(dthird[step], new_b[2])


def update_keep_kernel(k_kept, s_kept, w_gate, w_out, w_up, *outs):
    dact_r, third_r, activ_r, deriv_r, slope_r, second_r, dfirst_r, dthird_r, act_r = outs
    gate_b, out_b, up_b = (w[...].astype(BF16) for w in (w_gate, w_out, w_up))
    for step in range(k_kept.shape[0]):
        keys, scaled = k_kept[step], s_kept[step]
        first = mm(keys, gate_b)
        third = mm(keys, up_b)
        dact = mm_t(scaled, out_b)
        sig = jax.nn.sigmoid(first)
        activ = first * sig
        slope = sig * (1.0 - sig)
        deriv = sig + first * slope
        third_deriv = third * deriv
        dact_r[step] = dact
        third_r[step] = third
        activ_r[step] = activ
        deriv_r[step] = deriv
        slope_r[step] = third_deriv
        second_r[step] = third * (slope * (2.0 + first * (1.0 - 2.0 * sig)))
        dfirst_r[step] = (dact * third_deriv).astype(BF16)
        dthird_r[step] = (dact * activ).astype(BF16)
        act_r[step] = (activ * third).astype(BF16)


def update_back_kernel(groups, depth, scale, place, *refs):
    (k_kept, s_kept), refs = refs[:2], refs[2:]
    kept, refs = refs[:9], refs[9:]
    dact_r, third_r, activ_r, deriv_r, slope_r, second_r, dfirst_r, dthird_r, act_r = kept
    parts, refs = refs[:depth], refs[depth:]
    w_gate, w_out, w_up = refs[:3]
    packed = len(packing(groups))
    outs, slices = unpacked(groups, refs[3 : packed + 3]), refs[packed + 3 : -2]
    whole, sums = refs[-2:]
    assemble(place, parts, whole)
    gate_b, out_b, up_b = (w[...].astype(BF16) for w in (w_gate, w_out, w_up))
    cot_gate, cot_out, cot_up = ((whole[i] * scale).astype(BF16) for i in range(3))
    total = [0.0, 0.0, 0.0]
    for step in range(groups):
        keys, scaled = k_kept[step], s_kept[step]
        bar_dfirst = mm(keys, cot_gate)
        bar_dthird = mm(keys, cot_up)
        bar_act = mm_t(scaled, cot_out)
        dact, activ, deriv = dact_r[step], activ_r[step], deriv_r[step]
        bar_activ = bar_dthird * dact + bar_act * third_r[step]
        bar_dact = (bar_dfirst * slope_r[step] + bar_dthird * activ).astype(BF16)
        bar_df_dact = bar_dfirst * dact
        bar_third = (bar_df_dact * deriv + bar_act * activ).astype(BF16)
        bar_first = (bar_activ * deriv + bar_df_dact * second_r[step]).astype(BF16)
        outs[step][0][...] = (
            mm_t(dfirst_r[step], cot_gate)
            + mm_t(dthird_r[step], cot_up)
            + mm_t(bar_first, gate_b)
            + mm_t(bar_third, up_b)
        )
        outs[step][1][...] = mm(act_r[step], cot_out) + mm(bar_dact, out_b)
        total[0] += tmm(keys, bar_first)
        total[1] += tmm(bar_dact, scaled)
        total[2] += tmm(keys, bar_third)
    for i in range(3):
        sums[i] = total[i]
    send_slices(sums, slices, place[1], depth)


def join_query_kernel(groups, place, *refs):
    pieces, out, scratch = refs[:groups], refs[groups], refs[groups + 1]
    tokens, heads, width = out.shape
    for step, piece in enumerate(pieces):
        put_head(scratch, place[0] ^ step, piece[...], tokens, heads)
    out[...] = rows_of(scratch).reshape(tokens, heads, width).astype(BF16)


def join_update_kernel(groups, place, r, *refs):
    pieces, (out_k, out_v, sk, sv) = unpacked(groups, refs[:-4]), refs[-4:]
    tokens, heads, width = out_k.shape
    for step, piece in enumerate(pieces):
        head = place[0] ^ step
        put_head(sk, head, piece[0][...], tokens, heads)
        put_head(sv, head, piece[1][...] * rate_column(r, head), tokens, heads)
    out_k[...] = rows_of(sk).reshape(tokens, heads, width).astype(BF16)
    out_v[...] = rows_of(sv).reshape(tokens, heads, width).astype(BF16)


def join_rows_kernel(groups, place, *refs):
    parts, grads = refs[:groups], refs[groups:]
    for step, part in enumerate(parts):
        for i, grad in enumerate(grads):
            grad[place[0] ^ step] = part[0, i]


def rows_kernel(groups, place, *refs):
    parts, outs, total = refs[: -groups - 1], refs[-groups - 1 : -1], refs[-1]
    summed = parts[0][0]
    for part in parts[1:]:
        summed += part[0]
    total[...] = summed
    rows = total.shape[1] // groups
    for step, out in enumerate(outs):
        at = pl.multiple_of((place[0] ^ step) * rows, rows)
        out[0] = total[:, pl.ds(at, rows), :]


def local(queries, keys, values, rates, head_scale, gain, w_gate, w_out, w_up, cotangent):
    tokens, heads, width = keys.shape[1:]
    hidden = w_gate.shape[2]
    ctx = lax.axis_size("ctx")
    head_axis = lax.axis_size("head")
    groups = heads
    depth = ctx // groups
    assert groups & (groups - 1) == 0 and depth & (depth - 1) == 0
    scale = 1.0 / math.sqrt(tokens * ctx * width)
    count = float(heads * head_axis * width)
    me = lax.axis_index("ctx")
    mine, layer = lax.rem(me, groups), lax.div(me, groups)
    place = jnp.stack([mine, layer]).astype(jnp.int32)

    def move(x, axis, step):
        return lax.ppermute(x, axis, [(c, c ^ step) for c in range(lax.axis_size(axis))])

    def in_plane(parts):
        return [parts[0]] + [move(p, "ctx", step) for step, p in enumerate(parts) if step]

    def forwarded(got):
        return [got[:1]] if got.shape[0] == 1 else [got[i : i + 1] for i in range(got.shape[0])]

    def scatter(outs, count, unit):
        outs = list(outs)
        evens = list(range(2, count, 2))
        via = forwarded(move(outs.pop(0), "ctx", unit)) if evens else []
        via, outs[0] = after(via, outs[0])
        first = [move(outs[0], "ctx", unit)] if count > 1 else []
        even = [move(p + v, "ctx", r * unit) for p, v, r in zip(outs[1:], via, evens)]
        return [outs[-1]] + first + even

    def gather(part, count, unit):
        got = [part] * count
        for r in [2 * i for i in range(1, count // 2)]:
            got[r] = move(part, "ctx", r * unit)
            got[r + 1] = move(got[r], "ctx", unit)
        if count > 1:
            got[1] = move(part, "ctx", unit)
        return got

    def after(x, *others):
        return lax.optimization_barrier((x, *others))

    def shape(*dims, dtype=F32):
        return jax.ShapeDtypeStruct(dims, dtype)

    flops = 2 * groups * tokens * width * hidden
    pieces = [shape(tokens, width)] * groups
    slices = [shape(len(m), 3, hidden // depth, width) for m in send_groups(depth)]
    joined = shape(tokens, heads, width, dtype=BF16)
    scratch = pltpu.VMEM((width // LANES, tokens * heads, LANES), F32)
    square = pltpu.VMEM((3, hidden, width), F32)

    def split(body, *args):
        outs = [shape(tokens, width, dtype=BF16)] + pieces[1:]
        body = functools.partial(body, groups)
        return call(body, outs, [scratch], 16 * flops, place, *args, mib=8)

    k_in = in_plane(split(split_kernel, keys[0]))
    s_in = in_plane(split(split_scaled_kernel, values[0], rates[0]))
    own = [lax.dynamic_index_in_dim(w, mine, 0, keepdims=False) for w in (w_gate, w_out, w_up)]
    own_scale = lax.dynamic_index_in_dim(head_scale, mine, 0, keepdims=True)[None, :]
    k_in, s_in, queries, cotangent = after(k_in, s_in, queries, cotangent)

    def kept(*dims, dtype=F32):
        return shape(*dims, tokens, width, dtype=dtype)

    out = call(
        functools.partial(update_kernel, groups, depth, scale),
        [kept(groups, dtype=BF16)] * 2 + slices, [square], 6 * flops,
        place, *k_in, *s_in, *own,
    )
    early, terms = out[:2], out[2:]
    *q_out, scale_row = call(
        functools.partial(split_apply_kernel, groups),
        [shape(2, tokens, width)] * groups + [shape(8, width)],
        [scratch], flops // 8, place, queries[0], cotangent[0], gain, own_scale,
    )
    q_in = in_plane(q_out[:-1])
    new = functools.reduce(jnp.add, scatter(terms, depth, groups))
    new, q_in, q_last = after(new, q_in, q_out[-1])
    q_in.append(move(q_last, "ctx", groups - 1))
    new = gather(new, depth, groups)
    *passed, stats = call(
        functools.partial(apply_kernel, groups, depth),
        [kept(groups), kept(groups), kept(groups, dtype=BF16), kept(groups)]
        + [shape(3, hidden, width, dtype=BF16), shape(2, groups, tokens)],
        [square], 3 * flops, place, scale_row, *q_in, *new,
    )
    for axis, size in (("head", lax.axis_size("head")), ("ctx", groups)):
        bit = 1
        while bit < size:
            stats = stats + move(stats, axis, bit)
            bit *= 2
    out = call(
        functools.partial(apply_back_kernel, groups, depth, count),
        [kept(groups, dtype=BF16)] * 2 + slices, [square], 6 * flops,
        place, scale_row, stats, *q_in, *passed,
    )
    q_sent = call(
        query_back_kernel, [shape(tokens, width)] * groups, [], 2 * flops, *out[:2], passed[-1]
    )
    out = out[2:]
    out, early = after(out, early)
    saved = call(
        update_keep_kernel, [kept(groups)] * 6 + [kept(groups, dtype=BF16)] * 3, [], 3 * flops,
        *early, *own,
    )
    part = functools.reduce(jnp.add, scatter(out, depth, groups))
    parts = gather(part, depth, groups)
    (grad_q,) = call(
        functools.partial(join_query_kernel, groups), [joined], [scratch], flops // 16,
        place, *in_plane(q_sent),
    )
    parts, grad_q, saved = after(parts, grad_q, saved)
    rows = hidden // depth
    out = call(
        functools.partial(update_back_kernel, groups, depth, scale),
        [kept(len(members)) for members in packing(groups)] + slices, [square] * 2, 12 * flops,
        place, *early, *saved, *parts, *own, mib=24,
    )
    packed = len(packing(groups))
    back = in_plane(out[:packed])
    ends = scatter(out[packed:], depth, groups)
    if groups == 4:
        ends, back = after(ends, back)
        back += [move(back[1][2], "ctx", 2), move(back[2][2], "ctx", 1)]
    own_rows = rows // groups
    sent = call(
        functools.partial(rows_kernel, groups),
        [shape(1, 3, own_rows, width)] * groups,
        [pltpu.VMEM((3, rows, width), F32)], flops // 100, place, part, *ends,
    )
    grad_k, grad_v = call(
        functools.partial(join_update_kernel, groups), [joined] * 2, [scratch] * 2, flops // 8,
        place, rates[0], *back,
    )
    got, grad_k, grad_v = after(in_plane(sent), grad_k, grad_v)
    grads = call(
        functools.partial(join_rows_kernel, groups), [shape(heads, own_rows, width)] * 3, [],
        flops // 100, place, *got,
    )
    if lax.axis_size("batch") > 1:
        grads = [lax.psum_scatter(x, "batch", scatter_dimension=1, tiled=True) for x in grads]
    return (grad_q[None], grad_k[None], grad_v[None], grads[0], grads[1], grads[2])


def solution(mesh):
    in_specs = (
        P("batch", "ctx", "head", None),
        P("batch", "ctx", "head", None),
        P("batch", "ctx", "head", None),
        P("batch", "head", "ctx"),
        P("head"),
        P("head", None),
        P("head", None, None),
        P("head", None, None),
        P("head", None, None),
        P("batch", "ctx", "head", None),
    )
    out_specs = (
        P("batch", "ctx", "head", None),
        P("batch", "ctx", "head", None),
        P("batch", "ctx", "head", None),
        P("head", ("ctx", "batch"), None),
        P("head", ("ctx", "batch"), None),
        P("head", ("ctx", "batch"), None),
    )
    return jax.shard_map(local, mesh=mesh, in_specs=in_specs, out_specs=out_specs, check_vma=False)
```

```python
import functools
import math

import jax
import jax.numpy as jnp
from jax import lax
from jax.experimental import pallas as pl
from jax.experimental.pallas import tpu as pltpu
from jax.sharding import PartitionSpec as P

F32 = jnp.float32
BF16 = jnp.bfloat16
LANES = 128
MIB = 1024 * 1024


def mm(a, b):
    return jnp.dot(a, b, preferred_element_type=F32)


def mm_t(a, b):
    return lax.dot_general(a, b, (((1,), (1,)), ((), ())), preferred_element_type=F32)


def tmm(a, b):
    return lax.dot_general(a, b, (((0,), (0,)), ((), ())), preferred_element_type=F32)


def call(body, out_shape, scratch, flops, *args, mib=16):
    smem = pl.BlockSpec(memory_space=pltpu.SMEM)
    vmem = pl.BlockSpec(memory_space=pltpu.VMEM)
    size = sum(a.size * a.dtype.itemsize for a in args)
    size += sum(math.prod(o.shape) * o.dtype.itemsize for o in out_shape)
    return pl.pallas_call(
        body,
        out_shape=out_shape,
        in_specs=[smem if a.dtype == jnp.int32 else vmem for a in args],
        out_specs=[vmem] * len(out_shape),
        scratch_shapes=scratch,
        compiler_params=pltpu.CompilerParams(vmem_limit_bytes=mib * MIB),
        cost_estimate=pl.CostEstimate(flops=flops, bytes_accessed=size, transcendentals=0),
    )(*args)


def put_rows(scratch, x):
    for i in range(scratch.shape[0]):
        scratch[i] = x[:, i * LANES : (i + 1) * LANES]


def take_head(scratch, head, tokens, heads):
    parts = [scratch[i, pl.ds(head, tokens, stride=heads), :] for i in range(scratch.shape[0])]
    return jnp.concatenate(parts, axis=1)


def put_head(scratch, head, x, tokens, heads):
    for i in range(scratch.shape[0]):
        scratch[i, pl.ds(head, tokens, stride=heads), :] = x[:, i * LANES : (i + 1) * LANES]


def rows_of(scratch):
    return jnp.concatenate([scratch[i] for i in range(scratch.shape[0])], axis=1)


def split_kernel(groups, place, x, *rest):
    outs, scratch = rest[:groups], rest[groups]
    tokens, heads, width = x.shape
    put_rows(scratch, x[...].astype(F32).reshape(tokens * heads, width))
    for step, out in enumerate(outs):
        out[...] = take_head(scratch, place[0] ^ step, tokens, heads).astype(out.dtype)


def split_scaled_kernel(groups, place, x, r, *rest):
    outs = rest[:groups]
    split_kernel(groups, place, x, *rest)
    for step in range(groups):
        scaled = outs[step][...].astype(F32) * rate_column(r, place[0] ^ step)
        outs[step][...] = scaled.astype(BF16).astype(outs[step].dtype)


def split_apply_kernel(groups, place, q, cot, gain, scale, *rest):
    outs, scale_row, scratch = rest[:-2], rest[-2], rest[-1]
    scale_row[...] = jnp.broadcast_to(scale[...], scale_row.shape)
    pieces = query_refs(groups, outs)
    split_kernel(groups, place, q, *[one for one, _ in pieces], scratch)
    split_kernel(groups, place, cot, *[two for _, two in pieces], scratch)
    for step in range(groups):
        pieces[step][1][...] *= gain[pl.ds(place[0] ^ step, 1), :]


def packing(groups):
    if groups == 4:
        return [[(0, 0), (0, 1)], [(1, 0), (1, 1), (3, 0)], [(2, 0), (2, 1), (3, 1)]]
    return [[(step, 0), (step, 1)] for step in range(groups)]


def unpacked(groups, refs):
    found = {}
    for ref, members in zip(refs, packing(groups)):
        for i, member in enumerate(members):
            found[member] = ref.at[i]
    for i, ref in enumerate(refs[len(packing(groups)) :]):
        found[(groups - 1, i)] = ref
    return [(found[(step, 0)], found[(step, 1)]) for step in range(groups)]


def rate_column(r, head):
    return jnp.broadcast_to(r[pl.ds(head, 1), :], (8, r.shape[1])).T[:, 0:1]


def send_groups(count):
    odd = list(range(3, count, 2))
    return ([odd] if odd else []) + [[r] for r in [1] + list(range(2, count, 2)) if r < count] + [[0]]


def send_slices(sums, outs, own, count):
    rows = sums.shape[1] // count
    for out, members in zip(outs, send_groups(count)):
        for i, step in enumerate(members):
            at = pl.multiple_of((own ^ step) * rows, rows)
            out[i] = sums[:, pl.ds(at, rows), :]


def update_sums(keys_in, scaled_in, weights, key_kept, scaled_kept):
    gate_b, out_b, up_b = (w[...].astype(BF16) for w in weights)
    total = [0.0, 0.0, 0.0]
    for step, (key, value) in enumerate(zip(keys_in, scaled_in)):
        keys = key[...].astype(BF16)
        scaled = value[...].astype(BF16)
        key_kept[step] = keys
        scaled_kept[step] = scaled
        first = mm(keys, gate_b)
        third = mm(keys, up_b)
        sig = jax.nn.sigmoid(first)
        activ = first * sig
        act = (activ * third).astype(BF16)
        dact = mm_t(scaled, out_b)
        deriv = sig * (1.0 + first * (1.0 - sig))
        dfirst = (dact * third * deriv).astype(BF16)
        dthird = (dact * activ).astype(BF16)
        total[0] += tmm(keys, dfirst)
        total[1] += tmm(act, scaled)
        total[2] += tmm(keys, dthird)
    return total


def update_kernel(count, depth, scale, place, *refs):
    keys_in, scaled_in, weights = refs[:count], refs[count : 2 * count], refs[2 * count :][:3]
    key_kept, scaled_kept = refs[2 * count + 3 : 2 * count + 5]
    outs, sums = refs[2 * count + 5 : -1], refs[-1]
    total = update_sums(keys_in, scaled_in, weights, key_kept, scaled_kept)
    for i in range(3):
        sums[i] = total[i] * scale
    send_slices(sums, outs, place[1], depth)
    rows = sums.shape[1] // depth
    at = pl.multiple_of(place[1] * rows, rows)
    for i, w in enumerate(weights):
        outs[-1][0, i] += w[pl.ds(at, rows), :]


def assemble(place, parts, whole):
    rows = parts[0].shape[2]
    for i, part in enumerate(parts):
        at = pl.multiple_of((place[1] ^ (i if i < 2 else i // 2 + 1)) * rows, rows)
        low, high = {3: (0, 3), 2: (0, 2), 1: (2, 3)}[part.shape[1]]
        whole[low:high, pl.ds(at, rows), :] = part[0]


def gathered(depth):
    return max(2 * depth - 2, depth)


def query_refs(groups, refs):
    return [(ref.at[0], ref.at[1]) for ref in refs[:groups]]


def apply_kernel(groups, depth, place, scale_row, *refs):
    pieces, refs = query_refs(groups, refs), refs[groups:]
    parts = refs[: gathered(depth)]
    activ_ref, slope_ref, hidden_ref, os_ref, new_b, stats, whole = refs[gathered(depth) :]
    assemble(place, parts, whole)
    new_b[...] = whole[...].astype(BF16)
    for step in range(groups):
        queries = pieces[step][0][...].astype(BF16)
        tokens = queries.shape[0]
        first = mm(queries, new_b[0])
        third = mm(queries, new_b[2])
        sig = jax.nn.sigmoid(first)
        activ = first * sig
        hidden = (activ * third).astype(BF16)
        scaled = mm(hidden, new_b[1]) * scale_row[0:1, :]
        activ_ref[step] = activ
        slope_ref[step] = third * (sig * (1.0 + first * (1.0 - sig)))
        hidden_ref[step] = hidden
        os_ref[step] = scaled
        sq = jnp.sum(scaled * scaled, axis=1, keepdims=True)
        ps = jnp.sum(scaled * pieces[step][1][...], axis=1, keepdims=True)
        lane = lax.broadcasted_iota(jnp.int32, (tokens, LANES), 1)
        both = jnp.where(lane == 0, sq, jnp.where(lane == 1, ps, 0.0)).T
        source = place[0] ^ step
        stats[0, pl.ds(source, 1), :] = both[0:1, :]
        stats[1, pl.ds(source, 1), :] = both[1:2, :]


def apply_back_kernel(groups, depth, count, place, scale_row, stats, *refs):
    pieces, refs = query_refs(groups, refs), refs[groups:]
    activ_ref, slope_ref, hidden_ref, os_ref, new_b = refs[:5]
    dfirst_ref, dthird_ref, slices, sums = refs[5], refs[6], refs[7:-1], refs[-1]
    total = [0.0, 0.0, 0.0]
    for step in range(groups):
        queries = pieces[step][0][...].astype(BF16)
        source = place[0] ^ step
        sq = rate_column(stats.at[0], source)
        ps = rate_column(stats.at[1], source)
        inv = lax.rsqrt(sq / count + 1e-06)
        dos = inv * pieces[step][1][...] - os_ref[step] * (inv * inv * inv * ps / count)
        dout = (dos * scale_row[0:1, :]).astype(BF16)
        dhidden = mm_t(dout, new_b[1])
        dthird = (dhidden * activ_ref[step]).astype(BF16)
        dfirst = (dhidden * slope_ref[step]).astype(BF16)
        dfirst_ref[step] = dfirst
        dthird_ref[step] = dthird
        total[0] += tmm(queries, dfirst)
        total[1] += tmm(hidden_ref[step], dout)
        total[2] += tmm(queries, dthird)
    for i in range(3):
        sums[i] = total[i]
    send_slices(sums, slices, place[1], depth)


def query_back_kernel(dfirst, dthird, new_b, *outs):
    for step, out in enumerate(outs):
        out[...] = mm_t(dfirst[step], new_b[0]) + mm_t(dthird[step], new_b[2])


def update_keep_kernel(k_kept, s_kept, w_gate, w_out, w_up, *outs):
    dact_r, third_r, activ_r, deriv_r, slope_r, second_r, dfirst_r, dthird_r, act_r = outs
    gate_b, out_b, up_b = (w[...].astype(BF16) for w in (w_gate, w_out, w_up))
    for step in range(k_kept.shape[0]):
        keys, scaled = k_kept[step], s_kept[step]
        first = mm(keys, gate_b)
        third = mm(keys, up_b)
        dact = mm_t(scaled, out_b)
        sig = jax.nn.sigmoid(first)
        activ = first * sig
        slope = sig * (1.0 - sig)
        deriv = sig + first * slope
        third_deriv = third * deriv
        dact_r[step] = dact
        third_r[step] = third
        activ_r[step] = activ
        deriv_r[step] = deriv
        slope_r[step] = third_deriv
        second_r[step] = third * (slope * (2.0 + first * (1.0 - 2.0 * sig)))
        dfirst_r[step] = (dact * third_deriv).astype(BF16)
        dthird_r[step] = (dact * activ).astype(BF16)
        act_r[step] = (activ * third).astype(BF16)


def update_back_kernel(groups, depth, scale, place, *refs):
    (k_kept, s_kept), refs = refs[:2], refs[2:]
    kept, refs = refs[:9], refs[9:]
    dact_r, third_r, activ_r, deriv_r, slope_r, second_r, dfirst_r, dthird_r, act_r = kept
    parts, refs = refs[: gathered(depth)], refs[gathered(depth) :]
    w_gate, w_out, w_up = refs[:3]
    packed = len(packing(groups))
    outs, slices = unpacked(groups, refs[3 : packed + 3]), refs[packed + 3 : -2]
    whole, sums = refs[-2:]
    assemble(place, parts, whole)
    gate_b, out_b, up_b = (w[...].astype(BF16) for w in (w_gate, w_out, w_up))
    cot_gate, cot_out, cot_up = ((whole[i] * scale).astype(BF16) for i in range(3))
    total = [0.0, 0.0, 0.0]
    for step in range(groups):
        keys, scaled = k_kept[step], s_kept[step]
        bar_dfirst = mm(keys, cot_gate)
        bar_dthird = mm(keys, cot_up)
        bar_act = mm_t(scaled, cot_out)
        dact, activ, deriv = dact_r[step], activ_r[step], deriv_r[step]
        bar_activ = bar_dthird * dact + bar_act * third_r[step]
        bar_dact = (bar_dfirst * slope_r[step] + bar_dthird * activ).astype(BF16)
        bar_df_dact = bar_dfirst * dact
        bar_third = (bar_df_dact * deriv + bar_act * activ).astype(BF16)
        bar_first = (bar_activ * deriv + bar_df_dact * second_r[step]).astype(BF16)
        outs[step][0][...] = (
            mm_t(dfirst_r[step], cot_gate)
            + mm_t(dthird_r[step], cot_up)
            + mm_t(bar_first, gate_b)
            + mm_t(bar_third, up_b)
        )
        outs[step][1][...] = mm(act_r[step], cot_out) + mm(bar_dact, out_b)
        total[0] += tmm(keys, bar_first)
        total[1] += tmm(bar_dact, scaled)
        total[2] += tmm(keys, bar_third)
    for i in range(3):
        sums[i] = total[i]
    send_slices(sums, slices, place[1], depth)


def join_query_kernel(groups, place, *refs):
    pieces, out, scratch = refs[:groups], refs[groups], refs[groups + 1]
    tokens, heads, width = out.shape
    for step, piece in enumerate(pieces):
        put_head(scratch, place[0] ^ step, piece[...], tokens, heads)
    out[...] = rows_of(scratch).reshape(tokens, heads, width).astype(BF16)


def join_update_kernel(groups, place, r, *refs):
    pieces, (out_k, out_v, sk, sv) = unpacked(groups, refs[:-4]), refs[-4:]
    tokens, heads, width = out_k.shape
    for step, piece in enumerate(pieces):
        head = place[0] ^ step
        put_head(sk, head, piece[0][...], tokens, heads)
        put_head(sv, head, piece[1][...] * rate_column(r, head), tokens, heads)
    out_k[...] = rows_of(sk).reshape(tokens, heads, width).astype(BF16)
    out_v[...] = rows_of(sv).reshape(tokens, heads, width).astype(BF16)


def join_rows_kernel(groups, place, *refs):
    parts, grads = refs[:groups], refs[groups:]
    for step, part in enumerate(parts):
        for i, grad in enumerate(grads):
            grad[place[0] ^ step] = part[0, i]


def rows_kernel(groups, place, *refs):
    parts, outs, total = refs[: -groups - 1], refs[-groups - 1 : -1], refs[-1]
    summed = parts[0][0]
    for part in parts[1:]:
        summed += part[0]
    total[...] = summed
    rows = total.shape[1] // groups
    for step, out in enumerate(outs):
        at = pl.multiple_of((place[0] ^ step) * rows, rows)
        out[0] = total[:, pl.ds(at, rows), :]


def local(queries, keys, values, rates, head_scale, gain, w_gate, w_out, w_up, cotangent):
    tokens, heads, width = keys.shape[1:]
    hidden = w_gate.shape[2]
    ctx = lax.axis_size("ctx")
    head_axis = lax.axis_size("head")
    groups = heads
    depth = ctx // groups
    assert groups & (groups - 1) == 0 and depth & (depth - 1) == 0
    scale = 1.0 / math.sqrt(tokens * ctx * width)
    count = float(heads * head_axis * width)
    me = lax.axis_index("ctx")
    mine, layer = lax.rem(me, groups), lax.div(me, groups)
    place = jnp.stack([mine, layer]).astype(jnp.int32)

    def move(x, axis, step):
        return lax.ppermute(x, axis, [(c, c ^ step) for c in range(lax.axis_size(axis))])

    def in_plane(parts):
        return [parts[0]] + [move(p, "ctx", step) for step, p in enumerate(parts) if step]

    def forwarded(got):
        return [got[:1]] if got.shape[0] == 1 else [got[i : i + 1] for i in range(got.shape[0])]

    def scatter(outs, count, unit):
        outs = list(outs)
        evens = list(range(2, count, 2))
        via = forwarded(move(outs.pop(0), "ctx", unit)) if evens else []
        via, outs[0] = after(via, outs[0])
        first = [move(outs[0], "ctx", unit)] if count > 1 else []
        even = [move(p + v, "ctx", r * unit) for p, v, r in zip(outs[1:], via, evens)]
        return [outs[-1]] + first + even

    def gather(part, count, unit):
        got = [part, move(part, "ctx", unit)][:count]
        for r in range(2, count, 2):
            sent = [move(part[:, i : i + 2], "ctx", r * unit) for i in (0, 2)]
            got += sent + [move(x, "ctx", unit) for x in sent]
        return got

    def after(x, *others):
        return lax.optimization_barrier((x, *others))

    def shape(*dims, dtype=F32):
        return jax.ShapeDtypeStruct(dims, dtype)

    flops = 2 * groups * tokens * width * hidden
    pieces = [shape(tokens, width)] * groups
    slices = [shape(len(m), 3, hidden // depth, width) for m in send_groups(depth)]
    joined = shape(tokens, heads, width, dtype=BF16)
    scratch = pltpu.VMEM((width // LANES, tokens * heads, LANES), F32)
    square = pltpu.VMEM((3, hidden, width), F32)

    def split(body, *args):
        outs = [shape(tokens, width, dtype=BF16)] + pieces[1:]
        body = functools.partial(body, groups)
        return call(body, outs, [scratch], 16 * flops, place, *args, mib=8)

    k_in = in_plane(split(split_kernel, keys[0]))
    s_in = in_plane(split(split_scaled_kernel, values[0], rates[0]))
    own = [lax.dynamic_index_in_dim(w, mine, 0, keepdims=False) for w in (w_gate, w_out, w_up)]
    own_scale = lax.dynamic_index_in_dim(head_scale, mine, 0, keepdims=True)[None, :]
    k_in, s_in, queries, cotangent = after(k_in, s_in, queries, cotangent)

    def kept(*dims, dtype=F32):
        return shape(*dims, tokens, width, dtype=dtype)

    out = call(
        functools.partial(update_kernel, groups, depth, scale),
        [kept(groups, dtype=BF16)] * 2 + slices, [square], 6 * flops,
        place, *k_in, *s_in, *own,
    )
    early, terms = out[:2], out[2:]
    *q_out, scale_row = call(
        functools.partial(split_apply_kernel, groups),
        [shape(2, tokens, width)] * groups + [shape(8, width)],
        [scratch], flops // 8, place, queries[0], cotangent[0], gain, own_scale,
    )
    q_in = in_plane(q_out[:-1])
    new = functools.reduce(jnp.add, scatter(terms, depth, groups))
    new, q_in, q_last = after(new, q_in, q_out[-1])
    q_in.append(move(q_last, "ctx", groups - 1))
    new = gather(new, depth, groups)
    *passed, stats = call(
        functools.partial(apply_kernel, groups, depth),
        [kept(groups), kept(groups), kept(groups, dtype=BF16), kept(groups)]
        + [shape(3, hidden, width, dtype=BF16), shape(2, groups, tokens)],
        [square], 3 * flops, place, scale_row, *q_in, *new,
    )
    for axis, size in (("head", lax.axis_size("head")), ("ctx", groups)):
        bit = 1
        while bit < size:
            stats = stats + move(stats, axis, bit)
            bit *= 2
    out = call(
        functools.partial(apply_back_kernel, groups, depth, count),
        [kept(groups, dtype=BF16)] * 2 + slices, [square], 6 * flops,
        place, scale_row, stats, *q_in, *passed,
    )
    q_sent = call(
        query_back_kernel, [shape(tokens, width)] * groups, [], 2 * flops, *out[:2], passed[-1]
    )
    out = out[2:]
    out, early = after(out, early)
    saved = call(
        update_keep_kernel, [kept(groups)] * 6 + [kept(groups, dtype=BF16)] * 3, [], 3 * flops,
        *early, *own,
    )
    part = functools.reduce(jnp.add, scatter(out, depth, groups))
    parts = gather(part, depth, groups)
    q_back = in_plane(q_sent)
    parts, saved, q_back = after(parts, saved, q_back)
    (grad_q,) = call(
        functools.partial(join_query_kernel, groups), [joined], [scratch], flops // 16,
        place, *q_back,
    )
    rows = hidden // depth
    out = call(
        functools.partial(update_back_kernel, groups, depth, scale),
        [kept(len(members)) for members in packing(groups)] + slices, [square] * 2, 12 * flops,
        place, *early, *saved, *parts, *own, mib=24,
    )
    packed = len(packing(groups))
    back = in_plane(out[:packed])
    ends = scatter(out[packed:], depth, groups)
    if groups == 4:
        ends, back, grad_q = after(ends, back, grad_q)
        back += [move(back[1][2], "ctx", 2), move(back[2][2], "ctx", 1)]
    own_rows = rows // groups
    sent = call(
        functools.partial(rows_kernel, groups),
        [shape(1, 3, own_rows, width)] * groups,
        [pltpu.VMEM((3, rows, width), F32)], flops // 100, place, part, *ends,
    )
    grad_k, grad_v = call(
        functools.partial(join_update_kernel, groups), [joined] * 2, [scratch] * 2, flops // 8,
        place, rates[0], *back,
    )
    got, grad_k, grad_v = after(in_plane(sent), grad_k, grad_v)
    grads = call(
        functools.partial(join_rows_kernel, groups), [shape(heads, own_rows, width)] * 3, [],
        flops // 100, place, *got,
    )
    if lax.axis_size("batch") > 1:
        grads = [lax.psum_scatter(x, "batch", scatter_dimension=1, tiled=True) for x in grads]
    return (grad_q[None], grad_k[None], grad_v[None], grads[0], grads[1], grads[2])


def solution(mesh):
    in_specs = (
        P("batch", "ctx", "head", None),
        P("batch", "ctx", "head", None),
        P("batch", "ctx", "head", None),
        P("batch", "head", "ctx"),
        P("head"),
        P("head", None),
        P("head", None, None),
        P("head", None, None),
        P("head", None, None),
        P("batch", "ctx", "head", None),
    )
    out_specs = (
        P("batch", "ctx", "head", None),
        P("batch", "ctx", "head", None),
        P("batch", "ctx", "head", None),
        P("head", ("ctx", "batch"), None),
        P("head", ("ctx", "batch"), None),
        P("head", ("ctx", "batch"), None),
    )
    return jax.shard_map(local, mesh=mesh, in_specs=in_specs, out_specs=out_specs, check_vma=False)
```

```python
import functools
import math

import jax
import jax.numpy as jnp
from jax import lax
from jax.experimental import pallas as pl
from jax.experimental.pallas import tpu as pltpu
from jax.sharding import PartitionSpec as P

F32 = jnp.float32
BF16 = jnp.bfloat16
LANES = 128
MIB = 1024 * 1024


def mm(a, b):
    return jnp.dot(a, b, preferred_element_type=F32)


def mm_t(a, b):
    return lax.dot_general(a, b, (((1,), (1,)), ((), ())), preferred_element_type=F32)


def tmm(a, b):
    return lax.dot_general(a, b, (((0,), (0,)), ((), ())), preferred_element_type=F32)


def call(body, out_shape, scratch, flops, *args, mib=16):
    smem = pl.BlockSpec(memory_space=pltpu.SMEM)
    vmem = pl.BlockSpec(memory_space=pltpu.VMEM)
    size = sum(a.size * a.dtype.itemsize for a in args)
    size += sum(math.prod(o.shape) * o.dtype.itemsize for o in out_shape)
    return pl.pallas_call(
        body,
        out_shape=out_shape,
        in_specs=[smem if a.dtype == jnp.int32 else vmem for a in args],
        out_specs=[vmem] * len(out_shape),
        scratch_shapes=scratch,
        compiler_params=pltpu.CompilerParams(vmem_limit_bytes=mib * MIB),
        cost_estimate=pl.CostEstimate(flops=flops, bytes_accessed=size, transcendentals=0),
    )(*args)


def put_rows(scratch, x):
    for i in range(scratch.shape[0]):
        scratch[i] = x[:, i * LANES : (i + 1) * LANES]


def take_head(scratch, head, tokens, heads):
    parts = [scratch[i, pl.ds(head, tokens, stride=heads), :] for i in range(scratch.shape[0])]
    return jnp.concatenate(parts, axis=1)


def put_head(scratch, head, x, tokens, heads):
    for i in range(scratch.shape[0]):
        scratch[i, pl.ds(head, tokens, stride=heads), :] = x[:, i * LANES : (i + 1) * LANES]


def rows_of(scratch):
    return jnp.concatenate([scratch[i] for i in range(scratch.shape[0])], axis=1)


def split_kernel(groups, place, x, *rest):
    outs, scratch = rest[:groups], rest[groups]
    tokens, heads, width = x.shape
    put_rows(scratch, x[...].astype(F32).reshape(tokens * heads, width))
    for step, out in enumerate(outs):
        out[...] = take_head(scratch, place[0] ^ step, tokens, heads).astype(out.dtype)


def split_scaled_kernel(groups, place, x, r, *rest):
    outs = rest[:groups]
    split_kernel(groups, place, x, *rest)
    for step in range(groups):
        scaled = outs[step][...].astype(F32) * rate_column(r, place[0] ^ step)
        outs[step][...] = scaled.astype(BF16).astype(outs[step].dtype)


def split_apply_kernel(groups, place, q, cot, gain, scale, *rest):
    outs, scale_row, scratch = rest[:-2], rest[-2], rest[-1]
    scale_row[...] = jnp.broadcast_to(scale[...], scale_row.shape)
    pieces = query_refs(groups, outs)
    split_kernel(groups, place, q, *[one for one, _ in pieces], scratch)
    split_kernel(groups, place, cot, *[two for _, two in pieces], scratch)
    for step in range(groups):
        pieces[step][1][...] *= gain[pl.ds(place[0] ^ step, 1), :]


def packing(groups):
    if groups == 4:
        return [[(0, 0), (0, 1)], [(1, 0), (1, 1), (3, 0)], [(2, 0), (2, 1), (3, 1)]]
    return [[(step, 0), (step, 1)] for step in range(groups)]


def unpacked(groups, refs):
    found = {}
    for ref, members in zip(refs, packing(groups)):
        for i, member in enumerate(members):
            found[member] = ref.at[i]
    for i, ref in enumerate(refs[len(packing(groups)) :]):
        found[(groups - 1, i)] = ref
    return [(found[(step, 0)], found[(step, 1)]) for step in range(groups)]


def rate_column(r, head):
    return jnp.broadcast_to(r[pl.ds(head, 1), :], (8, r.shape[1])).T[:, 0:1]


def send_groups(count):
    odd = list(range(3, count, 2))
    return ([odd] if odd else []) + [[r] for r in [1] + list(range(2, count, 2)) if r < count] + [[0]]


def send_slices(sums, outs, own, count):
    rows = sums.shape[1] // count
    for out, members in zip(outs, send_groups(count)):
        for i, step in enumerate(members):
            at = pl.multiple_of((own ^ step) * rows, rows)
            out[i] = sums[:, pl.ds(at, rows), :]


def update_sums(keys_in, scaled_in, weights, key_kept, scaled_kept):
    gate_b, out_b, up_b = (w[...].astype(BF16) for w in weights)
    acts, dfirsts, dthirds = [], [], []
    for step, (key, value) in enumerate(zip(keys_in, scaled_in)):
        keys = key[...].astype(BF16)
        scaled = value[...].astype(BF16)
        key_kept[step] = keys
        scaled_kept[step] = scaled
        first = mm(keys, gate_b)
        third = mm(keys, up_b)
        sig = jax.nn.sigmoid(first)
        activ = first * sig
        act = (activ * third).astype(BF16)
        dact = mm_t(scaled, out_b)
        deriv = sig * (1.0 + first * (1.0 - sig))
        dfirst = (dact * third * deriv).astype(BF16)
        dthird = (dact * activ).astype(BF16)
        acts.append(act)
        dfirsts.append(dfirst)
        dthirds.append(dthird)
    keys, scaled = tokens_of(key_kept), tokens_of(scaled_kept)
    return (
        tmm(keys, jnp.concatenate(dfirsts)),
        tmm(jnp.concatenate(acts), scaled),
        tmm(keys, jnp.concatenate(dthirds)),
    )


def update_kernel(count, depth, scale, place, *refs):
    keys_in, scaled_in, weights = refs[:count], refs[count : 2 * count], refs[2 * count :][:3]
    key_kept, scaled_kept = refs[2 * count + 3 : 2 * count + 5]
    outs, sums = refs[2 * count + 5 : -1], refs[-1]
    total = update_sums(keys_in, scaled_in, weights, key_kept, scaled_kept)
    for i in range(3):
        sums[i] = total[i] * scale
    send_slices(sums, outs, place[1], depth)
    rows = sums.shape[1] // depth
    at = pl.multiple_of(place[1] * rows, rows)
    for i, w in enumerate(weights):
        outs[-1][0, i] += w[pl.ds(at, rows), :]


def assemble(place, parts, whole):
    rows = parts[0].shape[2]
    for step, part in enumerate(parts):
        at = pl.multiple_of((place[1] ^ step) * rows, rows)
        whole[:, pl.ds(at, rows), :] = part[0]


def query_refs(groups, refs):
    return [(ref.at[0], ref.at[1]) for ref in refs[: groups - 1]] + [refs[groups - 1 : groups + 1]]


def tokens_of(ref):
    return ref[...].reshape(ref.shape[0] * ref.shape[1], ref.shape[2])


def apply_kernel(groups, depth, place, scale_row, *refs):
    pieces, refs = query_refs(groups, refs), refs[groups + 1 :]
    parts = refs[:depth]
    activ_ref, slope_ref, hidden_ref, os_ref, new_b, stats, whole = refs[depth:]
    assemble(place, parts, whole)
    new_b[...] = whole[...].astype(BF16)
    for step in range(groups):
        queries = pieces[step][0][...].astype(BF16)
        tokens = queries.shape[0]
        first = mm(queries, new_b[0])
        third = mm(queries, new_b[2])
        sig = jax.nn.sigmoid(first)
        activ = first * sig
        hidden = (activ * third).astype(BF16)
        scaled = mm(hidden, new_b[1]) * scale_row[0:1, :]
        activ_ref[step] = activ
        slope_ref[step] = third * (sig * (1.0 + first * (1.0 - sig)))
        hidden_ref[step] = hidden
        os_ref[step] = scaled
        sq = jnp.sum(scaled * scaled, axis=1, keepdims=True)
        ps = jnp.sum(scaled * pieces[step][1][...], axis=1, keepdims=True)
        lane = lax.broadcasted_iota(jnp.int32, (tokens, LANES), 1)
        both = jnp.where(lane == 0, sq, jnp.where(lane == 1, ps, 0.0)).T
        source = place[0] ^ step
        stats[0, pl.ds(source, 1), :] = both[0:1, :]
        stats[1, pl.ds(source, 1), :] = both[1:2, :]


def apply_back_kernel(groups, depth, count, place, scale_row, *refs):
    stats, refs = refs[:groups], refs[groups:]
    pieces, refs = query_refs(groups, refs), refs[groups + 1 :]
    activ_ref, slope_ref, hidden_ref, os_ref, new_b = refs[:5]
    dfirst_ref, dthird_ref, slices, sums, both = refs[5], refs[6], refs[7:-2], refs[-2], refs[-1]
    both[...] = functools.reduce(jnp.add, [ref[...] for ref in stats])
    douts = []
    for step in range(groups):
        source = place[0] ^ step
        sq = rate_column(both.at[0], source)
        ps = rate_column(both.at[1], source)
        inv = lax.rsqrt(sq / count + 1e-06)
        dos = inv * pieces[step][1][...] - os_ref[step] * (inv * inv * inv * ps / count)
        dout = (dos * scale_row[0:1, :]).astype(BF16)
        dhidden = mm_t(dout, new_b[1])
        dthird = (dhidden * activ_ref[step]).astype(BF16)
        dfirst = (dhidden * slope_ref[step]).astype(BF16)
        dfirst_ref[step] = dfirst
        dthird_ref[step] = dthird
        douts.append(dout)
    queries = jnp.concatenate([piece[0][...].astype(BF16) for piece in pieces])
    sums[0] = tmm(queries, tokens_of(dfirst_ref))
    sums[1] = tmm(tokens_of(hidden_ref), jnp.concatenate(douts))
    sums[2] = tmm(queries, tokens_of(dthird_ref))
    send_slices(sums, slices, place[1], depth)


def query_back_kernel(dfirst, dthird, new_b, *outs):
    for step, out in enumerate(outs):
        out[...] = mm_t(dfirst[step], new_b[0]) + mm_t(dthird[step], new_b[2])


def update_keep_kernel(k_kept, s_kept, w_gate, w_out, w_up, *outs):
    dact_r, third_r, activ_r, deriv_r, slope_r, second_r, dfirst_r, dthird_r, act_r = outs
    gate_b, out_b, up_b = (w[...].astype(BF16) for w in (w_gate, w_out, w_up))
    for step in range(k_kept.shape[0]):
        keys, scaled = k_kept[step], s_kept[step]
        first = mm(keys, gate_b)
        third = mm(keys, up_b)
        dact = mm_t(scaled, out_b)
        sig = jax.nn.sigmoid(first)
        activ = first * sig
        slope = sig * (1.0 - sig)
        deriv = sig + first * slope
        third_deriv = third * deriv
        dact_r[step] = dact
        third_r[step] = third
        activ_r[step] = activ
        deriv_r[step] = deriv
        slope_r[step] = third_deriv
        second_r[step] = third * (slope * (2.0 + first * (1.0 - 2.0 * sig)))
        dfirst_r[step] = (dact * third_deriv).astype(BF16)
        dthird_r[step] = (dact * activ).astype(BF16)
        act_r[step] = (activ * third).astype(BF16)


def update_back_kernel(groups, depth, scale, place, *refs):
    (k_kept, s_kept), refs = refs[:2], refs[2:]
    kept, refs = refs[:9], refs[9:]
    dact_r, third_r, activ_r, deriv_r, slope_r, second_r, dfirst_r, dthird_r, act_r = kept
    parts, refs = refs[:depth], refs[depth:]
    w_gate, w_out, w_up = refs[:3]
    packed = len(packing(groups))
    outs, slices = unpacked(groups, refs[3 : packed + 3]), refs[packed + 3 : -2]
    whole, sums = refs[-2:]
    assemble(place, parts, whole)
    gate_b, out_b, up_b = (w[...].astype(BF16) for w in (w_gate, w_out, w_up))
    cot_gate, cot_out, cot_up = ((whole[i] * scale).astype(BF16) for i in range(3))
    firsts, thirds, dacts = [], [], []
    for step in range(groups):
        keys, scaled = k_kept[step], s_kept[step]
        bar_dfirst = mm(keys, cot_gate)
        bar_dthird = mm(keys, cot_up)
        bar_act = mm_t(scaled, cot_out)
        dact, activ, deriv = dact_r[step], activ_r[step], deriv_r[step]
        bar_activ = bar_dthird * dact + bar_act * third_r[step]
        bar_dact = (bar_dfirst * slope_r[step] + bar_dthird * activ).astype(BF16)
        bar_df_dact = bar_dfirst * dact
        bar_third = (bar_df_dact * deriv + bar_act * activ).astype(BF16)
        bar_first = (bar_activ * deriv + bar_df_dact * second_r[step]).astype(BF16)
        outs[step][0][...] = (
            mm_t(dfirst_r[step], cot_gate)
            + mm_t(dthird_r[step], cot_up)
            + mm_t(bar_first, gate_b)
            + mm_t(bar_third, up_b)
        )
        outs[step][1][...] = mm(act_r[step], cot_out) + mm(bar_dact, out_b)
        firsts.append(bar_first)
        thirds.append(bar_third)
        dacts.append(bar_dact)
    keys = tokens_of(k_kept)
    sums[0] = tmm(keys, jnp.concatenate(firsts))
    sums[1] = tmm(jnp.concatenate(dacts), tokens_of(s_kept))
    sums[2] = tmm(keys, jnp.concatenate(thirds))
    send_slices(sums, slices, place[1], depth)


def join_query_kernel(groups, place, *refs):
    pieces, out, scratch = refs[:groups], refs[groups], refs[groups + 1]
    tokens, heads, width = out.shape
    for step, piece in enumerate(pieces):
        put_head(scratch, place[0] ^ step, piece[...], tokens, heads)
    out[...] = rows_of(scratch).reshape(tokens, heads, width).astype(BF16)


def join_update_kernel(groups, place, r, *refs):
    pieces, (out_k, out_v, sk, sv) = unpacked(groups, refs[:-4]), refs[-4:]
    tokens, heads, width = out_k.shape
    for step, piece in enumerate(pieces):
        head = place[0] ^ step
        put_head(sk, head, piece[0][...], tokens, heads)
        put_head(sv, head, piece[1][...] * rate_column(r, head), tokens, heads)
    out_k[...] = rows_of(sk).reshape(tokens, heads, width).astype(BF16)
    out_v[...] = rows_of(sv).reshape(tokens, heads, width).astype(BF16)


def join_rows_kernel(groups, place, *refs):
    parts, grads = refs[:groups], refs[groups:]
    for step, part in enumerate(parts):
        for i, grad in enumerate(grads):
            grad[place[0] ^ step] = part[0, i]


def rows_kernel(groups, place, *refs):
    parts, outs, total = refs[: -groups - 1], refs[-groups - 1 : -1], refs[-1]
    summed = parts[0][0]
    for part in parts[1:]:
        summed += part[0]
    total[...] = summed
    rows = total.shape[1] // groups
    for step, out in enumerate(outs):
        at = pl.multiple_of((place[0] ^ step) * rows, rows)
        out[0] = total[:, pl.ds(at, rows), :]


def local(queries, keys, values, rates, head_scale, gain, w_gate, w_out, w_up, cotangent):
    tokens, heads, width = keys.shape[1:]
    hidden = w_gate.shape[2]
    ctx = lax.axis_size("ctx")
    head_axis = lax.axis_size("head")
    groups = heads
    depth = ctx // groups
    assert groups & (groups - 1) == 0 and depth & (depth - 1) == 0
    scale = 1.0 / math.sqrt(tokens * ctx * width)
    count = float(heads * head_axis * width)
    me = lax.axis_index("ctx")
    mine, layer = lax.rem(me, groups), lax.div(me, groups)
    place = jnp.stack([mine, layer]).astype(jnp.int32)

    def move(x, axis, step):
        return lax.ppermute(x, axis, [(c, c ^ step) for c in range(lax.axis_size(axis))])

    def in_plane(parts):
        return [parts[0]] + [move(p, "ctx", step) for step, p in enumerate(parts) if step]

    def forwarded(got):
        return [got[:1]] if got.shape[0] == 1 else [got[i : i + 1] for i in range(got.shape[0])]

    def scatter(outs, count, unit):
        outs = list(outs)
        evens = list(range(2, count, 2))
        via = forwarded(move(outs.pop(0), "ctx", unit)) if evens else []
        via, outs[0] = after(via, outs[0])
        first = [move(outs[0], "ctx", unit)] if count > 1 else []
        even = [move(p + v, "ctx", r * unit) for p, v, r in zip(outs[1:], via, evens)]
        return [outs[-1]] + first + even

    def gather(part, count, unit):
        got = [part] * count
        for r in [2 * i for i in range(1, count // 2)]:
            got[r] = move(part, "ctx", r * unit)
            got[r + 1] = move(got[r], "ctx", unit)
        if count > 1:
            got[1] = move(part, "ctx", unit)
        return got

    def after(x, *others):
        return lax.optimization_barrier((x, *others))

    def shape(*dims, dtype=F32):
        return jax.ShapeDtypeStruct(dims, dtype)

    flops = 2 * groups * tokens * width * hidden
    pieces = [shape(tokens, width)] * groups
    slices = [shape(len(m), 3, hidden // depth, width) for m in send_groups(depth)]
    joined = shape(tokens, heads, width, dtype=BF16)
    scratch = pltpu.VMEM((width // LANES, tokens * heads, LANES), F32)
    square = pltpu.VMEM((3, hidden, width), F32)

    def split(body, *args):
        outs = [shape(tokens, width, dtype=BF16)] + pieces[1:]
        body = functools.partial(body, groups)
        return call(body, outs, [scratch], 16 * flops, place, *args, mib=8)

    k_in = in_plane(split(split_kernel, keys[0]))
    s_in = in_plane(split(split_scaled_kernel, values[0], rates[0]))
    own = [lax.dynamic_index_in_dim(w, mine, 0, keepdims=False) for w in (w_gate, w_out, w_up)]
    own_scale = lax.dynamic_index_in_dim(head_scale, mine, 0, keepdims=True)[None, :]
    k_in, s_in, queries, cotangent = after(k_in, s_in, queries, cotangent)

    def kept(*dims, dtype=F32):
        return shape(*dims, tokens, width, dtype=dtype)

    out = call(
        functools.partial(update_kernel, groups, depth, scale),
        [kept(groups, dtype=BF16)] * 2 + slices, [square], 6 * flops,
        place, *k_in, *s_in, *own,
    )
    early, terms = out[:2], out[2:]
    *q_out, scale_row = call(
        functools.partial(split_apply_kernel, groups),
        [shape(2, tokens, width)] * (groups - 1) + [shape(tokens, width)] * 2 + [shape(8, width)],
        [scratch], flops // 8, place, queries[0], cotangent[0], gain, own_scale,
    )
    q_in = in_plane(q_out[:-2])
    new = functools.reduce(jnp.add, scatter(terms, depth, groups))
    new, q_in, q_last = after(new, q_in, q_out[-2:])
    q_in += [move(x, "ctx", groups - 1) for x in q_last]
    new = gather(new, depth, groups)
    *passed, stats = call(
        functools.partial(apply_kernel, groups, depth),
        [kept(groups), kept(groups), kept(groups, dtype=BF16), kept(groups)]
        + [shape(3, hidden, width, dtype=BF16), shape(2, groups, tokens)],
        [square], 3 * flops, place, scale_row, *q_in, *new,
    )
    bit = 1
    while bit < head_axis:
        stats = stats + move(stats, "head", bit)
        bit *= 2
    out = call(
        functools.partial(apply_back_kernel, groups, depth, count),
        [kept(groups, dtype=BF16)] * 2 + slices,
        [square, pltpu.VMEM((2, groups, tokens), F32)], 6 * flops,
        place, scale_row, *in_plane([stats] * groups), *q_in, *passed,
    )
    q_sent = call(
        query_back_kernel, [shape(tokens, width)] * groups, [], 2 * flops, *out[:2], passed[-1]
    )
    out = out[2:]
    out, early = after(out, early)
    saved = call(
        update_keep_kernel, [kept(groups)] * 6 + [kept(groups, dtype=BF16)] * 3, [], 3 * flops,
        *early, *own,
    )
    part = functools.reduce(jnp.add, scatter(out, depth, groups))
    parts = gather(part, depth, groups)
    q_back = in_plane(q_sent)
    parts, saved, q_back = after(parts, saved, q_back)
    (grad_q,) = call(
        functools.partial(join_query_kernel, groups), [joined], [scratch], flops // 16,
        place, *q_back,
    )
    rows = hidden // depth
    out = call(
        functools.partial(update_back_kernel, groups, depth, scale),
        [kept(len(members)) for members in packing(groups)] + slices, [square] * 2, 12 * flops,
        place, *early, *saved, *parts, *own, mib=24,
    )
    packed = len(packing(groups))
    back = in_plane(out[:packed])
    ends = scatter(out[packed:], depth, groups)
    if groups == 4:
        ends, back, grad_q = after(ends, back, grad_q)
        back += [move(back[1][2], "ctx", 2), move(back[2][2], "ctx", 1)]
    own_rows = rows // groups
    sent = call(
        functools.partial(rows_kernel, groups),
        [shape(1, 3, own_rows, width)] * groups,
        [pltpu.VMEM((3, rows, width), F32)], flops // 100, place, part, *ends,
    )
    grad_k, grad_v = call(
        functools.partial(join_update_kernel, groups), [joined] * 2, [scratch] * 2, flops // 8,
        place, rates[0], *back,
    )
    got, grad_k, grad_v = after(in_plane(sent), grad_k, grad_v)
    grads = call(
        functools.partial(join_rows_kernel, groups), [shape(heads, own_rows, width)] * 3, [],
        flops // 100, place, *got,
    )
    if lax.axis_size("batch") > 1:
        grads = [lax.psum_scatter(x, "batch", scatter_dimension=1, tiled=True) for x in grads]
    return (grad_q[None], grad_k[None], grad_v[None], grads[0], grads[1], grads[2])


def solution(mesh):
    in_specs = (
        P("batch", "ctx", "head", None),
        P("batch", "ctx", "head", None),
        P("batch", "ctx", "head", None),
        P("batch", "head", "ctx"),
        P("head"),
        P("head", None),
        P("head", None, None),
        P("head", None, None),
        P("head", None, None),
        P("batch", "ctx", "head", None),
    )
    out_specs = (
        P("batch", "ctx", "head", None),
        P("batch", "ctx", "head", None),
        P("batch", "ctx", "head", None),
        P("head", ("ctx", "batch"), None),
        P("head", ("ctx", "batch"), None),
        P("head", ("ctx", "batch"), None),
    )
    return jax.shard_map(local, mesh=mesh, in_specs=in_specs, out_specs=out_specs, check_vma=False)
```

```python
import functools
import math

import jax
import jax.numpy as jnp
from jax import lax
from jax.experimental import pallas as pl
from jax.experimental.pallas import tpu as pltpu
from jax.sharding import PartitionSpec as P

F32 = jnp.float32
BF16 = jnp.bfloat16
LANES = 128
MIB = 1024 * 1024


def mm(a, b):
    return jnp.dot(a, b, preferred_element_type=F32)


def mm_t(a, b):
    return lax.dot_general(a, b, (((1,), (1,)), ((), ())), preferred_element_type=F32)


def tmm(a, b):
    return lax.dot_general(a, b, (((0,), (0,)), ((), ())), preferred_element_type=F32)


def call(body, out_shape, scratch, flops, *args, mib=16):
    smem = pl.BlockSpec(memory_space=pltpu.SMEM)
    vmem = pl.BlockSpec(memory_space=pltpu.VMEM)
    size = sum(a.size * a.dtype.itemsize for a in args)
    size += sum(math.prod(o.shape) * o.dtype.itemsize for o in out_shape)
    return pl.pallas_call(
        body,
        out_shape=out_shape,
        in_specs=[smem if a.dtype == jnp.int32 else vmem for a in args],
        out_specs=[vmem] * len(out_shape),
        scratch_shapes=scratch,
        compiler_params=pltpu.CompilerParams(vmem_limit_bytes=mib * MIB),
        cost_estimate=pl.CostEstimate(flops=flops, bytes_accessed=size, transcendentals=0),
    )(*args)


def put_rows(scratch, x):
    for i in range(scratch.shape[0]):
        scratch[i] = x[:, i * LANES : (i + 1) * LANES]


def take_head(scratch, head, tokens, heads):
    parts = [scratch[i, pl.ds(head, tokens, stride=heads), :] for i in range(scratch.shape[0])]
    return jnp.concatenate(parts, axis=1)


def put_head(scratch, head, x, tokens, heads):
    for i in range(scratch.shape[0]):
        scratch[i, pl.ds(head, tokens, stride=heads), :] = x[:, i * LANES : (i + 1) * LANES]


def rows_of(scratch):
    return jnp.concatenate([scratch[i] for i in range(scratch.shape[0])], axis=1)


def split_kernel(groups, place, x, *rest):
    outs, scratch = rest[:groups], rest[groups]
    tokens, heads, width = x.shape
    put_rows(scratch, x[...].astype(F32).reshape(tokens * heads, width))
    for step, out in enumerate(outs):
        out[...] = take_head(scratch, place[0] ^ step, tokens, heads).astype(out.dtype)


def split_scaled_kernel(groups, place, x, r, *rest):
    outs = rest[:groups]
    split_kernel(groups, place, x, *rest)
    for step in range(groups):
        scaled = outs[step][...].astype(F32) * rate_column(r, place[0] ^ step)
        outs[step][...] = scaled.astype(BF16).astype(outs[step].dtype)


def split_apply_kernel(groups, place, q, cot, gain, scale, *rest):
    outs, scale_row, scratch = rest[:-2], rest[-2], rest[-1]
    scale_row[...] = jnp.broadcast_to(scale[...], scale_row.shape)
    pieces = query_refs(groups, outs)
    split_kernel(groups, place, q, *[one for one, _ in pieces], scratch)
    split_kernel(groups, place, cot, *[two for _, two in pieces], scratch)
    for step in range(groups):
        pieces[step][1][...] *= gain[pl.ds(place[0] ^ step, 1), :]


def packing(groups):
    if groups == 4:
        return [[(0, 0), (0, 1)], [(1, 0), (1, 1), (3, 0)], [(2, 0), (2, 1), (3, 1)]]
    return [[(step, 0), (step, 1)] for step in range(groups)]


def unpacked(groups, refs):
    found = {}
    for ref, members in zip(refs, packing(groups)):
        for i, member in enumerate(members):
            found[member] = ref.at[i] if ref is not None else None
    for i, ref in enumerate(refs[len(packing(groups)) :]):
        found[(groups - 1, i)] = ref
    return [(found[(step, 0)], found[(step, 1)]) for step in range(groups)]


def rate_column(r, head):
    return jnp.broadcast_to(r[pl.ds(head, 1), :], (8, r.shape[1])).T[:, 0:1]


def send_groups(count):
    odd = list(range(3, count, 2))
    return ([odd] if odd else []) + [[r] for r in [1] + list(range(2, count, 2)) if r < count] + [[0]]


def send_slices(sums, outs, own, count):
    rows = sums.shape[1] // count
    for out, members in zip(outs, send_groups(count)):
        for i, step in enumerate(members):
            at = pl.multiple_of((own ^ step) * rows, rows)
            out[i] = sums[:, pl.ds(at, rows), :]


def update_sums(keys_in, scaled_in, weights, key_kept, scaled_kept):
    gate_b, out_b, up_b = (w[...].astype(BF16) for w in weights)
    acts, dfirsts, dthirds = [], [], []
    for step, (key, value) in enumerate(zip(keys_in, scaled_in)):
        keys = key[...].astype(BF16)
        scaled = value[...].astype(BF16)
        key_kept[step] = keys
        scaled_kept[step] = scaled
        first = mm(keys, gate_b)
        third = mm(keys, up_b)
        sig = jax.nn.sigmoid(first)
        activ = first * sig
        act = (activ * third).astype(BF16)
        dact = mm_t(scaled, out_b)
        deriv = sig * (1.0 + first * (1.0 - sig))
        dfirst = (dact * third * deriv).astype(BF16)
        dthird = (dact * activ).astype(BF16)
        acts.append(act)
        dfirsts.append(dfirst)
        dthirds.append(dthird)
    keys, scaled = tokens_of(key_kept), tokens_of(scaled_kept)
    return (
        tmm(keys, jnp.concatenate(dfirsts)),
        tmm(jnp.concatenate(acts), scaled),
        tmm(keys, jnp.concatenate(dthirds)),
    )


def update_kernel(count, depth, scale, place, *refs):
    keys_in, scaled_in, weights = refs[:count], refs[count : 2 * count], refs[2 * count :][:3]
    key_kept, scaled_kept = refs[2 * count + 3 : 2 * count + 5]
    outs, sums = refs[2 * count + 5 : -1], refs[-1]
    total = update_sums(keys_in, scaled_in, weights, key_kept, scaled_kept)
    for i in range(3):
        sums[i] = total[i] * scale
    send_slices(sums, outs, place[1], depth)
    rows = sums.shape[1] // depth
    at = pl.multiple_of(place[1] * rows, rows)
    for i, w in enumerate(weights):
        outs[-1][0, i] += w[pl.ds(at, rows), :]


def assemble(place, parts, whole):
    rows = parts[0].shape[2]
    for step, part in enumerate(parts):
        at = pl.multiple_of((place[1] ^ step) * rows, rows)
        whole[:, pl.ds(at, rows), :] = part[0]


def query_refs(groups, refs):
    return [(ref.at[0], ref.at[1]) for ref in refs[: groups - 1]] + [refs[groups - 1 : groups + 1]]


def tokens_of(ref):
    return ref[...].reshape(ref.shape[0] * ref.shape[1], ref.shape[2])


def apply_kernel(groups, depth, place, scale_row, *refs):
    pieces, refs = query_refs(groups, refs), refs[groups + 1 :]
    parts = refs[:depth]
    activ_ref, slope_ref, hidden_ref, os_ref, new_b, stats, whole = refs[depth:]
    assemble(place, parts, whole)
    new_b[...] = whole[...].astype(BF16)
    for step in range(groups):
        queries = pieces[step][0][...].astype(BF16)
        tokens = queries.shape[0]
        first = mm(queries, new_b[0])
        third = mm(queries, new_b[2])
        sig = jax.nn.sigmoid(first)
        activ = first * sig
        hidden = (activ * third).astype(BF16)
        scaled = mm(hidden, new_b[1]) * scale_row[0:1, :]
        activ_ref[step] = activ
        slope_ref[step] = third * (sig * (1.0 + first * (1.0 - sig)))
        hidden_ref[step] = hidden
        os_ref[step] = scaled
        sq = jnp.sum(scaled * scaled, axis=1, keepdims=True)
        ps = jnp.sum(scaled * pieces[step][1][...], axis=1, keepdims=True)
        lane = lax.broadcasted_iota(jnp.int32, (tokens, LANES), 1)
        both = jnp.where(lane == 0, sq, jnp.where(lane == 1, ps, 0.0)).T
        source = place[0] ^ step
        stats[0, pl.ds(source, 1), :] = both[0:1, :]
        stats[1, pl.ds(source, 1), :] = both[1:2, :]


def apply_back_kernel(groups, depth, count, place, scale_row, *refs):
    stats, refs = refs[:groups], refs[groups:]
    pieces, refs = query_refs(groups, refs), refs[groups + 1 :]
    activ_ref, slope_ref, hidden_ref, os_ref, new_b = refs[:5]
    dfirst_ref, dthird_ref, slices, sums, both = refs[5], refs[6], refs[7:-2], refs[-2], refs[-1]
    both[...] = functools.reduce(jnp.add, [ref[...] for ref in stats])
    douts = []
    for step in range(groups):
        source = place[0] ^ step
        sq = rate_column(both.at[0], source)
        ps = rate_column(both.at[1], source)
        inv = lax.rsqrt(sq / count + 1e-06)
        dos = inv * pieces[step][1][...] - os_ref[step] * (inv * inv * inv * ps / count)
        dout = (dos * scale_row[0:1, :]).astype(BF16)
        dhidden = mm_t(dout, new_b[1])
        dthird = (dhidden * activ_ref[step]).astype(BF16)
        dfirst = (dhidden * slope_ref[step]).astype(BF16)
        dfirst_ref[step] = dfirst
        dthird_ref[step] = dthird
        douts.append(dout)
    queries = jnp.concatenate([piece[0][...].astype(BF16) for piece in pieces])
    sums[0] = tmm(queries, tokens_of(dfirst_ref))
    sums[1] = tmm(tokens_of(hidden_ref), jnp.concatenate(douts))
    sums[2] = tmm(queries, tokens_of(dthird_ref))
    send_slices(sums, slices, place[1], depth)


def query_back_kernel(dfirst, dthird, new_b, *outs):
    for step, out in enumerate(outs):
        out[...] = mm_t(dfirst[step], new_b[0]) + mm_t(dthird[step], new_b[2])


def update_keep_kernel(k_kept, s_kept, w_gate, w_out, w_up, *outs):
    dact_r, third_r, activ_r, deriv_r, slope_r, second_r, dfirst_r, dthird_r, act_r = outs
    gate_b, out_b, up_b = (w[...].astype(BF16) for w in (w_gate, w_out, w_up))
    for step in range(k_kept.shape[0]):
        keys, scaled = k_kept[step], s_kept[step]
        first = mm(keys, gate_b)
        third = mm(keys, up_b)
        dact = mm_t(scaled, out_b)
        sig = jax.nn.sigmoid(first)
        activ = first * sig
        slope = sig * (1.0 - sig)
        deriv = sig + first * slope
        third_deriv = third * deriv
        dact_r[step] = dact
        third_r[step] = third
        activ_r[step] = activ
        deriv_r[step] = deriv
        slope_r[step] = third_deriv
        second_r[step] = third * (slope * (2.0 + first * (1.0 - 2.0 * sig)))
        dfirst_r[step] = (dact * third_deriv).astype(BF16)
        dthird_r[step] = (dact * activ).astype(BF16)
        act_r[step] = (activ * third).astype(BF16)


def update_back_steps(steps, outs, refs, weights, cots):
    k_kept, s_kept, dact_r, third_r, activ_r, deriv_r, slope_r, second_r, dfirst_r, dthird_r, act_r = refs
    gate_b, out_b, up_b = weights
    cot_gate, cot_out, cot_up = cots
    firsts, thirds, dacts = [], [], []
    for step in steps:
        keys, scaled = k_kept[step], s_kept[step]
        bar_dfirst = mm(keys, cot_gate)
        bar_dthird = mm(keys, cot_up)
        bar_act = mm_t(scaled, cot_out)
        dact, activ, deriv = dact_r[step], activ_r[step], deriv_r[step]
        bar_activ = bar_dthird * dact + bar_act * third_r[step]
        bar_dact = (bar_dfirst * slope_r[step] + bar_dthird * activ).astype(BF16)
        bar_df_dact = bar_dfirst * dact
        bar_third = (bar_df_dact * deriv + bar_act * activ).astype(BF16)
        bar_first = (bar_activ * deriv + bar_df_dact * second_r[step]).astype(BF16)
        outs[step][0][...] = (
            mm_t(dfirst_r[step], cot_gate)
            + mm_t(dthird_r[step], cot_up)
            + mm_t(bar_first, gate_b)
            + mm_t(bar_third, up_b)
        )
        outs[step][1][...] = mm(act_r[step], cot_out) + mm(bar_dact, out_b)
        firsts.append(bar_first)
        thirds.append(bar_third)
        dacts.append(bar_dact)
    return firsts, thirds, dacts


def update_away_kernel(groups, depth, scale, place, *refs):
    kept, refs = refs[:11], refs[11:]
    parts, refs = refs[:depth], refs[depth:]
    weights = [w[...].astype(BF16) for w in refs[:3]]
    outs, (cots, firsts, thirds, dacts, whole) = refs[3:-5], refs[-5:]
    assemble(place, parts, whole)
    cots[...] = (whole[...] * scale).astype(BF16)
    outs = unpacked(groups, [None] + list(outs))
    found = update_back_steps(range(1, groups), outs, kept, weights, [cots[i] for i in range(3)])
    for to, values in zip((firsts, thirds, dacts), found):
        for i, value in enumerate(values):
            to[i] = value


def update_home_kernel(depth, place, *refs):
    kept, refs = refs[:11], refs[11:]
    weights = [w[...].astype(BF16) for w in refs[:3]]
    cots, firsts, thirds, dacts = refs[3:7]
    out, slices, sums = refs[7], refs[8:-1], refs[-1]
    outs = [(out.at[0], out.at[1])]
    found = update_back_steps([0], outs, kept, weights, [cots[i] for i in range(3)])
    first, third, dact = (
        jnp.concatenate(mine + [tokens_of(ref)])
        for mine, ref in zip(found, (firsts, thirds, dacts))
    )
    keys = tokens_of(kept[0])
    sums[0] = tmm(keys, first)
    sums[1] = tmm(dact, tokens_of(kept[1]))
    sums[2] = tmm(keys, third)
    send_slices(sums, slices, place[1], depth)


def join_query_kernel(groups, place, *refs):
    pieces, out, scratch = refs[:groups], refs[groups], refs[groups + 1]
    tokens, heads, width = out.shape
    for step, piece in enumerate(pieces):
        put_head(scratch, place[0] ^ step, piece[...], tokens, heads)
    out[...] = rows_of(scratch).reshape(tokens, heads, width).astype(BF16)


def join_update_kernel(groups, place, r, *refs):
    pieces, (out_k, out_v, sk, sv) = unpacked(groups, refs[:-4]), refs[-4:]
    tokens, heads, width = out_k.shape
    for step, piece in enumerate(pieces):
        head = place[0] ^ step
        put_head(sk, head, piece[0][...], tokens, heads)
        put_head(sv, head, piece[1][...] * rate_column(r, head), tokens, heads)
    out_k[...] = rows_of(sk).reshape(tokens, heads, width).astype(BF16)
    out_v[...] = rows_of(sv).reshape(tokens, heads, width).astype(BF16)


def join_rows_kernel(groups, place, *refs):
    parts, grads = refs[:groups], refs[groups:]
    for step, part in enumerate(parts):
        for i, grad in enumerate(grads):
            grad[place[0] ^ step] = part[0, i]


def rows_kernel(groups, place, *refs):
    parts, outs, total = refs[: -groups - 1], refs[-groups - 1 : -1], refs[-1]
    summed = parts[0][0]
    for part in parts[1:]:
        summed += part[0]
    total[...] = summed
    rows = total.shape[1] // groups
    for step, out in enumerate(outs):
        at = pl.multiple_of((place[0] ^ step) * rows, rows)
        out[0] = total[:, pl.ds(at, rows), :]


def local(queries, keys, values, rates, head_scale, gain, w_gate, w_out, w_up, cotangent):
    tokens, heads, width = keys.shape[1:]
    hidden = w_gate.shape[2]
    ctx = lax.axis_size("ctx")
    head_axis = lax.axis_size("head")
    groups = heads
    depth = ctx // groups
    assert groups & (groups - 1) == 0 and depth & (depth - 1) == 0
    scale = 1.0 / math.sqrt(tokens * ctx * width)
    count = float(heads * head_axis * width)
    me = lax.axis_index("ctx")
    mine, layer = lax.rem(me, groups), lax.div(me, groups)
    place = jnp.stack([mine, layer]).astype(jnp.int32)

    def move(x, axis, step):
        return lax.ppermute(x, axis, [(c, c ^ step) for c in range(lax.axis_size(axis))])

    def in_plane(parts):
        return [parts[0]] + [move(p, "ctx", step) for step, p in enumerate(parts) if step]

    def forwarded(got):
        return [got[:1]] if got.shape[0] == 1 else [got[i : i + 1] for i in range(got.shape[0])]

    def scatter(outs, count, unit):
        outs = list(outs)
        evens = list(range(2, count, 2))
        via = forwarded(move(outs.pop(0), "ctx", unit)) if evens else []
        via, outs[0] = after(via, outs[0])
        first = [move(outs[0], "ctx", unit)] if count > 1 else []
        even = [move(p + v, "ctx", r * unit) for p, v, r in zip(outs[1:], via, evens)]
        return [outs[-1]] + first + even

    def gather(part, count, unit):
        got = [part] * count
        for r in [2 * i for i in range(1, count // 2)]:
            got[r] = move(part, "ctx", r * unit)
            got[r + 1] = move(got[r], "ctx", unit)
        if count > 1:
            got[1] = move(part, "ctx", unit)
        return got

    def after(x, *others):
        return lax.optimization_barrier((x, *others))

    def shape(*dims, dtype=F32):
        return jax.ShapeDtypeStruct(dims, dtype)

    flops = 2 * groups * tokens * width * hidden
    pieces = [shape(tokens, width)] * groups
    slices = [shape(len(m), 3, hidden // depth, width) for m in send_groups(depth)]
    joined = shape(tokens, heads, width, dtype=BF16)
    scratch = pltpu.VMEM((width // LANES, tokens * heads, LANES), F32)
    square = pltpu.VMEM((3, hidden, width), F32)

    def split(body, *args):
        outs = [shape(tokens, width, dtype=BF16)] + pieces[1:]
        body = functools.partial(body, groups)
        return call(body, outs, [scratch], 16 * flops, place, *args, mib=8)

    k_in = in_plane(split(split_kernel, keys[0]))
    k_in[0], values, rates = after(k_in[0], values, rates)
    s_in = in_plane(split(split_scaled_kernel, values[0], rates[0]))
    own = [lax.dynamic_index_in_dim(w, mine, 0, keepdims=False) for w in (w_gate, w_out, w_up)]
    own_scale = lax.dynamic_index_in_dim(head_scale, mine, 0, keepdims=True)[None, :]
    k_in, s_in, queries, cotangent = after(k_in, s_in, queries, cotangent)

    def kept(*dims, dtype=F32):
        return shape(*dims, tokens, width, dtype=dtype)

    out = call(
        functools.partial(update_kernel, groups, depth, scale),
        [kept(groups, dtype=BF16)] * 2 + slices, [square], 6 * flops,
        place, *k_in, *s_in, *own,
    )
    early, terms = out[:2], out[2:]
    *q_out, scale_row = call(
        functools.partial(split_apply_kernel, groups),
        [shape(2, tokens, width)] * (groups - 1) + [shape(tokens, width)] * 2 + [shape(8, width)],
        [scratch], flops // 8, place, queries[0], cotangent[0], gain, own_scale,
    )
    q_in = in_plane(q_out[:-2])
    new = functools.reduce(jnp.add, scatter(terms, depth, groups))
    new, q_in, q_last = after(new, q_in, q_out[-2:])
    q_in += [move(x, "ctx", groups - 1) for x in q_last]
    new = gather(new, depth, groups)
    *passed, stats = call(
        functools.partial(apply_kernel, groups, depth),
        [kept(groups), kept(groups), kept(groups, dtype=BF16), kept(groups)]
        + [shape(3, hidden, width, dtype=BF16), shape(2, groups, tokens)],
        [square], 3 * flops, place, scale_row, *q_in, *new,
    )
    bit = 1
    while bit < head_axis:
        stats = stats + move(stats, "head", bit)
        bit *= 2
    out = call(
        functools.partial(apply_back_kernel, groups, depth, count),
        [kept(groups, dtype=BF16)] * 2 + slices,
        [square, pltpu.VMEM((2, groups, tokens), F32)], 6 * flops,
        place, scale_row, *in_plane([stats] * groups), *q_in, *passed,
    )
    q_sent = call(
        query_back_kernel, [shape(tokens, width)] * groups, [], 2 * flops, *out[:2], passed[-1]
    )
    out = out[2:]
    out, early = after(out, early)
    saved = call(
        update_keep_kernel, [kept(groups)] * 6 + [kept(groups, dtype=BF16)] * 3, [], 3 * flops,
        *early, *own,
    )
    part = functools.reduce(jnp.add, scatter(out, depth, groups))
    parts = gather(part, depth, groups)
    q_back = in_plane(q_sent)
    parts, saved, q_back = after(parts, saved, q_back)
    (grad_q,) = call(
        functools.partial(join_query_kernel, groups), [joined], [scratch], flops // 16,
        place, *q_back,
    )
    rows = hidden // depth
    away = [kept(len(members)) for members in packing(groups)[1:]]
    *sent, cots, firsts, thirds, dacts = call(
        functools.partial(update_away_kernel, groups, depth, scale),
        away + [shape(3, hidden, width, dtype=BF16)] + [kept(groups - 1, dtype=BF16)] * 3,
        [square], 9 * flops, place, *early, *saved, *parts, *own, mib=24,
    )
    mine_back, *ends = call(
        functools.partial(update_home_kernel, depth), [kept(2)] + slices, [square], 5 * flops,
        place, *early, *saved, *own, cots, firsts, thirds, dacts,
    )
    back = in_plane([mine_back] + sent)
    ends = scatter(ends, depth, groups)
    if groups == 4:
        ends, back, grad_q = after(ends, back, grad_q)
        back += [move(back[1][2], "ctx", 2), move(back[2][2], "ctx", 1)]
    own_rows = rows // groups
    sent = call(
        functools.partial(rows_kernel, groups),
        [shape(1, 3, own_rows, width)] * groups,
        [pltpu.VMEM((3, rows, width), F32)], flops // 100, place, part, *ends,
    )
    grad_k, grad_v = call(
        functools.partial(join_update_kernel, groups), [joined] * 2, [scratch] * 2, flops // 8,
        place, rates[0], *back,
    )
    got, grad_k, grad_v = after(in_plane(sent), grad_k, grad_v)
    grads = call(
        functools.partial(join_rows_kernel, groups), [shape(heads, own_rows, width)] * 3, [],
        flops // 100, place, *got,
    )
    if lax.axis_size("batch") > 1:
        grads = [lax.psum_scatter(x, "batch", scatter_dimension=1, tiled=True) for x in grads]
    return (grad_q[None], grad_k[None], grad_v[None], grads[0], grads[1], grads[2])


def solution(mesh):
    in_specs = (
        P("batch", "ctx", "head", None),
        P("batch", "ctx", "head", None),
        P("batch", "ctx", "head", None),
        P("batch", "head", "ctx"),
        P("head"),
        P("head", None),
        P("head", None, None),
        P("head", None, None),
        P("head", None, None),
        P("batch", "ctx", "head", None),
    )
    out_specs = (
        P("batch", "ctx", "head", None),
        P("batch", "ctx", "head", None),
        P("batch", "ctx", "head", None),
        P("head", ("ctx", "batch"), None),
        P("head", ("ctx", "batch"), None),
        P("head", ("ctx", "batch"), None),
    )
    return jax.shard_map(local, mesh=mesh, in_specs=in_specs, out_specs=out_specs, check_vma=False)
```

```python
import functools
import math

import jax
import jax.numpy as jnp
from jax import lax
from jax.experimental import pallas as pl
from jax.experimental.pallas import tpu as pltpu
from jax.sharding import PartitionSpec as P

F32 = jnp.float32
BF16 = jnp.bfloat16
LANES = 128
MIB = 1024 * 1024


def mm(a, b):
    return jnp.dot(a, b, preferred_element_type=F32)


def mm_t(a, b):
    return lax.dot_general(a, b, (((1,), (1,)), ((), ())), preferred_element_type=F32)


def tmm(a, b):
    return lax.dot_general(a, b, (((0,), (0,)), ((), ())), preferred_element_type=F32)


def call(body, out_shape, scratch, flops, *args, mib=16):
    smem = pl.BlockSpec(memory_space=pltpu.SMEM)
    vmem = pl.BlockSpec(memory_space=pltpu.VMEM)
    size = sum(a.size * a.dtype.itemsize for a in args)
    size += sum(math.prod(o.shape) * o.dtype.itemsize for o in out_shape)
    return pl.pallas_call(
        body,
        out_shape=out_shape,
        in_specs=[smem if a.dtype == jnp.int32 else vmem for a in args],
        out_specs=[vmem] * len(out_shape),
        scratch_shapes=scratch,
        compiler_params=pltpu.CompilerParams(vmem_limit_bytes=mib * MIB),
        cost_estimate=pl.CostEstimate(flops=flops, bytes_accessed=size, transcendentals=0),
    )(*args)


def put_rows(scratch, x):
    for i in range(scratch.shape[0]):
        scratch[i] = x[:, i * LANES : (i + 1) * LANES]


def take_head(scratch, head, tokens, heads):
    parts = [scratch[i, pl.ds(head, tokens, stride=heads), :] for i in range(scratch.shape[0])]
    return jnp.concatenate(parts, axis=1)


def put_head(scratch, head, x, tokens, heads):
    for i in range(scratch.shape[0]):
        scratch[i, pl.ds(head, tokens, stride=heads), :] = x[:, i * LANES : (i + 1) * LANES]


def rows_of(scratch):
    return jnp.concatenate([scratch[i] for i in range(scratch.shape[0])], axis=1)


def split_kernel(groups, place, x, *rest):
    outs, scratch = rest[:groups], rest[groups]
    tokens, heads, width = x.shape
    put_rows(scratch, x[...].astype(F32).reshape(tokens * heads, width))
    for step, out in enumerate(outs):
        out[...] = take_head(scratch, place[0] ^ step, tokens, heads).astype(out.dtype)


def split_scaled_kernel(groups, place, x, r, *rest):
    outs = rest[:groups]
    split_kernel(groups, place, x, *rest)
    for step in range(groups):
        scaled = outs[step][...].astype(F32) * rate_column(r, place[0] ^ step)
        outs[step][...] = scaled.astype(BF16).astype(outs[step].dtype)


def split_apply_kernel(groups, place, q, cot, gain, scale, *rest):
    outs, scale_row, scratch = rest[:-2], rest[-2], rest[-1]
    scale_row[...] = jnp.broadcast_to(scale[...], scale_row.shape)
    pieces = query_refs(groups, outs)
    split_kernel(groups, place, q, *[one for one, _ in pieces], scratch)
    split_kernel(groups, place, cot, *[two for _, two in pieces], scratch)
    for step in range(groups):
        pieces[step][1][...] *= gain[pl.ds(place[0] ^ step, 1), :]


def packing(groups):
    if groups == 4:
        return [[(0, 0), (0, 1)], [(1, 0), (1, 1), (3, 0)], [(2, 0), (2, 1), (3, 1)]]
    return [[(step, 0), (step, 1)] for step in range(groups)]


def unpacked(groups, refs):
    found = {}
    for ref, members in zip(refs, packing(groups)):
        for i, member in enumerate(members):
            found[member] = ref.at[i]
    for i, ref in enumerate(refs[len(packing(groups)) :]):
        found[(groups - 1, i)] = ref
    return [(found[(step, 0)], found[(step, 1)]) for step in range(groups)]


def rate_column(r, head):
    return jnp.broadcast_to(r[pl.ds(head, 1), :], (8, r.shape[1])).T[:, 0:1]


def send_groups(count):
    odd = list(range(3, count, 2))
    return ([odd] if odd else []) + [[r] for r in [1] + list(range(2, count, 2)) if r < count] + [[0]]


def send_slices(sums, outs, own, count):
    rows = sums.shape[1] // count
    for out, members in zip(outs, send_groups(count)):
        for i, step in enumerate(members):
            at = pl.multiple_of((own ^ step) * rows, rows)
            out[i] = sums[:, pl.ds(at, rows), :]


def update_sums(keys_in, scaled_in, weights, key_kept, scaled_kept):
    gate_b, out_b, up_b = (w[...].astype(BF16) for w in weights)
    acts, dfirsts, dthirds = [], [], []
    for step, (key, value) in enumerate(zip(keys_in, scaled_in)):
        keys = key[...].astype(BF16)
        scaled = value[...].astype(BF16)
        key_kept[step] = keys
        scaled_kept[step] = scaled
        first = mm(keys, gate_b)
        third = mm(keys, up_b)
        sig = jax.nn.sigmoid(first)
        activ = first * sig
        act = (activ * third).astype(BF16)
        dact = mm_t(scaled, out_b)
        deriv = sig * (1.0 + first * (1.0 - sig))
        dfirst = (dact * third * deriv).astype(BF16)
        dthird = (dact * activ).astype(BF16)
        acts.append(act)
        dfirsts.append(dfirst)
        dthirds.append(dthird)
    keys, scaled = tokens_of(key_kept), tokens_of(scaled_kept)
    return (
        tmm(keys, jnp.concatenate(dfirsts)),
        tmm(jnp.concatenate(acts), scaled),
        tmm(keys, jnp.concatenate(dthirds)),
    )


def update_kernel(count, depth, scale, place, *refs):
    keys_in, scaled_in, weights = refs[:count], refs[count : 2 * count], refs[2 * count :][:3]
    key_kept, scaled_kept = refs[2 * count + 3 : 2 * count + 5]
    outs, sums = refs[2 * count + 5 : -1], refs[-1]
    total = update_sums(keys_in, scaled_in, weights, key_kept, scaled_kept)
    for i in range(3):
        sums[i] = total[i] * scale
    send_slices(sums, outs, place[1], depth)
    rows = sums.shape[1] // depth
    at = pl.multiple_of(place[1] * rows, rows)
    for i, w in enumerate(weights):
        outs[-1][0, i] += w[pl.ds(at, rows), :]


def assemble(place, parts, whole):
    rows = parts[0].shape[2]
    for step, part in enumerate(parts):
        at = pl.multiple_of((place[1] ^ step) * rows, rows)
        whole[:, pl.ds(at, rows), :] = part[0]


def query_refs(groups, refs):
    return [(ref.at[0], ref.at[1]) for ref in refs[:groups]]


def tokens_of(ref):
    return ref[...].reshape(ref.shape[0] * ref.shape[1], ref.shape[2])


def apply_kernel(groups, depth, place, scale_row, *refs):
    pieces, refs = query_refs(groups, refs), refs[groups:]
    parts = refs[:depth]
    activ_ref, slope_ref, hidden_ref, os_ref, new_b, stats, whole = refs[depth:]
    assemble(place, parts, whole)
    new_b[...] = whole[...].astype(BF16)
    for step in range(groups):
        queries = pieces[step][0][...].astype(BF16)
        tokens = queries.shape[0]
        first = mm(queries, new_b[0])
        third = mm(queries, new_b[2])
        sig = jax.nn.sigmoid(first)
        activ = first * sig
        hidden = (activ * third).astype(BF16)
        scaled = mm(hidden, new_b[1]) * scale_row[0:1, :]
        activ_ref[step] = activ
        slope_ref[step] = third * (sig * (1.0 + first * (1.0 - sig)))
        hidden_ref[step] = hidden
        os_ref[step] = scaled
        sq = jnp.sum(scaled * scaled, axis=1, keepdims=True)
        ps = jnp.sum(scaled * pieces[step][1][...], axis=1, keepdims=True)
        lane = lax.broadcasted_iota(jnp.int32, (tokens, LANES), 1)
        both = jnp.where(lane == 0, sq, jnp.where(lane == 1, ps, 0.0)).T
        source = place[0] ^ step
        stats[0, pl.ds(source, 1), :] = both[0:1, :]
        stats[1, pl.ds(source, 1), :] = both[1:2, :]


def apply_back_kernel(groups, depth, count, place, scale_row, *refs):
    stats, refs = refs[:groups], refs[groups:]
    pieces, refs = query_refs(groups, refs), refs[groups:]
    activ_ref, slope_ref, hidden_ref, os_ref, new_b = refs[:5]
    dfirst_ref, dthird_ref, slices, sums, both = refs[5], refs[6], refs[7:-2], refs[-2], refs[-1]
    both[...] = functools.reduce(jnp.add, [ref[...] for ref in stats])
    douts = []
    for step in range(groups):
        source = place[0] ^ step
        sq = rate_column(both.at[0], source)
        ps = rate_column(both.at[1], source)
        inv = lax.rsqrt(sq / count + 1e-06)
        dos = inv * pieces[step][1][...] - os_ref[step] * (inv * inv * inv * ps / count)
        dout = (dos * scale_row[0:1, :]).astype(BF16)
        dhidden = mm_t(dout, new_b[1])
        dthird = (dhidden * activ_ref[step]).astype(BF16)
        dfirst = (dhidden * slope_ref[step]).astype(BF16)
        dfirst_ref[step] = dfirst
        dthird_ref[step] = dthird
        douts.append(dout)
    queries = jnp.concatenate([piece[0][...].astype(BF16) for piece in pieces])
    sums[0] = tmm(queries, tokens_of(dfirst_ref))
    sums[1] = tmm(tokens_of(hidden_ref), jnp.concatenate(douts))
    sums[2] = tmm(queries, tokens_of(dthird_ref))
    send_slices(sums, slices, place[1], depth)


def query_back_kernel(dfirst, dthird, new_b, *outs):
    for step, out in enumerate(outs):
        out[...] = mm_t(dfirst[step], new_b[0]) + mm_t(dthird[step], new_b[2])


def update_keep_kernel(k_kept, s_kept, w_gate, w_out, w_up, *outs):
    dact_r, third_r, activ_r, deriv_r, slope_r, second_r, dfirst_r, dthird_r, act_r = outs
    gate_b, out_b, up_b = (w[...].astype(BF16) for w in (w_gate, w_out, w_up))
    for step in range(k_kept.shape[0]):
        keys, scaled = k_kept[step], s_kept[step]
        first = mm(keys, gate_b)
        third = mm(keys, up_b)
        dact = mm_t(scaled, out_b)
        sig = jax.nn.sigmoid(first)
        activ = first * sig
        slope = sig * (1.0 - sig)
        deriv = sig + first * slope
        third_deriv = third * deriv
        dact_r[step] = dact
        third_r[step] = third
        activ_r[step] = activ
        deriv_r[step] = deriv
        slope_r[step] = third_deriv
        second_r[step] = third * (slope * (2.0 + first * (1.0 - 2.0 * sig)))
        dfirst_r[step] = (dact * third_deriv).astype(BF16)
        dthird_r[step] = (dact * activ).astype(BF16)
        act_r[step] = (activ * third).astype(BF16)


def update_back_kernel(groups, depth, scale, place, *refs):
    (k_kept, s_kept), refs = refs[:2], refs[2:]
    kept, refs = refs[:9], refs[9:]
    dact_r, third_r, activ_r, deriv_r, slope_r, second_r, dfirst_r, dthird_r, act_r = kept
    parts, refs = refs[:depth], refs[depth:]
    w_gate, w_out, w_up = refs[:3]
    packed = len(packing(groups))
    outs, slices = unpacked(groups, refs[3 : packed + 3]), refs[packed + 3 : -2]
    whole, sums = refs[-2:]
    assemble(place, parts, whole)
    gate_b, out_b, up_b = (w[...].astype(BF16) for w in (w_gate, w_out, w_up))
    cot_gate, cot_out, cot_up = ((whole[i] * scale).astype(BF16) for i in range(3))
    firsts, thirds, dacts = [], [], []
    for step in range(groups):
        keys, scaled = k_kept[step], s_kept[step]
        bar_dfirst = mm(keys, cot_gate)
        bar_dthird = mm(keys, cot_up)
        bar_act = mm_t(scaled, cot_out)
        dact, activ, deriv = dact_r[step], activ_r[step], deriv_r[step]
        bar_activ = bar_dthird * dact + bar_act * third_r[step]
        bar_dact = (bar_dfirst * slope_r[step] + bar_dthird * activ).astype(BF16)
        bar_df_dact = bar_dfirst * dact
        bar_third = (bar_df_dact * deriv + bar_act * activ).astype(BF16)
        bar_first = (bar_activ * deriv + bar_df_dact * second_r[step]).astype(BF16)
        outs[step][0][...] = (
            mm_t(dfirst_r[step], cot_gate)
            + mm_t(dthird_r[step], cot_up)
            + mm_t(bar_first, gate_b)
            + mm_t(bar_third, up_b)
        )
        outs[step][1][...] = mm(act_r[step], cot_out) + mm(bar_dact, out_b)
        firsts.append(bar_first)
        thirds.append(bar_third)
        dacts.append(bar_dact)
    keys = tokens_of(k_kept)
    sums[0] = tmm(keys, jnp.concatenate(firsts))
    sums[1] = tmm(jnp.concatenate(dacts), tokens_of(s_kept))
    sums[2] = tmm(keys, jnp.concatenate(thirds))
    send_slices(sums, slices, place[1], depth)


def join_query_kernel(groups, place, *refs):
    pieces, out, scratch = refs[:groups], refs[groups], refs[groups + 1]
    tokens, heads, width = out.shape
    for step, piece in enumerate(pieces):
        put_head(scratch, place[0] ^ step, piece[...], tokens, heads)
    out[...] = rows_of(scratch).reshape(tokens, heads, width).astype(BF16)


def join_update_kernel(groups, place, r, *refs):
    pieces, (out_k, out_v, sk, sv) = unpacked(groups, refs[:-4]), refs[-4:]
    tokens, heads, width = out_k.shape
    for step, piece in enumerate(pieces):
        head = place[0] ^ step
        put_head(sk, head, piece[0][...], tokens, heads)
        put_head(sv, head, piece[1][...] * rate_column(r, head), tokens, heads)
    out_k[...] = rows_of(sk).reshape(tokens, heads, width).astype(BF16)
    out_v[...] = rows_of(sv).reshape(tokens, heads, width).astype(BF16)


def join_rows_kernel(groups, place, *refs):
    parts, grads = refs[:groups], refs[groups:]
    for step, part in enumerate(parts):
        for i, grad in enumerate(grads):
            grad[place[0] ^ step] = part[0, i]


def rows_kernel(groups, place, *refs):
    parts, outs, total = refs[: -groups - 1], refs[-groups - 1 : -1], refs[-1]
    summed = parts[0][0]
    for part in parts[1:]:
        summed += part[0]
    total[...] = summed
    rows = total.shape[1] // groups
    for step, out in enumerate(outs):
        at = pl.multiple_of((place[0] ^ step) * rows, rows)
        out[0] = total[:, pl.ds(at, rows), :]


def local(queries, keys, values, rates, head_scale, gain, w_gate, w_out, w_up, cotangent):
    tokens, heads, width = keys.shape[1:]
    hidden = w_gate.shape[2]
    ctx = lax.axis_size("ctx")
    head_axis = lax.axis_size("head")
    groups = heads
    depth = ctx // groups
    assert groups & (groups - 1) == 0 and depth & (depth - 1) == 0
    scale = 1.0 / math.sqrt(tokens * ctx * width)
    count = float(heads * head_axis * width)
    me = lax.axis_index("ctx")
    mine, layer = lax.rem(me, groups), lax.div(me, groups)
    place = jnp.stack([mine, layer]).astype(jnp.int32)

    def move(x, axis, step):
        return lax.ppermute(x, axis, [(c, c ^ step) for c in range(lax.axis_size(axis))])

    def in_plane(parts):
        return [parts[0]] + [move(p, "ctx", step) for step, p in enumerate(parts) if step]

    def forwarded(got):
        return [got[:1]] if got.shape[0] == 1 else [got[i : i + 1] for i in range(got.shape[0])]

    def scatter(outs, count, unit):
        outs = list(outs)
        evens = list(range(2, count, 2))
        via = forwarded(move(outs.pop(0), "ctx", unit)) if evens else []
        via, outs[0] = after(via, outs[0])
        first = [move(outs[0], "ctx", unit)] if count > 1 else []
        even = [move(p + v, "ctx", r * unit) for p, v, r in zip(outs[1:], via, evens)]
        return [outs[-1]] + first + even

    def gather(part, count, unit):
        got = [part] * count
        for r in [2 * i for i in range(1, count // 2)]:
            got[r] = move(part, "ctx", r * unit)
            got[r + 1] = move(got[r], "ctx", unit)
        if count > 1:
            got[1] = move(part, "ctx", unit)
        return got

    def after(x, *others):
        return lax.optimization_barrier((x, *others))

    def shape(*dims, dtype=F32):
        return jax.ShapeDtypeStruct(dims, dtype)

    flops = 2 * groups * tokens * width * hidden
    pieces = [shape(tokens, width)] * groups
    slices = [shape(len(m), 3, hidden // depth, width) for m in send_groups(depth)]
    joined = shape(tokens, heads, width, dtype=BF16)
    scratch = pltpu.VMEM((width // LANES, tokens * heads, LANES), F32)
    square = pltpu.VMEM((3, hidden, width), F32)

    def split(body, *args):
        outs = [shape(tokens, width, dtype=BF16)] + pieces[1:]
        body = functools.partial(body, groups)
        return call(body, outs, [scratch], 16 * flops, place, *args, mib=8)

    k_in = in_plane(split(split_kernel, keys[0]))
    s_in = in_plane(split(split_scaled_kernel, values[0], rates[0]))
    own = [lax.dynamic_index_in_dim(w, mine, 0, keepdims=False) for w in (w_gate, w_out, w_up)]
    own_scale = lax.dynamic_index_in_dim(head_scale, mine, 0, keepdims=True)[None, :]
    k_in, s_in, queries, cotangent = after(k_in, s_in, queries, cotangent)

    def kept(*dims, dtype=F32):
        return shape(*dims, tokens, width, dtype=dtype)

    out = call(
        functools.partial(update_kernel, groups, depth, scale),
        [kept(groups, dtype=BF16)] * 2 + slices, [square], 6 * flops,
        place, *k_in, *s_in, *own,
    )
    early, terms = out[:2], out[2:]
    *q_out, scale_row = call(
        functools.partial(split_apply_kernel, groups),
        [shape(2, tokens, width)] * groups + [shape(8, width)],
        [scratch], flops // 8, place, queries[0], cotangent[0], gain, own_scale,
    )
    q_in = in_plane(q_out[:-1])
    new = functools.reduce(jnp.add, scatter(terms, depth, groups))
    new, q_in, q_last = after(new, q_in, q_out[-1])
    q_in.append(move(q_last, "ctx", groups - 1))
    new = gather(new, depth, groups)
    *passed, stats = call(
        functools.partial(apply_kernel, groups, depth),
        [kept(groups), kept(groups), kept(groups, dtype=BF16), kept(groups)]
        + [shape(3, hidden, width, dtype=BF16), shape(2, groups, tokens)],
        [square], 3 * flops, place, scale_row, *q_in, *new,
    )
    bit = 1
    while bit < head_axis:
        stats = stats + move(stats, "head", bit)
        bit *= 2
    out = call(
        functools.partial(apply_back_kernel, groups, depth, count),
        [kept(groups, dtype=BF16)] * 2 + slices,
        [square, pltpu.VMEM((2, groups, tokens), F32)], 6 * flops,
        place, scale_row, *in_plane([stats] * groups), *q_in, *passed,
    )
    q_sent = call(
        query_back_kernel, [shape(tokens, width)] * groups, [], 2 * flops, *out[:2], passed[-1]
    )
    out = out[2:]
    out, early = after(out, early)
    saved = call(
        update_keep_kernel, [kept(groups)] * 6 + [kept(groups, dtype=BF16)] * 3, [], 3 * flops,
        *early, *own,
    )
    part = functools.reduce(jnp.add, scatter(out, depth, groups))
    parts = gather(part, depth, groups)
    q_back = in_plane(q_sent)
    parts, saved, q_back = after(parts, saved, q_back)
    (grad_q,) = call(
        functools.partial(join_query_kernel, groups), [joined], [scratch], flops // 16,
        place, *q_back,
    )
    rows = hidden // depth
    out = call(
        functools.partial(update_back_kernel, groups, depth, scale),
        [kept(len(members)) for members in packing(groups)] + slices, [square] * 2, 12 * flops,
        place, *early, *saved, *parts, *own, mib=24,
    )
    packed = len(packing(groups))
    back = in_plane(out[:packed])
    ends = scatter(out[packed:], depth, groups)
    if groups == 4:
        ends, back, grad_q = after(ends, back, grad_q)
        back += [move(back[1][2], "ctx", 2), move(back[2][2], "ctx", 1)]
    own_rows = rows // groups
    sent = call(
        functools.partial(rows_kernel, groups),
        [shape(1, 3, own_rows, width)] * groups,
        [pltpu.VMEM((3, rows, width), F32)], flops // 100, place, part, *ends,
    )
    grad_k, grad_v = call(
        functools.partial(join_update_kernel, groups), [joined] * 2, [scratch] * 2, flops // 8,
        place, rates[0], *back,
    )
    got, grad_k, grad_v = after(in_plane(sent), grad_k, grad_v)
    grads = call(
        functools.partial(join_rows_kernel, groups), [shape(heads, own_rows, width)] * 3, [],
        flops // 100, place, *got,
    )
    if lax.axis_size("batch") > 1:
        grads = [lax.psum_scatter(x, "batch", scatter_dimension=1, tiled=True) for x in grads]
    return (grad_q[None], grad_k[None], grad_v[None], grads[0], grads[1], grads[2])


def solution(mesh):
    in_specs = (
        P("batch", "ctx", "head", None),
        P("batch", "ctx", "head", None),
        P("batch", "ctx", "head", None),
        P("batch", "head", "ctx"),
        P("head"),
        P("head", None),
        P("head", None, None),
        P("head", None, None),
        P("head", None, None),
        P("batch", "ctx", "head", None),
    )
    out_specs = (
        P("batch", "ctx", "head", None),
        P("batch", "ctx", "head", None),
        P("batch", "ctx", "head", None),
        P("head", ("ctx", "batch"), None),
        P("head", ("ctx", "batch"), None),
        P("head", ("ctx", "batch"), None),
    )
    return jax.shard_map(local, mesh=mesh, in_specs=in_specs, out_specs=out_specs, check_vma=False)
```

```python
import functools
import math

import jax
import jax.numpy as jnp
from jax import lax
from jax.experimental import pallas as pl
from jax.experimental.pallas import tpu as pltpu
from jax.sharding import PartitionSpec as P

F32 = jnp.float32
BF16 = jnp.bfloat16
LANES = 128
MIB = 1024 * 1024


def mm(a, b):
    return jnp.dot(a, b, preferred_element_type=F32)


def mm_t(a, b):
    return lax.dot_general(a, b, (((1,), (1,)), ((), ())), preferred_element_type=F32)


def tmm(a, b):
    return lax.dot_general(a, b, (((0,), (0,)), ((), ())), preferred_element_type=F32)


def call(body, out_shape, scratch, flops, *args, mib=16):
    smem = pl.BlockSpec(memory_space=pltpu.SMEM)
    vmem = pl.BlockSpec(memory_space=pltpu.VMEM)
    size = sum(a.size * a.dtype.itemsize for a in args)
    size += sum(math.prod(o.shape) * o.dtype.itemsize for o in out_shape)
    return pl.pallas_call(
        body,
        out_shape=out_shape,
        in_specs=[smem if a.dtype == jnp.int32 else vmem for a in args],
        out_specs=[vmem] * len(out_shape),
        scratch_shapes=scratch,
        compiler_params=pltpu.CompilerParams(vmem_limit_bytes=mib * MIB),
        cost_estimate=pl.CostEstimate(flops=flops, bytes_accessed=size, transcendentals=0),
    )(*args)


def put_rows(scratch, x):
    for i in range(scratch.shape[0]):
        scratch[i] = x[:, i * LANES : (i + 1) * LANES]


def take_head(scratch, head, tokens, heads):
    parts = [scratch[i, pl.ds(head, tokens, stride=heads), :] for i in range(scratch.shape[0])]
    return jnp.concatenate(parts, axis=1)


def put_head(scratch, head, x, tokens, heads):
    for i in range(scratch.shape[0]):
        scratch[i, pl.ds(head, tokens, stride=heads), :] = x[:, i * LANES : (i + 1) * LANES]


def rows_of(scratch):
    return jnp.concatenate([scratch[i] for i in range(scratch.shape[0])], axis=1)


def split_kernel(groups, place, x, *rest):
    outs, scratch = rest[:groups], rest[groups]
    tokens, heads, width = x.shape
    put_rows(scratch, x[...].astype(F32).reshape(tokens * heads, width))
    for step, out in enumerate(outs):
        out[...] = take_head(scratch, place[0] ^ step, tokens, heads).astype(out.dtype)


def split_scaled_kernel(groups, place, x, r, *rest):
    outs = rest[:groups]
    split_kernel(groups, place, x, *rest)
    for step in range(groups):
        scaled = outs[step][...].astype(F32) * rate_column(r, place[0] ^ step)
        outs[step][...] = scaled.astype(BF16).astype(outs[step].dtype)


def split_apply_kernel(groups, place, q, cot, gain, scale, *rest):
    outs, scale_row, scratch = rest[:-2], rest[-2], rest[-1]
    scale_row[...] = jnp.broadcast_to(scale[...], scale_row.shape)
    pieces = query_refs(groups, outs)
    split_kernel(groups, place, q, *[one for one, _ in pieces], scratch)
    split_kernel(groups, place, cot, *[two for _, two in pieces], scratch)
    for step in range(groups):
        pieces[step][1][...] *= gain[pl.ds(place[0] ^ step, 1), :]


def packing(groups):
    if groups == 4:
        return [[(0, 0), (0, 1)], [(1, 0), (1, 1), (3, 0)], [(2, 0), (2, 1), (3, 1)]]
    return [[(step, 0), (step, 1)] for step in range(groups)]


def unpacked(groups, refs):
    found = {}
    for ref, members in zip(refs, packing(groups)):
        for i, member in enumerate(members):
            found[member] = ref.at[i]
    for i, ref in enumerate(refs[len(packing(groups)) :]):
        found[(groups - 1, i)] = ref
    return [(found[(step, 0)], found[(step, 1)]) for step in range(groups)]


def rate_column(r, head):
    return jnp.broadcast_to(r[pl.ds(head, 1), :], (8, r.shape[1])).T[:, 0:1]


def send_groups(count):
    odd = list(range(3, count, 2))
    return ([odd] if odd else []) + [[r] for r in [1] + list(range(2, count, 2)) if r < count] + [[0]]


def send_slices(sums, outs, own, count):
    rows = sums.shape[1] // count
    for out, members in zip(outs, send_groups(count)):
        for i, step in enumerate(members):
            at = pl.multiple_of((own ^ step) * rows, rows)
            out[i] = sums[:, pl.ds(at, rows), :]


def update_sums(keys_in, scaled_in, weights, key_kept, scaled_kept):
    gate_b, out_b, up_b = (w[...].astype(BF16) for w in weights)
    acts, dfirsts, dthirds = [], [], []
    for step, (key, value) in enumerate(zip(keys_in, scaled_in)):
        keys = key[...].astype(BF16)
        scaled = value[...].astype(BF16)
        key_kept[step] = keys
        scaled_kept[step] = scaled
        first = mm(keys, gate_b)
        third = mm(keys, up_b)
        sig = jax.nn.sigmoid(first)
        activ = first * sig
        act = (activ * third).astype(BF16)
        dact = mm_t(scaled, out_b)
        deriv = sig * (1.0 + first * (1.0 - sig))
        dfirst = (dact * third * deriv).astype(BF16)
        dthird = (dact * activ).astype(BF16)
        acts.append(act)
        dfirsts.append(dfirst)
        dthirds.append(dthird)
    keys, scaled = tokens_of(key_kept), tokens_of(scaled_kept)
    return (
        tmm(keys, jnp.concatenate(dfirsts)),
        tmm(jnp.concatenate(acts), scaled),
        tmm(keys, jnp.concatenate(dthirds)),
    )


def update_kernel(count, depth, scale, place, *refs):
    keys_in, scaled_in, weights = refs[:count], refs[count : 2 * count], refs[2 * count :][:3]
    key_kept, scaled_kept = refs[2 * count + 3 : 2 * count + 5]
    outs, sums = refs[2 * count + 5 : -1], refs[-1]
    total = update_sums(keys_in, scaled_in, weights, key_kept, scaled_kept)
    for i in range(3):
        sums[i] = total[i] * scale
    send_slices(sums, outs, place[1], depth)
    rows = sums.shape[1] // depth
    at = pl.multiple_of(place[1] * rows, rows)
    for i, w in enumerate(weights):
        outs[-1][0, i] += w[pl.ds(at, rows), :]


def assemble(place, parts, whole):
    rows = parts[0].shape[2]
    for step, part in enumerate(parts):
        at = pl.multiple_of((place[1] ^ step) * rows, rows)
        whole[:, pl.ds(at, rows), :] = part[0]


def query_refs(groups, refs):
    return [(ref.at[0], ref.at[1]) for ref in refs[: groups - 1]] + [refs[groups - 1 : groups + 1]]


def tokens_of(ref):
    return ref[...].reshape(ref.shape[0] * ref.shape[1], ref.shape[2])


def apply_kernel(groups, depth, place, scale_row, *refs):
    pieces, refs = query_refs(groups, refs), refs[groups + 1 :]
    parts = refs[:depth]
    activ_ref, slope_ref, hidden_ref, os_ref, new_b, stats, whole = refs[depth:]
    assemble(place, parts, whole)
    new_b[...] = whole[...].astype(BF16)
    for step in range(groups):
        queries = pieces[step][0][...].astype(BF16)
        tokens = queries.shape[0]
        first = mm(queries, new_b[0])
        third = mm(queries, new_b[2])
        sig = jax.nn.sigmoid(first)
        activ = first * sig
        hidden = (activ * third).astype(BF16)
        scaled = mm(hidden, new_b[1]) * scale_row[0:1, :]
        activ_ref[step] = activ
        slope_ref[step] = third * (sig * (1.0 + first * (1.0 - sig)))
        hidden_ref[step] = hidden
        os_ref[step] = scaled
        sq = jnp.sum(scaled * scaled, axis=1, keepdims=True)
        ps = jnp.sum(scaled * pieces[step][1][...], axis=1, keepdims=True)
        lane = lax.broadcasted_iota(jnp.int32, (tokens, LANES), 1)
        both = jnp.where(lane == 0, sq, jnp.where(lane == 1, ps, 0.0)).T
        source = place[0] ^ step
        stats[0, pl.ds(source, 1), :] = both[0:1, :]
        stats[1, pl.ds(source, 1), :] = both[1:2, :]


def apply_back_kernel(groups, depth, count, place, scale_row, *refs):
    stats, refs = refs[:groups], refs[groups:]
    pieces, refs = query_refs(groups, refs), refs[groups + 1 :]
    activ_ref, slope_ref, hidden_ref, os_ref, new_b = refs[:5]
    dfirst_ref, dthird_ref, slices, sums, both = refs[5], refs[6], refs[7:-2], refs[-2], refs[-1]
    both[...] = functools.reduce(jnp.add, [ref[...] for ref in stats])
    douts = []
    for step in range(groups):
        source = place[0] ^ step
        sq = rate_column(both.at[0], source)
        ps = rate_column(both.at[1], source)
        inv = lax.rsqrt(sq / count + 1e-06)
        dos = inv * pieces[step][1][...] - os_ref[step] * (inv * inv * inv * ps / count)
        dout = (dos * scale_row[0:1, :]).astype(BF16)
        dhidden = mm_t(dout, new_b[1])
        dthird = (dhidden * activ_ref[step]).astype(BF16)
        dfirst = (dhidden * slope_ref[step]).astype(BF16)
        dfirst_ref[step] = dfirst
        dthird_ref[step] = dthird
        douts.append(dout)
    queries = jnp.concatenate([piece[0][...].astype(BF16) for piece in pieces])
    sums[0] = tmm(queries, tokens_of(dfirst_ref))
    sums[1] = tmm(tokens_of(hidden_ref), jnp.concatenate(douts))
    sums[2] = tmm(queries, tokens_of(dthird_ref))
    send_slices(sums, slices, place[1], depth)


def query_back_kernel(dfirst, dthird, new_b, *outs):
    for step, out in enumerate(outs):
        out[...] = mm_t(dfirst[step], new_b[0]) + mm_t(dthird[step], new_b[2])


def update_keep_kernel(k_kept, s_kept, w_gate, w_out, w_up, *outs):
    dact_r, third_r, activ_r, deriv_r, slope_r, second_r, dfirst_r, dthird_r, act_r = outs
    gate_b, out_b, up_b = (w[...].astype(BF16) for w in (w_gate, w_out, w_up))
    for step in range(k_kept.shape[0]):
        keys, scaled = k_kept[step], s_kept[step]
        first = mm(keys, gate_b)
        third = mm(keys, up_b)
        dact = mm_t(scaled, out_b)
        sig = jax.nn.sigmoid(first)
        activ = first * sig
        slope = sig * (1.0 - sig)
        deriv = sig + first * slope
        third_deriv = third * deriv
        dact_r[step] = dact
        third_r[step] = third
        activ_r[step] = activ
        deriv_r[step] = deriv
        slope_r[step] = third_deriv
        second_r[step] = third * (slope * (2.0 + first * (1.0 - 2.0 * sig)))
        dfirst_r[step] = (dact * third_deriv).astype(BF16)
        dthird_r[step] = (dact * activ).astype(BF16)
        act_r[step] = (activ * third).astype(BF16)


def update_back_kernel(groups, depth, scale, place, *refs):
    (k_kept, s_kept), refs = refs[:2], refs[2:]
    kept, refs = refs[:9], refs[9:]
    dact_r, third_r, activ_r, deriv_r, slope_r, second_r, dfirst_r, dthird_r, act_r = kept
    parts, refs = refs[:depth], refs[depth:]
    w_gate, w_out, w_up = refs[:3]
    packed = len(packing(groups))
    outs, slices = unpacked(groups, refs[3 : packed + 3]), refs[packed + 3 : -2]
    whole, sums = refs[-2:]
    assemble(place, parts, whole)
    gate_b, out_b, up_b = (w[...].astype(BF16) for w in (w_gate, w_out, w_up))
    cot_gate, cot_out, cot_up = ((whole[i] * scale).astype(BF16) for i in range(3))
    firsts, thirds, dacts = [], [], []
    for step in range(groups):
        keys, scaled = k_kept[step], s_kept[step]
        bar_dfirst = mm(keys, cot_gate)
        bar_dthird = mm(keys, cot_up)
        bar_act = mm_t(scaled, cot_out)
        dact, activ, deriv = dact_r[step], activ_r[step], deriv_r[step]
        bar_activ = bar_dthird * dact + bar_act * third_r[step]
        bar_dact = (bar_dfirst * slope_r[step] + bar_dthird * activ).astype(BF16)
        bar_df_dact = bar_dfirst * dact
        bar_third = (bar_df_dact * deriv + bar_act * activ).astype(BF16)
        bar_first = (bar_activ * deriv + bar_df_dact * second_r[step]).astype(BF16)
        outs[step][0][...] = (
            mm_t(dfirst_r[step], cot_gate)
            + mm_t(dthird_r[step], cot_up)
            + mm_t(bar_first, gate_b)
            + mm_t(bar_third, up_b)
        )
        outs[step][1][...] = mm(act_r[step], cot_out) + mm(bar_dact, out_b)
        firsts.append(bar_first)
        thirds.append(bar_third)
        dacts.append(bar_dact)
    keys = tokens_of(k_kept)
    sums[0] = tmm(keys, jnp.concatenate(firsts))
    sums[1] = tmm(jnp.concatenate(dacts), tokens_of(s_kept))
    sums[2] = tmm(keys, jnp.concatenate(thirds))
    send_slices(sums, slices, place[1], depth)


def join_query_kernel(groups, place, *refs):
    pieces, out, scratch = refs[:groups], refs[groups], refs[groups + 1]
    tokens, heads, width = out.shape
    for step, piece in enumerate(pieces):
        put_head(scratch, place[0] ^ step, piece[...], tokens, heads)
    out[...] = rows_of(scratch).reshape(tokens, heads, width).astype(BF16)


def join_update_kernel(groups, place, r, *refs):
    pieces, (out_k, out_v, sk, sv) = unpacked(groups, refs[:-4]), refs[-4:]
    tokens, heads, width = out_k.shape
    for step, piece in enumerate(pieces):
        head = place[0] ^ step
        put_head(sk, head, piece[0][...], tokens, heads)
        put_head(sv, head, piece[1][...] * rate_column(r, head), tokens, heads)
    out_k[...] = rows_of(sk).reshape(tokens, heads, width).astype(BF16)
    out_v[...] = rows_of(sv).reshape(tokens, heads, width).astype(BF16)


def join_rows_kernel(groups, place, *refs):
    parts, grads = refs[:groups], refs[groups:]
    for step, part in enumerate(parts):
        for i, grad in enumerate(grads):
            grad[place[0] ^ step] = part[0, i]


def rows_kernel(groups, place, *refs):
    parts, outs, total = refs[: -groups - 1], refs[-groups - 1 : -1], refs[-1]
    summed = parts[0][0]
    for part in parts[1:]:
        summed += part[0]
    total[...] = summed
    rows = total.shape[1] // groups
    for step, out in enumerate(outs):
        at = pl.multiple_of((place[0] ^ step) * rows, rows)
        out[0] = total[:, pl.ds(at, rows), :]


def local(queries, keys, values, rates, head_scale, gain, w_gate, w_out, w_up, cotangent):
    tokens, heads, width = keys.shape[1:]
    hidden = w_gate.shape[2]
    ctx = lax.axis_size("ctx")
    head_axis = lax.axis_size("head")
    groups = heads
    depth = ctx // groups
    assert groups & (groups - 1) == 0 and depth & (depth - 1) == 0
    scale = 1.0 / math.sqrt(tokens * ctx * width)
    count = float(heads * head_axis * width)
    me = lax.axis_index("ctx")
    mine, layer = lax.rem(me, groups), lax.div(me, groups)
    place = jnp.stack([mine, layer]).astype(jnp.int32)

    def move(x, axis, step):
        return lax.ppermute(x, axis, [(c, c ^ step) for c in range(lax.axis_size(axis))])

    def in_plane(parts):
        return [parts[0]] + [move(p, "ctx", step) for step, p in enumerate(parts) if step]

    def forwarded(got):
        return [got[:1]] if got.shape[0] == 1 else [got[i : i + 1] for i in range(got.shape[0])]

    def scatter(outs, count, unit):
        outs = list(outs)
        evens = list(range(2, count, 2))
        via = forwarded(move(outs.pop(0), "ctx", unit)) if evens else []
        via, outs[0] = after(via, outs[0])
        first = [move(outs[0], "ctx", unit)] if count > 1 else []
        even = [move(p + v, "ctx", r * unit) for p, v, r in zip(outs[1:], via, evens)]
        return [outs[-1]] + first + even

    def gather(part, count, unit):
        got = [part] * count
        for r in [2 * i for i in range(1, count // 2)]:
            got[r] = move(part, "ctx", r * unit)
            got[r + 1] = move(got[r], "ctx", unit)
        if count > 1:
            got[1] = move(part, "ctx", unit)
        return got

    def after(x, *others):
        return lax.optimization_barrier((x, *others))

    def shape(*dims, dtype=F32):
        return jax.ShapeDtypeStruct(dims, dtype)

    flops = 2 * groups * tokens * width * hidden
    pieces = [shape(tokens, width)] * groups
    slices = [shape(len(m), 3, hidden // depth, width) for m in send_groups(depth)]
    joined = shape(tokens, heads, width, dtype=BF16)
    scratch = pltpu.VMEM((width // LANES, tokens * heads, LANES), F32)
    square = pltpu.VMEM((3, hidden, width), F32)

    def split(body, *args):
        outs = [shape(tokens, width, dtype=BF16)] + pieces[1:]
        body = functools.partial(body, groups)
        return call(body, outs, [scratch], 16 * flops, place, *args, mib=8)

    k_in = in_plane(split(split_kernel, keys[0]))
    s_in = in_plane(split(split_scaled_kernel, values[0], rates[0]))
    own = [lax.dynamic_index_in_dim(w, mine, 0, keepdims=False) for w in (w_gate, w_out, w_up)]
    own_scale = lax.dynamic_index_in_dim(head_scale, mine, 0, keepdims=True)[None, :]
    k_in, s_in, queries, cotangent = after(k_in, s_in, queries, cotangent)

    def kept(*dims, dtype=F32):
        return shape(*dims, tokens, width, dtype=dtype)

    out = call(
        functools.partial(update_kernel, groups, depth, scale),
        [kept(groups, dtype=BF16)] * 2 + slices, [square], 6 * flops,
        place, *k_in, *s_in, *own,
    )
    early, terms = out[:2], out[2:]
    *q_out, scale_row = call(
        functools.partial(split_apply_kernel, groups),
        [shape(2, tokens, width)] * (groups - 1) + [shape(tokens, width)] * 2 + [shape(8, width)],
        [scratch], flops // 8, place, queries[0], cotangent[0], gain, own_scale,
    )
    q_in = in_plane(q_out[:-2])
    new = functools.reduce(jnp.add, scatter(terms, depth, groups))
    new, q_in, q_last = after(new, q_in, q_out[-2:])
    q_in += [move(x, "ctx", groups - 1) for x in q_last]
    new = gather(new, depth, groups)
    *passed, stats = call(
        functools.partial(apply_kernel, groups, depth),
        [kept(groups), kept(groups), kept(groups, dtype=BF16), kept(groups)]
        + [shape(3, hidden, width, dtype=BF16), shape(2, groups, tokens)],
        [square], 3 * flops, place, scale_row, *q_in, *new,
    )
    bit = 1
    while bit < head_axis:
        stats = stats + move(stats, "head", bit)
        bit *= 2
    out = call(
        functools.partial(apply_back_kernel, groups, depth, count),
        [kept(groups, dtype=BF16)] * 2 + slices,
        [square, pltpu.VMEM((2, groups, tokens), F32)], 6 * flops,
        place, scale_row, *in_plane([stats] * groups), *q_in, *passed,
    )
    q_sent = call(
        query_back_kernel, [shape(tokens, width)] * groups, [], 2 * flops, *out[:2], passed[-1]
    )
    out = out[2:]
    out, early = after(out, early)
    saved = call(
        update_keep_kernel, [kept(groups)] * 6 + [kept(groups, dtype=BF16)] * 3, [], 3 * flops,
        *early, *own,
    )
    part = functools.reduce(jnp.add, scatter(out, depth, groups))
    parts = gather(part, depth, groups)
    (grad_q,) = call(
        functools.partial(join_query_kernel, groups), [joined], [scratch], flops // 16,
        place, *in_plane(q_sent),
    )
    parts, grad_q, saved = after(parts, grad_q, saved)
    rows = hidden // depth
    out = call(
        functools.partial(update_back_kernel, groups, depth, scale),
        [kept(len(members)) for members in packing(groups)] + slices, [square] * 2, 12 * flops,
        place, *early, *saved, *parts, *own, mib=24,
    )
    packed = len(packing(groups))
    back = in_plane(out[:packed])
    ends = scatter(out[packed:], depth, groups)
    if groups == 4:
        ends, back = after(ends, back)
        back += [move(back[1][2], "ctx", 2), move(back[2][2], "ctx", 1)]
    own_rows = rows // groups
    sent = call(
        functools.partial(rows_kernel, groups),
        [shape(1, 3, own_rows, width)] * groups,
        [pltpu.VMEM((3, rows, width), F32)], flops // 100, place, part, *ends,
    )
    grad_k, grad_v = call(
        functools.partial(join_update_kernel, groups), [joined] * 2, [scratch] * 2, flops // 8,
        place, rates[0], *back,
    )
    got, grad_k, grad_v = after(in_plane(sent), grad_k, grad_v)
    grads = call(
        functools.partial(join_rows_kernel, groups), [shape(heads, own_rows, width)] * 3, [],
        flops // 100, place, *got,
    )
    if lax.axis_size("batch") > 1:
        grads = [lax.psum_scatter(x, "batch", scatter_dimension=1, tiled=True) for x in grads]
    return (grad_q[None], grad_k[None], grad_v[None], grads[0], grads[1], grads[2])


def solution(mesh):
    in_specs = (
        P("batch", "ctx", "head", None),
        P("batch", "ctx", "head", None),
        P("batch", "ctx", "head", None),
        P("batch", "head", "ctx"),
        P("head"),
        P("head", None),
        P("head", None, None),
        P("head", None, None),
        P("head", None, None),
        P("batch", "ctx", "head", None),
    )
    out_specs = (
        P("batch", "ctx", "head", None),
        P("batch", "ctx", "head", None),
        P("batch", "ctx", "head", None),
        P("head", ("ctx", "batch"), None),
        P("head", ("ctx", "batch"), None),
        P("head", ("ctx", "batch"), None),
    )
    return jax.shard_map(local, mesh=mesh, in_specs=in_specs, out_specs=out_specs, check_vma=False)
```

```python
import functools
import math

import jax
import jax.numpy as jnp
from jax import lax
from jax.experimental import pallas as pl
from jax.experimental.pallas import tpu as pltpu
from jax.sharding import PartitionSpec as P

F32 = jnp.float32
BF16 = jnp.bfloat16
LANES = 128
MIB = 1024 * 1024


def mm(a, b):
    return jnp.dot(a, b, preferred_element_type=F32)


def mm_t(a, b):
    return lax.dot_general(a, b, (((1,), (1,)), ((), ())), preferred_element_type=F32)


def tmm(a, b):
    return lax.dot_general(a, b, (((0,), (0,)), ((), ())), preferred_element_type=F32)


def call(body, out_shape, scratch, flops, *args, mib=16):
    smem = pl.BlockSpec(memory_space=pltpu.SMEM)
    vmem = pl.BlockSpec(memory_space=pltpu.VMEM)
    size = sum(a.size * a.dtype.itemsize for a in args)
    size += sum(math.prod(o.shape) * o.dtype.itemsize for o in out_shape)
    return pl.pallas_call(
        body,
        out_shape=out_shape,
        in_specs=[smem if a.dtype == jnp.int32 else vmem for a in args],
        out_specs=[vmem] * len(out_shape),
        scratch_shapes=scratch,
        compiler_params=pltpu.CompilerParams(vmem_limit_bytes=mib * MIB),
        cost_estimate=pl.CostEstimate(flops=flops, bytes_accessed=size, transcendentals=0),
    )(*args)


def put_rows(scratch, x):
    for i in range(scratch.shape[0]):
        scratch[i, : x.shape[0], :] = x[:, i * LANES : (i + 1) * LANES]


def take_head(scratch, head, tokens, heads):
    parts = [scratch[i, pl.ds(head, tokens, stride=heads), :] for i in range(scratch.shape[0])]
    return jnp.concatenate(parts, axis=1)


def put_head(scratch, head, x, tokens, heads):
    for i in range(scratch.shape[0]):
        scratch[i, pl.ds(head, tokens, stride=heads), :] = x[:, i * LANES : (i + 1) * LANES]


def rows_of(scratch, rows):
    return jnp.concatenate([scratch[i, :rows, :] for i in range(scratch.shape[0])], axis=1)


def split_kernel(groups, place, x, *rest):
    outs, scratch = rest[:groups], rest[groups]
    tokens, heads, width = x.shape
    put_rows(scratch, x[...].astype(F32).reshape(tokens * heads, width))
    for step, out in enumerate(outs):
        out[...] = take_head(scratch, place[0] ^ step, tokens, heads).astype(out.dtype)


def split_scaled_kernel(groups, place, x, r, *rest):
    outs = rest[:groups]
    split_kernel(groups, place, x, *rest)
    for step in range(groups):
        scaled = outs[step][...].astype(F32) * rate_column(r, place[0] ^ step)
        outs[step][...] = scaled.astype(BF16).astype(outs[step].dtype)


def split_apply_kernel(groups, place, q, cot, gain, scale, *rest):
    outs, scale_row, scratch = rest[:groups], rest[groups], rest[groups + 1]
    scale_row[...] = jnp.broadcast_to(scale[...], scale_row.shape)
    split_kernel(groups, place, q, *[out.at[0] for out in outs], scratch)
    split_kernel(groups, place, cot, *[out.at[1] for out in outs], scratch)
    for step in range(groups):
        outs[step][1] *= gain[pl.ds(place[0] ^ step, 1), :]


def packing(groups):
    if groups == 4:
        return [[(0, 0), (0, 1)], [(1, 0), (1, 1), (3, 0)], [(2, 0), (2, 1), (3, 1)]]
    return [[(step, 0), (step, 1)] for step in range(groups)]


def unpacked(groups, refs):
    found = {}
    for ref, members in zip(refs, packing(groups)):
        for i, member in enumerate(members):
            found[member] = ref.at[i]
    for i, ref in enumerate(refs[len(packing(groups)) :]):
        found[(groups - 1, i)] = ref
    return [(found[(step, 0)], found[(step, 1)]) for step in range(groups)]


def rate_column(r, head):
    return jnp.broadcast_to(r[pl.ds(head, 1), :], (8, r.shape[1])).T[:, 0:1]


def send_groups(count):
    odd = list(range(3, count, 2))
    return ([odd] if odd else []) + [[r] for r in [1] + list(range(2, count, 2)) if r < count] + [[0]]


def send_slices(sums, outs, own, count):
    rows = sums.shape[1] // count
    for out, members in zip(outs, send_groups(count)):
        for i, step in enumerate(members):
            at = pl.multiple_of((own ^ step) * rows, rows)
            out[i] = sums[:, pl.ds(at, rows), :]


def update_sums(keys_in, scaled_in, weights, key_kept, scaled_kept):
    gate_b, out_b, up_b = (w[...].astype(BF16) for w in weights)
    total = [0.0, 0.0, 0.0]
    for step, (key, value) in enumerate(zip(keys_in, scaled_in)):
        keys = key[...].astype(BF16)
        scaled = value[...].astype(BF16)
        key_kept[step] = keys
        scaled_kept[step] = scaled
        first = mm(keys, gate_b)
        third = mm(keys, up_b)
        sig = jax.nn.sigmoid(first)
        activ = first * sig
        act = (activ * third).astype(BF16)
        dact = mm_t(scaled, out_b)
        deriv = sig * (1.0 + first * (1.0 - sig))
        dfirst = (dact * third * deriv).astype(BF16)
        dthird = (dact * activ).astype(BF16)
        total[0] += tmm(keys, dfirst)
        total[1] += tmm(act, scaled)
        total[2] += tmm(keys, dthird)
    return total


def update_kernel(count, depth, scale, place, *refs):
    keys_in, scaled_in, weights = refs[:count], refs[count : 2 * count], refs[2 * count :][:3]
    key_kept, scaled_kept = refs[2 * count + 3 : 2 * count + 5]
    outs, sums = refs[2 * count + 5 : -1], refs[-1]
    total = update_sums(keys_in, scaled_in, weights, key_kept, scaled_kept)
    for i in range(3):
        sums[i] = total[i] * scale
    send_slices(sums, outs, place[1], depth)
    rows = sums.shape[1] // depth
    at = pl.multiple_of(place[1] * rows, rows)
    for i, w in enumerate(weights):
        outs[-1][0, i] += w[pl.ds(at, rows), :]


def assemble(place, parts, whole):
    rows = parts[0].shape[2]
    for step, part in enumerate(parts):
        at = pl.multiple_of((place[1] ^ step) * rows, rows)
        whole[:, pl.ds(at, rows), :] = part[0]


def apply_kernel(groups, depth, place, scale_row, *refs):
    pieces = refs[:groups]
    parts = refs[groups : groups + depth]
    activ_ref, slope_ref, hidden_ref, os_ref, new_b, stats, whole = refs[groups + depth :]
    assemble(place, parts, whole)
    new_b[...] = whole[...].astype(BF16)
    for step in range(groups):
        queries = pieces[step][0].astype(BF16)
        tokens = queries.shape[0]
        first = mm(queries, new_b[0])
        third = mm(queries, new_b[2])
        sig = jax.nn.sigmoid(first)
        activ = first * sig
        hidden = (activ * third).astype(BF16)
        scaled = mm(hidden, new_b[1]) * scale_row[0:1, :]
        activ_ref[step] = activ
        slope_ref[step] = third * (sig * (1.0 + first * (1.0 - sig)))
        hidden_ref[step] = hidden
        os_ref[step] = scaled
        sq = jnp.sum(scaled * scaled, axis=1, keepdims=True)
        ps = jnp.sum(scaled * pieces[step][1], axis=1, keepdims=True)
        lane = lax.broadcasted_iota(jnp.int32, (tokens, LANES), 1)
        both = jnp.where(lane == 0, sq, jnp.where(lane == 1, ps, 0.0)).T
        source = place[0] ^ step
        stats[0, pl.ds(source, 1), :] = both[0:1, :]
        stats[1, pl.ds(source, 1), :] = both[1:2, :]


def apply_back_kernel(groups, depth, count, place, scale_row, stats, *refs):
    pieces, refs = refs[:groups], refs[groups:]
    activ_ref, slope_ref, hidden_ref, os_ref, new_b = refs[:5]
    dfirst_ref, dthird_ref, slices, sums = refs[5], refs[6], refs[7:-1], refs[-1]
    total = [0.0, 0.0, 0.0]
    for step in range(groups):
        queries = pieces[step][0].astype(BF16)
        source = place[0] ^ step
        sq = rate_column(stats.at[0], source)
        ps = rate_column(stats.at[1], source)
        inv = lax.rsqrt(sq / count + 1e-06)
        dos = inv * pieces[step][1] - os_ref[step] * (inv * inv * inv * ps / count)
        dout = (dos * scale_row[0:1, :]).astype(BF16)
        dhidden = mm_t(dout, new_b[1])
        dthird = (dhidden * activ_ref[step]).astype(BF16)
        dfirst = (dhidden * slope_ref[step]).astype(BF16)
        dfirst_ref[step] = dfirst
        dthird_ref[step] = dthird
        total[0] += tmm(queries, dfirst)
        total[1] += tmm(hidden_ref[step], dout)
        total[2] += tmm(queries, dthird)
    for i in range(3):
        sums[i] = total[i]
    send_slices(sums, slices, place[1], depth)


def query_back_kernel(dfirst, dthird, new_b, *outs):
    for step, out in enumerate(outs):
        out[...] = mm_t(dfirst[step], new_b[0]) + mm_t(dthird[step], new_b[2])


def update_keep_kernel(k_kept, s_kept, w_gate, w_out, w_up, *outs):
    dact_r, third_r, activ_r, deriv_r, slope_r, second_r, dfirst_r, dthird_r, act_r = outs
    gate_b, out_b, up_b = (w[...].astype(BF16) for w in (w_gate, w_out, w_up))
    for step in range(k_kept.shape[0]):
        keys, scaled = k_kept[step], s_kept[step]
        first = mm(keys, gate_b)
        third = mm(keys, up_b)
        dact = mm_t(scaled, out_b)
        sig = jax.nn.sigmoid(first)
        activ = first * sig
        slope = sig * (1.0 - sig)
        deriv = sig + first * slope
        third_deriv = third * deriv
        dact_r[step] = dact
        third_r[step] = third
        activ_r[step] = activ
        deriv_r[step] = deriv
        slope_r[step] = third_deriv
        second_r[step] = third * (slope * (2.0 + first * (1.0 - 2.0 * sig)))
        dfirst_r[step] = (dact * third_deriv).astype(BF16)
        dthird_r[step] = (dact * activ).astype(BF16)
        act_r[step] = (activ * third).astype(BF16)


def update_back_kernel(groups, depth, scale, place, *refs):
    (k_kept, s_kept), refs = refs[:2], refs[2:]
    kept, refs = refs[:9], refs[9:]
    dact_r, third_r, activ_r, deriv_r, slope_r, second_r, dfirst_r, dthird_r, act_r = kept
    parts, refs = refs[:depth], refs[depth:]
    w_gate, w_out, w_up = refs[:3]
    packed = len(packing(groups))
    outs, slices = unpacked(groups, refs[3 : packed + 3]), refs[packed + 3 : -2]
    whole, sums = refs[-2:]
    assemble(place, parts, whole)
    gate_b, out_b, up_b = (w[...].astype(BF16) for w in (w_gate, w_out, w_up))
    cot_gate, cot_out, cot_up = ((whole[i] * scale).astype(BF16) for i in range(3))
    total = [0.0, 0.0, 0.0]
    for step in range(groups):
        keys, scaled = k_kept[step], s_kept[step]
        bar_dfirst = mm(keys, cot_gate)
        bar_dthird = mm(keys, cot_up)
        bar_act = mm_t(scaled, cot_out)
        dact, activ, deriv = dact_r[step], activ_r[step], deriv_r[step]
        bar_activ = bar_dthird * dact + bar_act * third_r[step]
        bar_dact = (bar_dfirst * slope_r[step] + bar_dthird * activ).astype(BF16)
        bar_df_dact = bar_dfirst * dact
        bar_third = (bar_df_dact * deriv + bar_act * activ).astype(BF16)
        bar_first = (bar_activ * deriv + bar_df_dact * second_r[step]).astype(BF16)
        outs[step][0][...] = (
            mm_t(dfirst_r[step], cot_gate)
            + mm_t(dthird_r[step], cot_up)
            + mm_t(bar_first, gate_b)
            + mm_t(bar_third, up_b)
        )
        outs[step][1][...] = mm(act_r[step], cot_out) + mm(bar_dact, out_b)
        total[0] += tmm(keys, bar_first)
        total[1] += tmm(bar_dact, scaled)
        total[2] += tmm(keys, bar_third)
    for i in range(3):
        sums[i] = total[i]
    send_slices(sums, slices, place[1], depth)


def join_query_kernel(groups, place, *refs):
    pieces, out, scratch = refs[:groups], refs[groups], refs[groups + 1]
    tokens, heads, width = out.shape
    for step, piece in enumerate(pieces):
        put_head(scratch, place[0] ^ step, piece[...], tokens, heads)
    out[...] = rows_of(scratch, tokens * heads).reshape(tokens, heads, width).astype(BF16)


def join_update_kernel(groups, place, r, *refs):
    pieces, (out_k, out_v, sk, sv) = unpacked(groups, refs[:-4]), refs[-4:]
    tokens, heads, width = out_k.shape
    for step, piece in enumerate(pieces):
        head = place[0] ^ step
        put_head(sk, head, piece[0][...], tokens, heads)
        put_head(sv, head, piece[1][...] * rate_column(r, head), tokens, heads)
    out_k[...] = rows_of(sk, tokens * heads).reshape(tokens, heads, width).astype(BF16)
    out_v[...] = rows_of(sv, tokens * heads).reshape(tokens, heads, width).astype(BF16)


def join_rows_kernel(groups, place, *refs):
    parts, grads = refs[:groups], refs[groups:]
    for step, part in enumerate(parts):
        for i, grad in enumerate(grads):
            grad[place[0] ^ step] = part[0, i]


def rows_kernel(groups, place, *refs):
    parts, outs, total = refs[: -groups - 1], refs[-groups - 1 : -1], refs[-1]
    summed = parts[0][0]
    for part in parts[1:]:
        summed += part[0]
    total[...] = summed
    rows = total.shape[1] // groups
    for step, out in enumerate(outs):
        at = pl.multiple_of((place[0] ^ step) * rows, rows)
        out[0] = total[:, pl.ds(at, rows), :]


def local(queries, keys, values, rates, head_scale, gain, w_gate, w_out, w_up, cotangent):
    tokens, heads, width = keys.shape[1:]
    hidden = w_gate.shape[2]
    ctx = lax.axis_size("ctx")
    head_axis = lax.axis_size("head")
    groups = heads
    depth = ctx // groups
    assert groups & (groups - 1) == 0 and depth & (depth - 1) == 0
    scale = 1.0 / math.sqrt(tokens * ctx * width)
    count = float(heads * head_axis * width)
    me = lax.axis_index("ctx")
    mine, layer = lax.rem(me, groups), lax.div(me, groups)
    place = jnp.stack([mine, layer]).astype(jnp.int32)

    def move(x, axis, step):
        return lax.ppermute(x, axis, [(c, c ^ step) for c in range(lax.axis_size(axis))])

    def in_plane(parts):
        return [parts[0]] + [move(p, "ctx", step) for step, p in enumerate(parts) if step]

    def forwarded(got):
        return [got[:1]] if got.shape[0] == 1 else [got[i : i + 1] for i in range(got.shape[0])]

    def scatter(outs, count, unit):
        outs = list(outs)
        evens = list(range(2, count, 2))
        via = forwarded(move(outs.pop(0), "ctx", unit)) if evens else []
        via, outs[0] = after(via, outs[0])
        first = [move(outs[0], "ctx", unit)] if count > 1 else []
        even = [move(p + v, "ctx", r * unit) for p, v, r in zip(outs[1:], via, evens)]
        return [outs[-1]] + first + even

    def gather(part, count, unit):
        got = [part] * count
        for r in [2 * i for i in range(1, count // 2)]:
            got[r] = move(part, "ctx", r * unit)
            got[r + 1] = move(got[r], "ctx", unit)
        if count > 1:
            got[1] = move(part, "ctx", unit)
        return got

    def after(x, *others):
        return lax.optimization_barrier((x, *others))

    def shape(*dims, dtype=F32):
        return jax.ShapeDtypeStruct(dims, dtype)

    flops = 2 * groups * tokens * width * hidden
    pieces = [shape(tokens, width)] * groups
    slices = [shape(len(m), 3, hidden // depth, width) for m in send_groups(depth)]
    joined = shape(tokens, heads, width, dtype=BF16)
    scratch = pltpu.VMEM((width // LANES, tokens * heads + 8 * heads, LANES), F32)
    square = pltpu.VMEM((3, hidden, width), F32)

    def split(body, *args):
        outs = [shape(tokens, width, dtype=BF16)] + pieces[1:]
        body = functools.partial(body, groups)
        return call(body, outs, [scratch], 16 * flops, place, *args, mib=8)

    k_in = in_plane(split(split_kernel, keys[0]))
    s_in = in_plane(split(split_scaled_kernel, values[0], rates[0]))
    own = [lax.dynamic_index_in_dim(w, mine, 0, keepdims=False) for w in (w_gate, w_out, w_up)]
    own_scale = lax.dynamic_index_in_dim(head_scale, mine, 0, keepdims=True)[None, :]
    k_in, s_in, queries, cotangent = after(k_in, s_in, queries, cotangent)

    def kept(*dims, dtype=F32):
        return shape(*dims, tokens, width, dtype=dtype)

    out = call(
        functools.partial(update_kernel, groups, depth, scale),
        [kept(groups, dtype=BF16)] * 2 + slices, [square], 6 * flops,
        place, *k_in, *s_in, *own,
    )
    early, terms = out[:2], out[2:]
    *q_out, scale_row = call(
        functools.partial(split_apply_kernel, groups),
        [shape(2, tokens, width)] * groups + [shape(8, width)],
        [scratch], flops // 8, place, queries[0], cotangent[0], gain, own_scale,
    )
    q_in = in_plane(q_out[:-1])
    new = functools.reduce(jnp.add, scatter(terms, depth, groups))
    new, q_in, q_last = after(new, q_in, q_out[-1])
    q_in.append(move(q_last, "ctx", groups - 1))
    new = gather(new, depth, groups)
    *passed, stats = call(
        functools.partial(apply_kernel, groups, depth),
        [kept(groups), kept(groups), kept(groups, dtype=BF16), kept(groups)]
        + [shape(3, hidden, width, dtype=BF16), shape(2, groups, tokens)],
        [square], 3 * flops, place, scale_row, *q_in, *new,
    )
    for axis, size in (("head", lax.axis_size("head")), ("ctx", groups)):
        bit = 1
        while bit < size:
            stats = stats + move(stats, axis, bit)
            bit *= 2
    out = call(
        functools.partial(apply_back_kernel, groups, depth, count),
        [kept(groups, dtype=BF16)] * 2 + slices, [square], 6 * flops,
        place, scale_row, stats, *q_in, *passed,
    )
    q_sent = call(
        query_back_kernel, [shape(tokens, width)] * groups, [], 2 * flops, *out[:2], passed[-1]
    )
    out = out[2:]
    out, early = after(out, early)
    saved = call(
        update_keep_kernel, [kept(groups)] * 6 + [kept(groups, dtype=BF16)] * 3, [], 3 * flops,
        *early, *own,
    )
    part = functools.reduce(jnp.add, scatter(out, depth, groups))
    parts = gather(part, depth, groups)
    (grad_q,) = call(
        functools.partial(join_query_kernel, groups), [joined], [scratch], flops // 16,
        place, *in_plane(q_sent),
    )
    parts, grad_q, saved = after(parts, grad_q, saved)
    rows = hidden // depth
    out = call(
        functools.partial(update_back_kernel, groups, depth, scale),
        [kept(len(members)) for members in packing(groups)] + slices, [square] * 2, 12 * flops,
        place, *early, *saved, *parts, *own, mib=24,
    )
    packed = len(packing(groups))
    back = in_plane(out[:packed])
    ends = scatter(out[packed:], depth, groups)
    if groups == 4:
        ends, back = after(ends, back)
        back += [move(back[1][2], "ctx", 2), move(back[2][2], "ctx", 1)]
    own_rows = rows // groups
    sent = call(
        functools.partial(rows_kernel, groups),
        [shape(1, 3, own_rows, width)] * groups,
        [pltpu.VMEM((3, rows, width), F32)], flops // 100, place, part, *ends,
    )
    grad_k, grad_v = call(
        functools.partial(join_update_kernel, groups), [joined] * 2, [scratch] * 2, flops // 8,
        place, rates[0], *back,
    )
    got, grad_k, grad_v = after(in_plane(sent), grad_k, grad_v)
    grads = call(
        functools.partial(join_rows_kernel, groups), [shape(heads, own_rows, width)] * 3, [],
        flops // 100, place, *got,
    )
    if lax.axis_size("batch") > 1:
        grads = [lax.psum_scatter(x, "batch", scatter_dimension=1, tiled=True) for x in grads]
    return (grad_q[None], grad_k[None], grad_v[None], grads[0], grads[1], grads[2])


def solution(mesh):
    in_specs = (
        P("batch", "ctx", "head", None),
        P("batch", "ctx", "head", None),
        P("batch", "ctx", "head", None),
        P("batch", "head", "ctx"),
        P("head"),
        P("head", None),
        P("head", None, None),
        P("head", None, None),
        P("head", None, None),
        P("batch", "ctx", "head", None),
    )
    out_specs = (
        P("batch", "ctx", "head", None),
        P("batch", "ctx", "head", None),
        P("batch", "ctx", "head", None),
        P("head", ("ctx", "batch"), None),
        P("head", ("ctx", "batch"), None),
        P("head", ("ctx", "batch"), None),
    )
    return jax.shard_map(local, mesh=mesh, in_specs=in_specs, out_specs=out_specs, check_vma=False)
```
